32 devices in a mesh: pair: 8 (over y, x, core), slab: 4 (over z).
Axes of the slice: x: 2, y: 2, z: 4, core: 2. Of those that a mesh axis runs over, the one named last changes fastest.
Arguments:
- amplitudes: bfloat16 [8, 8, 160000], P('pair'), may hold values from -6 to 6
- integrals: bfloat16 [160000, 1024], P('pair', 'slab'), may hold values from -0.0390625 to 0.0390625
- virt_irrep: int32 [400], replicated, may hold values from 0 to 7
- occ_energy: float32 [8], replicated, may hold values from -1.2 to -0.3
- slab_energy: float32 [32], replicated, may hold values from 0.1 to 1.5
Outputs:
- update: float32 [8, 8, 32, 32], P('pair', None, 'slab')
The draws below stay inside these ranges and needn't reach their ends.
All inputs are finite; a program needn't handle non-finite values.
Results may differ from the reference program's by a relative error of at most 0.0003.
Values may be sent and summed in bfloat16 or wider, within the bound.
No kernel may reach another device: no remote copies, remote signals or barrier semaphores. Data moves between devices by JAX's collectives and lax.ppermute only.
A program may use at most 256 MiB of HBM per device.

```python
import jax
import jax.numpy as jnp
from jax import lax

V = 400
VS = 32
OCC = 8


def plant(values, key, least, high):
    dims = values.shape
    index_at = [jax.random.randint(jax.random.fold_in(key, axis), (), 0, dims[axis]) for axis in range(len(dims))]
    values = values.at[tuple(index_at)].set(least)
    longest = dims.index(max(dims))
    index_at[longest] = (index_at[longest] + 1) % dims[longest]
    return values.at[tuple(index_at)].set(high)


def level_of(key, dims, pieces, low, high):
    factor_of = 1.0
    for dim, parts in pieces:
        draws = jax.random.uniform(jax.random.fold_in(jax.random.fold_in(key, 6), dim), (parts,), jnp.float32, low / len(pieces), high / len(pieces))
        factor_of = factor_of * jnp.repeat(jnp.exp(draws), dims[dim] // parts).reshape((-1,) + (1,) * (len(dims) - 1 - dim))
    return factor_of


def centred(rng, shape, width, limit, pieces=(), kind=jnp.bfloat16):
    entries = width * jax.random.normal(rng, shape, jnp.float32)
    if pieces:
        entries = entries * level_of(rng, shape, pieces, -0.22, 0.18)
    return jnp.clip(entries, -limit, limit).astype(kind)


def setup_inputs(seed: int = 0) -> dict:
    seeds = jax.random.split(jax.random.key(seed), 6)
    amplitudes = centred(seeds[0], (OCC, OCC, V * V), 1.0, 6.0, ((0, 8),))
    integrals = centred(seeds[1], (V * V, VS * VS), (V * V // 8) ** -0.5, 0.0390625, ((0, 8), (1, 4)))
    virt_irrep = plant(jax.random.randint(seeds[2], (V,), 0, 8), jax.random.fold_in(seeds[2], 1), 0, 7).astype(jnp.int32)
    occ_energy = jnp.clip(jax.random.uniform(seeds[3], (OCC,), jnp.float32, -1.2, -0.3), -1.2, -0.3)
    slab_energy = jnp.clip(jax.random.uniform(seeds[4], (VS,), jnp.float32, 0.1, 1.5), 0.1, 1.5)
    return {"amplitudes": amplitudes, "integrals": integrals, "virt_irrep": virt_irrep, "occ_energy": occ_energy, "slab_energy": slab_energy}


def reference(amplitudes, integrals, virt_irrep, occ_energy, slab_energy):
    pair_total = OCC * OCC
    flat_amps = amplitudes.reshape(pair_total, V * V)
    irrep_cd = jnp.bitwise_xor(virt_irrep[:, None], virt_irrep[None, :]).reshape(V * V)
    slab_irrep = virt_irrep[:VS]
    irrep_ab = jnp.bitwise_xor(slab_irrep[:, None], slab_irrep[None, :]).reshape(VS * VS)
    block_rows = 16 * V

    def accumulate(carry, block_index):
        offset = (block_index * block_rows).astype(jnp.int32)
        amps_block = lax.dynamic_slice_in_dim(flat_amps, offset, block_rows, 1).astype(jnp.float32)
        ints_block = lax.dynamic_slice_in_dim(integrals, offset, block_rows, 0).astype(jnp.float32)
        rows_irrep = lax.dynamic_slice_in_dim(irrep_cd, offset, block_rows, 0)
        allowed = rows_irrep[:, None] == irrep_ab[None, :]
        ints_block = jnp.where(allowed, ints_block, jnp.zeros_like(ints_block))
        return carry + jnp.dot(amps_block, ints_block, preferred_element_type=jnp.float32), None

    ladder, _ = lax.scan(accumulate, jnp.zeros((pair_total, VS * VS), jnp.float32),
                         jnp.arange(V * V // block_rows, dtype=jnp.int32))
    residual = ladder.reshape(OCC, OCC, VS, VS)
    symmetric = residual + jnp.transpose(residual, (1, 0, 3, 2))
    denominator = (slab_energy[None, None, :, None] + slab_energy[None, None, None, :]
                   - occ_energy[:, None, None, None] - occ_energy[None, :, None, None])
    return symmetric / denominator
```

```python
import functools
import math

import jax
import jax.numpy as jnp
from jax import lax
from jax.experimental import pallas as pl
from jax.experimental.pallas import tpu as pltpu
from jax.sharding import PartitionSpec as P

IRREPS = 8
VMEM_BYTES = 56 * 2**20


def pack_kernel(rows_local, amps_ref, out_ref):
    for dest in range(out_ref.shape[0]):
        out_ref[dest] = amps_ref[:, dest * rows_local : (dest + 1) * rows_local]


def pack(amps, pair_count):
    rows, virt_pairs = amps.shape
    rows_local = virt_pairs // pair_count
    return pl.pallas_call(
        functools.partial(pack_kernel, rows_local),
        out_shape=jax.ShapeDtypeStruct((pair_count, rows, rows_local), amps.dtype),
        in_specs=[pl.BlockSpec(memory_space=pltpu.VMEM)],
        out_specs=pl.BlockSpec(memory_space=pltpu.VMEM),
        compiler_params=pltpu.CompilerParams(vmem_limit_bytes=VMEM_BYTES),
        cost_estimate=pl.CostEstimate(flops=0, bytes_accessed=4 * rows * virt_pairs, transcendentals=0),
        name="pack_amplitudes",
    )(amps)


def mask_kernel(per_step, parts, first_ref, irrep_ref, irrep_d_ref, irrep_ab_ref, ints_ref, out_ref, table):
    step = pl.program_id(0)

    @pl.when(step == 0)
    def _():
        for part in range(parts):
            needed = irrep_d_ref[part] ^ irrep_ab_ref[...]
            for irrep in range(IRREPS):
                table[irrep * parts + part] = jnp.where(needed == irrep, 1.0, 0.0).astype(table.dtype)

    for k in range(per_step):
        index = first_ref[0] + step * per_step + k
        irrep_c = irrep_ref[index // parts]
        out_ref[k] = ints_ref[k] * table[irrep_c * parts + index % parts]


def mask(integrals, virt_irrep, irrep_ab, first_row):
    virtuals = virt_irrep.shape[0]
    rows_local, cols_local = integrals.shape
    chunk = math.gcd(virtuals, rows_local)
    parts = virtuals // chunk
    chunks = rows_local // chunk
    per_step = next(n for n in (10, 5, 4, 2, 1) if chunks % n == 0)
    block = pl.BlockSpec((per_step, chunk, cols_local), lambda step, *_: (step, 0, 0))
    masked = pl.pallas_call(
        functools.partial(mask_kernel, per_step, parts),
        grid_spec=pltpu.PrefetchScalarGridSpec(
            num_scalar_prefetch=2,
            grid=(chunks // per_step,),
            in_specs=[
                pl.BlockSpec((parts, chunk, 1), lambda step, *_: (0, 0, 0)),
                pl.BlockSpec((1, cols_local), lambda step, *_: (0, 0)),
                block,
            ],
            out_specs=block,
            scratch_shapes=[pltpu.VMEM((IRREPS * parts, chunk, cols_local), integrals.dtype)],
        ),
        out_shape=jax.ShapeDtypeStruct((chunks, chunk, cols_local), integrals.dtype),
        compiler_params=pltpu.CompilerParams(vmem_limit_bytes=VMEM_BYTES),
        cost_estimate=pl.CostEstimate(
            flops=rows_local * cols_local, bytes_accessed=4 * rows_local * cols_local, transcendentals=0
        ),
        name="mask_integrals",
    )(
        (first_row // chunk).astype(jnp.int32).reshape(1),
        virt_irrep,
        virt_irrep.reshape(parts, chunk, 1),
        irrep_ab.reshape(1, cols_local),
        integrals.reshape(chunks, chunk, cols_local),
    )
    return masked.reshape(rows_local, cols_local)


def dot_kernel(bounds, amps_ref, ints_ref, out_ref, buffer, sems):
    copies = [
        pltpu.make_async_copy(
            ints_ref.at[pl.ds(start, stop - start)], buffer.at[pl.ds(start, stop - start)], sems.at[k]
        )
        for k, (start, stop) in enumerate(bounds)
    ]
    for copy in copies:
        copy.start()
    total = None
    for copy, (start, stop) in zip(copies, bounds):
        copy.wait()
        part = jnp.dot(amps_ref[:, start:stop], buffer[start:stop], preferred_element_type=jnp.float32)
        total = part if total is None else total + part
    out_ref[...] = total


def contract(amps, ints):
    count, rows = amps.shape
    cols = ints.shape[1]
    size = 2560
    bounds = [(start, min(start + size, rows)) for start in range(0, rows, size)]
    return pl.pallas_call(
        functools.partial(dot_kernel, bounds),
        out_shape=jax.ShapeDtypeStruct((count, cols), jnp.float32),
        in_specs=[pl.BlockSpec(memory_space=pltpu.VMEM), pl.BlockSpec(memory_space=pl.ANY)],
        out_specs=pl.BlockSpec(memory_space=pltpu.VMEM),
        scratch_shapes=[pltpu.VMEM((rows, cols), ints.dtype), pltpu.SemaphoreType.DMA((len(bounds),))],
        compiler_params=pltpu.CompilerParams(vmem_limit_bytes=VMEM_BYTES),
        cost_estimate=pl.CostEstimate(
            flops=2 * count * rows * cols, bytes_accessed=2 * rows * (cols + count), transcendentals=0
        ),
        name="contract",
    )(amps, ints)


def local(amplitudes, integrals, virt_irrep, occ_energy, slab_energy):
    pair_count = lax.axis_size("pair")
    slab_count = lax.axis_size("slab")
    pair_index = lax.axis_index("pair")
    slab_index = lax.axis_index("slab")
    occ_local, occupied, virt_pairs = amplitudes.shape
    rows_local, cols_local = integrals.shape
    slab_virt = slab_energy.shape[0]
    first_local = slab_virt // slab_count

    slab_irrep = virt_irrep[:slab_virt]
    own_irrep = lax.dynamic_slice_in_dim(slab_irrep, slab_index * first_local, first_local, 0)
    irrep_ab = jnp.bitwise_xor(own_irrep[:, None], slab_irrep[None, :]).reshape(-1)

    packed = pack(amplitudes.reshape(occ_local * occupied, virt_pairs), pair_count)
    received = lax.all_to_all(packed, "pair", split_axis=0, concat_axis=0, tiled=True)
    masked = mask(integrals, virt_irrep, irrep_ab, pair_index * rows_local)
    product = contract(received.reshape(pair_count * occ_local * occupied, rows_local), masked)

    direct = product.reshape(pair_count, occ_local * occupied, cols_local)
    direct = lax.all_to_all(direct, "pair", split_axis=0, concat_axis=0, tiled=True)
    mirror = product.reshape(occupied, pair_count, occ_local, first_local, slab_count, first_local)
    mirror = mirror.transpose(1, 4, 2, 0, 3, 5)
    mirror = mirror.reshape(pair_count * slab_count, occ_local * occupied, first_local * first_local)
    mirror = lax.all_to_all(mirror, ("pair", "slab"), split_axis=0, concat_axis=0, tiled=True)

    ladder = jnp.sum(direct, axis=0).reshape(occ_local, occupied, first_local, slab_virt)
    mirror = jnp.sum(mirror.reshape(pair_count, slab_count, -1), axis=0)
    mirror = mirror.reshape(slab_count, occ_local, occupied, first_local, first_local)
    mirror = mirror.transpose(1, 2, 4, 0, 3).reshape(occ_local, occupied, first_local, slab_virt)

    energy_i = lax.dynamic_slice_in_dim(occ_energy, pair_index * occ_local, occ_local, 0)
    energy_a = lax.dynamic_slice_in_dim(slab_energy, slab_index * first_local, first_local, 0)
    denominator = (
        energy_a[None, None, :, None]
        + slab_energy[None, None, None, :]
        - energy_i[:, None, None, None]
        - occ_energy[None, :, None, None]
    )
    return (ladder + mirror) / denominator


def solution(mesh):
    placed = (P("pair", None, None), P("pair", "slab"), P(), P(), P())
    return jax.shard_map(
        local, mesh=mesh, in_specs=placed, out_specs=P("pair", None, "slab", None), check_vma=False
    )
```

```python
import functools
import math

import jax
import jax.numpy as jnp
from jax import lax
from jax.experimental import pallas as pl
from jax.experimental.pallas import tpu as pltpu
from jax.sharding import PartitionSpec as P

IRREPS = 8
MIB = 2**20


def pack_kernel(rows_local, me_ref, amps_ref, *refs):
    count = amps_ref.shape[1] // rows_local
    outs, (held, packed, in_sems, out_sems) = refs[:count], refs[count:]
    bounds = [-(-dest * rows_local // 128) * 128 for dest in range(count + 1)]
    loads = []
    for dest in range(count):
        window = pl.ds(bounds[dest], bounds[dest + 1] - bounds[dest])
        loads.append(pltpu.make_async_copy(amps_ref.at[:, window], held.at[:, window], in_sems.at[dest]))
        loads[-1].start()
    for dest in range(count):
        loads[dest].wait()
        packed[me_ref[0] ^ dest] = held[:, dest * rows_local : (dest + 1) * rows_local]
    stores = [pltpu.make_async_copy(packed.at[k], outs[k], out_sems.at[k]) for k in range(count)]
    for store in stores:
        store.start()
    for store in stores:
        store.wait()


def pack(amps, me, pair_count):
    rows, virt_pairs = amps.shape
    rows_local = virt_pairs // pair_count
    part = jax.ShapeDtypeStruct((rows, rows_local), amps.dtype)
    return pl.pallas_call(
        functools.partial(pack_kernel, rows_local),
        out_shape=[part] * pair_count,
        in_specs=[pl.BlockSpec(memory_space=pltpu.SMEM), pl.BlockSpec(memory_space=pl.ANY)],
        out_specs=[pl.BlockSpec(memory_space=pl.ANY)] * pair_count,
        scratch_shapes=[
            pltpu.VMEM((rows, virt_pairs), amps.dtype),
            pltpu.VMEM((pair_count, rows, rows_local), amps.dtype),
            pltpu.SemaphoreType.DMA((pair_count,)),
            pltpu.SemaphoreType.DMA((pair_count,)),
        ],
        compiler_params=pltpu.CompilerParams(vmem_limit_bytes=32 * MIB),
        cost_estimate=pl.CostEstimate(flops=0, bytes_accessed=4 * rows * virt_pairs, transcendentals=0),
        name="pack_amplitudes",
    )(me, amps)


def mask_kernel(per_step, parts, first_ref, irrep_ref, irrep_d_ref, irrep_ab_ref, ints_ref, out_ref, table):
    step = pl.program_id(0)

    @pl.when(step == 0)
    def _():
        for part in range(parts):
            needed = irrep_d_ref[part] ^ irrep_ab_ref[...]
            for irrep in range(IRREPS):
                table[irrep * parts + part] = jnp.where(needed == irrep, 1.0, 0.0).astype(table.dtype)

    for k in range(per_step):
        index = first_ref[0] + step * per_step + k
        irrep_c = irrep_ref[index // parts]
        out_ref[k] = ints_ref[k] * table[irrep_c * parts + index % parts]


def mask(integrals, virt_irrep, irrep_ab, first_row):
    virtuals = virt_irrep.shape[0]
    rows_local, cols_local = integrals.shape
    chunk = math.gcd(virtuals, rows_local)
    parts = virtuals // chunk
    chunks = rows_local // chunk
    per_step = next(n for n in (10, 5, 4, 2, 1) if chunks % n == 0)
    block = pl.BlockSpec((per_step, chunk, cols_local), lambda step, *_: (step, 0, 0))
    masked = pl.pallas_call(
        functools.partial(mask_kernel, per_step, parts),
        grid_spec=pltpu.PrefetchScalarGridSpec(
            num_scalar_prefetch=2,
            grid=(chunks // per_step,),
            in_specs=[
                pl.BlockSpec((parts, chunk, 1), lambda step, *_: (0, 0, 0)),
                pl.BlockSpec((1, cols_local), lambda step, *_: (0, 0)),
                block,
            ],
            out_specs=block,
            scratch_shapes=[pltpu.VMEM((IRREPS * parts, chunk, cols_local), integrals.dtype)],
        ),
        out_shape=jax.ShapeDtypeStruct((chunks, chunk, cols_local), integrals.dtype),
        compiler_params=pltpu.CompilerParams(vmem_limit_bytes=20 * MIB),
        cost_estimate=pl.CostEstimate(
            flops=rows_local * cols_local, bytes_accessed=4 * rows_local * cols_local, transcendentals=0
        ),
        name="mask_integrals",
    )(
        (first_row // chunk).astype(jnp.int32).reshape(1),
        virt_irrep,
        virt_irrep.reshape(parts, chunk, 1),
        irrep_ab.reshape(1, cols_local),
        integrals.reshape(chunks, chunk, cols_local),
    )
    return masked.reshape(rows_local, cols_local)


def contract_kernel(bounds, pair_count, me_ref, *refs):
    amps, ints_ref, outs = refs[:pair_count], refs[pair_count], refs[pair_count + 1 : 2 * pair_count + 1]
    buffer, partial, sems = refs[2 * pair_count + 1 :]
    copies = [
        pltpu.make_async_copy(
            ints_ref.at[pl.ds(start, stop - start)], buffer.at[pl.ds(start, stop - start)], sems.at[k]
        )
        for k, (start, stop) in enumerate(bounds)
    ]
    for copy in copies:
        copy.start()
    total = None
    for copy, (start, stop) in zip(copies, bounds):
        copy.wait()
        rows = jnp.concatenate([ref[:, start:stop] for ref in amps], axis=0)
        part = jnp.dot(rows, buffer[start:stop], preferred_element_type=jnp.float32)
        total = part if total is None else total + part
    partial[...] = total.reshape(partial.shape)
    me = me_ref[0]
    for k in range(pair_count):
        outs[k][:pair_count] = partial[k]
        for i in range(pair_count):
            outs[k][pair_count + i : pair_count + i + 1] = partial[me ^ i, pl.ds(me ^ k, 1)]


def contract(amps, ints, me):
    pair_count = len(amps)
    occupied, rows = amps[0].shape
    cols = ints.shape[1]
    size = 2560
    bounds = [(start, min(start + size, rows)) for start in range(0, rows, size)]
    part = jax.ShapeDtypeStruct((2 * pair_count, cols), jnp.float32)
    vmem = pl.BlockSpec(memory_space=pltpu.VMEM)
    return pl.pallas_call(
        functools.partial(contract_kernel, bounds, pair_count),
        out_shape=[part] * pair_count,
        in_specs=[pl.BlockSpec(memory_space=pltpu.SMEM)] + [vmem] * pair_count + [pl.BlockSpec(memory_space=pl.ANY)],
        out_specs=[vmem] * pair_count,
        scratch_shapes=[
            pltpu.VMEM((rows, cols), ints.dtype),
            pltpu.VMEM((pair_count, occupied, cols), jnp.float32),
            pltpu.SemaphoreType.DMA((len(bounds),)),
        ],
        compiler_params=pltpu.CompilerParams(vmem_limit_bytes=36 * MIB),
        cost_estimate=pl.CostEstimate(
            flops=2 * pair_count * occupied * rows * cols,
            bytes_accessed=2 * rows * (cols + pair_count * occupied),
            transcendentals=0,
        ),
        name="contract",
    )(me, *amps, ints)


def add_kernel(*refs):
    parts, (ladder_ref, mirror_ref) = refs[:-2], refs[-2:]
    total = parts[0][...]
    for part in parts[1:]:
        total = total + part[...]
    half = total.shape[0] // 2
    ladder_ref[...] = total[:half]
    mirror_ref[...] = total[half:]


def add_parts(parts):
    rows, cols = parts[0].shape
    half = jax.ShapeDtypeStruct((rows // 2, cols), jnp.float32)
    vmem = pl.BlockSpec(memory_space=pltpu.VMEM)
    return pl.pallas_call(
        add_kernel,
        out_shape=[half, half],
        in_specs=[vmem] * len(parts),
        out_specs=[vmem, vmem],
        cost_estimate=pl.CostEstimate(
            flops=len(parts) * rows * cols, bytes_accessed=4 * len(parts) * rows * cols, transcendentals=0
        ),
        name="add_parts",
    )(*parts)


def finish_kernel(first_local, ladder_ref, denominator_ref, select_ref, *refs):
    mirrors, out_ref = refs[:-1], refs[-1]
    rows = ladder_ref.shape[0]
    total = jnp.concatenate([mirror[...] for mirror in mirrors], axis=1)
    high = total.astype(jnp.bfloat16)
    rest = total - high.astype(jnp.float32)
    middle = rest.astype(jnp.bfloat16)
    low = (rest - middle.astype(jnp.float32)).astype(jnp.bfloat16)
    terms = [jnp.dot(term, select_ref[...], preferred_element_type=jnp.float32) for term in (high, middle, low)]
    update = (ladder_ref[...] + (terms[0] + terms[1] + terms[2])) / denominator_ref[...]
    width = out_ref.shape[2]
    for a in range(first_local):
        out_ref[:, a, :] = update[:, a * width : (a + 1) * width]


def finish(ladder, mirrors, denominator, select, first_local, slab_virt):
    rows = ladder.shape[0]
    return pl.pallas_call(
        functools.partial(finish_kernel, first_local),
        out_shape=jax.ShapeDtypeStruct((rows, first_local, slab_virt), jnp.float32),
        in_specs=[pl.BlockSpec(memory_space=pltpu.VMEM)] * (3 + len(mirrors)),
        out_specs=pl.BlockSpec(memory_space=pltpu.VMEM),
        compiler_params=pltpu.CompilerParams(vmem_limit_bytes=16 * MIB),
        cost_estimate=pl.CostEstimate(
            flops=6 * rows * select.size, bytes_accessed=2 * select.size, transcendentals=0
        ),
        name="finish",
    )(ladder, denominator, select, *mirrors)


def exchange(parts, axis, me_count):
    received = [parts[0]]
    for k in range(1, me_count):
        received.append(lax.ppermute(parts[k], axis, [(p, p ^ k) for p in range(me_count)]))
    return received


def local(amplitudes, integrals, virt_irrep, occ_energy, slab_energy):
    pair_count = lax.axis_size("pair")
    slab_count = lax.axis_size("slab")
    pair_index = lax.axis_index("pair")
    slab_index = lax.axis_index("slab")
    occ_local, occupied, virt_pairs = amplitudes.shape
    rows_local, cols_local = integrals.shape
    slab_virt = slab_energy.shape[0]
    first_local = slab_virt // slab_count
    assert occ_local == 1
    me = pair_index.astype(jnp.int32).reshape(1)

    slab_irrep = virt_irrep[:slab_virt]
    own_irrep = lax.dynamic_slice_in_dim(slab_irrep, slab_index * first_local, first_local, 0)
    irrep_ab = jnp.bitwise_xor(own_irrep[:, None], slab_irrep[None, :]).reshape(-1)

    energy_i = lax.dynamic_slice_in_dim(occ_energy, pair_index, 1, 0)
    energy_a = lax.dynamic_slice_in_dim(slab_energy, slab_index * first_local, first_local, 0)
    energy_ab = (energy_a[:, None] + slab_energy[None, :]).reshape(1, cols_local)
    denominator = energy_ab - energy_i - occ_energy[:, None]

    shape = (slab_count * cols_local, cols_local)
    row, col = (lax.broadcasted_iota(jnp.int32, shape, axis) for axis in (0, 1))
    source = jnp.bitwise_xor(row // cols_local, slab_index.astype(jnp.int32))
    row = row % cols_local
    same_a = row % slab_virt == slab_index * first_local + col // slab_virt
    same_b = source * first_local + row // slab_virt == col % slab_virt
    select = jnp.where(same_a & same_b, 1.0, 0.0).astype(jnp.bfloat16)

    amps = exchange(pack(amplitudes.reshape(occupied, virt_pairs), me, pair_count), "pair", pair_count)
    masked = mask(integrals, virt_irrep, irrep_ab, pair_index * rows_local)
    parts = exchange(contract(amps, masked, me), "pair", pair_count)
    ladder, mirror = add_parts(parts)
    mirrors = exchange([mirror] * slab_count, "slab", slab_count)
    update = finish(ladder, mirrors, denominator, select, first_local, slab_virt)
    return update.reshape(occ_local, occupied, first_local, slab_virt)


def solution(mesh):
    placed = (P("pair", None, None), P("pair", "slab"), P(), P(), P())
    return jax.shard_map(
        local, mesh=mesh, in_specs=placed, out_specs=P("pair", None, "slab", None), check_vma=False
    )
```

```python
import functools
import math

import jax
import jax.numpy as jnp
import numpy as np
from jax import lax
from jax.experimental import pallas as pl
from jax.experimental.pallas import tpu as pltpu
from jax.sharding import PartitionSpec as P

IRREPS = 8
MIB = 2**20
SHARE = 0.24


def pack_kernel(rows_local, start_ref, amps_ref, out_ref, held, sems):
    count, _, size = out_ref.shape
    start = pl.multiple_of(start_ref[0], 128)
    loads, shifts = [], []
    for dest in range(count):
        first = dest * rows_local // 128 * 128
        shifts.append(dest * rows_local - first)
        width = -(-(shifts[dest] + size) // 128) * 128
        loads.append(
            pltpu.make_async_copy(
                amps_ref.at[:, pl.ds(start + first, width)], held.at[dest, :, pl.ds(0, width)], sems.at[dest]
            )
        )
        loads[-1].start()
    for dest in range(count):
        loads[dest].wait()
        out_ref[dest] = held[dest, :, shifts[dest] : shifts[dest] + size]


def pack(amps, start, size, pair_count, vmem):
    rows, virt_pairs = amps.shape
    return pl.pallas_call(
        functools.partial(pack_kernel, virt_pairs // pair_count),
        out_shape=jax.ShapeDtypeStruct((pair_count, rows, size), amps.dtype),
        in_specs=[pl.BlockSpec(memory_space=pltpu.SMEM), pl.BlockSpec(memory_space=pltpu.HBM)],
        out_specs=pl.BlockSpec(memory_space=pltpu.VMEM),
        scratch_shapes=[
            pltpu.VMEM((pair_count, rows, -(-size // 128) * 128 + 128), amps.dtype),
            pltpu.SemaphoreType.DMA((pair_count,)),
        ],
        compiler_params=pltpu.CompilerParams(vmem_limit_bytes=vmem),
        cost_estimate=pl.CostEstimate(flops=0, bytes_accessed=4 * pair_count * rows * size, transcendentals=0),
        name="pack_amplitudes",
    )(start, amps)


def mask_kernel(per_step, parts, first_ref, irrep_ref, irrep_d_ref, irrep_ab_ref, ints_ref, out_ref, table):
    step = pl.program_id(0)

    @pl.when(step == 0)
    def _():
        for part in range(parts):
            needed = irrep_d_ref[part] ^ irrep_ab_ref[...]
            for irrep in range(IRREPS):
                table[irrep * parts + part] = jnp.where(needed == irrep, 1.0, 0.0).astype(table.dtype)

    for k in range(per_step):
        index = first_ref[0] + step * per_step + k
        irrep_c = irrep_ref[index // parts]
        out_ref[k] = ints_ref[k] * table[irrep_c * parts + index % parts]


def mask(integrals, virt_irrep, irrep_ab, first_row):
    virtuals = virt_irrep.shape[0]
    rows_local, cols_local = integrals.shape
    chunk = math.gcd(virtuals, rows_local)
    parts = virtuals // chunk
    chunks = rows_local // chunk
    per_step = next(n for n in (10, 5, 4, 2, 1) if chunks % n == 0)
    block = pl.BlockSpec((per_step, chunk, cols_local), lambda step, *_: (step, 0, 0))
    masked = pl.pallas_call(
        functools.partial(mask_kernel, per_step, parts),
        grid_spec=pltpu.PrefetchScalarGridSpec(
            num_scalar_prefetch=2,
            grid=(chunks // per_step,),
            in_specs=[
                pl.BlockSpec((parts, chunk, 1), lambda step, *_: (0, 0, 0)),
                pl.BlockSpec((1, cols_local), lambda step, *_: (0, 0)),
                block,
            ],
            out_specs=block,
            scratch_shapes=[pltpu.VMEM((IRREPS * parts, chunk, cols_local), integrals.dtype)],
        ),
        out_shape=jax.ShapeDtypeStruct((chunks, chunk, cols_local), integrals.dtype),
        compiler_params=pltpu.CompilerParams(vmem_limit_bytes=14 * MIB),
        cost_estimate=pl.CostEstimate(
            flops=rows_local * cols_local, bytes_accessed=4 * rows_local * cols_local, transcendentals=0
        ),
        name="mask_integrals",
    )(
        (first_row // chunk).astype(jnp.int32).reshape(1),
        virt_irrep,
        virt_irrep.reshape(parts, chunk, 1),
        irrep_ab.reshape(1, cols_local),
        integrals.reshape(chunks, chunk, cols_local),
    )
    return masked.reshape(rows_local, cols_local)


def accumulate(start_ref, amps_ref, ints_ref):
    count, rows, size = amps_ref.shape
    start = pl.multiple_of(start_ref[0], 128)
    step = 2560
    total = None
    for first in range(0, size, step):
        last = min(first + step, size)
        lhs = amps_ref[:, :, first:last].reshape(count * rows, last - first)
        part = jnp.dot(lhs, ints_ref[pl.ds(start + first, last - first)], preferred_element_type=jnp.float32)
        total = part if total is None else total + part
    return total


def contract_kernel(start_ref, amps_ref, ints_ref, *refs):
    out_ref = refs[-1]
    total = accumulate(start_ref, amps_ref, ints_ref)
    if len(refs) == 2:
        total = total + refs[0][...]
    out_ref[...] = total


def select_exactly(values, select):
    rows = values.shape[0]
    high = values.astype(jnp.bfloat16)
    rest = values - high.astype(jnp.float32)
    middle = rest.astype(jnp.bfloat16)
    low = (rest - middle.astype(jnp.float32)).astype(jnp.bfloat16)
    terms = [jnp.dot(term, select, preferred_element_type=jnp.float32) for term in (high, middle, low)]
    return terms[0] + terms[1] + terms[2]


def contract_last_kernel(start_ref, amps_ref, ints_ref, before_ref, select_ref, direct_ref, mirror_ref, sorted_ref):
    total = accumulate(start_ref, amps_ref, ints_ref) + before_ref[...]
    pair_count, occupied, _ = direct_ref.shape
    slab_count = mirror_ref.shape[0] // pair_count
    half, width = mirror_ref.shape[1], mirror_ref.shape[2] // 2
    direct_ref[...] = total.reshape(direct_ref.shape)
    sorted_ref[...] = select_exactly(total, select_ref[...]).reshape(sorted_ref.shape)
    for p in range(pair_count):
        block = sorted_ref[:, p, :]
        for s in range(slab_count):
            part = block[:, s * width : (s + 1) * width]
            mirror_ref[p * slab_count + s, :, :width] = part[:half]
            mirror_ref[p * slab_count + s, :, width:] = part[half:]


def contract(amps, ints, start, before=None, select=None, slab_count=None):
    pair_count, occupied, size = amps.shape
    cols = ints.shape[1]
    vmem = pl.BlockSpec(memory_space=pltpu.VMEM)
    operands = [operand for operand in (before, select) if operand is not None]
    scratch = []
    if select is None:
        kernel = contract_kernel
        out_shape = jax.ShapeDtypeStruct((pair_count * occupied, cols), jnp.float32)
        out_specs = vmem
    else:
        kernel = contract_last_kernel
        width = cols // slab_count
        out_shape = [
            jax.ShapeDtypeStruct((pair_count, occupied, cols), jnp.float32),
            jax.ShapeDtypeStruct((pair_count * slab_count, occupied // 2, 2 * width), jnp.float32),
        ]
        out_specs = [vmem, vmem]
        scratch = [pltpu.VMEM((pair_count, occupied, cols), jnp.float32)]
    return pl.pallas_call(
        kernel,
        out_shape=out_shape,
        in_specs=[pl.BlockSpec(memory_space=pltpu.SMEM)] + [vmem] * (2 + len(operands)),
        out_specs=out_specs,
        scratch_shapes=scratch,
        compiler_params=pltpu.CompilerParams(vmem_limit_bytes=24 * MIB),
        cost_estimate=pl.CostEstimate(
            flops=2 * pair_count * occupied * size * cols,
            bytes_accessed=2 * size * (cols + pair_count * occupied),
            transcendentals=0,
        ),
        name="contract",
    )(start, amps, ints, *operands)


def finish_kernel(direct_ref, mirror_ref, denominator_ref, select_ref, out_ref):
    pair_count = direct_ref.shape[0]
    slab_count = mirror_ref.shape[0] // pair_count
    width = mirror_ref.shape[2] // 2
    ladder = direct_ref[0]
    for q in range(1, pair_count):
        ladder = ladder + direct_ref[q]
    blocks = []
    for s in range(slab_count):
        block = mirror_ref[s]
        for q in range(1, pair_count):
            block = block + mirror_ref[q * slab_count + s]
        blocks.append(jnp.concatenate([block[:, :width], block[:, width:]], axis=0))
    mirror = select_exactly(jnp.concatenate(blocks, axis=1), select_ref[...])
    update = (ladder + mirror) / denominator_ref[...]
    _, first_local, slab_virt = out_ref.shape
    for a in range(first_local):
        out_ref[:, a, :] = update[:, a * slab_virt : (a + 1) * slab_virt]


def finish(direct, mirror, denominator, select, first_local, slab_virt):
    occupied = direct.shape[1]
    return pl.pallas_call(
        finish_kernel,
        out_shape=jax.ShapeDtypeStruct((occupied, first_local, slab_virt), jnp.float32),
        in_specs=[pl.BlockSpec(memory_space=pltpu.VMEM)] * 4,
        out_specs=pl.BlockSpec(memory_space=pltpu.VMEM),
        compiler_params=pltpu.CompilerParams(vmem_limit_bytes=8 * MIB),
        cost_estimate=pl.CostEstimate(flops=2 * direct.size, bytes_accessed=8 * direct.size, transcendentals=0),
        name="finish",
    )(direct, mirror, denominator, select)


def selection(source):
    matrix = np.zeros((source.size, source.size), np.float32)
    matrix[source.reshape(-1), np.arange(source.size)] = 1.0
    return jnp.asarray(matrix, jnp.bfloat16)


def local(amplitudes, integrals, virt_irrep, occ_energy, slab_energy):
    pair_count = lax.axis_size("pair")
    slab_count = lax.axis_size("slab")
    pair_index = lax.axis_index("pair")
    slab_index = lax.axis_index("slab").astype(jnp.int32)
    occ_local, occupied, virt_pairs = amplitudes.shape
    rows_local, cols_local = integrals.shape
    slab_virt = slab_energy.shape[0]
    first_local = slab_virt // slab_count
    assert occ_local == 1

    slab_irrep = virt_irrep[:slab_virt]
    own_irrep = lax.dynamic_slice_in_dim(slab_irrep, slab_index * first_local, first_local, 0)
    irrep_ab = jnp.bitwise_xor(own_irrep[:, None], slab_irrep[None, :]).reshape(-1)

    energy_i = lax.dynamic_slice_in_dim(occ_energy, pair_index, 1, 0)
    energy_a = lax.dynamic_slice_in_dim(slab_energy, slab_index * first_local, first_local, 0)
    energy_ab = (energy_a[:, None] + slab_energy[None, :]).reshape(1, cols_local)
    denominator = energy_ab - energy_i - occ_energy[:, None]

    columns = np.arange(cols_local)
    by_slab = selection(columns.reshape(first_local, slab_count, first_local).transpose(1, 0, 2))
    by_first = selection(columns.reshape(slab_count, first_local, first_local).transpose(2, 0, 1))

    shared = int(SHARE * rows_local) // 128 * 128
    parity = slab_index % 2
    own = (parity * shared).reshape(1)
    other = ((1 - parity) * shared).reshape(1)
    rest = jnp.full((1,), 2 * shared, jnp.int32)
    amps = amplitudes.reshape(occupied, virt_pairs)

    def spread(start, size, vmem):
        packed = pack(amps, start, size, pair_count, vmem)
        return lax.all_to_all(packed, "pair", split_axis=0, concat_axis=0, tiled=True)

    own_amps = spread(own, shared, 60 * MIB)
    other_amps = lax.ppermute(own_amps, "slab", [(s, s ^ 1) for s in range(slab_count)])
    rest_amps = spread(rest, rows_local - 2 * shared, 8 * MIB)
    masked = mask(integrals, virt_irrep, irrep_ab, pair_index * rows_local)
    partial = contract(own_amps, masked, own)
    partial = contract(rest_amps, masked, rest, partial)
    direct, mirror = contract(other_amps, masked, other, partial, by_slab, slab_count)

    mirror = lax.all_to_all(mirror, ("pair", "slab"), split_axis=0, concat_axis=0, tiled=True)
    direct = lax.all_to_all(direct, "pair", split_axis=0, concat_axis=0, tiled=True)
    update = finish(direct, mirror, denominator, by_first, first_local, slab_virt)
    return update.reshape(occ_local, occupied, first_local, slab_virt)


def solution(mesh):
    placed = (P("pair", None, None), P("pair", "slab"), P(), P(), P())
    return jax.shard_map(
        local, mesh=mesh, in_specs=placed, out_specs=P("pair", None, "slab", None), check_vma=False
    )
```

```python
import functools
import math

import jax
import jax.numpy as jnp
from jax import lax
from jax.experimental import pallas as pl
from jax.experimental.pallas import tpu as pltpu
from jax.sharding import PartitionSpec as P

IRREPS = 8
MIB = 2**20
SHARE = 0.24


def pack_kernel(rows_local, home, me_ref, start_ref, amps_ref, after_ref, *refs):
    outs, (held, packed, sems) = refs[:-3], refs[-3:]
    _, _, size = packed.shape
    count = sems.shape[0]
    me = me_ref[0]
    start = pl.multiple_of(start_ref[0], 128)
    loads, shifts = [], []
    for dest in range(count):
        first = dest * rows_local // 128 * 128
        shifts.append(dest * rows_local - first)
        width = -(-(shifts[dest] + size) // 128) * 128
        slot = dest ^ me if home else dest
        loads.append(
            pltpu.make_async_copy(
                amps_ref.at[:, pl.ds(start + first, width)], held.at[slot, :, pl.ds(0, width)], sems.at[dest]
            )
        )

    def wanted(dest):
        return (dest ^ me) // 2 == 0 if home else True

    for dest in range(count):
        pl.when(wanted(dest))(loads[dest].start)
    for dest in range(count):

        @pl.when(wanted(dest))
        def _():
            loads[dest].wait()
            packed[dest ^ me] = held[dest ^ me if home else dest, :, shifts[dest] : shifts[dest] + size]

    for k, out in enumerate(outs):
        slot = 0 if home else 2 * k + 2
        out[...] = packed[slot : slot + 2]


def pack(amps, me, start, size, pair_count, home, after=None):
    rows, virt_pairs = amps.shape
    held = (2 if home else pair_count, rows, -(-size // 128) * 128 + 128)
    packed = (held[0], rows, size)
    outs = 1 if home else pair_count // 2 - 1
    vmem = 60 * MIB if after is None else 2 * MIB + 6 * held[0] * rows * held[2]
    return pl.pallas_call(
        functools.partial(pack_kernel, virt_pairs // pair_count, home),
        out_shape=[jax.ShapeDtypeStruct((2, rows, size), amps.dtype)] * outs,
        in_specs=[pl.BlockSpec(memory_space=pltpu.SMEM)] * 2
        + [pl.BlockSpec(memory_space=pltpu.HBM), pl.BlockSpec(memory_space=pl.ANY)],
        out_specs=[pl.BlockSpec(memory_space=pltpu.VMEM)] * outs,
        scratch_shapes=[
            pltpu.VMEM(held, amps.dtype),
            pltpu.VMEM(packed, amps.dtype),
            pltpu.SemaphoreType.DMA((pair_count,)),
        ],
        compiler_params=pltpu.CompilerParams(vmem_limit_bytes=vmem),
        cost_estimate=pl.CostEstimate(flops=0, bytes_accessed=4 * held[0] * rows * size, transcendentals=0),
        name="pack_home" if home else "pack_amplitudes",
    )(me, start, amps, me if after is None else after)


def mask_kernel(per_step, parts, first_ref, irrep_ref, irrep_d_ref, irrep_ab_ref, ints_ref, out_ref, table):
    step = pl.program_id(0)

    @pl.when(step == 0)
    def _():
        for part in range(parts):
            needed = irrep_d_ref[part] ^ irrep_ab_ref[...]
            for irrep in range(IRREPS):
                table[irrep * parts + part] = jnp.where(needed == irrep, 1.0, 0.0).astype(table.dtype)

    for k in range(per_step):
        index = first_ref[0] + step * per_step + k
        irrep_c = irrep_ref[index // parts]
        out_ref[k] = ints_ref[k] * table[irrep_c * parts + index % parts]


def mask(integrals, virt_irrep, irrep_ab, first_row):
    virtuals = virt_irrep.shape[0]
    rows_local, cols_local = integrals.shape
    chunk = math.gcd(virtuals, rows_local)
    parts = virtuals // chunk
    chunks = rows_local // chunk
    per_step = next(n for n in (10, 5, 4, 2, 1) if chunks % n == 0)
    block = pl.BlockSpec((per_step, chunk, cols_local), lambda step, *_: (step, 0, 0))
    masked = pl.pallas_call(
        functools.partial(mask_kernel, per_step, parts),
        grid_spec=pltpu.PrefetchScalarGridSpec(
            num_scalar_prefetch=2,
            grid=(chunks // per_step,),
            in_specs=[
                pl.BlockSpec((parts, chunk, 1), lambda step, *_: (0, 0, 0)),
                pl.BlockSpec((1, cols_local), lambda step, *_: (0, 0)),
                block,
            ],
            out_specs=block,
            scratch_shapes=[pltpu.VMEM((IRREPS * parts, chunk, cols_local), integrals.dtype)],
        ),
        out_shape=jax.ShapeDtypeStruct((chunks, chunk, cols_local), integrals.dtype),
        compiler_params=pltpu.CompilerParams(vmem_limit_bytes=14 * MIB),
        cost_estimate=pl.CostEstimate(
            flops=rows_local * cols_local, bytes_accessed=4 * rows_local * cols_local, transcendentals=0
        ),
        name="mask_integrals",
    )(
        (first_row // chunk).astype(jnp.int32).reshape(1),
        virt_irrep,
        virt_irrep.reshape(parts, chunk, 1),
        irrep_ab.reshape(1, cols_local),
        integrals.reshape(chunks, chunk, cols_local),
    )
    return masked.reshape(rows_local, cols_local)


def merge_kernel(*refs):
    for k, ref in enumerate(refs[:-1]):
        refs[-1][k] = ref[...]


def merge(parts):
    return pl.pallas_call(
        merge_kernel,
        out_shape=jax.ShapeDtypeStruct((len(parts),) + parts[0].shape, parts[0].dtype),
        in_specs=[pl.BlockSpec(memory_space=pltpu.VMEM)] * len(parts),
        out_specs=pl.BlockSpec(memory_space=pltpu.VMEM),
        compiler_params=pltpu.CompilerParams(vmem_limit_bytes=4 * MIB),
        cost_estimate=pl.CostEstimate(flops=0, bytes_accessed=4 * len(parts) * parts[0].size, transcendentals=0),
        name="merge",
    )(*parts)


def accumulate(start_ref, home_ref, home_other_ref, ints_ref, mine, others, size):
    start = pl.multiple_of(start_ref[0], 128)
    step = 2560
    total = None
    for first in range(0, size, step):
        width = min(step, size - first)
        rows = pl.ds(start + first, width)
        blocks = [home_ref[0, :, rows], home_other_ref[1, :, rows]]
        for own, other in zip(mine, others):
            blocks += [own[0, :, first : first + width], other[1, :, first : first + width]]
        lhs = jnp.concatenate(blocks, axis=0)
        part = jnp.dot(lhs, ints_ref[rows], preferred_element_type=jnp.float32)
        total = part if total is None else total + part
    return total


def views(refs):
    return [refs[0].at[k] for k in range(refs[0].shape[0])] if len(refs[0].shape) == 4 else list(refs)


def contract_kernel(arrays, last, start_ref, me_ref, home_ref, home_other_ref, ints_ref, *refs):
    mine, others, refs = views(refs[:arrays]), views(refs[arrays : 2 * arrays]), refs[2 * arrays :]
    total = accumulate(start_ref, home_ref, home_other_ref, ints_ref, mine, others, mine[0].shape[2])
    if not last:
        before, out_ref = refs[:-1], refs[-1]
        out_ref[...] = total + before[0][...] if before else total
        return
    before_ref, out_ref, partial = refs
    me = me_ref[0]
    partial[...] = (total + before_ref[...]).reshape(partial.shape)
    count = partial.shape[0]
    for p in range(count):
        out_ref[p, :count] = partial[p ^ me]
        for i in range(count):
            out_ref[p, count + i : count + i + 1] = partial[i ^ me, p : p + 1]


def contract(mine, others, home, home_other, ints, start, me, before=None, last=False):
    occupied, size = mine[0].shape[-2:]
    cols = ints.shape[1]
    vmem = pl.BlockSpec(memory_space=pltpu.VMEM)
    operands = [*mine, *others] + ([] if before is None else [before])
    if last:
        out_shape = jax.ShapeDtypeStruct((occupied, 2 * occupied, cols), jnp.float32)
        scratch = [pltpu.VMEM((occupied, occupied, cols), jnp.float32)]
    else:
        out_shape = jax.ShapeDtypeStruct((occupied * occupied, cols), jnp.float32)
        scratch = []
    return pl.pallas_call(
        functools.partial(contract_kernel, len(mine), last),
        out_shape=out_shape,
        in_specs=[pl.BlockSpec(memory_space=pltpu.SMEM)] * 2 + [vmem] * (3 + len(operands)),
        out_specs=vmem,
        scratch_shapes=scratch,
        compiler_params=pltpu.CompilerParams(vmem_limit_bytes=8 * MIB),
        cost_estimate=pl.CostEstimate(
            flops=2 * occupied * occupied * size * cols,
            bytes_accessed=2 * size * (cols + occupied * occupied),
            transcendentals=0,
        ),
        name="contract",
    )(start, me, home, home_other, ints, *operands)


def select_exactly(values, select):
    rows = values.shape[0]
    high = values.astype(jnp.bfloat16)
    rest = values - high.astype(jnp.float32)
    middle = rest.astype(jnp.bfloat16)
    low = (rest - middle.astype(jnp.float32)).astype(jnp.bfloat16)
    terms = [jnp.dot(term, select, preferred_element_type=jnp.float32) for term in (high, middle, low)]
    return terms[0] + terms[1] + terms[2]


def add_kernel(parts_ref, ladder_ref, mirror_ref):
    total = parts_ref[0]
    for q in range(1, parts_ref.shape[0]):
        total = total + parts_ref[q]
    half = total.shape[0] // 2
    ladder_ref[...] = total[:half]
    mirror_ref[...] = total[half:]


def add_parts(parts):
    _, rows, cols = parts.shape
    half = jax.ShapeDtypeStruct((rows // 2, cols), jnp.float32)
    vmem = pl.BlockSpec(memory_space=pltpu.VMEM)
    return pl.pallas_call(
        add_kernel,
        out_shape=[half, half],
        in_specs=[vmem],
        out_specs=[vmem, vmem],
        compiler_params=pltpu.CompilerParams(vmem_limit_bytes=4 * MIB),
        cost_estimate=pl.CostEstimate(flops=parts.size, bytes_accessed=4 * parts.size, transcendentals=0),
        name="add_parts",
    )(parts)


def finish_kernel(ladder_ref, denominator_ref, select_ref, *refs):
    mirrors, out_ref = refs[:-1], refs[-1]
    mirror = select_exactly(jnp.concatenate([ref[...] for ref in mirrors], axis=1), select_ref[...])
    update = (ladder_ref[...] + mirror) / denominator_ref[...]
    _, first_local, slab_virt = out_ref.shape
    for a in range(first_local):
        out_ref[:, a, :] = update[:, a * slab_virt : (a + 1) * slab_virt]


def finish(ladder, mirrors, denominator, select, first_local, slab_virt):
    rows = ladder.shape[0]
    return pl.pallas_call(
        finish_kernel,
        out_shape=jax.ShapeDtypeStruct((rows, first_local, slab_virt), jnp.float32),
        in_specs=[pl.BlockSpec(memory_space=pltpu.VMEM)] * (3 + len(mirrors)),
        out_specs=pl.BlockSpec(memory_space=pltpu.VMEM),
        compiler_params=pltpu.CompilerParams(vmem_limit_bytes=6 * MIB),
        cost_estimate=pl.CostEstimate(flops=6 * rows * select.size, bytes_accessed=2 * select.size, transcendentals=0),
        name="finish",
    )(ladder, denominator, select, *mirrors)


def swap(values, axis, bits):
    return lax.ppermute(values, axis, [(p, p ^ bits) for p in range(lax.axis_size(axis))])


def local(amplitudes, integrals, virt_irrep, occ_energy, slab_energy):
    pair_count = lax.axis_size("pair")
    slab_count = lax.axis_size("slab")
    pair_index = lax.axis_index("pair")
    slab_index = lax.axis_index("slab").astype(jnp.int32)
    occ_local, occupied, virt_pairs = amplitudes.shape
    rows_local, cols_local = integrals.shape
    slab_virt = slab_energy.shape[0]
    first_local = slab_virt // slab_count
    assert occ_local == 1
    me = pair_index.astype(jnp.int32).reshape(1)

    slab_irrep = virt_irrep[:slab_virt]
    own_irrep = lax.dynamic_slice_in_dim(slab_irrep, slab_index * first_local, first_local, 0)
    irrep_ab = jnp.bitwise_xor(own_irrep[:, None], slab_irrep[None, :]).reshape(-1)

    energy_i = lax.dynamic_slice_in_dim(occ_energy, pair_index, 1, 0)
    energy_a = lax.dynamic_slice_in_dim(slab_energy, slab_index * first_local, first_local, 0)
    energy_ab = (energy_a[:, None] + slab_energy[None, :]).reshape(1, cols_local)
    denominator = energy_ab - energy_i - occ_energy[:, None]

    shape = (slab_count * cols_local, cols_local)
    row, col = (lax.broadcasted_iota(jnp.int32, shape, axis) for axis in (0, 1))
    source = jnp.bitwise_xor(row // cols_local, slab_index)
    row = row % cols_local
    same_a = row % slab_virt == slab_index * first_local + col // slab_virt
    same_b = source * first_local + row // slab_virt == col % slab_virt
    select = jnp.where(same_a & same_b, 1.0, 0.0).astype(jnp.bfloat16)

    shared = int(SHARE * rows_local) // 128 * 128
    parity = slab_index % 2
    own = (parity * shared).reshape(1)
    other = ((1 - parity) * shared).reshape(1)
    rest = jnp.full((1,), 2 * shared, jnp.int32)
    whole = jnp.zeros((1,), jnp.int32)
    amps = amplitudes.reshape(occupied, virt_pairs)
    chips = [2 * k for k in range(1, pair_count // 2)]

    parts = pack(amps, me, own, shared, pair_count, False)
    own_mine = [swap(part, "pair", bits) for part, bits in zip(parts, chips)]
    parts = pack(amps, me, rest, rows_local - 2 * shared, pair_count, False, parts[-1])
    rest_mine = [swap(part, "pair", bits) for part, bits in zip(parts, chips)]

    own_mine = merge(own_mine)
    (home,) = pack(amps, me, whole, rows_local, pair_count, True, own_mine)
    home_other = swap(home, "pair", 1)
    other_mine = swap(own_mine, "slab", 1)
    own_others = swap(own_mine, "pair", 1)
    rest_others = [swap(part, "pair", 1) for part in rest_mine]
    other_others = swap(other_mine, "pair", 1)

    masked = mask(integrals, virt_irrep, irrep_ab, pair_index * rows_local)
    partial = contract([own_mine], [own_others], home, home_other, masked, own, me)
    partial = contract(rest_mine, rest_others, home, home_other, masked, rest, me, partial)
    parts = contract([other_mine], [other_others], home, home_other, masked, other, me, partial, True)

    parts = lax.all_to_all(parts, "pair", split_axis=0, concat_axis=0, tiled=True)
    ladder, mirror = add_parts(parts)
    mirrors = [mirror] + [swap(mirror, "slab", bits) for bits in range(1, slab_count)]
    update = finish(ladder, mirrors, denominator, select, first_local, slab_virt)
    return update.reshape(occ_local, occupied, first_local, slab_virt)


def solution(mesh):
    placed = (P("pair", None, None), P("pair", "slab"), P(), P(), P())
    return jax.shard_map(
        local, mesh=mesh, in_specs=placed, out_specs=P("pair", None, "slab", None), check_vma=False
    )
```

```python
import functools
import math

import jax
import jax.numpy as jnp
from jax import lax
from jax.experimental import pallas as pl
from jax.experimental.pallas import tpu as pltpu
from jax.sharding import PartitionSpec as P

IRREPS = 8
MIB = 2**20
SHARE = 0.24
LATE_FLOPS = 10**10


def pack_kernel(rows_local, home, me_ref, start_ref, amps_ref, after_ref, *refs):
    outs, (held, packed, sems) = refs[:-3], refs[-3:]
    _, _, size = packed.shape
    count = sems.shape[0]
    me = me_ref[0]
    start = pl.multiple_of(start_ref[0], 128)
    loads, shifts = [], []
    for dest in range(count):
        first = dest * rows_local // 128 * 128
        shifts.append(dest * rows_local - first)
        width = -(-(shifts[dest] + size) // 128) * 128
        slot = dest ^ me if home else dest
        loads.append(
            pltpu.make_async_copy(
                amps_ref.at[:, pl.ds(start + first, width)], held.at[slot, :, pl.ds(0, width)], sems.at[dest]
            )
        )

    def wanted(dest):
        return (dest ^ me) // 2 == 0 if home else True

    for dest in range(count):
        pl.when(wanted(dest))(loads[dest].start)
    for dest in range(count):

        @pl.when(wanted(dest))
        def _():
            loads[dest].wait()
            packed[dest ^ me] = held[dest ^ me if home else dest, :, shifts[dest] : shifts[dest] + size]

    for k, out in enumerate(outs):
        slot = 0 if home else 2 * k + 2
        out[...] = packed[slot : slot + 2]


def pack(amps, me, start, size, pair_count, home, after=None):
    rows, virt_pairs = amps.shape
    held = (2 if home else pair_count, rows, -(-size // 128) * 128 + 128)
    packed = (held[0], rows, size)
    outs = 1 if home else pair_count // 2 - 1
    vmem = 2 * MIB + 6 * held[0] * rows * held[2]
    return pl.pallas_call(
        functools.partial(pack_kernel, virt_pairs // pair_count, home),
        out_shape=[jax.ShapeDtypeStruct((2, rows, size), amps.dtype)] * outs,
        in_specs=[pl.BlockSpec(memory_space=pltpu.SMEM)] * 2
        + [pl.BlockSpec(memory_space=pltpu.HBM), pl.BlockSpec(memory_space=pl.ANY)],
        out_specs=[pl.BlockSpec(memory_space=pltpu.VMEM)] * outs,
        scratch_shapes=[
            pltpu.VMEM(held, amps.dtype),
            pltpu.VMEM(packed, amps.dtype),
            pltpu.SemaphoreType.DMA((pair_count,)),
        ],
        compiler_params=pltpu.CompilerParams(vmem_limit_bytes=vmem),
        cost_estimate=pl.CostEstimate(flops=0, bytes_accessed=4 * held[0] * rows * size, transcendentals=0),
        name="pack_home" if home else "pack_amplitudes",
    )(me, start, pltpu.with_memory_space_constraint(amps, pltpu.HBM), me if after is None else after)


def mask_kernel(per_step, parts, me_ref, slab_ref, irrep_ref, occ_ref, virt_ref, row_ref, ints_ref, *refs):
    out_ref, select_ref, denominator_ref, table, padded, by_row = refs
    step = pl.program_id(0)
    chunk, cols = ints_ref.shape[1:]
    slab_virt = virt_ref.shape[0]
    first_local = cols // slab_virt
    bits = slab_virt.bit_length() - 1
    me, slab = me_ref[0], slab_ref[0]

    @pl.when(step == 0)
    def _():
        padded[:, : row_ref.shape[1]] = row_ref[...]
        for k in range(padded.shape[1] // 128):
            lanes = slice(k * 128, (k + 1) * 128)
            by_row[lanes] = jnp.transpose(jnp.broadcast_to(padded[:, lanes], (128, 128)))

        col = lax.broadcasted_iota(jnp.int32, (1, cols), 1)
        a_of, b_of = col >> bits, col & (slab_virt - 1)
        irrep_a = irrep_b = jnp.zeros_like(col)
        energy_a = energy_b = jnp.zeros(col.shape, jnp.float32)
        for a in range(first_local):
            irrep_a = jnp.where(a_of == a, irrep_ref[slab * first_local + a], irrep_a)
            energy_a = jnp.where(a_of == a, virt_ref[slab * first_local + a], energy_a)
        for b in range(slab_virt):
            irrep_b = jnp.where(b_of == b, irrep_ref[b], irrep_b)
            energy_b = jnp.where(b_of == b, virt_ref[b], energy_b)
        irrep_ab = irrep_a ^ irrep_b

        for part in range(parts):
            for lanes in (slice(k, k + 128) for k in range(0, cols, 128)):
                needed = by_row[part * chunk : (part + 1) * chunk] ^ irrep_ab[:, lanes]
                for irrep in range(IRREPS):
                    table[irrep * parts + part, :, lanes] = jnp.where(needed == irrep, 1.0, 0.0).astype(table.dtype)

        occupied = denominator_ref.shape[0]
        j_of = lax.broadcasted_iota(jnp.int32, (occupied, cols), 0)
        energy_j = jnp.zeros((occupied, cols), jnp.float32)
        for j in range(occupied):
            energy_j = jnp.where(j_of == j, occ_ref[j], energy_j)
        denominator_ref[...] = energy_a + energy_b - occ_ref[me] - energy_j

        row = lax.broadcasted_iota(jnp.int32, (cols, cols), 0)
        col = lax.broadcasted_iota(jnp.int32, (cols, cols), 1)
        same_a = (row & (slab_virt - 1)) == slab * first_local + (col >> bits)
        for t in range(select_ref.shape[0] // cols):
            same_b = (slab ^ t) * first_local + (row >> bits) == (col & (slab_virt - 1))
            chosen = jnp.where(same_a & same_b, 1.0, 0.0)
            select_ref[t * cols : (t + 1) * cols] = chosen.astype(select_ref.dtype)

    chunks = per_step * pl.num_programs(0)
    for k in range(per_step):
        index = me * chunks + step * per_step + k
        irrep_c = irrep_ref[index // parts]
        out_ref[k] = ints_ref[k] * table[irrep_c * parts + index % parts]


def mask(integrals, me, slab, virt_irrep, occ_energy, slab_energy):
    virtuals = virt_irrep.shape[0]
    slab_virt = slab_energy.shape[0]
    occupied = occ_energy.shape[0]
    rows_local, cols_local = integrals.shape
    chunk = math.gcd(virtuals, rows_local)
    parts = virtuals // chunk
    chunks = rows_local // chunk
    per_step = next(n for n in (10, 5, 4, 2, 1) if chunks % n == 0)
    padded = -(-virtuals // 128) * 128
    select_rows = slab_virt * slab_virt
    block = pl.BlockSpec((per_step, chunk, cols_local), lambda step: (step, 0, 0))
    scalars = pl.BlockSpec(memory_space=pltpu.SMEM)
    masked, select, denominator = pl.pallas_call(
        functools.partial(mask_kernel, per_step, parts),
        grid=(chunks // per_step,),
        in_specs=[scalars] * 5 + [pl.BlockSpec((1, virtuals), lambda step: (0, 0)), block],
        out_specs=[
            block,
            pl.BlockSpec((select_rows, cols_local), lambda step: (0, 0)),
            pl.BlockSpec((occupied, cols_local), lambda step: (0, 0)),
        ],
        scratch_shapes=[
            pltpu.VMEM((IRREPS * parts, chunk, cols_local), integrals.dtype),
            pltpu.VMEM((1, padded), jnp.int32),
            pltpu.VMEM((padded, 128), jnp.int32),
        ],
        out_shape=[
            jax.ShapeDtypeStruct((chunks, chunk, cols_local), integrals.dtype),
            jax.ShapeDtypeStruct((select_rows, cols_local), jnp.bfloat16),
            jax.ShapeDtypeStruct((occupied, cols_local), jnp.float32),
        ],
        compiler_params=pltpu.CompilerParams(vmem_limit_bytes=16 * MIB),
        cost_estimate=pl.CostEstimate(
            flops=LATE_FLOPS, bytes_accessed=4 * rows_local * cols_local, transcendentals=0
        ),
        name="mask_integrals",
    )(
        me,
        slab,
        virt_irrep,
        occ_energy,
        slab_energy,
        virt_irrep.reshape(1, virtuals),
        pltpu.with_memory_space_constraint(integrals.reshape(chunks, chunk, cols_local), pltpu.HBM),
    )
    return masked.reshape(rows_local, cols_local), select, denominator


def merge_kernel(*refs):
    parts, home_ref, all_ref, other_ref = refs[:-3], refs[-3], refs[-2], refs[-1]
    size = parts[0].shape[2]
    for k, part in enumerate(parts):
        all_ref[k] = part[...]
        other_ref[:, k * size : (k + 1) * size] = part[1]
    other_ref[:, len(parts) * size :] = home_ref[1]


def merge(parts, home):
    count = len(parts)
    _, rows, size = parts[0].shape
    other = (rows, count * size + home.shape[2])
    vmem = pl.BlockSpec(memory_space=pltpu.VMEM)
    return pl.pallas_call(
        merge_kernel,
        out_shape=[
            jax.ShapeDtypeStruct((count,) + parts[0].shape, home.dtype),
            jax.ShapeDtypeStruct(other, home.dtype),
        ],
        in_specs=[vmem] * (count + 1),
        out_specs=[vmem, vmem],
        compiler_params=pltpu.CompilerParams(vmem_limit_bytes=4 * MIB),
        cost_estimate=pl.CostEstimate(flops=0, bytes_accessed=6 * rows * other[1], transcendentals=0),
        name="merge",
    )(*parts, home)


def other_core_kernel(*refs):
    parts, out_ref = refs[:-2], refs[-1]
    for k, part in enumerate(parts):
        out_ref[k] = part[1]


def for_other_core(parts, after):
    vmem = pl.BlockSpec(memory_space=pltpu.VMEM)
    _, rows, size = parts[0].shape
    out = jax.ShapeDtypeStruct((len(parts), rows, size), parts[0].dtype)
    return pl.pallas_call(
        other_core_kernel,
        out_shape=out,
        in_specs=[vmem] * len(parts) + [pl.BlockSpec(memory_space=pl.ANY)],
        out_specs=vmem,
        compiler_params=pltpu.CompilerParams(vmem_limit_bytes=4 * MIB),
        cost_estimate=pl.CostEstimate(flops=0, bytes_accessed=4 * out.size, transcendentals=0),
        name="for_other_core",
    )(*parts, after)


def contract_kernel(arrays, packed_other, last, start_ref, me_ref, home_ref, home_other_ref, ints_ref, *refs):
    lhs = refs[-2] if last else refs[-1]
    count, rows, size = lhs.shape
    chips = count // 2 - 1
    start = pl.multiple_of(start_ref[0], 128)
    home_first = home_other_ref.shape[1] - home_ref.shape[2]
    columns = pl.ds(start, size)
    lhs[0] = home_ref[0, :, columns]
    lhs[1] = home_other_ref[:, pl.ds(home_first + start, size)]
    mine, refs = refs[:arrays], refs[arrays:]
    for k in range(chips):
        lhs[2 * k + 2] = mine[0][k, 0] if arrays == 1 else mine[k][0]
        if packed_other:
            lhs[2 * k + 3] = home_other_ref[:, k * size : (k + 1) * size]
        else:
            lhs[2 * k + 3] = refs[0][k, 1] if arrays == 1 else refs[0][k]
    refs = refs if packed_other else refs[1:]
    step = 2560
    total = None
    for first in range(0, size, step):
        width = min(step, size - first)
        block = lhs[:, :, first : first + width].reshape(count * rows, width)
        part = jnp.dot(block, ints_ref[pl.ds(start + first, width)], preferred_element_type=jnp.float32)
        total = part if total is None else total + part
    if not last:
        before, out_ref = refs[:-2], refs[-2]
        out_ref[...] = total + before[0][...] if before else total
        return
    before_ref, out_ref, _, partial = refs
    me = me_ref[0]
    partial[...] = (total + before_ref[...]).reshape(partial.shape)
    for p in range(count):
        out_ref[p, :count] = partial[p ^ me]
        for i in range(count):
            out_ref[p, count + i : count + i + 1] = partial[i ^ me, p : p + 1]


def contract(mine, others, home, home_other, ints, start, me, before=None, last=False, flops=0):
    occupied, size = mine[0].shape[-2:]
    cols = ints.shape[1]
    vmem = pl.BlockSpec(memory_space=pltpu.VMEM)
    operands = [*mine, *others] + ([] if before is None else [before])
    scratch = [pltpu.VMEM((occupied, occupied, size), home.dtype)]
    if last:
        out_shape = jax.ShapeDtypeStruct((occupied, 2 * occupied, cols), jnp.float32)
        scratch.append(pltpu.VMEM((occupied, occupied, cols), jnp.float32))
    else:
        out_shape = jax.ShapeDtypeStruct((occupied * occupied, cols), jnp.float32)
    return pl.pallas_call(
        functools.partial(contract_kernel, len(mine), not others, last),
        out_shape=out_shape,
        in_specs=[pl.BlockSpec(memory_space=pltpu.SMEM)] * 2 + [vmem] * (3 + len(operands)),
        out_specs=vmem,
        scratch_shapes=scratch,
        compiler_params=pltpu.CompilerParams(vmem_limit_bytes=4 * MIB + 16 * occupied * occupied * cols + 4 * occupied * occupied * size),
        cost_estimate=pl.CostEstimate(
            flops=2 * occupied * occupied * size * cols + flops,
            bytes_accessed=2 * size * (cols + occupied * occupied),
            transcendentals=0,
        ),
        name="contract",
    )(start, me, home, home_other, ints, *operands)


def select_exactly(values, select):
    rows = values.shape[0]
    high = values.astype(jnp.bfloat16)
    rest = values - high.astype(jnp.float32)
    middle = rest.astype(jnp.bfloat16)
    low = (rest - middle.astype(jnp.float32)).astype(jnp.bfloat16)
    terms = [jnp.dot(term, select, preferred_element_type=jnp.float32) for term in (high, middle, low)]
    return terms[0] + terms[1] + terms[2]


def add_kernel(parts_ref, ladder_ref, mirror_ref):
    total = parts_ref[0]
    for q in range(1, parts_ref.shape[0]):
        total = total + parts_ref[q]
    half = total.shape[0] // 2
    ladder_ref[...] = total[:half]
    mirror_ref[...] = total[half:]


def add_parts(parts):
    _, rows, cols = parts.shape
    half = jax.ShapeDtypeStruct((rows // 2, cols), jnp.float32)
    vmem = pl.BlockSpec(memory_space=pltpu.VMEM)
    return pl.pallas_call(
        add_kernel,
        out_shape=[half, half],
        in_specs=[vmem],
        out_specs=[vmem, vmem],
        compiler_params=pltpu.CompilerParams(vmem_limit_bytes=4 * MIB),
        cost_estimate=pl.CostEstimate(flops=parts.size, bytes_accessed=4 * parts.size, transcendentals=0),
        name="add_parts",
    )(parts)


def finish_kernel(ladder_ref, denominator_ref, select_ref, *refs):
    mirrors, out_ref = refs[:-1], refs[-1]
    mirror = select_exactly(jnp.concatenate([ref[...] for ref in mirrors], axis=1), select_ref[...])
    update = (ladder_ref[...] + mirror) / denominator_ref[...]
    _, first_local, slab_virt = out_ref.shape
    for a in range(first_local):
        out_ref[:, a, :] = update[:, a * slab_virt : (a + 1) * slab_virt]


def finish(ladder, mirrors, denominator, select, first_local, slab_virt):
    rows = ladder.shape[0]
    return pl.pallas_call(
        finish_kernel,
        out_shape=jax.ShapeDtypeStruct((rows, first_local, slab_virt), jnp.float32),
        in_specs=[pl.BlockSpec(memory_space=pltpu.VMEM)] * (3 + len(mirrors)),
        out_specs=pl.BlockSpec(memory_space=pltpu.VMEM),
        compiler_params=pltpu.CompilerParams(vmem_limit_bytes=6 * MIB),
        cost_estimate=pl.CostEstimate(flops=6 * rows * select.size, bytes_accessed=2 * select.size, transcendentals=0),
        name="finish",
    )(ladder, denominator, select, *mirrors)


def swap(values, axis, bits):
    return lax.ppermute(values, axis, [(p, p ^ bits) for p in range(lax.axis_size(axis))])


def local(amplitudes, integrals, virt_irrep, occ_energy, slab_energy):
    pair_count = lax.axis_size("pair")
    slab_count = lax.axis_size("slab")
    occ_local, occupied, virt_pairs = amplitudes.shape
    rows_local, cols_local = integrals.shape
    slab_virt = slab_energy.shape[0]
    first_local = slab_virt // slab_count
    assert occ_local == 1
    slab_index = lax.axis_index("slab").astype(jnp.int32)
    me = lax.axis_index("pair").astype(jnp.int32).reshape(1)
    slab = slab_index.reshape(1)

    shared = int(SHARE * rows_local) // 128 * 128
    parity = slab_index % 2
    own = (parity * shared).reshape(1)
    other = ((1 - parity) * shared).reshape(1)
    rest = jnp.full((1,), 2 * shared, jnp.int32)
    whole = jnp.zeros((1,), jnp.int32)
    amps = amplitudes.reshape(occupied, virt_pairs)
    chips = [2 * k for k in range(1, pair_count // 2)]

    parts = pack(amps, me, own, shared, pair_count, False)
    own_mine = [swap(part, "pair", bits) for part, bits in zip(parts, chips)]
    parts = pack(amps, me, rest, rows_local - 2 * shared, pair_count, False, parts[-1])
    rest_mine = [swap(part, "pair", bits) for part, bits in zip(parts, chips)]
    (home,) = pack(amps, me, whole, rows_local, pair_count, True, parts[-1])

    own_mine, for_other = merge(own_mine, home)
    other_mine = swap(own_mine, "slab", 1)
    home_other = swap(for_other, "pair", 1)
    other_others = swap(other_mine, "pair", 1)
    masked, select, denominator = mask(integrals, me, slab, virt_irrep, occ_energy, slab_energy)
    rest_others = swap(for_other_core(rest_mine, masked), "pair", 1)
    partial = contract([own_mine], [], home, home_other, masked, own, me)
    partial = contract(rest_mine, [rest_others], home, home_other, masked, rest, me, partial)
    parts = contract([other_mine], [other_others], home, home_other, masked, other, me, partial, True)

    parts = lax.all_to_all(parts, "pair", split_axis=0, concat_axis=0, tiled=True)
    ladder, mirror = add_parts(parts)
    mirrors = [mirror] + [swap(mirror, "slab", bits) for bits in range(1, slab_count)]
    update = finish(ladder, mirrors, denominator, select, first_local, slab_virt)
    return update.reshape(occ_local, occupied, first_local, slab_virt)


def solution(mesh):
    placed = (P("pair", None, None), P("pair", "slab"), P(), P(), P())
    return jax.shard_map(
        local, mesh=mesh, in_specs=placed, out_specs=P("pair", None, "slab", None), check_vma=False
    )
```

```python
import functools
import math

import jax
import jax.numpy as jnp
from jax import lax
from jax.experimental import pallas as pl
from jax.experimental.pallas import tpu as pltpu
from jax.sharding import PartitionSpec as P

IRREPS = 8
MIB = 2**20
SHARE = 0.24
LATE_FLOPS = 10**10


def pack_kernel(rows_local, home, me_ref, start_ref, amps_ref, after_ref, *refs):
    outs, (held, packed, sems) = refs[:-3], refs[-3:]
    _, _, size = packed.shape
    count = sems.shape[0]
    me = me_ref[0]
    start = pl.multiple_of(start_ref[0], 128)
    loads, shifts = [], []
    for dest in range(count):
        first = dest * rows_local // 128 * 128
        shifts.append(dest * rows_local - first)
        width = -(-(shifts[dest] + size) // 128) * 128
        slot = dest ^ me if home else dest
        loads.append(
            pltpu.make_async_copy(
                amps_ref.at[:, pl.ds(start + first, width)], held.at[slot, :, pl.ds(0, width)], sems.at[dest]
            )
        )

    def wanted(dest):
        return (dest ^ me) // 2 == 0 if home else True

    for dest in range(count):
        pl.when(wanted(dest))(loads[dest].start)
    for dest in range(count):

        @pl.when(wanted(dest))
        def _():
            loads[dest].wait()
            packed[dest ^ me] = held[dest ^ me if home else dest, :, shifts[dest] : shifts[dest] + size]

    for k, out in enumerate(outs):
        slot = 0 if home else 2 * k + 2
        out[...] = packed[slot : slot + 2]


def pack(amps, me, start, size, pair_count, home, after=None):
    rows, virt_pairs = amps.shape
    held = (2 if home else pair_count, rows, -(-size // 128) * 128 + 128)
    packed = (held[0], rows, size)
    outs = 1 if home else pair_count // 2 - 1
    vmem = 2 * MIB + 6 * held[0] * rows * held[2]
    return pl.pallas_call(
        functools.partial(pack_kernel, virt_pairs // pair_count, home),
        out_shape=[jax.ShapeDtypeStruct((2, rows, size), amps.dtype)] * outs,
        in_specs=[pl.BlockSpec(memory_space=pltpu.SMEM)] * 2
        + [pl.BlockSpec(memory_space=pltpu.HBM), pl.BlockSpec(memory_space=pl.ANY)],
        out_specs=[pl.BlockSpec(memory_space=pltpu.VMEM)] * outs,
        scratch_shapes=[
            pltpu.VMEM(held, amps.dtype),
            pltpu.VMEM(packed, amps.dtype),
            pltpu.SemaphoreType.DMA((pair_count,)),
        ],
        compiler_params=pltpu.CompilerParams(vmem_limit_bytes=vmem),
        cost_estimate=pl.CostEstimate(flops=0, bytes_accessed=4 * held[0] * rows * size, transcendentals=0),
        name="pack_home" if home else "pack_amplitudes",
    )(me, start, pltpu.with_memory_space_constraint(amps, pltpu.HBM), me if after is None else after)


def mask_kernel(per_step, parts, me_ref, slab_ref, irrep_ref, occ_ref, virt_ref, row_ref, ints_ref, *refs):
    out_ref, select_ref, denominator_ref, table, padded, by_row = refs
    step = pl.program_id(0)
    chunk, cols = ints_ref.shape[1:]
    slab_virt = virt_ref.shape[0]
    first_local = cols // slab_virt
    bits = slab_virt.bit_length() - 1
    me, slab = me_ref[0], slab_ref[0]

    @pl.when(step == 0)
    def _():
        padded[:, : row_ref.shape[1]] = row_ref[...]
        for k in range(padded.shape[1] // 128):
            lanes = slice(k * 128, (k + 1) * 128)
            by_row[lanes] = jnp.transpose(jnp.broadcast_to(padded[:, lanes], (128, 128)))

        col = lax.broadcasted_iota(jnp.int32, (1, cols), 1)
        a_of, b_of = col >> bits, col & (slab_virt - 1)
        irrep_a = irrep_b = jnp.zeros_like(col)
        energy_a = energy_b = jnp.zeros(col.shape, jnp.float32)
        for a in range(first_local):
            irrep_a = jnp.where(a_of == a, irrep_ref[slab * first_local + a], irrep_a)
            energy_a = jnp.where(a_of == a, virt_ref[slab * first_local + a], energy_a)
        for b in range(slab_virt):
            irrep_b = jnp.where(b_of == b, irrep_ref[b], irrep_b)
            energy_b = jnp.where(b_of == b, virt_ref[b], energy_b)
        irrep_ab = irrep_a ^ irrep_b

        for part in range(parts):
            for lanes in (slice(k, k + 128) for k in range(0, cols, 128)):
                needed = by_row[part * chunk : (part + 1) * chunk] ^ irrep_ab[:, lanes]
                for irrep in range(IRREPS):
                    table[irrep * parts + part, :, lanes] = jnp.where(needed == irrep, 1.0, 0.0).astype(table.dtype)

        occupied = denominator_ref.shape[0]
        j_of = lax.broadcasted_iota(jnp.int32, (occupied, cols), 0)
        energy_j = jnp.zeros((occupied, cols), jnp.float32)
        for j in range(occupied):
            energy_j = jnp.where(j_of == j, occ_ref[j], energy_j)
        denominator_ref[...] = energy_a + energy_b - occ_ref[me] - energy_j

        row = lax.broadcasted_iota(jnp.int32, (cols, cols), 0)
        col = lax.broadcasted_iota(jnp.int32, (cols, cols), 1)
        same_a = (row & (slab_virt - 1)) == slab * first_local + (col >> bits)
        for t in range(select_ref.shape[0] // cols):
            same_b = (slab ^ t) * first_local + (row >> bits) == (col & (slab_virt - 1))
            chosen = jnp.where(same_a & same_b, 1.0, 0.0)
            select_ref[t * cols : (t + 1) * cols] = chosen.astype(select_ref.dtype)

    chunks = per_step * pl.num_programs(0)
    for k in range(per_step):
        index = me * chunks + step * per_step + k
        irrep_c = irrep_ref[index // parts]
        out_ref[k] = ints_ref[k] * table[irrep_c * parts + index % parts]


def in_hbm(array):
    return pltpu.with_memory_space_constraint(array, pltpu.HBM)


def mask(integrals, me, slab, virt_irrep, occ_energy, slab_energy):
    virtuals = virt_irrep.shape[0]
    slab_virt = slab_energy.shape[0]
    occupied = occ_energy.shape[0]
    rows_local, cols_local = integrals.shape
    chunk = math.gcd(virtuals, rows_local)
    parts = virtuals // chunk
    chunks = rows_local // chunk
    per_step = next(n for n in (10, 5, 4, 2, 1) if chunks % n == 0)
    padded = -(-virtuals // 128) * 128
    select_rows = slab_virt * slab_virt
    block = pl.BlockSpec((per_step, chunk, cols_local), lambda step: (step, 0, 0))
    scalars = pl.BlockSpec(memory_space=pltpu.SMEM)
    masked, select, denominator = pl.pallas_call(
        functools.partial(mask_kernel, per_step, parts),
        grid=(chunks // per_step,),
        in_specs=[scalars] * 5 + [pl.BlockSpec((1, virtuals), lambda step: (0, 0)), block],
        out_specs=[
            block,
            pl.BlockSpec((select_rows, cols_local), lambda step: (0, 0)),
            pl.BlockSpec((occupied, cols_local), lambda step: (0, 0)),
        ],
        scratch_shapes=[
            pltpu.VMEM((IRREPS * parts, chunk, cols_local), integrals.dtype),
            pltpu.VMEM((1, padded), jnp.int32),
            pltpu.VMEM((padded, 128), jnp.int32),
        ],
        out_shape=[
            pltpu.VMEM((chunks, chunk, cols_local), integrals.dtype),
            jax.ShapeDtypeStruct((select_rows, cols_local), jnp.bfloat16),
            jax.ShapeDtypeStruct((occupied, cols_local), jnp.float32),
        ],
        compiler_params=pltpu.CompilerParams(vmem_limit_bytes=16 * MIB),
        cost_estimate=pl.CostEstimate(
            flops=LATE_FLOPS, bytes_accessed=4 * rows_local * cols_local, transcendentals=0
        ),
        name="mask_integrals",
    )(
        me,
        slab,
        *(in_hbm(array) for array in (virt_irrep, occ_energy, slab_energy, virt_irrep.reshape(1, virtuals))),
        in_hbm(integrals.reshape(chunks, chunk, cols_local)),
    )
    return masked.reshape(rows_local, cols_local), select, denominator


def merge_kernel(*refs):
    parts, home_ref, all_ref, other_ref = refs[:-3], refs[-3], refs[-2], refs[-1]
    size = parts[0].shape[2]
    for k, part in enumerate(parts):
        all_ref[k] = part[...]
        other_ref[:, k * size : (k + 1) * size] = part[1]
    other_ref[:, len(parts) * size :] = home_ref[1]


def merge(parts, home):
    count = len(parts)
    _, rows, size = parts[0].shape
    other = (rows, count * size + home.shape[2])
    vmem = pl.BlockSpec(memory_space=pltpu.VMEM)
    return pl.pallas_call(
        merge_kernel,
        out_shape=[
            jax.ShapeDtypeStruct((count,) + parts[0].shape, home.dtype),
            jax.ShapeDtypeStruct(other, home.dtype),
        ],
        in_specs=[vmem] * (count + 1),
        out_specs=[vmem, vmem],
        compiler_params=pltpu.CompilerParams(vmem_limit_bytes=4 * MIB),
        cost_estimate=pl.CostEstimate(flops=0, bytes_accessed=6 * rows * other[1], transcendentals=0),
        name="merge",
    )(*parts, home)


def other_core_kernel(*refs):
    parts, out_ref = refs[:-2], refs[-1]
    for k, part in enumerate(parts):
        out_ref[k] = part[1]


def for_other_core(parts, after):
    vmem = pl.BlockSpec(memory_space=pltpu.VMEM)
    _, rows, size = parts[0].shape
    out = jax.ShapeDtypeStruct((len(parts), rows, size), parts[0].dtype)
    return pl.pallas_call(
        other_core_kernel,
        out_shape=out,
        in_specs=[vmem] * len(parts) + [pl.BlockSpec(memory_space=pl.ANY)],
        out_specs=vmem,
        compiler_params=pltpu.CompilerParams(vmem_limit_bytes=4 * MIB),
        cost_estimate=pl.CostEstimate(flops=0, bytes_accessed=4 * out.size, transcendentals=0),
        name="for_other_core",
    )(*parts, after)


def contract_kernel(arrays, packed_other, last, start_ref, me_ref, home_ref, home_other_ref, ints_ref, *refs):
    lhs = refs[-2] if last else refs[-1]
    count, rows, size = lhs.shape
    chips = count // 2 - 1
    start = pl.multiple_of(start_ref[0], 128)
    home_first = home_other_ref.shape[1] - home_ref.shape[2]
    columns = pl.ds(start, size)
    lhs[0] = home_ref[0, :, columns]
    lhs[1] = home_other_ref[:, pl.ds(home_first + start, size)]
    mine, refs = refs[:arrays], refs[arrays:]
    for k in range(chips):
        lhs[2 * k + 2] = mine[0][k, 0] if arrays == 1 else mine[k][0]
        if packed_other:
            lhs[2 * k + 3] = home_other_ref[:, k * size : (k + 1) * size]
        else:
            lhs[2 * k + 3] = refs[0][k, 1] if arrays == 1 else refs[0][k]
    refs = refs if packed_other else refs[1:]
    step = 2560
    total = None
    for first in range(0, size, step):
        width = min(step, size - first)
        block = lhs[:, :, first : first + width].reshape(count * rows, width)
        part = jnp.dot(block, ints_ref[pl.ds(start + first, width)], preferred_element_type=jnp.float32)
        total = part if total is None else total + part
    if not last:
        before, out_ref = refs[:-2], refs[-2]
        out_ref[...] = total + before[0][...] if before else total
        return
    before_ref, out_ref, _, partial = refs
    me = me_ref[0]
    partial[...] = (total + before_ref[...]).reshape(partial.shape)
    for p in range(count):
        out_ref[p, :count] = partial[p ^ me]
        for i in range(count):
            out_ref[p, count + i : count + i + 1] = partial[i ^ me, p : p + 1]


def contract(mine, others, home, home_other, ints, start, me, before=None, last=False, flops=0):
    occupied, size = mine[0].shape[-2:]
    cols = ints.shape[1]
    vmem = pl.BlockSpec(memory_space=pltpu.VMEM)
    operands = [*mine, *others] + ([] if before is None else [before])
    scratch = [pltpu.VMEM((occupied, occupied, size), home.dtype)]
    if last:
        out_shape = jax.ShapeDtypeStruct((occupied, 2 * occupied, cols), jnp.float32)
        scratch.append(pltpu.VMEM((occupied, occupied, cols), jnp.float32))
    else:
        out_shape = jax.ShapeDtypeStruct((occupied * occupied, cols), jnp.float32)
    return pl.pallas_call(
        functools.partial(contract_kernel, len(mine), not others, last),
        out_shape=out_shape,
        in_specs=[pl.BlockSpec(memory_space=pltpu.SMEM)] * 2 + [vmem] * (3 + len(operands)),
        out_specs=vmem,
        scratch_shapes=scratch,
        compiler_params=pltpu.CompilerParams(vmem_limit_bytes=4 * MIB + 16 * occupied * occupied * cols + 4 * occupied * occupied * size),
        cost_estimate=pl.CostEstimate(
            flops=2 * occupied * occupied * size * cols + flops,
            bytes_accessed=2 * size * (cols + occupied * occupied),
            transcendentals=0,
        ),
        name="contract",
    )(start, me, home, home_other, pltpu.with_memory_space_constraint(ints, pltpu.VMEM), *operands)


def select_exactly(values, select):
    rows = values.shape[0]
    high = values.astype(jnp.bfloat16)
    rest = values - high.astype(jnp.float32)
    middle = rest.astype(jnp.bfloat16)
    low = (rest - middle.astype(jnp.float32)).astype(jnp.bfloat16)
    terms = [jnp.dot(term, select, preferred_element_type=jnp.float32) for term in (high, middle, low)]
    return terms[0] + terms[1] + terms[2]


def add_kernel(parts_ref, ladder_ref, mirror_ref):
    total = parts_ref[0]
    for q in range(1, parts_ref.shape[0]):
        total = total + parts_ref[q]
    half = total.shape[0] // 2
    ladder_ref[...] = total[:half]
    mirror_ref[...] = total[half:]


def add_parts(parts):
    _, rows, cols = parts.shape
    half = jax.ShapeDtypeStruct((rows // 2, cols), jnp.float32)
    vmem = pl.BlockSpec(memory_space=pltpu.VMEM)
    return pl.pallas_call(
        add_kernel,
        out_shape=[half, half],
        in_specs=[vmem],
        out_specs=[vmem, vmem],
        compiler_params=pltpu.CompilerParams(vmem_limit_bytes=4 * MIB),
        cost_estimate=pl.CostEstimate(flops=parts.size, bytes_accessed=4 * parts.size, transcendentals=0),
        name="add_parts",
    )(parts)


def finish_kernel(ladder_ref, denominator_ref, select_ref, *refs):
    mirrors, out_ref = refs[:-1], refs[-1]
    mirror = select_exactly(jnp.concatenate([ref[...] for ref in mirrors], axis=1), select_ref[...])
    update = (ladder_ref[...] + mirror) / denominator_ref[...]
    _, first_local, slab_virt = out_ref.shape
    for a in range(first_local):
        out_ref[:, a, :] = update[:, a * slab_virt : (a + 1) * slab_virt]


def finish(ladder, mirrors, denominator, select, first_local, slab_virt):
    rows = ladder.shape[0]
    return pl.pallas_call(
        finish_kernel,
        out_shape=jax.ShapeDtypeStruct((rows, first_local, slab_virt), jnp.float32),
        in_specs=[pl.BlockSpec(memory_space=pltpu.VMEM)] * (3 + len(mirrors)),
        out_specs=pl.BlockSpec(memory_space=pltpu.VMEM),
        compiler_params=pltpu.CompilerParams(vmem_limit_bytes=6 * MIB),
        cost_estimate=pl.CostEstimate(flops=6 * rows * select.size, bytes_accessed=2 * select.size, transcendentals=0),
        name="finish",
    )(ladder, denominator, select, *mirrors)


def swap(values, axis, bits):
    return lax.ppermute(values, axis, [(p, p ^ bits) for p in range(lax.axis_size(axis))])


def local(amplitudes, integrals, virt_irrep, occ_energy, slab_energy):
    pair_count = lax.axis_size("pair")
    slab_count = lax.axis_size("slab")
    occ_local, occupied, virt_pairs = amplitudes.shape
    rows_local, cols_local = integrals.shape
    slab_virt = slab_energy.shape[0]
    first_local = slab_virt // slab_count
    assert occ_local == 1
    slab_index = lax.axis_index("slab").astype(jnp.int32)
    me = lax.axis_index("pair").astype(jnp.int32).reshape(1)
    slab = slab_index.reshape(1)

    shared = int(SHARE * rows_local) // 128 * 128
    parity = slab_index % 2
    own = (parity * shared).reshape(1)
    other = ((1 - parity) * shared).reshape(1)
    rest = jnp.full((1,), 2 * shared, jnp.int32)
    whole = jnp.zeros((1,), jnp.int32)
    amps = amplitudes.reshape(occupied, virt_pairs)
    chips = [2 * k for k in range(1, pair_count // 2)]

    parts = pack(amps, me, own, shared, pair_count, False)
    own_mine = [swap(part, "pair", bits) for part, bits in zip(parts, chips)]
    parts = pack(amps, me, rest, rows_local - 2 * shared, pair_count, False, parts[-1])
    rest_mine = [swap(part, "pair", bits) for part, bits in zip(parts, chips)]
    (home,) = pack(amps, me, whole, rows_local, pair_count, True, parts[-1])

    own_mine, for_other = merge(own_mine, home)
    other_mine = swap(own_mine, "slab", 1)
    home_other = swap(for_other, "pair", 1)
    other_others = swap(other_mine, "pair", 1)
    masked, select, denominator = mask(integrals, me, slab, virt_irrep, occ_energy, slab_energy)
    rest_others = swap(for_other_core(rest_mine, denominator), "pair", 1)
    partial = contract([own_mine], [], home, home_other, masked, own, me)
    partial = contract(rest_mine, [rest_others], home, home_other, masked, rest, me, partial)
    parts = contract([other_mine], [other_others], home, home_other, masked, other, me, partial, True)

    parts = lax.all_to_all(parts, "pair", split_axis=0, concat_axis=0, tiled=True)
    ladder, mirror = add_parts(parts)
    mirrors = [mirror] + [swap(mirror, "slab", bits) for bits in range(1, slab_count)]
    update = finish(ladder, mirrors, denominator, select, first_local, slab_virt)
    return update.reshape(occ_local, occupied, first_local, slab_virt)


def solution(mesh):
    placed = (P("pair", None, None), P("pair", "slab"), P(), P(), P())
    return jax.shard_map(
        local, mesh=mesh, in_specs=placed, out_specs=P("pair", None, "slab", None), check_vma=False
    )
```

```python
import functools
import math

import jax
import jax.numpy as jnp
from jax import lax
from jax.experimental import pallas as pl
from jax.experimental.pallas import tpu as pltpu
from jax.sharding import PartitionSpec as P

IRREPS = 8
MIB = 2**20
SHARE = 0.24
LATE_FLOPS = 10**10
PIECE = 1280


def pack_kernel(rows_local, chip_pairs, me_ref, start_ref, amps_ref, after_ref, *refs):
    outs, (held, packed, sems) = refs[:-3], refs[-3:]
    _, _, size = packed.shape
    count = held.shape[0]
    me = me_ref[0]
    start = pl.multiple_of(start_ref[0], 128)
    loads, shifts = [], []
    for dest in range(count):
        first = dest * rows_local // 128 * 128
        shifts.append(dest * rows_local - first)
        width = -(-(shifts[dest] + size) // 128) * 128
        loads.append(
            pltpu.make_async_copy(
                amps_ref.at[:, pl.ds(start + first, width)], held.at[dest, :, pl.ds(0, width)], sems.at[dest]
            )
        )
        loads[-1].start()
    for dest in range(count):
        loads[dest].wait()
        block = held[dest, :, shifts[dest] : shifts[dest] + size]
        if chip_pairs:
            packed[dest ^ me] = block
        else:
            outs[0][dest] = block
    if chip_pairs:
        for k, out in enumerate(outs):
            out[...] = packed[2 * k : 2 * k + 2]


def pack(amps, me, start, size, pair_count, chip_pairs, after):
    rows, virt_pairs = amps.shape
    held = (pair_count, rows, -(-size // 128) * 128 + 128)
    if chip_pairs:
        out_shape = [jax.ShapeDtypeStruct((2, rows, size), amps.dtype)] * (pair_count // 2)
    else:
        out_shape = [jax.ShapeDtypeStruct((pair_count, rows, size), amps.dtype)]
    return pl.pallas_call(
        functools.partial(pack_kernel, virt_pairs // pair_count, chip_pairs),
        out_shape=out_shape,
        in_specs=[pl.BlockSpec(memory_space=pltpu.SMEM)] * 2
        + [pl.BlockSpec(memory_space=pltpu.HBM), pl.BlockSpec(memory_space=pl.ANY)],
        out_specs=[pl.BlockSpec(memory_space=pltpu.VMEM)] * len(out_shape),
        scratch_shapes=[
            pltpu.VMEM(held, amps.dtype),
            pltpu.VMEM((pair_count if chip_pairs else 1, rows, size), amps.dtype),
            pltpu.SemaphoreType.DMA((pair_count,)),
        ],
        compiler_params=pltpu.CompilerParams(vmem_limit_bytes=2 * MIB + 6 * held[0] * rows * held[2]),
        cost_estimate=pl.CostEstimate(flops=0, bytes_accessed=4 * held[0] * rows * size, transcendentals=0),
        name="pack_chips" if chip_pairs else "pack_devices",
    )(me, start, in_hbm(amps), after)


def in_hbm(array):
    return pltpu.with_memory_space_constraint(array, pltpu.HBM)


def mask_kernel(per_step, parts, me_ref, slab_ref, irrep_ref, occ_ref, virt_ref, row_ref, ints_ref, *refs):
    out_ref, select_ref, denominator_ref, table, padded, by_row = refs
    step = pl.program_id(0)
    chunk, cols = ints_ref.shape[1:]
    slab_virt = virt_ref.shape[0]
    first_local = cols // slab_virt
    bits = slab_virt.bit_length() - 1
    me, slab = me_ref[0], slab_ref[0]

    @pl.when(step == 0)
    def _():
        padded[:, : row_ref.shape[1]] = row_ref[...]
        for k in range(padded.shape[1] // 128):
            lanes = slice(k * 128, (k + 1) * 128)
            by_row[lanes] = jnp.transpose(jnp.broadcast_to(padded[:, lanes], (128, 128)))

        col = lax.broadcasted_iota(jnp.int32, (1, cols), 1)
        a_of, b_of = col >> bits, col & (slab_virt - 1)
        irrep_a = irrep_b = jnp.zeros_like(col)
        energy_a = energy_b = jnp.zeros(col.shape, jnp.float32)
        for a in range(first_local):
            irrep_a = jnp.where(a_of == a, irrep_ref[slab * first_local + a], irrep_a)
            energy_a = jnp.where(a_of == a, virt_ref[slab * first_local + a], energy_a)
        for b in range(slab_virt):
            irrep_b = jnp.where(b_of == b, irrep_ref[b], irrep_b)
            energy_b = jnp.where(b_of == b, virt_ref[b], energy_b)
        irrep_ab = irrep_a ^ irrep_b

        for part in range(parts):
            for lanes in (slice(k, k + 128) for k in range(0, cols, 128)):
                needed = by_row[part * chunk : (part + 1) * chunk] ^ irrep_ab[:, lanes]
                for irrep in range(IRREPS):
                    table[irrep * parts + part, :, lanes] = jnp.where(needed == irrep, 1.0, 0.0).astype(table.dtype)

        occupied = denominator_ref.shape[0]
        j_of = lax.broadcasted_iota(jnp.int32, (occupied, cols), 0)
        energy_j = jnp.zeros((occupied, cols), jnp.float32)
        for j in range(occupied):
            energy_j = jnp.where(j_of == j, occ_ref[j], energy_j)
        denominator_ref[...] = energy_a + energy_b - occ_ref[me] - energy_j

        row = lax.broadcasted_iota(jnp.int32, (cols, cols), 0)
        col = lax.broadcasted_iota(jnp.int32, (cols, cols), 1)
        same_a = (row & (slab_virt - 1)) == slab * first_local + (col >> bits)
        for t in range(select_ref.shape[0] // cols):
            same_b = (slab ^ t) * first_local + (row >> bits) == (col & (slab_virt - 1))
            chosen = jnp.where(same_a & same_b, 1.0, 0.0)
            select_ref[t * cols : (t + 1) * cols] = chosen.astype(select_ref.dtype)

    chunks = per_step * pl.num_programs(0)
    for k in range(per_step):
        index = me * chunks + step * per_step + k
        irrep_c = irrep_ref[index // parts]
        out_ref[k] = ints_ref[k] * table[irrep_c * parts + index % parts]


def mask(integrals, me, slab, virt_irrep, occ_energy, slab_energy):
    virtuals = virt_irrep.shape[0]
    slab_virt = slab_energy.shape[0]
    occupied = occ_energy.shape[0]
    rows_local, cols_local = integrals.shape
    chunk = math.gcd(virtuals, rows_local)
    parts = virtuals // chunk
    chunks = rows_local // chunk
    per_step = next(n for n in (10, 5, 4, 2, 1) if chunks % n == 0)
    padded = -(-virtuals // 128) * 128
    select_rows = slab_virt * slab_virt
    block = pl.BlockSpec((per_step, chunk, cols_local), lambda step: (step, 0, 0))
    scalars = pl.BlockSpec(memory_space=pltpu.SMEM)
    masked, select, denominator = pl.pallas_call(
        functools.partial(mask_kernel, per_step, parts),
        grid=(chunks // per_step,),
        in_specs=[scalars] * 5 + [pl.BlockSpec((1, virtuals), lambda step: (0, 0)), block],
        out_specs=[
            block,
            pl.BlockSpec((select_rows, cols_local), lambda step: (0, 0)),
            pl.BlockSpec((occupied, cols_local), lambda step: (0, 0)),
        ],
        scratch_shapes=[
            pltpu.VMEM((IRREPS * parts, chunk, cols_local), integrals.dtype),
            pltpu.VMEM((1, padded), jnp.int32),
            pltpu.VMEM((padded, 128), jnp.int32),
        ],
        out_shape=[
            pltpu.HBM((chunks, chunk, cols_local), integrals.dtype),
            jax.ShapeDtypeStruct((select_rows, cols_local), jnp.bfloat16),
            jax.ShapeDtypeStruct((occupied, cols_local), jnp.float32),
        ],
        compiler_params=pltpu.CompilerParams(vmem_limit_bytes=16 * MIB),
        cost_estimate=pl.CostEstimate(
            flops=LATE_FLOPS, bytes_accessed=4 * rows_local * cols_local, transcendentals=0
        ),
        name="mask_integrals",
    )(
        me,
        slab,
        *(in_hbm(array) for array in (virt_irrep, occ_energy, slab_energy, virt_irrep.reshape(1, virtuals))),
        in_hbm(integrals.reshape(chunks, chunk, cols_local)),
    )
    return masked.reshape(rows_local, cols_local), select, denominator


def merge_kernel(*refs):
    parts, all_ref, other_ref = refs[:-2], refs[-2], refs[-1]
    for k, part in enumerate(parts):
        other_ref[k] = part[1]
        if k:
            all_ref[k - 1] = part[...]


def merge(parts):
    count = len(parts)
    _, rows, size = parts[0].shape
    vmem = pl.BlockSpec(memory_space=pltpu.VMEM)
    return pl.pallas_call(
        merge_kernel,
        out_shape=[
            jax.ShapeDtypeStruct((count - 1, 2, rows, size), parts[0].dtype),
            jax.ShapeDtypeStruct((count, rows, size), parts[0].dtype),
        ],
        in_specs=[vmem] * count,
        out_specs=[vmem, vmem],
        compiler_params=pltpu.CompilerParams(vmem_limit_bytes=4 * MIB),
        cost_estimate=pl.CostEstimate(flops=0, bytes_accessed=6 * count * rows * size, transcendentals=0),
        name="merge",
    )(*parts)


def stream_dot(lhs, start, size, ints_ref, buffer, sems):
    copies, bounds = [], []
    for first in range(0, size, PIECE):
        width = min(PIECE, size - first)
        rows = pl.ds(first, width)
        copies.append(pltpu.make_async_copy(ints_ref.at[pl.ds(start + first, width)], buffer.at[rows], sems.at[len(copies)]))
        bounds.append((first, first + width))
        copies[-1].start()
    yield
    total = None
    for copy, (first, last) in zip(copies, bounds):
        copy.wait()
        block = lhs[:, :, first:last].reshape(lhs.shape[0] * lhs.shape[1], last - first)
        part = jnp.dot(block, buffer[first:last], preferred_element_type=jnp.float32)
        total = part if total is None else total + part
    yield total


def shared_kernel(start_ref, home_ref, mine_ref, others_ref, ints_ref, before_ref, out_ref, lhs, buffer, sems):
    count, _, size = lhs.shape
    product = stream_dot(lhs, pl.multiple_of(start_ref[0], 128), size, ints_ref, buffer, sems)
    next(product)
    lhs[0] = home_ref[0]
    for k in range(1, count // 2):
        lhs[2 * k] = mine_ref[k - 1, 0]
    for k in range(count // 2):
        lhs[2 * k + 1] = others_ref[k]
    out_ref[...] = next(product) + before_ref[...]


def contract_shared(home, mine, others, ints, start, before):
    count, rows, size = others.shape
    count *= 2
    cols = ints.shape[1]
    vmem = pl.BlockSpec(memory_space=pltpu.VMEM)
    return pl.pallas_call(
        shared_kernel,
        out_shape=jax.ShapeDtypeStruct((count * rows, cols), jnp.float32),
        in_specs=[pl.BlockSpec(memory_space=pltpu.SMEM), vmem, vmem, vmem, pl.BlockSpec(memory_space=pltpu.HBM), vmem],
        out_specs=vmem,
        scratch_shapes=[
            pltpu.VMEM((count, rows, size), ints.dtype),
            pltpu.VMEM((size, cols), ints.dtype),
            pltpu.SemaphoreType.DMA((-(-size // PIECE),)),
        ],
        compiler_params=pltpu.CompilerParams(
            vmem_limit_bytes=4 * MIB + 4 * size * (count * rows + cols) + 16 * count * rows * cols
        ),
        cost_estimate=pl.CostEstimate(
            flops=2 * count * rows * size * cols, bytes_accessed=2 * size * (cols + count * rows), transcendentals=0
        ),
        name="contract_shared",
    )(start, home, mine, others, in_hbm(ints), before)


def rest_kernel(start, me_ref, amps_ref, ints_ref, before_ref, out_ref, partial, buffer, sems):
    count, rows, size = amps_ref.shape
    product = stream_dot(amps_ref, start, size, ints_ref, buffer, sems)
    next(product)
    partial[...] = next(product).reshape(partial.shape)
    me = me_ref[0]
    for i in range(count):
        block = partial[i] + before_ref[i ^ me]
        out_ref[i, :rows] = block
        for j in range(rows):
            out_ref[j, rows + i : rows + i + 1] = block[j : j + 1]


def contract_rest(amps, ints, start, me, before):
    count, rows, size = amps.shape
    cols = ints.shape[1]
    vmem = pl.BlockSpec(memory_space=pltpu.VMEM)
    return pl.pallas_call(
        functools.partial(rest_kernel, start),
        out_shape=jax.ShapeDtypeStruct((count, 2 * rows, cols), jnp.float32),
        in_specs=[pl.BlockSpec(memory_space=pltpu.SMEM), vmem, pl.BlockSpec(memory_space=pltpu.HBM), vmem],
        out_specs=vmem,
        scratch_shapes=[
            pltpu.VMEM((count, rows, cols), jnp.float32),
            pltpu.VMEM((size, cols), ints.dtype),
            pltpu.SemaphoreType.DMA((-(-size // PIECE),)),
        ],
        compiler_params=pltpu.CompilerParams(
            vmem_limit_bytes=4 * MIB + 2 * size * (count * rows + cols) + 24 * count * rows * cols
        ),
        cost_estimate=pl.CostEstimate(
            flops=2 * count * rows * size * cols, bytes_accessed=2 * size * (cols + count * rows), transcendentals=0
        ),
        name="contract_rest",
    )(me, amps, in_hbm(ints), before.reshape(count, rows, cols))


def others_kernel(home_ref, mine_ref, out_ref):
    out_ref[0] = home_ref[1]
    for k in range(1, out_ref.shape[0]):
        out_ref[k] = mine_ref[k - 1, 1]


def merge_others(home, mine):
    vmem = pl.BlockSpec(memory_space=pltpu.VMEM)
    out = jax.ShapeDtypeStruct((mine.shape[0] + 1,) + mine.shape[2:], mine.dtype)
    return pl.pallas_call(
        others_kernel,
        out_shape=out,
        in_specs=[vmem, vmem],
        out_specs=vmem,
        compiler_params=pltpu.CompilerParams(vmem_limit_bytes=4 * MIB),
        cost_estimate=pl.CostEstimate(flops=0, bytes_accessed=4 * out.size, transcendentals=0),
        name="merge_others",
    )(home, mine)


def select_exactly(values, select):
    rows = values.shape[0]
    high = values.astype(jnp.bfloat16)
    rest = values - high.astype(jnp.float32)
    middle = rest.astype(jnp.bfloat16)
    low = (rest - middle.astype(jnp.float32)).astype(jnp.bfloat16)
    terms = [jnp.dot(term, select, preferred_element_type=jnp.float32) for term in (high, middle, low)]
    return terms[0] + terms[1] + terms[2]


def add_kernel(parts_ref, ladder_ref, mirror_ref):
    total = parts_ref[0]
    for q in range(1, parts_ref.shape[0]):
        total = total + parts_ref[q]
    half = total.shape[0] // 2
    ladder_ref[...] = total[:half]
    mirror_ref[...] = total[half:]


def add_parts(parts):
    _, rows, cols = parts.shape
    half = jax.ShapeDtypeStruct((rows // 2, cols), jnp.float32)
    vmem = pl.BlockSpec(memory_space=pltpu.VMEM)
    return pl.pallas_call(
        add_kernel,
        out_shape=[half, half],
        in_specs=[vmem],
        out_specs=[vmem, vmem],
        compiler_params=pltpu.CompilerParams(vmem_limit_bytes=4 * MIB),
        cost_estimate=pl.CostEstimate(flops=parts.size, bytes_accessed=4 * parts.size, transcendentals=0),
        name="add_parts",
    )(parts)


def finish_kernel(ladder_ref, denominator_ref, select_ref, *refs):
    mirrors, out_ref = refs[:-1], refs[-1]
    mirror = select_exactly(jnp.concatenate([ref[...] for ref in mirrors], axis=1), select_ref[...])
    update = (ladder_ref[...] + mirror) / denominator_ref[...]
    _, first_local, slab_virt = out_ref.shape
    for a in range(first_local):
        out_ref[:, a, :] = update[:, a * slab_virt : (a + 1) * slab_virt]


def finish(ladder, mirrors, denominator, select, first_local, slab_virt):
    rows = ladder.shape[0]
    return pl.pallas_call(
        finish_kernel,
        out_shape=jax.ShapeDtypeStruct((rows, first_local, slab_virt), jnp.float32),
        in_specs=[pl.BlockSpec(memory_space=pltpu.VMEM)] * (3 + len(mirrors)),
        out_specs=pl.BlockSpec(memory_space=pltpu.VMEM),
        compiler_params=pltpu.CompilerParams(vmem_limit_bytes=6 * MIB),
        cost_estimate=pl.CostEstimate(flops=6 * rows * select.size, bytes_accessed=2 * select.size, transcendentals=0),
        name="finish",
    )(ladder, denominator, select, *mirrors)


def swap(values, axis, bits):
    return lax.ppermute(values, axis, [(p, p ^ bits) for p in range(lax.axis_size(axis))])


def local(amplitudes, integrals, virt_irrep, occ_energy, slab_energy):
    pair_count = lax.axis_size("pair")
    slab_count = lax.axis_size("slab")
    occ_local, occupied, virt_pairs = amplitudes.shape
    rows_local, cols_local = integrals.shape
    slab_virt = slab_energy.shape[0]
    first_local = slab_virt // slab_count
    assert occ_local == 1
    slab_index = lax.axis_index("slab").astype(jnp.int32)
    me = lax.axis_index("pair").astype(jnp.int32).reshape(1)
    slab = slab_index.reshape(1)

    shared = int(SHARE * rows_local) // 128 * 128
    parity = slab_index % 2
    own = (parity * shared).reshape(1)
    other = ((1 - parity) * shared).reshape(1)
    rest = jnp.full((1,), 2 * shared, jnp.int32)
    amps = amplitudes.reshape(occupied, virt_pairs)

    parts = pack(amps, me, own, shared, pair_count, True, me)
    mine = [parts[0]] + [swap(parts[k], "pair", 2 * k) for k in range(1, pair_count // 2)]
    (packed,) = pack(amps, me, rest, rows_local - 2 * shared, pair_count, False, parts[-1])
    rest_amps = lax.all_to_all(packed, "pair", split_axis=0, concat_axis=0, tiled=True)
    home = pack(amps, me, other, shared, pair_count, True, packed)[0]

    own_mine, for_other = merge(mine)
    other_mine = swap(own_mine, "slab", 1)
    own_others = swap(for_other, "pair", 1)
    masked, select, denominator = mask(integrals, me, slab, virt_irrep, occ_energy, slab_energy)
    zero = jnp.zeros((pair_count * occupied, cols_local), jnp.float32)
    partial = contract_shared(parts[0], own_mine, own_others, masked, own, zero)
    other_others = swap(merge_others(home, other_mine), "pair", 1)
    partial = contract_shared(home, other_mine, other_others, masked, other, partial)
    parts = contract_rest(rest_amps, masked, 2 * shared, me, partial)

    parts = lax.all_to_all(parts, "pair", split_axis=0, concat_axis=0, tiled=True)
    ladder, mirror = add_parts(parts)
    mirrors = [mirror] + [swap(mirror, "slab", bits) for bits in range(1, slab_count)]
    update = finish(ladder, mirrors, denominator, select, first_local, slab_virt)
    return update.reshape(occ_local, occupied, first_local, slab_virt)


def solution(mesh):
    placed = (P("pair", None, None), P("pair", "slab"), P(), P(), P())
    return jax.shard_map(
        local, mesh=mesh, in_specs=placed, out_specs=P("pair", None, "slab", None), check_vma=False
    )
```

```python
import functools
import math

import jax
import jax.numpy as jnp
from jax import lax
from jax.experimental import pallas as pl
from jax.experimental.pallas import tpu as pltpu
from jax.sharding import PartitionSpec as P

IRREPS = 8
MIB = 2**20
SHARE = 0.24
LATE_FLOPS = 10**10


def start_of(part, slab_ref, shared):
    parity = slab_ref[0] % 2
    return pl.multiple_of({"own": parity * shared, "other": (1 - parity) * shared, "rest": 2 * shared, "all": 0}[part], 128)


def pack_kernel(rows_local, shared, which, me_ref, slab_ref, amps_ref, after_ref, *refs):
    outs, (held, packed, sems) = refs[:-3], refs[-3:]
    _, _, size = packed.shape
    count = sems.shape[0]
    home = which == "all"
    me = me_ref[0]
    start = start_of(which, slab_ref, shared)
    loads, shifts = [], []
    for dest in range(count):
        first = dest * rows_local // 128 * 128
        shifts.append(dest * rows_local - first)
        width = -(-(shifts[dest] + size) // 128) * 128
        slot = dest ^ me if home else dest
        loads.append(
            pltpu.make_async_copy(
                amps_ref.at[:, pl.ds(start + first, width)], held.at[slot, :, pl.ds(0, width)], sems.at[dest]
            )
        )

    def wanted(dest):
        return (dest ^ me) // 2 == 0 if home else True

    for dest in range(count):
        pl.when(wanted(dest))(loads[dest].start)
    for dest in range(count):

        @pl.when(wanted(dest))
        def _():
            loads[dest].wait()
            packed[dest ^ me] = held[dest ^ me if home else dest, :, shifts[dest] : shifts[dest] + size]

    for k, out in enumerate(outs):
        slot = 0 if home else 2 * k + 2
        out[...] = packed[slot : slot + 2]


def pack(amps, me, slab, shared, which, pair_count, after=None):
    rows, virt_pairs = amps.shape
    rows_local = virt_pairs // pair_count
    home = which == "all"
    size = {"own": shared, "rest": rows_local - 2 * shared, "all": rows_local}[which]
    held = (2 if home else pair_count, rows, -(-size // 128) * 128 + 128)
    packed = (held[0], rows, size)
    outs = 1 if home else pair_count // 2 - 1
    vmem = 2 * MIB + 6 * held[0] * rows * held[2]
    return pl.pallas_call(
        functools.partial(pack_kernel, rows_local, shared, which),
        out_shape=[jax.ShapeDtypeStruct((2, rows, size), amps.dtype)] * outs,
        in_specs=[pl.BlockSpec(memory_space=pltpu.SMEM)] * 2
        + [pl.BlockSpec(memory_space=pltpu.HBM), pl.BlockSpec(memory_space=pl.ANY)],
        out_specs=[pl.BlockSpec(memory_space=pltpu.VMEM)] * outs,
        scratch_shapes=[
            pltpu.VMEM(held, amps.dtype),
            pltpu.VMEM(packed, amps.dtype),
            pltpu.SemaphoreType.DMA((pair_count,)),
        ],
        compiler_params=pltpu.CompilerParams(vmem_limit_bytes=vmem),
        cost_estimate=pl.CostEstimate(flops=0, bytes_accessed=4 * held[0] * rows * size, transcendentals=0),
        name="pack_home" if home else "pack_amplitudes",
    )(me, slab, pltpu.with_memory_space_constraint(amps, pltpu.HBM), me if after is None else after)


def mask_kernel(per_step, parts, me_ref, slab_ref, irrep_ref, occ_ref, virt_ref, row_ref, ints_ref, *refs):
    out_ref, select_ref, denominator_ref, table, padded, by_row = refs
    step = pl.program_id(0)
    chunk, cols = ints_ref.shape[1:]
    slab_virt = virt_ref.shape[0]
    first_local = cols // slab_virt
    bits = slab_virt.bit_length() - 1
    me, slab = me_ref[0], slab_ref[0]

    @pl.when(step == 0)
    def _():
        padded[:, : row_ref.shape[1]] = row_ref[...]
        for k in range(padded.shape[1] // 128):
            lanes = slice(k * 128, (k + 1) * 128)
            by_row[lanes] = jnp.transpose(jnp.broadcast_to(padded[:, lanes], (128, 128)))

        col = lax.broadcasted_iota(jnp.int32, (1, cols), 1)
        a_of, b_of = col >> bits, col & (slab_virt - 1)
        irrep_a = irrep_b = jnp.zeros_like(col)
        energy_a = energy_b = jnp.zeros(col.shape, jnp.float32)
        for a in range(first_local):
            irrep_a = jnp.where(a_of == a, irrep_ref[slab * first_local + a], irrep_a)
            energy_a = jnp.where(a_of == a, virt_ref[slab * first_local + a], energy_a)
        for b in range(slab_virt):
            irrep_b = jnp.where(b_of == b, irrep_ref[b], irrep_b)
            energy_b = jnp.where(b_of == b, virt_ref[b], energy_b)
        irrep_ab = irrep_a ^ irrep_b

        for part in range(parts):
            for lanes in (slice(k, k + 128) for k in range(0, cols, 128)):
                needed = by_row[part * chunk : (part + 1) * chunk] ^ irrep_ab[:, lanes]
                for irrep in range(IRREPS):
                    table[irrep * parts + part, :, lanes] = jnp.where(needed == irrep, 1.0, 0.0).astype(table.dtype)

        occupied = denominator_ref.shape[0]
        j_of = lax.broadcasted_iota(jnp.int32, (occupied, cols), 0)
        energy_j = jnp.zeros((occupied, cols), jnp.float32)
        for j in range(occupied):
            energy_j = jnp.where(j_of == j, occ_ref[j], energy_j)
        denominator_ref[...] = energy_a + energy_b - occ_ref[me] - energy_j

        row = lax.broadcasted_iota(jnp.int32, (cols, cols), 0)
        col = lax.broadcasted_iota(jnp.int32, (cols, cols), 1)
        same_a = (row & (slab_virt - 1)) == slab * first_local + (col >> bits)
        for t in range(select_ref.shape[0] // cols):
            same_b = (slab ^ t) * first_local + (row >> bits) == (col & (slab_virt - 1))
            chosen = jnp.where(same_a & same_b, 1.0, 0.0)
            select_ref[t * cols : (t + 1) * cols] = chosen.astype(select_ref.dtype)

    chunks = per_step * pl.num_programs(0)
    for k in range(per_step):
        index = me * chunks + step * per_step + k
        irrep_c = irrep_ref[index // parts]
        out_ref[k] = ints_ref[k] * table[irrep_c * parts + index % parts]


def in_hbm(array):
    return pltpu.with_memory_space_constraint(array, pltpu.HBM)


def mask(integrals, me, slab, virt_irrep, occ_energy, slab_energy):
    virtuals = virt_irrep.shape[0]
    slab_virt = slab_energy.shape[0]
    occupied = occ_energy.shape[0]
    rows_local, cols_local = integrals.shape
    chunk = math.gcd(virtuals, rows_local)
    parts = virtuals // chunk
    chunks = rows_local // chunk
    per_step = next(n for n in (10, 5, 4, 2, 1) if chunks % n == 0)
    padded = -(-virtuals // 128) * 128
    select_rows = slab_virt * slab_virt
    block = pl.BlockSpec((per_step, chunk, cols_local), lambda step: (step, 0, 0))
    scalars = pl.BlockSpec(memory_space=pltpu.SMEM)
    masked, select, denominator = pl.pallas_call(
        functools.partial(mask_kernel, per_step, parts),
        grid=(chunks // per_step,),
        in_specs=[scalars] * 5 + [pl.BlockSpec((1, virtuals), lambda step: (0, 0)), block],
        out_specs=[
            block,
            pl.BlockSpec((select_rows, cols_local), lambda step: (0, 0)),
            pl.BlockSpec((occupied, cols_local), lambda step: (0, 0)),
        ],
        scratch_shapes=[
            pltpu.VMEM((IRREPS * parts, chunk, cols_local), integrals.dtype),
            pltpu.VMEM((1, padded), jnp.int32),
            pltpu.VMEM((padded, 128), jnp.int32),
        ],
        out_shape=[
            pltpu.VMEM((chunks, chunk, cols_local), integrals.dtype),
            jax.ShapeDtypeStruct((select_rows, cols_local), jnp.bfloat16),
            jax.ShapeDtypeStruct((occupied, cols_local), jnp.float32),
        ],
        compiler_params=pltpu.CompilerParams(vmem_limit_bytes=16 * MIB),
        cost_estimate=pl.CostEstimate(
            flops=LATE_FLOPS, bytes_accessed=4 * rows_local * cols_local, transcendentals=0
        ),
        name="mask_integrals",
    )(
        me,
        slab,
        *(in_hbm(array) for array in (virt_irrep, occ_energy, slab_energy, virt_irrep.reshape(1, virtuals))),
        in_hbm(integrals.reshape(chunks, chunk, cols_local)),
    )
    return masked.reshape(rows_local, cols_local), select, denominator


def merge_kernel(*refs):
    parts, home_ref, all_ref, other_ref = refs[:-3], refs[-3], refs[-2], refs[-1]
    size = parts[0].shape[2]
    for k, part in enumerate(parts):
        all_ref[k] = part[...]
        other_ref[:, k * size : (k + 1) * size] = part[1]
    other_ref[:, len(parts) * size :] = home_ref[1]


def merge(parts, home):
    count = len(parts)
    _, rows, size = parts[0].shape
    other = (rows, count * size + home.shape[2])
    vmem = pl.BlockSpec(memory_space=pltpu.VMEM)
    return pl.pallas_call(
        merge_kernel,
        out_shape=[
            jax.ShapeDtypeStruct((count,) + parts[0].shape, home.dtype),
            jax.ShapeDtypeStruct(other, home.dtype),
        ],
        in_specs=[vmem] * (count + 1),
        out_specs=[vmem, vmem],
        compiler_params=pltpu.CompilerParams(vmem_limit_bytes=4 * MIB),
        cost_estimate=pl.CostEstimate(flops=0, bytes_accessed=6 * rows * other[1], transcendentals=0),
        name="merge",
    )(*parts, home)


def other_core_kernel(*refs):
    parts, out_ref = refs[:-2], refs[-1]
    for k, part in enumerate(parts):
        out_ref[k] = part[1]


def for_other_core(parts, after):
    vmem = pl.BlockSpec(memory_space=pltpu.VMEM)
    _, rows, size = parts[0].shape
    out = jax.ShapeDtypeStruct((len(parts), rows, size), parts[0].dtype)
    return pl.pallas_call(
        other_core_kernel,
        out_shape=out,
        in_specs=[vmem] * len(parts) + [pl.BlockSpec(memory_space=pl.ANY)],
        out_specs=vmem,
        compiler_params=pltpu.CompilerParams(vmem_limit_bytes=4 * MIB),
        cost_estimate=pl.CostEstimate(flops=0, bytes_accessed=4 * out.size, transcendentals=0),
        name="for_other_core",
    )(*parts, after)


def contract_kernel(arrays, packed_other, last, shared, which, slab_ref, me_ref, home_ref, home_other_ref, ints_ref, *refs):
    lhs = refs[-2] if last else refs[-1]
    count, rows, size = lhs.shape
    chips = count // 2 - 1
    start = start_of(which, slab_ref, shared)
    home_first = home_other_ref.shape[1] - home_ref.shape[2]
    columns = pl.ds(start, size)
    lhs[0] = home_ref[0, :, columns]
    lhs[1] = home_other_ref[:, pl.ds(home_first + start, size)]
    mine, refs = refs[:arrays], refs[arrays:]
    for k in range(chips):
        lhs[2 * k + 2] = mine[0][k, 0] if arrays == 1 else mine[k][0]
        if packed_other:
            lhs[2 * k + 3] = home_other_ref[:, k * size : (k + 1) * size]
        else:
            lhs[2 * k + 3] = refs[0][k, 1] if arrays == 1 else refs[0][k]
    refs = refs if packed_other else refs[1:]
    step = 2560
    total = None
    for first in range(0, size, step):
        width = min(step, size - first)
        block = lhs[:, :, first : first + width].reshape(count * rows, width)
        part = jnp.dot(block, ints_ref[pl.ds(start + first, width)], preferred_element_type=jnp.float32)
        total = part if total is None else total + part
    if not last:
        before, out_ref = refs[:-2], refs[-2]
        out_ref[...] = total + before[0][...] if before else total
        return
    before_ref, out_ref, _, partial = refs
    me = me_ref[0]
    partial[...] = (total + before_ref[...]).reshape(partial.shape)
    for i in range(count):
        block = partial[i ^ me]
        out_ref[i, :count] = block
        for j in range(count):
            out_ref[j, count + i : count + i + 1] = block[j : j + 1]


def contract(mine, others, home, home_other, ints, me, slab, shared, which, before=None, last=False):
    occupied, size = mine[0].shape[-2:]
    cols = ints.shape[1]
    vmem = pl.BlockSpec(memory_space=pltpu.VMEM)
    operands = [*mine, *others] + ([] if before is None else [before])
    scratch = [pltpu.VMEM((occupied, occupied, size), home.dtype)]
    if last:
        out_shape = jax.ShapeDtypeStruct((occupied, 2 * occupied, cols), jnp.float32)
        scratch.append(pltpu.VMEM((occupied, occupied, cols), jnp.float32))
    else:
        out_shape = jax.ShapeDtypeStruct((occupied * occupied, cols), jnp.float32)
    return pl.pallas_call(
        functools.partial(contract_kernel, len(mine), not others, last, shared, which),
        out_shape=out_shape,
        in_specs=[pl.BlockSpec(memory_space=pltpu.SMEM)] * 2 + [vmem] * (3 + len(operands)),
        out_specs=vmem,
        scratch_shapes=scratch,
        compiler_params=pltpu.CompilerParams(vmem_limit_bytes=4 * MIB + 16 * occupied * occupied * cols + 4 * occupied * occupied * size),
        cost_estimate=pl.CostEstimate(
            flops=2 * occupied * occupied * size * cols,
            bytes_accessed=2 * size * (cols + occupied * occupied),
            transcendentals=0,
        ),
        name="contract",
    )(slab, me, home, home_other, pltpu.with_memory_space_constraint(ints, pltpu.VMEM), *operands)


def select_exactly(values, select):
    rows = values.shape[0]
    high = values.astype(jnp.bfloat16)
    rest = values - high.astype(jnp.float32)
    middle = rest.astype(jnp.bfloat16)
    low = (rest - middle.astype(jnp.float32)).astype(jnp.bfloat16)
    terms = [jnp.dot(term, select, preferred_element_type=jnp.float32) for term in (high, middle, low)]
    return terms[0] + terms[1] + terms[2]


def add_kernel(parts_ref, ladder_ref, mirror_ref):
    total = parts_ref[0]
    for q in range(1, parts_ref.shape[0]):
        total = total + parts_ref[q]
    half = total.shape[0] // 2
    ladder_ref[...] = total[:half]
    mirror_ref[...] = total[half:]


def add_parts(parts):
    _, rows, cols = parts.shape
    half = jax.ShapeDtypeStruct((rows // 2, cols), jnp.float32)
    vmem = pl.BlockSpec(memory_space=pltpu.VMEM)
    return pl.pallas_call(
        add_kernel,
        out_shape=[half, half],
        in_specs=[vmem],
        out_specs=[vmem, vmem],
        compiler_params=pltpu.CompilerParams(vmem_limit_bytes=4 * MIB),
        cost_estimate=pl.CostEstimate(flops=parts.size, bytes_accessed=4 * parts.size, transcendentals=0),
        name="add_parts",
    )(parts)


def finish_kernel(ladder_ref, denominator_ref, select_ref, *refs):
    mirrors, out_ref = refs[:-1], refs[-1]
    mirror = select_exactly(jnp.concatenate([ref[...] for ref in mirrors], axis=1), select_ref[...])
    update = (ladder_ref[...] + mirror) / denominator_ref[...]
    _, first_local, slab_virt = out_ref.shape
    for a in range(first_local):
        out_ref[:, a, :] = update[:, a * slab_virt : (a + 1) * slab_virt]


def finish(ladder, mirrors, denominator, select, first_local, slab_virt):
    rows = ladder.shape[0]
    return pl.pallas_call(
        finish_kernel,
        out_shape=jax.ShapeDtypeStruct((rows, first_local, slab_virt), jnp.float32),
        in_specs=[pl.BlockSpec(memory_space=pltpu.VMEM)] * (3 + len(mirrors)),
        out_specs=pl.BlockSpec(memory_space=pltpu.VMEM),
        compiler_params=pltpu.CompilerParams(vmem_limit_bytes=6 * MIB),
        cost_estimate=pl.CostEstimate(flops=6 * rows * select.size, bytes_accessed=2 * select.size, transcendentals=0),
        name="finish",
    )(ladder, denominator, select, *mirrors)


def swap(values, axis, bits):
    return lax.ppermute(values, axis, [(p, p ^ bits) for p in range(lax.axis_size(axis))])


def local(amplitudes, integrals, virt_irrep, occ_energy, slab_energy):
    pair_count = lax.axis_size("pair")
    slab_count = lax.axis_size("slab")
    occ_local, occupied, virt_pairs = amplitudes.shape
    rows_local, cols_local = integrals.shape
    slab_virt = slab_energy.shape[0]
    first_local = slab_virt // slab_count
    assert occ_local == 1
    me = lax.axis_index("pair").astype(jnp.int32).reshape(1)
    slab = lax.axis_index("slab").astype(jnp.int32).reshape(1)

    shared = int(SHARE * rows_local) // 128 * 128
    amps = amplitudes.reshape(occupied, virt_pairs)
    chips = [2 * k for k in range(1, pair_count // 2)]

    parts = pack(amps, me, slab, shared, "own", pair_count)
    own_mine = [swap(part, "pair", bits) for part, bits in zip(parts, chips)]
    parts = pack(amps, me, slab, shared, "rest", pair_count, parts[-1])
    rest_mine = [swap(part, "pair", bits) for part, bits in zip(parts, chips)]
    (home,) = pack(amps, me, slab, shared, "all", pair_count, parts[-1])

    own_mine, for_other = merge(own_mine, home)
    other_mine = swap(own_mine, "slab", 1)
    home_other = swap(for_other, "pair", 1)
    other_others = swap(other_mine, "pair", 1)
    masked, select, denominator = mask(integrals, me, slab, virt_irrep, occ_energy, slab_energy)
    rest_others = swap(for_other_core(rest_mine, denominator), "pair", 1)
    partial = contract([own_mine], [], home, home_other, masked, me, slab, shared, "own")
    partial = contract(rest_mine, [rest_others], home, home_other, masked, me, slab, shared, "rest", partial)
    parts = contract([other_mine], [other_others], home, home_other, masked, me, slab, shared, "other", partial, True)

    parts = lax.all_to_all(parts, "pair", split_axis=0, concat_axis=0, tiled=True)
    ladder, mirror = add_parts(parts)
    mirrors = [mirror] + [swap(mirror, "slab", bits) for bits in range(1, slab_count)]
    update = finish(ladder, mirrors, denominator, select, first_local, slab_virt)
    return update.reshape(occ_local, occupied, first_local, slab_virt)


def solution(mesh):
    placed = (P("pair", None, None), P("pair", "slab"), P(), P(), P())
    return jax.shard_map(
        local, mesh=mesh, in_specs=placed, out_specs=P("pair", None, "slab", None), check_vma=False
    )
```

```python
import functools
import math

import jax
import jax.numpy as jnp
from jax import lax
from jax.experimental import pallas as pl
from jax.experimental.pallas import tpu as pltpu
from jax.sharding import PartitionSpec as P

IRREPS = 8
MIB = 2**20
SHARE = 0.27
LATE_FLOPS = 10**10


def start_of(part, slab_ref, shared):
    parity = slab_ref[0] % 2
    return pl.multiple_of({"own": parity * shared, "other": (1 - parity) * shared, "rest": 2 * shared, "all": 0}[part], 128)


def pack_kernel(rows_local, shared, which, me_ref, slab_ref, amps_ref, after_ref, *refs):
    outs, (held, packed, sems) = refs[:-3], refs[-3:]
    _, _, size = packed.shape
    count = sems.shape[0]
    home = which == "all"
    me = me_ref[0]
    start = start_of(which, slab_ref, shared)
    loads, shifts = [], []
    for dest in range(count):
        first = dest * rows_local // 128 * 128
        shifts.append(dest * rows_local - first)
        width = -(-(shifts[dest] + size) // 128) * 128
        slot = dest ^ me if home else dest
        loads.append(
            pltpu.make_async_copy(
                amps_ref.at[:, pl.ds(start + first, width)], held.at[slot, :, pl.ds(0, width)], sems.at[dest]
            )
        )

    def wanted(dest):
        return (dest ^ me) // 2 == 0 if home else True

    for dest in range(count):
        pl.when(wanted(dest))(loads[dest].start)
    for dest in range(count):

        @pl.when(wanted(dest))
        def _():
            loads[dest].wait()
            packed[dest ^ me] = held[dest ^ me if home else dest, :, shifts[dest] : shifts[dest] + size]

    for k, out in enumerate(outs):
        slot = 0 if home else 2 * k + 2
        out[...] = packed[slot : slot + 2]


def pack(amps, me, slab, shared, which, pair_count, after=None):
    rows, virt_pairs = amps.shape
    rows_local = virt_pairs // pair_count
    home = which == "all"
    size = {"own": shared, "rest": rows_local - 2 * shared, "all": rows_local}[which]
    held = (2 if home else pair_count, rows, -(-size // 128) * 128 + 128)
    packed = (held[0], rows, size)
    outs = 1 if home else pair_count // 2 - 1
    vmem = 2 * MIB + 6 * held[0] * rows * held[2]
    return pl.pallas_call(
        functools.partial(pack_kernel, rows_local, shared, which),
        out_shape=[jax.ShapeDtypeStruct((2, rows, size), amps.dtype)] * outs,
        in_specs=[pl.BlockSpec(memory_space=pltpu.SMEM)] * 2
        + [pl.BlockSpec(memory_space=pltpu.HBM), pl.BlockSpec(memory_space=pl.ANY)],
        out_specs=[pl.BlockSpec(memory_space=pltpu.VMEM)] * outs,
        scratch_shapes=[
            pltpu.VMEM(held, amps.dtype),
            pltpu.VMEM(packed, amps.dtype),
            pltpu.SemaphoreType.DMA((pair_count,)),
        ],
        compiler_params=pltpu.CompilerParams(vmem_limit_bytes=vmem),
        cost_estimate=pl.CostEstimate(flops=0, bytes_accessed=4 * held[0] * rows * size, transcendentals=0),
        name="pack_home" if home else "pack_amplitudes",
    )(me, slab, pltpu.with_memory_space_constraint(amps, pltpu.HBM), me if after is None else after)


def mask_kernel(per_step, parts, me_ref, slab_ref, irrep_ref, occ_ref, virt_ref, row_ref, ints_ref, *refs):
    out_ref, select_ref, denominator_ref, table, padded, by_row = refs
    step = pl.program_id(0)
    chunk, cols = ints_ref.shape[1:]
    slab_virt = virt_ref.shape[0]
    first_local = cols // slab_virt
    bits = slab_virt.bit_length() - 1
    me, slab = me_ref[0], slab_ref[0]

    @pl.when(step == 0)
    def _():
        padded[:, : row_ref.shape[1]] = row_ref[...]
        for k in range(padded.shape[1] // 128):
            lanes = slice(k * 128, (k + 1) * 128)
            by_row[lanes] = jnp.transpose(jnp.broadcast_to(padded[:, lanes], (128, 128)))

        col = lax.broadcasted_iota(jnp.int32, (1, cols), 1)
        a_of, b_of = col >> bits, col & (slab_virt - 1)
        irrep_a = irrep_b = jnp.zeros_like(col)
        energy_a = energy_b = jnp.zeros(col.shape, jnp.float32)
        for a in range(first_local):
            irrep_a = jnp.where(a_of == a, irrep_ref[slab * first_local + a], irrep_a)
            energy_a = jnp.where(a_of == a, virt_ref[slab * first_local + a], energy_a)
        for b in range(slab_virt):
            irrep_b = jnp.where(b_of == b, irrep_ref[b], irrep_b)
            energy_b = jnp.where(b_of == b, virt_ref[b], energy_b)
        irrep_ab = irrep_a ^ irrep_b

        for part in range(parts):
            for lanes in (slice(k, k + 128) for k in range(0, cols, 128)):
                needed = by_row[part * chunk : (part + 1) * chunk] ^ irrep_ab[:, lanes]
                for irrep in range(IRREPS):
                    table[irrep * parts + part, :, lanes] = jnp.where(needed == irrep, 1.0, 0.0).astype(table.dtype)

        occupied = denominator_ref.shape[0]
        j_of = lax.broadcasted_iota(jnp.int32, (occupied, cols), 0)
        energy_j = jnp.zeros((occupied, cols), jnp.float32)
        for j in range(occupied):
            energy_j = jnp.where(j_of == j, occ_ref[j], energy_j)
        denominator_ref[...] = energy_a + energy_b - occ_ref[me] - energy_j

        row = lax.broadcasted_iota(jnp.int32, (cols, cols), 0)
        col = lax.broadcasted_iota(jnp.int32, (cols, cols), 1)
        same_a = (row & (slab_virt - 1)) == slab * first_local + (col >> bits)
        for t in range(select_ref.shape[0] // cols):
            same_b = (slab ^ t) * first_local + (row >> bits) == (col & (slab_virt - 1))
            chosen = jnp.where(same_a & same_b, 1.0, 0.0)
            select_ref[t * cols : (t + 1) * cols] = chosen.astype(select_ref.dtype)

    chunks = per_step * pl.num_programs(0)
    for k in range(per_step):
        index = me * chunks + step * per_step + k
        irrep_c = irrep_ref[index // parts]
        out_ref[k] = ints_ref[k] * table[irrep_c * parts + index % parts]


def in_hbm(array):
    return pltpu.with_memory_space_constraint(array, pltpu.HBM)


def mask(integrals, me, slab, virt_irrep, occ_energy, slab_energy):
    virtuals = virt_irrep.shape[0]
    slab_virt = slab_energy.shape[0]
    occupied = occ_energy.shape[0]
    rows_local, cols_local = integrals.shape
    chunk = math.gcd(virtuals, rows_local)
    parts = virtuals // chunk
    chunks = rows_local // chunk
    per_step = next(n for n in (10, 5, 4, 2, 1) if chunks % n == 0)
    padded = -(-virtuals // 128) * 128
    select_rows = slab_virt * slab_virt
    block = pl.BlockSpec((per_step, chunk, cols_local), lambda step: (step, 0, 0))
    scalars = pl.BlockSpec(memory_space=pltpu.SMEM)
    masked, select, denominator = pl.pallas_call(
        functools.partial(mask_kernel, per_step, parts),
        grid=(chunks // per_step,),
        in_specs=[scalars] * 5 + [pl.BlockSpec((1, virtuals), lambda step: (0, 0)), block],
        out_specs=[
            block,
            pl.BlockSpec((select_rows, cols_local), lambda step: (0, 0)),
            pl.BlockSpec((occupied, cols_local), lambda step: (0, 0)),
        ],
        scratch_shapes=[
            pltpu.VMEM((IRREPS * parts, chunk, cols_local), integrals.dtype),
            pltpu.VMEM((1, padded), jnp.int32),
            pltpu.VMEM((padded, 128), jnp.int32),
        ],
        out_shape=[
            pltpu.VMEM((chunks, chunk, cols_local), integrals.dtype),
            jax.ShapeDtypeStruct((select_rows, cols_local), jnp.bfloat16),
            jax.ShapeDtypeStruct((occupied, cols_local), jnp.float32),
        ],
        compiler_params=pltpu.CompilerParams(vmem_limit_bytes=16 * MIB),
        cost_estimate=pl.CostEstimate(
            flops=LATE_FLOPS, bytes_accessed=4 * rows_local * cols_local, transcendentals=0
        ),
        name="mask_integrals",
    )(
        me,
        slab,
        *(in_hbm(array) for array in (virt_irrep, occ_energy, slab_energy, virt_irrep.reshape(1, virtuals))),
        in_hbm(integrals.reshape(chunks, chunk, cols_local)),
    )
    return masked.reshape(rows_local, cols_local), select, denominator


def merge_kernel(*refs):
    parts, home_ref, all_ref, other_ref = refs[:-3], refs[-3], refs[-2], refs[-1]
    size = parts[0].shape[2]
    for k, part in enumerate(parts):
        all_ref[k] = part[...]
        other_ref[:, k * size : (k + 1) * size] = part[1]
    other_ref[:, len(parts) * size :] = home_ref[1]


def merge(parts, home):
    count = len(parts)
    _, rows, size = parts[0].shape
    other = (rows, count * size + home.shape[2])
    vmem = pl.BlockSpec(memory_space=pltpu.VMEM)
    return pl.pallas_call(
        merge_kernel,
        out_shape=[
            jax.ShapeDtypeStruct((count,) + parts[0].shape, home.dtype),
            jax.ShapeDtypeStruct(other, home.dtype),
        ],
        in_specs=[vmem] * (count + 1),
        out_specs=[vmem, vmem],
        compiler_params=pltpu.CompilerParams(vmem_limit_bytes=4 * MIB),
        cost_estimate=pl.CostEstimate(flops=0, bytes_accessed=6 * rows * other[1], transcendentals=0),
        name="merge",
    )(*parts, home)


def other_core_kernel(*refs):
    parts, out_ref = refs[:-2], refs[-1]
    for k, part in enumerate(parts):
        out_ref[k] = part[1]


def for_other_core(parts, after):
    vmem = pl.BlockSpec(memory_space=pltpu.VMEM)
    _, rows, size = parts[0].shape
    out = jax.ShapeDtypeStruct((len(parts), rows, size), parts[0].dtype)
    return pl.pallas_call(
        other_core_kernel,
        out_shape=out,
        in_specs=[vmem] * len(parts) + [pl.BlockSpec(memory_space=pl.ANY)],
        out_specs=vmem,
        compiler_params=pltpu.CompilerParams(vmem_limit_bytes=4 * MIB),
        cost_estimate=pl.CostEstimate(flops=LATE_FLOPS // 2, bytes_accessed=4 * out.size, transcendentals=0),
        name="for_other_core",
    )(*parts, after)


def contract_kernel(which, shared, slab_ref, me_ref, home_ref, home_other_ref, ints_ref, *refs):
    last = which == "other"
    lhs = refs[-2] if last else refs[-1]
    count, rows, size = lhs.shape
    chips = count // 2 - 1
    start = start_of(which, slab_ref, shared)
    home_first = home_other_ref.shape[1] - home_ref.shape[2]
    lhs[0] = home_ref[0, :, pl.ds(start, size)]
    lhs[1] = home_other_ref[:, pl.ds(home_first + start, size)]
    for k in range(chips):
        lhs[2 * k + 2] = refs[k][0] if which == "rest" else refs[0][k, 0]
        if which == "own":
            lhs[2 * k + 3] = home_other_ref[:, k * size : (k + 1) * size]
        elif which == "other":
            lhs[2 * k + 3] = refs[1][k, 1]
        else:
            lhs[2 * k + 3] = refs[chips][k]
    refs = refs[{"own": 1, "other": 2, "rest": chips + 1}[which] :]
    step = 2560
    total = None
    for first in range(0, size, step):
        width = min(step, size - first)
        block = lhs[:, :, first : first + width].reshape(count * rows, width)
        part = jnp.dot(block, ints_ref[pl.ds(start + first, width)], preferred_element_type=jnp.float32)
        total = part if total is None else total + part
    if not last:
        before, out_ref = refs[:-2], refs[-2]
        out_ref[...] = total + before[0][...] if before else total
        return
    before_ref, own_ref, other_ref, _, partial = refs
    me = me_ref[0]
    partial[:count, :rows] = (total + before_ref[...]).reshape(count, rows, total.shape[1])
    for i in range(count):
        block = partial[i ^ me, :rows]
        partial[count + (i ^ me), :rows] = block
        for j in range(rows):
            partial[count + (j ^ me), rows + i : rows + i + 1] = block[j : j + 1]
    for k in range(count // 2):
        own_ref[k] = partial[count + 2 * k]
        other_ref[k] = partial[count + 2 * k + 1]


def contract(amps, home, home_other, ints, me, slab, shared, which, before=None):
    occupied, size = amps[0].shape[-2:]
    cols = ints.shape[1]
    vmem = pl.BlockSpec(memory_space=pltpu.VMEM)
    operands = [*amps] + ([] if before is None else [before])
    scratch = [pltpu.VMEM((occupied, occupied, size), home.dtype)]
    if which == "other":
        out_shape = [jax.ShapeDtypeStruct((occupied // 2, 2 * occupied, cols), jnp.float32)] * 2
        scratch.append(pltpu.VMEM((2 * occupied, 2 * occupied, cols), jnp.float32))
    else:
        out_shape = [jax.ShapeDtypeStruct((occupied * occupied, cols), jnp.float32)]
    return pl.pallas_call(
        functools.partial(contract_kernel, which, shared),
        out_shape=out_shape,
        in_specs=[pl.BlockSpec(memory_space=pltpu.SMEM)] * 2 + [vmem] * (3 + len(operands)),
        out_specs=[vmem] * len(out_shape),
        scratch_shapes=scratch,
        compiler_params=pltpu.CompilerParams(
            vmem_limit_bytes=4 * MIB + 40 * occupied * occupied * cols + 4 * occupied * occupied * size
        ),
        cost_estimate=pl.CostEstimate(
            flops=2 * occupied * occupied * size * cols,
            bytes_accessed=2 * size * (cols + occupied * occupied),
            transcendentals=0,
        ),
        name="contract",
    )(slab, me, home, home_other, pltpu.with_memory_space_constraint(ints, pltpu.VMEM), *operands)


def select_exactly(values, select):
    rows = values.shape[0]
    high = values.astype(jnp.bfloat16)
    rest = values - high.astype(jnp.float32)
    middle = rest.astype(jnp.bfloat16)
    low = (rest - middle.astype(jnp.float32)).astype(jnp.bfloat16)
    terms = [jnp.dot(term, select, preferred_element_type=jnp.float32) for term in (high, middle, low)]
    return terms[0] + terms[1] + terms[2]


def add_cores_kernel(mine_ref, other_ref, *outs):
    for k, out in enumerate(outs):
        out[...] = mine_ref[k] + other_ref[k]


def add_cores(mine, other):
    count, rows, cols = mine.shape
    vmem = pl.BlockSpec(memory_space=pltpu.VMEM)
    return pl.pallas_call(
        add_cores_kernel,
        out_shape=[jax.ShapeDtypeStruct((rows, cols), jnp.float32)] * count,
        in_specs=[vmem, vmem],
        out_specs=[vmem] * count,
        compiler_params=pltpu.CompilerParams(vmem_limit_bytes=4 * MIB),
        cost_estimate=pl.CostEstimate(flops=mine.size, bytes_accessed=12 * mine.size, transcendentals=0),
        name="add_cores",
    )(mine, other)


def add_chips_kernel(*refs):
    parts, (ladder_ref, mirror_ref) = refs[:-2], refs[-2:]
    total = parts[0][...]
    for part in parts[1:]:
        total = total + part[...]
    half = total.shape[0] // 2
    ladder_ref[...] = total[:half]
    mirror_ref[...] = total[half:]


def add_chips(parts):
    rows, cols = parts[0].shape
    half = jax.ShapeDtypeStruct((rows // 2, cols), jnp.float32)
    vmem = pl.BlockSpec(memory_space=pltpu.VMEM)
    return pl.pallas_call(
        add_chips_kernel,
        out_shape=[half, half],
        in_specs=[vmem] * len(parts),
        out_specs=[vmem, vmem],
        compiler_params=pltpu.CompilerParams(vmem_limit_bytes=4 * MIB),
        cost_estimate=pl.CostEstimate(
            flops=len(parts) * rows * cols, bytes_accessed=4 * len(parts) * rows * cols, transcendentals=0
        ),
        name="add_chips",
    )(*parts)


def finish_kernel(ladder_ref, denominator_ref, select_ref, *refs):
    mirrors, out_ref = refs[:-1], refs[-1]
    mirror = select_exactly(jnp.concatenate([ref[...] for ref in mirrors], axis=1), select_ref[...])
    update = (ladder_ref[...] + mirror) / denominator_ref[...]
    _, first_local, slab_virt = out_ref.shape
    for a in range(first_local):
        out_ref[:, a, :] = update[:, a * slab_virt : (a + 1) * slab_virt]


def finish(ladder, mirrors, denominator, select, first_local, slab_virt):
    rows = ladder.shape[0]
    return pl.pallas_call(
        finish_kernel,
        out_shape=jax.ShapeDtypeStruct((rows, first_local, slab_virt), jnp.float32),
        in_specs=[pl.BlockSpec(memory_space=pltpu.VMEM)] * (3 + len(mirrors)),
        out_specs=pl.BlockSpec(memory_space=pltpu.VMEM),
        compiler_params=pltpu.CompilerParams(vmem_limit_bytes=6 * MIB),
        cost_estimate=pl.CostEstimate(flops=6 * rows * select.size, bytes_accessed=2 * select.size, transcendentals=0),
        name="finish",
    )(ladder, denominator, select, *mirrors)


def swap(values, axis, bits):
    return lax.ppermute(values, axis, [(p, p ^ bits) for p in range(lax.axis_size(axis))])


def local(amplitudes, integrals, virt_irrep, occ_energy, slab_energy):
    pair_count = lax.axis_size("pair")
    slab_count = lax.axis_size("slab")
    occ_local, occupied, virt_pairs = amplitudes.shape
    rows_local, cols_local = integrals.shape
    slab_virt = slab_energy.shape[0]
    first_local = slab_virt // slab_count
    assert occ_local == 1
    me = lax.axis_index("pair").astype(jnp.int32).reshape(1)
    slab = lax.axis_index("slab").astype(jnp.int32).reshape(1)

    shared = int(SHARE * rows_local) // 128 * 128
    amps = amplitudes.reshape(occupied, virt_pairs)
    chips = [2 * k for k in range(1, pair_count // 2)]

    def to_chips(parts):
        return [swap(part, "pair", bits) for part, bits in zip(parts, chips)]

    parts = pack(amps, me, slab, shared, "own", pair_count)
    own_amps = to_chips(parts)
    parts = pack(amps, me, slab, shared, "rest", pair_count, parts[-1])
    rest_amps = to_chips(parts)
    (home,) = pack(amps, me, slab, shared, "all", pair_count, parts[-1])

    own_amps, for_other = merge(own_amps, home)
    other_amps = swap(own_amps, "slab", 1)
    home_other = swap(for_other, "pair", 1)
    masked, select, denominator = mask(integrals, me, slab, virt_irrep, occ_energy, slab_energy)
    rest_others = swap(for_other_core(rest_amps, denominator), "pair", 1)
    place = (home, home_other, masked, me, slab, shared)
    (partial,) = contract([own_amps], *place, "own")
    (partial,) = contract([*rest_amps, rest_others], *place, "rest", partial)
    this_core, other_core = contract([other_amps, swap(other_amps, "pair", 1)], *place, "other", partial)

    parts = add_cores(this_core, swap(other_core, "pair", 1))
    ladder, mirror = add_chips([parts[0], *to_chips(parts[1:])])
    mirrors = [mirror] + [swap(mirror, "slab", bits) for bits in range(1, slab_count)]
    update = finish(ladder, mirrors, denominator, select, first_local, slab_virt)
    return update.reshape(occ_local, occupied, first_local, slab_virt)


def solution(mesh):
    placed = (P("pair", None, None), P("pair", "slab"), P(), P(), P())
    return jax.shard_map(
        local, mesh=mesh, in_specs=placed, out_specs=P("pair", None, "slab", None), check_vma=False
    )
```

```python
import functools
import math

import jax
import jax.numpy as jnp
from jax import lax
from jax.experimental import pallas as pl
from jax.experimental.pallas import tpu as pltpu
from jax.sharding import PartitionSpec as P

IRREPS = 8
MIB = 2**20
SHARE = 0.25
LATE_FLOPS = 10**10


def start_of(part, slab_ref, shared):
    parity = slab_ref[0] % 2
    return pl.multiple_of({"own": parity * shared, "other": (1 - parity) * shared, "rest": 2 * shared, "all": 0}[part], 128)


def pack_kernel(rows_local, shared, which, me_ref, slab_ref, amps_ref, after_ref, *refs):
    outs, (held, packed, sems) = refs[:-3], refs[-3:]
    _, _, size = packed.shape
    count = sems.shape[0]
    home = which == "all"
    me = me_ref[0]
    start = start_of(which, slab_ref, shared)
    loads, shifts = [], []
    for dest in range(count):
        first = dest * rows_local // 128 * 128
        shifts.append(dest * rows_local - first)
        width = -(-(shifts[dest] + size) // 128) * 128
        slot = dest ^ me if home else dest
        loads.append(
            pltpu.make_async_copy(
                amps_ref.at[:, pl.ds(start + first, width)], held.at[slot, :, pl.ds(0, width)], sems.at[dest]
            )
        )

    def wanted(dest):
        return (dest ^ me) // 2 == 0 if home else True

    for dest in range(count):
        pl.when(wanted(dest))(loads[dest].start)
    for dest in range(count):

        @pl.when(wanted(dest))
        def _():
            loads[dest].wait()
            packed[dest ^ me] = held[dest ^ me if home else dest, :, shifts[dest] : shifts[dest] + size]

    for k, out in enumerate(outs):
        slot = 0 if home else 2 * k + 2
        out[...] = packed[slot : slot + 2]


def pack(amps, me, slab, shared, which, pair_count, after=None):
    rows, virt_pairs = amps.shape
    rows_local = virt_pairs // pair_count
    home = which == "all"
    size = {"own": shared, "rest": rows_local - 2 * shared, "all": rows_local}[which]
    held = (2 if home else pair_count, rows, -(-size // 128) * 128 + 128)
    packed = (held[0], rows, size)
    outs = 1 if home else pair_count // 2 - 1
    vmem = 2 * MIB + 6 * held[0] * rows * held[2]
    return pl.pallas_call(
        functools.partial(pack_kernel, rows_local, shared, which),
        out_shape=[jax.ShapeDtypeStruct((2, rows, size), amps.dtype)] * outs,
        in_specs=[pl.BlockSpec(memory_space=pltpu.SMEM)] * 2
        + [pl.BlockSpec(memory_space=pltpu.HBM), pl.BlockSpec(memory_space=pl.ANY)],
        out_specs=[pl.BlockSpec(memory_space=pltpu.VMEM)] * outs,
        scratch_shapes=[
            pltpu.VMEM(held, amps.dtype),
            pltpu.VMEM(packed, amps.dtype),
            pltpu.SemaphoreType.DMA((pair_count,)),
        ],
        compiler_params=pltpu.CompilerParams(vmem_limit_bytes=vmem),
        cost_estimate=pl.CostEstimate(flops=0, bytes_accessed=4 * held[0] * rows * size, transcendentals=0),
        name="pack_home" if home else "pack_amplitudes",
    )(me, slab, pltpu.with_memory_space_constraint(amps, pltpu.HBM), me if after is None else after)


def mask_kernel(per_step, parts, me_ref, slab_ref, irrep_ref, occ_ref, virt_ref, row_ref, ints_ref, *refs):
    _, out_ref, select_ref, denominator_ref, table, padded, by_row = refs
    step = pl.program_id(0)
    chunk, cols = ints_ref.shape[1:]
    slab_virt = virt_ref.shape[0]
    first_local = cols // slab_virt
    bits = slab_virt.bit_length() - 1
    me, slab = me_ref[0], slab_ref[0]

    @pl.when(step == 0)
    def _():
        padded[:, : row_ref.shape[1]] = row_ref[...]
        for k in range(padded.shape[1] // 128):
            lanes = slice(k * 128, (k + 1) * 128)
            by_row[lanes] = jnp.transpose(jnp.broadcast_to(padded[:, lanes], (128, 128)))

        col = lax.broadcasted_iota(jnp.int32, (1, cols), 1)
        a_of, b_of = col >> bits, col & (slab_virt - 1)
        irrep_a = irrep_b = jnp.zeros_like(col)
        energy_a = energy_b = jnp.zeros(col.shape, jnp.float32)
        for a in range(first_local):
            irrep_a = jnp.where(a_of == a, irrep_ref[slab * first_local + a], irrep_a)
            energy_a = jnp.where(a_of == a, virt_ref[slab * first_local + a], energy_a)
        for b in range(slab_virt):
            irrep_b = jnp.where(b_of == b, irrep_ref[b], irrep_b)
            energy_b = jnp.where(b_of == b, virt_ref[b], energy_b)
        irrep_ab = irrep_a ^ irrep_b

        for part in range(parts):
            for lanes in (slice(k, k + 128) for k in range(0, cols, 128)):
                needed = by_row[part * chunk : (part + 1) * chunk] ^ irrep_ab[:, lanes]
                for irrep in range(IRREPS):
                    table[irrep * parts + part, :, lanes] = jnp.where(needed == irrep, 1.0, 0.0).astype(table.dtype)

        occupied = denominator_ref.shape[0]
        j_of = lax.broadcasted_iota(jnp.int32, (occupied, cols), 0)
        energy_j = jnp.zeros((occupied, cols), jnp.float32)
        for j in range(occupied):
            energy_j = jnp.where(j_of == j, occ_ref[j], energy_j)
        denominator_ref[...] = energy_a + energy_b - occ_ref[me] - energy_j

        row = lax.broadcasted_iota(jnp.int32, (cols, cols), 0)
        col = lax.broadcasted_iota(jnp.int32, (cols, cols), 1)
        same_a = (row & (slab_virt - 1)) == slab * first_local + (col >> bits)
        for t in range(select_ref.shape[0] // cols):
            same_b = (slab ^ t) * first_local + (row >> bits) == (col & (slab_virt - 1))
            chosen = jnp.where(same_a & same_b, 1.0, 0.0)
            select_ref[t * cols : (t + 1) * cols] = chosen.astype(select_ref.dtype)

    chunks = per_step * pl.num_programs(0)
    for k in range(per_step):
        index = me * chunks + step * per_step + k
        irrep_c = irrep_ref[index // parts]
        out_ref[k] = ints_ref[k] * table[irrep_c * parts + index % parts]


def in_hbm(array):
    return pltpu.with_memory_space_constraint(array, pltpu.HBM)


def mask(integrals, me, slab, virt_irrep, occ_energy, slab_energy, after):
    virtuals = virt_irrep.shape[0]
    slab_virt = slab_energy.shape[0]
    occupied = occ_energy.shape[0]
    rows_local, cols_local = integrals.shape
    chunk = math.gcd(virtuals, rows_local)
    parts = virtuals // chunk
    chunks = rows_local // chunk
    per_step = next(n for n in (10, 5, 4, 2, 1) if chunks % n == 0)
    padded = -(-virtuals // 128) * 128
    select_rows = slab_virt * slab_virt
    block = pl.BlockSpec((per_step, chunk, cols_local), lambda step: (step, 0, 0))
    scalars = pl.BlockSpec(memory_space=pltpu.SMEM)
    masked, select, denominator = pl.pallas_call(
        functools.partial(mask_kernel, per_step, parts),
        grid=(chunks // per_step,),
        in_specs=[scalars] * 5
        + [pl.BlockSpec((1, virtuals), lambda step: (0, 0)), block, pl.BlockSpec(memory_space=pl.ANY)],
        out_specs=[
            block,
            pl.BlockSpec((select_rows, cols_local), lambda step: (0, 0)),
            pl.BlockSpec((occupied, cols_local), lambda step: (0, 0)),
        ],
        scratch_shapes=[
            pltpu.VMEM((IRREPS * parts, chunk, cols_local), integrals.dtype),
            pltpu.VMEM((1, padded), jnp.int32),
            pltpu.VMEM((padded, 128), jnp.int32),
        ],
        out_shape=[
            pltpu.VMEM((chunks, chunk, cols_local), integrals.dtype),
            jax.ShapeDtypeStruct((select_rows, cols_local), jnp.bfloat16),
            jax.ShapeDtypeStruct((occupied, cols_local), jnp.float32),
        ],
        compiler_params=pltpu.CompilerParams(vmem_limit_bytes=16 * MIB),
        cost_estimate=pl.CostEstimate(
            flops=LATE_FLOPS, bytes_accessed=4 * rows_local * cols_local, transcendentals=0
        ),
        name="mask_integrals",
    )(
        me,
        slab,
        *(in_hbm(array) for array in (virt_irrep, occ_energy, slab_energy, virt_irrep.reshape(1, virtuals))),
        in_hbm(integrals.reshape(chunks, chunk, cols_local)),
        after,
    )
    return masked.reshape(rows_local, cols_local), select, denominator


def merge_kernel(*refs):
    parts, home_ref, all_ref, other_ref = refs[:-3], refs[-3], refs[-2], refs[-1]
    size = parts[0].shape[2]
    for k, part in enumerate(parts):
        all_ref[k] = part[...]
        other_ref[:, k * size : (k + 1) * size] = part[1]
    other_ref[:, len(parts) * size :] = home_ref[1]


def merge(parts, home):
    count = len(parts)
    _, rows, size = parts[0].shape
    other = (rows, count * size + home.shape[2])
    vmem = pl.BlockSpec(memory_space=pltpu.VMEM)
    return pl.pallas_call(
        merge_kernel,
        out_shape=[
            jax.ShapeDtypeStruct((count,) + parts[0].shape, home.dtype),
            jax.ShapeDtypeStruct(other, home.dtype),
        ],
        in_specs=[vmem] * (count + 1),
        out_specs=[vmem, vmem],
        compiler_params=pltpu.CompilerParams(vmem_limit_bytes=4 * MIB),
        cost_estimate=pl.CostEstimate(flops=0, bytes_accessed=6 * rows * other[1], transcendentals=0),
        name="merge",
    )(*parts, home)


def other_core_kernel(*refs):
    parts, out_ref = refs[:-2], refs[-1]
    for k, part in enumerate(parts):
        out_ref[k] = part[1]


def for_other_core(parts, after):
    vmem = pl.BlockSpec(memory_space=pltpu.VMEM)
    _, rows, size = parts[0].shape
    out = jax.ShapeDtypeStruct((len(parts), rows, size), parts[0].dtype)
    return pl.pallas_call(
        other_core_kernel,
        out_shape=out,
        in_specs=[vmem] * len(parts) + [pl.BlockSpec(memory_space=pl.ANY)],
        out_specs=vmem,
        compiler_params=pltpu.CompilerParams(vmem_limit_bytes=4 * MIB),
        cost_estimate=pl.CostEstimate(flops=LATE_FLOPS // 2, bytes_accessed=4 * out.size, transcendentals=0),
        name="for_other_core",
    )(*parts, after)


def contract_kernel(which, shared, slab_ref, me_ref, home_ref, home_other_ref, ints_ref, *refs):
    last = which == "other"
    lhs = refs[-2] if last else refs[-1]
    count, rows, size = lhs.shape
    chips = count // 2 - 1
    start = start_of(which, slab_ref, shared)
    home_first = home_other_ref.shape[1] - home_ref.shape[2]
    lhs[0] = home_ref[0, :, pl.ds(start, size)]
    lhs[1] = home_other_ref[:, pl.ds(home_first + start, size)]
    for k in range(chips):
        lhs[2 * k + 2] = refs[k][0] if which == "rest" else refs[0][k, 0]
        if which == "own":
            lhs[2 * k + 3] = home_other_ref[:, k * size : (k + 1) * size]
        elif which == "other":
            lhs[2 * k + 3] = refs[1][k, 1]
        else:
            lhs[2 * k + 3] = refs[chips][k]
    refs = refs[{"own": 1, "other": 2, "rest": chips + 1}[which] :]
    step = 2560
    total = None
    for first in range(0, size, step):
        width = min(step, size - first)
        block = lhs[:, :, first : first + width].reshape(count * rows, width)
        part = jnp.dot(block, ints_ref[pl.ds(start + first, width)], preferred_element_type=jnp.float32)
        total = part if total is None else total + part
    if not last:
        before, out_ref = refs[:-2], refs[-2]
        out_ref[...] = total + before[0][...] if before else total
        return
    before_ref, own_ref, other_ref, _, partial = refs
    me = me_ref[0]
    partial[:count, :rows] = (total + before_ref[...]).reshape(count, rows, total.shape[1])
    for i in range(count):
        block = partial[i ^ me, :rows]
        partial[count + (i ^ me), :rows] = block
        for j in range(rows):
            partial[count + (j ^ me), rows + i : rows + i + 1] = block[j : j + 1]
    for k in range(count // 2):
        own_ref[k] = partial[count + 2 * k]
        other_ref[k] = partial[count + 2 * k + 1]


def contract(amps, home, home_other, ints, me, slab, shared, which, before=None):
    occupied, size = amps[0].shape[-2:]
    cols = ints.shape[1]
    vmem = pl.BlockSpec(memory_space=pltpu.VMEM)
    operands = [*amps] + ([] if before is None else [before])
    scratch = [pltpu.VMEM((occupied, occupied, size), home.dtype)]
    if which == "other":
        out_shape = [jax.ShapeDtypeStruct((occupied // 2, 2 * occupied, cols), jnp.float32)] * 2
        scratch.append(pltpu.VMEM((2 * occupied, 2 * occupied, cols), jnp.float32))
    else:
        out_shape = [jax.ShapeDtypeStruct((occupied * occupied, cols), jnp.float32)]
    return pl.pallas_call(
        functools.partial(contract_kernel, which, shared),
        out_shape=out_shape,
        in_specs=[pl.BlockSpec(memory_space=pltpu.SMEM)] * 2 + [vmem] * (3 + len(operands)),
        out_specs=[vmem] * len(out_shape),
        scratch_shapes=scratch,
        compiler_params=pltpu.CompilerParams(
            vmem_limit_bytes=4 * MIB + 40 * occupied * occupied * cols + 4 * occupied * occupied * size
        ),
        cost_estimate=pl.CostEstimate(
            flops=2 * occupied * occupied * size * cols,
            bytes_accessed=2 * size * (cols + occupied * occupied),
            transcendentals=0,
        ),
        name="contract",
    )(slab, me, home, home_other, pltpu.with_memory_space_constraint(ints, pltpu.VMEM), *operands)


def select_exactly(values, select):
    rows = values.shape[0]
    high = values.astype(jnp.bfloat16)
    rest = values - high.astype(jnp.float32)
    middle = rest.astype(jnp.bfloat16)
    low = (rest - middle.astype(jnp.float32)).astype(jnp.bfloat16)
    terms = [jnp.dot(term, select, preferred_element_type=jnp.float32) for term in (high, middle, low)]
    return terms[0] + terms[1] + terms[2]


def add_kernel(kept_ref, got_ref, *outs):
    count = kept_ref.shape[0]
    if count == 1:
        total = kept_ref[0] + got_ref[0]
        half = total.shape[0] // 2
        for k, out in enumerate(outs):
            out[...] = total[k * half : (k + 1) * half]
        return
    for k in range(count):
        outs[k % 2][k // 2] = kept_ref[k] + got_ref[k]


def add(kept, got):
    count, rows, cols = kept.shape
    out = (rows // 2, cols) if count == 1 else (count // 2, rows, cols)
    vmem = pl.BlockSpec(memory_space=pltpu.VMEM)
    return pl.pallas_call(
        add_kernel,
        out_shape=[jax.ShapeDtypeStruct(out, jnp.float32)] * 2,
        in_specs=[vmem, vmem],
        out_specs=[vmem, vmem],
        compiler_params=pltpu.CompilerParams(vmem_limit_bytes=4 * MIB),
        cost_estimate=pl.CostEstimate(flops=kept.size, bytes_accessed=12 * kept.size, transcendentals=0),
        name="add",
    )(kept, got)


def stack_kernel(*refs):
    size = refs[0].shape[0]
    for k, ref in enumerate(refs[:-1]):
        refs[-1][k * size : (k + 1) * size] = ref[...]


def stack(parts):
    rows, cols = parts[0].shape
    vmem = pl.BlockSpec(memory_space=pltpu.VMEM)
    return pl.pallas_call(
        stack_kernel,
        out_shape=jax.ShapeDtypeStruct((len(parts) * rows, cols), jnp.float32),
        in_specs=[vmem] * len(parts),
        out_specs=vmem,
        compiler_params=pltpu.CompilerParams(vmem_limit_bytes=4 * MIB),
        cost_estimate=pl.CostEstimate(flops=0, bytes_accessed=8 * len(parts) * rows * cols, transcendentals=0),
        name="stack",
    )(*parts)


def finish_kernel(ladder_ref, denominator_ref, select_ref, *refs):
    mirrors, out_ref = refs[:-1], refs[-1]
    rows = ladder_ref.shape[0]
    blocks = [ref[k : k + rows] for ref in mirrors for k in range(0, ref.shape[0], rows)]
    mirror = select_exactly(jnp.concatenate(blocks, axis=1), select_ref[...])
    update = (ladder_ref[...] + mirror) / denominator_ref[...]
    _, first_local, slab_virt = out_ref.shape
    for a in range(first_local):
        out_ref[:, a, :] = update[:, a * slab_virt : (a + 1) * slab_virt]


def finish(ladder, mirrors, denominator, select, first_local, slab_virt):
    rows = ladder.shape[0]
    return pl.pallas_call(
        finish_kernel,
        out_shape=jax.ShapeDtypeStruct((rows, first_local, slab_virt), jnp.float32),
        in_specs=[pl.BlockSpec(memory_space=pltpu.VMEM)] * (3 + len(mirrors)),
        out_specs=pl.BlockSpec(memory_space=pltpu.VMEM),
        compiler_params=pltpu.CompilerParams(vmem_limit_bytes=6 * MIB),
        cost_estimate=pl.CostEstimate(flops=6 * rows * select.size, bytes_accessed=2 * select.size, transcendentals=0),
        name="finish",
    )(ladder, denominator, select, *mirrors)


def swap(values, axis, bits):
    return lax.ppermute(values, axis, [(p, p ^ bits) for p in range(lax.axis_size(axis))])


def local(amplitudes, integrals, virt_irrep, occ_energy, slab_energy):
    pair_count = lax.axis_size("pair")
    slab_count = lax.axis_size("slab")
    occ_local, occupied, virt_pairs = amplitudes.shape
    rows_local, cols_local = integrals.shape
    slab_virt = slab_energy.shape[0]
    first_local = slab_virt // slab_count
    assert occ_local == 1
    me = lax.axis_index("pair").astype(jnp.int32).reshape(1)
    slab = lax.axis_index("slab").astype(jnp.int32).reshape(1)

    shared = int(SHARE * rows_local) // 128 * 128
    amps = amplitudes.reshape(occupied, virt_pairs)
    chips = [2 * k for k in range(1, pair_count // 2)]

    def to_chips(parts):
        return [swap(part, "pair", bits) for part, bits in zip(parts, chips)]

    parts = pack(amps, me, slab, shared, "own", pair_count)
    own_amps = to_chips(parts)
    parts = pack(amps, me, slab, shared, "rest", pair_count, parts[-1])
    rest_amps = to_chips(parts)
    (home,) = pack(amps, me, slab, shared, "all", pair_count, parts[-1])

    own_amps, for_other = merge(own_amps, home)
    other_amps = swap(own_amps, "slab", 1)
    home_other = swap(for_other, "pair", 1)
    masked, select, denominator = mask(integrals, me, slab, virt_irrep, occ_energy, slab_energy, own_amps)
    rest_others = swap(for_other_core(rest_amps, denominator), "pair", 1)
    place = (home, home_other, masked, me, slab, shared)
    (partial,) = contract([own_amps], *place, "own")
    (partial,) = contract([*rest_amps, rest_others], *place, "rest", partial)
    even, odd = contract([other_amps, swap(other_amps, "pair", 1)], *place, "other", partial)

    bits = 1
    while bits < pair_count:
        even, odd = add(even, swap(odd, "pair", bits))
        bits *= 2
    ladder, mirrors = even, [odd]
    bits = 1
    while bits < slab_count:
        part = mirrors[0] if len(mirrors) == 1 else stack(mirrors)
        mirrors = [part, swap(part, "slab", bits)]
        bits *= 2
    update = finish(ladder, mirrors, denominator, select, first_local, slab_virt)
    return update.reshape(occ_local, occupied, first_local, slab_virt)


def solution(mesh):
    placed = (P("pair", None, None), P("pair", "slab"), P(), P(), P())
    return jax.shard_map(
        local, mesh=mesh, in_specs=placed, out_specs=P("pair", None, "slab", None), check_vma=False
    )
```

```python
import functools
import math

import jax
import jax.numpy as jnp
from jax import lax
from jax.experimental import pallas as pl
from jax.experimental.pallas import tpu as pltpu
from jax.sharding import PartitionSpec as P

IRREPS = 8
MIB = 2**20
SHARE = 0.3
LATE_FLOPS = 3 * 10**9


def start_of(part, slab_ref, shared):
    parity = slab_ref[0] % 2
    return pl.multiple_of({"own": parity * shared, "other": (1 - parity) * shared, "rest": 2 * shared, "all": 0}[part], 128)


def pack_kernel(rows_local, shared, which, me_ref, slab_ref, amps_ref, after_ref, *refs):
    outs, (held, packed, sems) = refs[:-3], refs[-3:]
    _, _, size = packed.shape
    count = sems.shape[0]
    home = which == "all"
    me = me_ref[0]
    start = start_of(which, slab_ref, shared)
    loads, shifts = [], []
    for dest in range(count):
        first = dest * rows_local // 128 * 128
        shifts.append(dest * rows_local - first)
        width = -(-(shifts[dest] + size) // 128) * 128
        slot = dest ^ me if home else dest
        loads.append(
            pltpu.make_async_copy(
                amps_ref.at[:, pl.ds(start + first, width)], held.at[slot, :, pl.ds(0, width)], sems.at[dest]
            )
        )

    def wanted(dest):
        return (dest ^ me) // 2 == 0 if home else True

    for dest in range(count):
        pl.when(wanted(dest))(loads[dest].start)
    for dest in range(count):

        @pl.when(wanted(dest))
        def _():
            loads[dest].wait()
            packed[dest ^ me] = held[dest ^ me if home else dest, :, shifts[dest] : shifts[dest] + size]

    for k, out in enumerate(outs):
        slot = 0 if home else 2 * k + 2
        out[...] = packed[slot : slot + 2]


def pack(amps, me, slab, shared, which, pair_count, after=None):
    rows, virt_pairs = amps.shape
    rows_local = virt_pairs // pair_count
    home = which == "all"
    size = {"own": shared, "rest": rows_local - 2 * shared, "all": rows_local}[which]
    held = (2 if home else pair_count, rows, -(-size // 128) * 128 + 128)
    packed = (held[0], rows, size)
    outs = 1 if home else pair_count // 2 - 1
    vmem = 2 * MIB + 6 * held[0] * rows * held[2]
    return pl.pallas_call(
        functools.partial(pack_kernel, rows_local, shared, which),
        out_shape=[jax.ShapeDtypeStruct((2, rows, size), amps.dtype)] * outs,
        in_specs=[pl.BlockSpec(memory_space=pltpu.SMEM)] * 2
        + [pl.BlockSpec(memory_space=pltpu.HBM), pl.BlockSpec(memory_space=pl.ANY)],
        out_specs=[pl.BlockSpec(memory_space=pltpu.VMEM)] * outs,
        scratch_shapes=[
            pltpu.VMEM(held, amps.dtype),
            pltpu.VMEM(packed, amps.dtype),
            pltpu.SemaphoreType.DMA((pair_count,)),
        ],
        compiler_params=pltpu.CompilerParams(vmem_limit_bytes=vmem),
        cost_estimate=pl.CostEstimate(flops=0, bytes_accessed=4 * held[0] * rows * size, transcendentals=0),
        name="pack_home" if home else "pack_amplitudes",
    )(me, slab, pltpu.with_memory_space_constraint(amps, pltpu.HBM), me if after is None else after)


def mask_kernel(per_step, parts, me_ref, slab_ref, irrep_ref, occ_ref, virt_ref, row_ref, ints_ref, *refs):
    _, out_ref, select_ref, denominator_ref, table, padded, by_row = refs
    step = pl.program_id(0)
    chunk, cols = ints_ref.shape[1:]
    slab_virt = virt_ref.shape[0]
    first_local = cols // slab_virt
    bits = slab_virt.bit_length() - 1
    me, slab = me_ref[0], slab_ref[0]

    @pl.when(step == 0)
    def _():
        padded[:, : row_ref.shape[1]] = row_ref[...]
        for k in range(padded.shape[1] // 128):
            lanes = slice(k * 128, (k + 1) * 128)
            by_row[lanes] = jnp.transpose(jnp.broadcast_to(padded[:, lanes], (128, 128)))

        col = lax.broadcasted_iota(jnp.int32, (1, cols), 1)
        a_of, b_of = col >> bits, col & (slab_virt - 1)
        irrep_a = irrep_b = jnp.zeros_like(col)
        energy_a = energy_b = jnp.zeros(col.shape, jnp.float32)
        for a in range(first_local):
            irrep_a = jnp.where(a_of == a, irrep_ref[slab * first_local + a], irrep_a)
            energy_a = jnp.where(a_of == a, virt_ref[slab * first_local + a], energy_a)
        for b in range(slab_virt):
            irrep_b = jnp.where(b_of == b, irrep_ref[b], irrep_b)
            energy_b = jnp.where(b_of == b, virt_ref[b], energy_b)
        irrep_ab = irrep_a ^ irrep_b

        for part in range(parts):
            for lanes in (slice(k, k + 128) for k in range(0, cols, 128)):
                needed = by_row[part * chunk : (part + 1) * chunk] ^ irrep_ab[:, lanes]
                for irrep in range(IRREPS):
                    table[irrep * parts + part, :, lanes] = jnp.where(needed == irrep, 1.0, 0.0).astype(table.dtype)

        occupied = denominator_ref.shape[0]
        j_of = lax.broadcasted_iota(jnp.int32, (occupied, cols), 0)
        energy_j = jnp.zeros((occupied, cols), jnp.float32)
        for j in range(occupied):
            energy_j = jnp.where(j_of == j, occ_ref[j], energy_j)
        denominator_ref[...] = energy_a + energy_b - occ_ref[me] - energy_j

        row = lax.broadcasted_iota(jnp.int32, (cols, cols), 0)
        col = lax.broadcasted_iota(jnp.int32, (cols, cols), 1)
        same_a = (row & (slab_virt - 1)) == slab * first_local + (col >> bits)
        for t in range(select_ref.shape[0] // cols):
            same_b = (slab ^ t) * first_local + (row >> bits) == (col & (slab_virt - 1))
            chosen = jnp.where(same_a & same_b, 1.0, 0.0)
            select_ref[t * cols : (t + 1) * cols] = chosen.astype(select_ref.dtype)

    chunks = per_step * pl.num_programs(0)
    for k in range(per_step):
        index = me * chunks + step * per_step + k
        irrep_c = irrep_ref[index // parts]
        out_ref[k] = ints_ref[k] * table[irrep_c * parts + index % parts]


def in_hbm(array):
    return pltpu.with_memory_space_constraint(array, pltpu.HBM)


def mask(integrals, me, slab, virt_irrep, occ_energy, slab_energy, after):
    virtuals = virt_irrep.shape[0]
    slab_virt = slab_energy.shape[0]
    occupied = occ_energy.shape[0]
    rows_local, cols_local = integrals.shape
    chunk = math.gcd(virtuals, rows_local)
    parts = virtuals // chunk
    chunks = rows_local // chunk
    per_step = next(n for n in (10, 5, 4, 2, 1) if chunks % n == 0)
    padded = -(-virtuals // 128) * 128
    select_rows = slab_virt * slab_virt
    block = pl.BlockSpec((per_step, chunk, cols_local), lambda step: (step, 0, 0))
    scalars = pl.BlockSpec(memory_space=pltpu.SMEM)
    masked, select, denominator = pl.pallas_call(
        functools.partial(mask_kernel, per_step, parts),
        grid=(chunks // per_step,),
        in_specs=[scalars] * 5
        + [pl.BlockSpec((1, virtuals), lambda step: (0, 0)), block, pl.BlockSpec(memory_space=pl.ANY)],
        out_specs=[
            block,
            pl.BlockSpec((select_rows, cols_local), lambda step: (0, 0)),
            pl.BlockSpec((occupied, cols_local), lambda step: (0, 0)),
        ],
        scratch_shapes=[
            pltpu.VMEM((IRREPS * parts, chunk, cols_local), integrals.dtype),
            pltpu.VMEM((1, padded), jnp.int32),
            pltpu.VMEM((padded, 128), jnp.int32),
        ],
        out_shape=[
            pltpu.VMEM((chunks, chunk, cols_local), integrals.dtype),
            jax.ShapeDtypeStruct((select_rows, cols_local), jnp.bfloat16),
            jax.ShapeDtypeStruct((occupied, cols_local), jnp.float32),
        ],
        compiler_params=pltpu.CompilerParams(vmem_limit_bytes=16 * MIB),
        cost_estimate=pl.CostEstimate(
            flops=LATE_FLOPS, bytes_accessed=4 * rows_local * cols_local, transcendentals=0
        ),
        name="mask_integrals",
    )(
        me,
        slab,
        *(in_hbm(array) for array in (virt_irrep, occ_energy, slab_energy, virt_irrep.reshape(1, virtuals))),
        in_hbm(integrals.reshape(chunks, chunk, cols_local)),
        after,
    )
    return masked.reshape(rows_local, cols_local), select, denominator


def merge_kernel(*refs):
    parts, home_ref, all_ref, other_ref = refs[:-3], refs[-3], refs[-2], refs[-1]
    size = parts[0].shape[2]
    for k, part in enumerate(parts):
        all_ref[k] = part[...]
        other_ref[:, k * size : (k + 1) * size] = part[1]
    other_ref[:, len(parts) * size :] = home_ref[1]


def merge(parts, home):
    count = len(parts)
    _, rows, size = parts[0].shape
    other = (rows, count * size + home.shape[2])
    vmem = pl.BlockSpec(memory_space=pltpu.VMEM)
    return pl.pallas_call(
        merge_kernel,
        out_shape=[
            jax.ShapeDtypeStruct((count,) + parts[0].shape, home.dtype),
            jax.ShapeDtypeStruct(other, home.dtype),
        ],
        in_specs=[vmem] * (count + 1),
        out_specs=[vmem, vmem],
        compiler_params=pltpu.CompilerParams(vmem_limit_bytes=4 * MIB),
        cost_estimate=pl.CostEstimate(flops=0, bytes_accessed=6 * rows * other[1], transcendentals=0),
        name="merge",
    )(*parts, home)


def tie_kernel(*refs):
    del refs


def tie(parts, after):
    count = len(parts)
    anywhere = pl.BlockSpec(memory_space=pl.ANY)
    return pl.pallas_call(
        tie_kernel,
        out_shape=[pltpu.VMEM(part.shape, part.dtype) for part in parts],
        in_specs=[anywhere] * (count + 1),
        out_specs=[anywhere] * count,
        input_output_aliases={k: k for k in range(count)},
        compiler_params=pltpu.CompilerParams(vmem_limit_bytes=2 * MIB),
        cost_estimate=pl.CostEstimate(flops=0, bytes_accessed=0, transcendentals=0),
        name="tie",
    )(*(pltpu.with_memory_space_constraint(part, pltpu.VMEM) for part in parts), after)


def other_core_kernel(*refs):
    parts, out_ref = refs[:-2], refs[-1]
    for k, part in enumerate(parts):
        out_ref[k] = part[1]


def for_other_core(parts, after):
    vmem = pl.BlockSpec(memory_space=pltpu.VMEM)
    _, rows, size = parts[0].shape
    out = jax.ShapeDtypeStruct((len(parts), rows, size), parts[0].dtype)
    return pl.pallas_call(
        other_core_kernel,
        out_shape=out,
        in_specs=[vmem] * len(parts) + [pl.BlockSpec(memory_space=pl.ANY)],
        out_specs=vmem,
        compiler_params=pltpu.CompilerParams(vmem_limit_bytes=4 * MIB),
        cost_estimate=pl.CostEstimate(flops=2 * LATE_FLOPS // 3, bytes_accessed=4 * out.size, transcendentals=0),
        name="for_other_core",
    )(*parts, after)


def contract_kernel(which, shared, slab_ref, me_ref, home_ref, home_other_ref, ints_ref, *refs):
    last = which == "other"
    lhs = refs[-2] if last else refs[-1]
    count, rows, size = lhs.shape
    chips = count // 2 - 1
    start = start_of(which, slab_ref, shared)
    home_first = home_other_ref.shape[1] - home_ref.shape[2]
    lhs[0] = home_ref[0, :, pl.ds(start, size)]
    lhs[1] = home_other_ref[:, pl.ds(home_first + start, size)]
    for k in range(chips):
        lhs[2 * k + 2] = refs[k][0] if which == "rest" else refs[0][k, 0]
        if which == "own":
            lhs[2 * k + 3] = home_other_ref[:, k * size : (k + 1) * size]
        elif which == "other":
            lhs[2 * k + 3] = refs[1][k, 1]
        else:
            lhs[2 * k + 3] = refs[chips][k]
    refs = refs[{"own": 1, "other": 2, "rest": chips + 1}[which] :]
    step = 2560
    total = None
    for first in range(0, size, step):
        width = min(step, size - first)
        block = lhs[:, :, first : first + width].reshape(count * rows, width)
        part = jnp.dot(block, ints_ref[pl.ds(start + first, width)], preferred_element_type=jnp.float32)
        total = part if total is None else total + part
    if not last:
        before, out_ref = refs[:-2], refs[-2]
        out_ref[...] = total + before[0][...] if before else total
        return
    before_ref, own_ref, other_ref, _, partial = refs
    me = me_ref[0]
    partial[:count, :rows] = (total + before_ref[...]).reshape(count, rows, total.shape[1])
    for i in range(count):
        block = partial[i ^ me, :rows]
        partial[count + (i ^ me), :rows] = block
        for j in range(rows):
            partial[count + (j ^ me), rows + i : rows + i + 1] = block[j : j + 1]
    for k in range(count // 2):
        own_ref[k] = partial[count + 2 * k]
        other_ref[k] = partial[count + 2 * k + 1]


def contract(amps, home, home_other, ints, me, slab, shared, which, before=None):
    occupied, size = amps[0].shape[-2:]
    cols = ints.shape[1]
    vmem = pl.BlockSpec(memory_space=pltpu.VMEM)
    operands = [*amps] + ([] if before is None else [before])
    scratch = [pltpu.VMEM((occupied, occupied, size), home.dtype)]
    if which == "other":
        out_shape = [jax.ShapeDtypeStruct((occupied // 2, 2 * occupied, cols), jnp.float32)] * 2
        scratch.append(pltpu.VMEM((2 * occupied, 2 * occupied, cols), jnp.float32))
    else:
        out_shape = [jax.ShapeDtypeStruct((occupied * occupied, cols), jnp.float32)]
    return pl.pallas_call(
        functools.partial(contract_kernel, which, shared),
        out_shape=out_shape,
        in_specs=[pl.BlockSpec(memory_space=pltpu.SMEM)] * 2 + [vmem] * (3 + len(operands)),
        out_specs=[vmem] * len(out_shape),
        scratch_shapes=scratch,
        compiler_params=pltpu.CompilerParams(
            vmem_limit_bytes=4 * MIB + 40 * occupied * occupied * cols + 4 * occupied * occupied * size
        ),
        cost_estimate=pl.CostEstimate(
            flops=2 * occupied * occupied * size * cols,
            bytes_accessed=2 * size * (cols + occupied * occupied),
            transcendentals=0,
        ),
        name="contract",
    )(slab, me, home, home_other, pltpu.with_memory_space_constraint(ints, pltpu.VMEM), *operands)


def select_exactly(values, select):
    rows = values.shape[0]
    high = values.astype(jnp.bfloat16)
    rest = values - high.astype(jnp.float32)
    middle = rest.astype(jnp.bfloat16)
    low = (rest - middle.astype(jnp.float32)).astype(jnp.bfloat16)
    terms = [jnp.dot(term, select, preferred_element_type=jnp.float32) for term in (high, middle, low)]
    return terms[0] + terms[1] + terms[2]


def add_kernel(kept_ref, got_ref, *outs):
    count = kept_ref.shape[0]
    if count == 1:
        total = kept_ref[0] + got_ref[0]
        half = total.shape[0] // 2
        for k, out in enumerate(outs):
            out[...] = total[k * half : (k + 1) * half]
        return
    for k in range(count):
        outs[k % 2][k // 2] = kept_ref[k] + got_ref[k]


def add(kept, got):
    count, rows, cols = kept.shape
    out = (rows // 2, cols) if count == 1 else (count // 2, rows, cols)
    vmem = pl.BlockSpec(memory_space=pltpu.VMEM)
    return pl.pallas_call(
        add_kernel,
        out_shape=[jax.ShapeDtypeStruct(out, jnp.float32)] * 2,
        in_specs=[vmem, vmem],
        out_specs=[vmem, vmem],
        compiler_params=pltpu.CompilerParams(vmem_limit_bytes=4 * MIB),
        cost_estimate=pl.CostEstimate(flops=kept.size, bytes_accessed=12 * kept.size, transcendentals=0),
        name="add",
    )(kept, got)


def stack_kernel(*refs):
    size = refs[0].shape[0]
    for k, ref in enumerate(refs[:-1]):
        refs[-1][k * size : (k + 1) * size] = ref[...]


def stack(parts):
    rows, cols = parts[0].shape
    vmem = pl.BlockSpec(memory_space=pltpu.VMEM)
    return pl.pallas_call(
        stack_kernel,
        out_shape=jax.ShapeDtypeStruct((len(parts) * rows, cols), jnp.float32),
        in_specs=[vmem] * len(parts),
        out_specs=vmem,
        compiler_params=pltpu.CompilerParams(vmem_limit_bytes=4 * MIB),
        cost_estimate=pl.CostEstimate(flops=0, bytes_accessed=8 * len(parts) * rows * cols, transcendentals=0),
        name="stack",
    )(*parts)


def finish_kernel(ladder_ref, denominator_ref, select_ref, *refs):
    mirrors, out_ref = refs[:-1], refs[-1]
    rows = ladder_ref.shape[0]
    blocks = [ref[k : k + rows] for ref in mirrors for k in range(0, ref.shape[0], rows)]
    mirror = select_exactly(jnp.concatenate(blocks, axis=1), select_ref[...])
    update = (ladder_ref[...] + mirror) / denominator_ref[...]
    _, first_local, slab_virt = out_ref.shape
    for a in range(first_local):
        out_ref[:, a, :] = update[:, a * slab_virt : (a + 1) * slab_virt]


def finish(ladder, mirrors, denominator, select, first_local, slab_virt):
    rows = ladder.shape[0]
    return pl.pallas_call(
        finish_kernel,
        out_shape=jax.ShapeDtypeStruct((rows, first_local, slab_virt), jnp.float32),
        in_specs=[pl.BlockSpec(memory_space=pltpu.VMEM)] * (3 + len(mirrors)),
        out_specs=pl.BlockSpec(memory_space=pltpu.VMEM),
        compiler_params=pltpu.CompilerParams(vmem_limit_bytes=6 * MIB),
        cost_estimate=pl.CostEstimate(flops=6 * rows * select.size, bytes_accessed=2 * select.size, transcendentals=0),
        name="finish",
    )(ladder, denominator, select, *mirrors)


def swap(values, axis, bits):
    return lax.ppermute(values, axis, [(p, p ^ bits) for p in range(lax.axis_size(axis))])


def local(amplitudes, integrals, virt_irrep, occ_energy, slab_energy):
    pair_count = lax.axis_size("pair")
    slab_count = lax.axis_size("slab")
    occ_local, occupied, virt_pairs = amplitudes.shape
    rows_local, cols_local = integrals.shape
    slab_virt = slab_energy.shape[0]
    first_local = slab_virt // slab_count
    assert occ_local == 1
    me = lax.axis_index("pair").astype(jnp.int32).reshape(1)
    slab = lax.axis_index("slab").astype(jnp.int32).reshape(1)

    shared = int(SHARE * rows_local) // 128 * 128
    amps = amplitudes.reshape(occupied, virt_pairs)
    chips = [2 * k for k in range(1, pair_count // 2)]

    def to_chips(parts):
        return [swap(part, "pair", bits) for part, bits in zip(parts, chips)]

    parts = pack(amps, me, slab, shared, "own", pair_count)
    own_amps = to_chips(parts)
    parts = pack(amps, me, slab, shared, "rest", pair_count, parts[-1])
    rest_amps = to_chips(tie(parts, own_amps[0]))
    (home,) = pack(amps, me, slab, shared, "all", pair_count, parts[-1])

    own_amps, for_other = merge(own_amps, home)
    other_amps = swap(own_amps, "slab", 1)
    home_other = swap(for_other, "pair", 1)
    masked, select, denominator = mask(integrals, me, slab, virt_irrep, occ_energy, slab_energy, own_amps)
    rest_others = swap(for_other_core(rest_amps, denominator), "pair", 1)
    place = (home, home_other, masked, me, slab, shared)
    (partial,) = contract([own_amps], *place, "own")
    (partial,) = contract([*rest_amps, rest_others], *place, "rest", partial)
    even, odd = contract([other_amps, swap(other_amps, "pair", 1)], *place, "other", partial)

    bits = 1
    while bits < pair_count:
        even, odd = add(even, swap(odd, "pair", bits))
        bits *= 2
    ladder, mirrors = even, [odd]
    bits = 1
    while bits < slab_count:
        part = mirrors[0] if len(mirrors) == 1 else stack(mirrors)
        mirrors = [part, swap(part, "slab", bits)]
        bits *= 2
    update = finish(ladder, mirrors, denominator, select, first_local, slab_virt)
    return update.reshape(occ_local, occupied, first_local, slab_virt)


def solution(mesh):
    placed = (P("pair", None, None), P("pair", "slab"), P(), P(), P())
    return jax.shard_map(
        local, mesh=mesh, in_specs=placed, out_specs=P("pair", None, "slab", None), check_vma=False
    )
```

```python
import functools
import math

import jax
import jax.numpy as jnp
from jax import lax
from jax.experimental import pallas as pl
from jax.experimental.pallas import tpu as pltpu
from jax.sharding import PartitionSpec as P

IRREPS = 8
MIB = 2**20
SHARE = 0.24
LATE_FLOPS = 10**10


def start_of(part, slab_ref, shared):
    parity = slab_ref[0] % 2
    return pl.multiple_of({"own": parity * shared, "other": (1 - parity) * shared, "rest": 2 * shared, "all": 0}[part], 128)


def pack_kernel(rows_local, shared, which, me_ref, slab_ref, amps_ref, after_ref, *refs):
    outs, (held, packed, sems) = refs[:-3], refs[-3:]
    _, _, size = packed.shape
    count = sems.shape[0]
    home = which == "all"
    me = me_ref[0]
    start = start_of(which, slab_ref, shared)
    loads, shifts = [], []
    for dest in range(count):
        first = dest * rows_local // 128 * 128
        shifts.append(dest * rows_local - first)
        width = -(-(shifts[dest] + size) // 128) * 128
        slot = dest ^ me if home else dest
        loads.append(
            pltpu.make_async_copy(
                amps_ref.at[:, pl.ds(start + first, width)], held.at[slot, :, pl.ds(0, width)], sems.at[dest]
            )
        )

    def wanted(dest):
        return (dest ^ me) // 2 == 0 if home else True

    for dest in range(count):
        pl.when(wanted(dest))(loads[dest].start)
    for dest in range(count):

        @pl.when(wanted(dest))
        def _():
            loads[dest].wait()
            packed[dest ^ me] = held[dest ^ me if home else dest, :, shifts[dest] : shifts[dest] + size]

    for k, out in enumerate(outs):
        slot = 0 if home else 2 * k + 2
        out[...] = packed[slot : slot + 2]


def pack(amps, me, slab, shared, which, pair_count, after=None):
    rows, virt_pairs = amps.shape
    rows_local = virt_pairs // pair_count
    home = which == "all"
    size = {"own": shared, "rest": rows_local - 2 * shared, "all": rows_local}[which]
    held = (2 if home else pair_count, rows, -(-size // 128) * 128 + 128)
    packed = (held[0], rows, size)
    outs = 1 if home else pair_count // 2 - 1
    vmem = 2 * MIB + 6 * held[0] * rows * held[2]
    return pl.pallas_call(
        functools.partial(pack_kernel, rows_local, shared, which),
        out_shape=[jax.ShapeDtypeStruct((2, rows, size), amps.dtype)] * outs,
        in_specs=[pl.BlockSpec(memory_space=pltpu.SMEM)] * 2
        + [pl.BlockSpec(memory_space=pltpu.HBM), pl.BlockSpec(memory_space=pl.ANY)],
        out_specs=[pl.BlockSpec(memory_space=pltpu.VMEM)] * outs,
        scratch_shapes=[
            pltpu.VMEM(held, amps.dtype),
            pltpu.VMEM(packed, amps.dtype),
            pltpu.SemaphoreType.DMA((pair_count,)),
        ],
        compiler_params=pltpu.CompilerParams(vmem_limit_bytes=vmem),
        cost_estimate=pl.CostEstimate(flops=0, bytes_accessed=4 * held[0] * rows * size, transcendentals=0),
        name="pack_home" if home else "pack_amplitudes",
    )(me, slab, pltpu.with_memory_space_constraint(amps, pltpu.HBM), me if after is None else after)


def mask_kernel(per_step, parts, me_ref, slab_ref, irrep_ref, occ_ref, virt_ref, row_ref, ints_ref, *refs):
    _, out_ref, select_ref, denominator_ref, table, padded, by_row = refs
    step = pl.program_id(0)
    chunk, cols = ints_ref.shape[1:]
    slab_virt = virt_ref.shape[0]
    first_local = cols // slab_virt
    bits = slab_virt.bit_length() - 1
    me, slab = me_ref[0], slab_ref[0]

    @pl.when(step == 0)
    def _():
        padded[:, : row_ref.shape[1]] = row_ref[...]
        for k in range(padded.shape[1] // 128):
            lanes = slice(k * 128, (k + 1) * 128)
            by_row[lanes] = jnp.transpose(jnp.broadcast_to(padded[:, lanes], (128, 128)))

        col = lax.broadcasted_iota(jnp.int32, (1, cols), 1)
        a_of, b_of = col >> bits, col & (slab_virt - 1)
        irrep_a = irrep_b = jnp.zeros_like(col)
        energy_a = energy_b = jnp.zeros(col.shape, jnp.float32)
        for a in range(first_local):
            irrep_a = jnp.where(a_of == a, irrep_ref[slab * first_local + a], irrep_a)
            energy_a = jnp.where(a_of == a, virt_ref[slab * first_local + a], energy_a)
        for b in range(slab_virt):
            irrep_b = jnp.where(b_of == b, irrep_ref[b], irrep_b)
            energy_b = jnp.where(b_of == b, virt_ref[b], energy_b)
        irrep_ab = irrep_a ^ irrep_b

        for part in range(parts):
            for lanes in (slice(k, k + 128) for k in range(0, cols, 128)):
                needed = by_row[part * chunk : (part + 1) * chunk] ^ irrep_ab[:, lanes]
                for irrep in range(IRREPS):
                    table[irrep * parts + part, :, lanes] = jnp.where(needed == irrep, 1.0, 0.0).astype(table.dtype)

        occupied = denominator_ref.shape[0]
        j_of = lax.broadcasted_iota(jnp.int32, (occupied, cols), 0)
        energy_j = jnp.zeros((occupied, cols), jnp.float32)
        for j in range(occupied):
            energy_j = jnp.where(j_of == j, occ_ref[j], energy_j)
        denominator_ref[...] = energy_a + energy_b - occ_ref[me] - energy_j

        row = lax.broadcasted_iota(jnp.int32, (cols, cols), 0)
        col = lax.broadcasted_iota(jnp.int32, (cols, cols), 1)
        same_a = (row & (slab_virt - 1)) == slab * first_local + (col >> bits)
        slab_count = select_ref.shape[0] // cols
        for t in range(slab_count):
            same_b = (slab + t) % slab_count * first_local + (row >> bits) == (col & (slab_virt - 1))
            chosen = jnp.where(same_a & same_b, 1.0, 0.0)
            select_ref[t * cols : (t + 1) * cols] = chosen.astype(select_ref.dtype)

    chunks = per_step * pl.num_programs(0)
    for k in range(per_step):
        index = me * chunks + step * per_step + k
        irrep_c = irrep_ref[index // parts]
        out_ref[k] = ints_ref[k] * table[irrep_c * parts + index % parts]


def in_hbm(array):
    return pltpu.with_memory_space_constraint(array, pltpu.HBM)


def mask(integrals, me, slab, virt_irrep, occ_energy, slab_energy, after):
    virtuals = virt_irrep.shape[0]
    slab_virt = slab_energy.shape[0]
    occupied = occ_energy.shape[0]
    rows_local, cols_local = integrals.shape
    chunk = math.gcd(virtuals, rows_local)
    parts = virtuals // chunk
    chunks = rows_local // chunk
    per_step = next(n for n in (10, 5, 4, 2, 1) if chunks % n == 0)
    padded = -(-virtuals // 128) * 128
    select_rows = slab_virt * slab_virt
    block = pl.BlockSpec((per_step, chunk, cols_local), lambda step: (step, 0, 0))
    scalars = pl.BlockSpec(memory_space=pltpu.SMEM)
    masked, select, denominator = pl.pallas_call(
        functools.partial(mask_kernel, per_step, parts),
        grid=(chunks // per_step,),
        in_specs=[scalars] * 5
        + [pl.BlockSpec((1, virtuals), lambda step: (0, 0)), block, pl.BlockSpec(memory_space=pl.ANY)],
        out_specs=[
            block,
            pl.BlockSpec((select_rows, cols_local), lambda step: (0, 0)),
            pl.BlockSpec((occupied, cols_local), lambda step: (0, 0)),
        ],
        scratch_shapes=[
            pltpu.VMEM((IRREPS * parts, chunk, cols_local), integrals.dtype),
            pltpu.VMEM((1, padded), jnp.int32),
            pltpu.VMEM((padded, 128), jnp.int32),
        ],
        out_shape=[
            pltpu.VMEM((chunks, chunk, cols_local), integrals.dtype),
            jax.ShapeDtypeStruct((select_rows, cols_local), jnp.bfloat16),
            jax.ShapeDtypeStruct((occupied, cols_local), jnp.float32),
        ],
        compiler_params=pltpu.CompilerParams(vmem_limit_bytes=16 * MIB),
        cost_estimate=pl.CostEstimate(
            flops=LATE_FLOPS, bytes_accessed=4 * rows_local * cols_local, transcendentals=0
        ),
        name="mask_integrals",
    )(
        me,
        slab,
        *(in_hbm(array) for array in (virt_irrep, occ_energy, slab_energy, virt_irrep.reshape(1, virtuals))),
        in_hbm(integrals.reshape(chunks, chunk, cols_local)),
        after,
    )
    return masked.reshape(rows_local, cols_local), select, denominator


def merge_kernel(*refs):
    parts, home_ref, all_ref, other_ref = refs[:-3], refs[-3], refs[-2], refs[-1]
    size = parts[0].shape[2]
    for k, part in enumerate(parts):
        all_ref[k] = part[...]
        other_ref[:, k * size : (k + 1) * size] = part[1]
    other_ref[:, len(parts) * size :] = home_ref[1]


def merge(parts, home):
    count = len(parts)
    _, rows, size = parts[0].shape
    other = (rows, count * size + home.shape[2])
    vmem = pl.BlockSpec(memory_space=pltpu.VMEM)
    return pl.pallas_call(
        merge_kernel,
        out_shape=[
            jax.ShapeDtypeStruct((count,) + parts[0].shape, home.dtype),
            jax.ShapeDtypeStruct(other, home.dtype),
        ],
        in_specs=[vmem] * (count + 1),
        out_specs=[vmem, vmem],
        compiler_params=pltpu.CompilerParams(vmem_limit_bytes=4 * MIB),
        cost_estimate=pl.CostEstimate(flops=0, bytes_accessed=6 * rows * other[1], transcendentals=0),
        name="merge",
    )(*parts, home)


def other_core_kernel(*refs):
    parts, out_ref = refs[:-2], refs[-1]
    for k, part in enumerate(parts):
        out_ref[k] = part[1]


def for_other_core(parts, after):
    vmem = pl.BlockSpec(memory_space=pltpu.VMEM)
    _, rows, size = parts[0].shape
    out = jax.ShapeDtypeStruct((len(parts), rows, size), parts[0].dtype)
    return pl.pallas_call(
        other_core_kernel,
        out_shape=out,
        in_specs=[vmem] * len(parts) + [pl.BlockSpec(memory_space=pl.ANY)],
        out_specs=vmem,
        compiler_params=pltpu.CompilerParams(vmem_limit_bytes=4 * MIB),
        cost_estimate=pl.CostEstimate(flops=LATE_FLOPS // 2, bytes_accessed=4 * out.size, transcendentals=0),
        name="for_other_core",
    )(*parts, after)


def contract_kernel(which, shared, slab_ref, me_ref, home_ref, home_other_ref, ints_ref, *refs):
    last = which == "other"
    lhs = refs[-2] if last else refs[-1]
    count, rows, size = lhs.shape
    chips = count // 2 - 1
    start = start_of(which, slab_ref, shared)
    home_first = home_other_ref.shape[1] - home_ref.shape[2]
    lhs[0] = home_ref[0, :, pl.ds(start, size)]
    lhs[1] = home_other_ref[:, pl.ds(home_first + start, size)]
    for k in range(chips):
        lhs[2 * k + 2] = refs[k][0] if which == "rest" else refs[0][k, 0]
        if which == "own":
            lhs[2 * k + 3] = home_other_ref[:, k * size : (k + 1) * size]
        elif which == "other":
            lhs[2 * k + 3] = refs[1][k, 1]
        else:
            lhs[2 * k + 3] = refs[chips][k]
    refs = refs[{"own": 1, "other": 2, "rest": chips + 1}[which] :]
    step = 2560
    total = None
    for first in range(0, size, step):
        width = min(step, size - first)
        block = lhs[:, :, first : first + width].reshape(count * rows, width)
        part = jnp.dot(block, ints_ref[pl.ds(start + first, width)], preferred_element_type=jnp.float32)
        total = part if total is None else total + part
    if not last:
        before, out_ref = refs[:-2], refs[-2]
        out_ref[...] = total + before[0][...] if before else total
        return
    before_ref, own_ref, other_ref, _, partial = refs
    me = me_ref[0]
    partial[:count, :rows] = (total + before_ref[...]).reshape(count, rows, total.shape[1])
    for i in range(count):
        block = partial[i ^ me, :rows]
        partial[count + (i ^ me), :rows] = block
        for j in range(rows):
            partial[count + (j ^ me), rows + i : rows + i + 1] = block[j : j + 1]
    for k in range(count // 2):
        own_ref[k] = partial[count + 2 * k]
        other_ref[k] = partial[count + 2 * k + 1]


def contract(amps, home, home_other, ints, me, slab, shared, which, before=None):
    occupied, size = amps[0].shape[-2:]
    cols = ints.shape[1]
    vmem = pl.BlockSpec(memory_space=pltpu.VMEM)
    operands = [*amps] + ([] if before is None else [before])
    scratch = [pltpu.VMEM((occupied, occupied, size), home.dtype)]
    if which == "other":
        out_shape = [jax.ShapeDtypeStruct((occupied // 2, 2 * occupied, cols), jnp.float32)] * 2
        scratch.append(pltpu.VMEM((2 * occupied, 2 * occupied, cols), jnp.float32))
    else:
        out_shape = [jax.ShapeDtypeStruct((occupied * occupied, cols), jnp.float32)]
    return pl.pallas_call(
        functools.partial(contract_kernel, which, shared),
        out_shape=out_shape,
        in_specs=[pl.BlockSpec(memory_space=pltpu.SMEM)] * 2 + [vmem] * (3 + len(operands)),
        out_specs=[vmem] * len(out_shape),
        scratch_shapes=scratch,
        compiler_params=pltpu.CompilerParams(
            vmem_limit_bytes=4 * MIB + 40 * occupied * occupied * cols + 4 * occupied * occupied * size
        ),
        cost_estimate=pl.CostEstimate(
            flops=2 * occupied * occupied * size * cols,
            bytes_accessed=2 * size * (cols + occupied * occupied),
            transcendentals=0,
        ),
        name="contract",
    )(slab, me, home, home_other, pltpu.with_memory_space_constraint(ints, pltpu.VMEM), *operands)


def select_exactly(values, select):
    rows = values.shape[0]
    high = values.astype(jnp.bfloat16)
    rest = values - high.astype(jnp.float32)
    middle = rest.astype(jnp.bfloat16)
    low = (rest - middle.astype(jnp.float32)).astype(jnp.bfloat16)
    terms = [jnp.dot(term, select, preferred_element_type=jnp.float32) for term in (high, middle, low)]
    return terms[0] + terms[1] + terms[2]


def add_cores_kernel(mine_ref, other_ref, *outs):
    for k, out in enumerate(outs):
        out[...] = mine_ref[k] + other_ref[k]


def add_cores(mine, other):
    count, rows, cols = mine.shape
    vmem = pl.BlockSpec(memory_space=pltpu.VMEM)
    return pl.pallas_call(
        add_cores_kernel,
        out_shape=[jax.ShapeDtypeStruct((rows, cols), jnp.float32)] * count,
        in_specs=[vmem, vmem],
        out_specs=[vmem] * count,
        compiler_params=pltpu.CompilerParams(vmem_limit_bytes=4 * MIB),
        cost_estimate=pl.CostEstimate(flops=mine.size, bytes_accessed=12 * mine.size, transcendentals=0),
        name="add_cores",
    )(mine, other)


def add_chips_kernel(*refs):
    parts, (ladder_ref, mirror_ref) = refs[:-2], refs[-2:]
    total = parts[0][...]
    for part in parts[1:]:
        total = total + part[...]
    half = total.shape[0] // 2
    ladder_ref[...] = total[:half]
    mirror_ref[...] = total[half:]


def add_chips(parts):
    rows, cols = parts[0].shape
    half = jax.ShapeDtypeStruct((rows // 2, cols), jnp.float32)
    vmem = pl.BlockSpec(memory_space=pltpu.VMEM)
    return pl.pallas_call(
        add_chips_kernel,
        out_shape=[half, half],
        in_specs=[vmem] * len(parts),
        out_specs=[vmem, vmem],
        compiler_params=pltpu.CompilerParams(vmem_limit_bytes=4 * MIB),
        cost_estimate=pl.CostEstimate(
            flops=len(parts) * rows * cols, bytes_accessed=4 * len(parts) * rows * cols, transcendentals=0
        ),
        name="add_chips",
    )(*parts)


def finish_kernel(ladder_ref, denominator_ref, select_ref, own_ref, *refs):
    down, up, out_ref = refs[: len(refs) // 2], refs[len(refs) // 2 : -1], refs[-1]
    blocks = [own_ref[...]] + [one[...] + other[...] for one, other in zip(down, up)]
    mirror = select_exactly(jnp.concatenate(blocks, axis=1), select_ref[...])
    update = (ladder_ref[...] + mirror) / denominator_ref[...]
    _, first_local, slab_virt = out_ref.shape
    for a in range(first_local):
        out_ref[:, a, :] = update[:, a * slab_virt : (a + 1) * slab_virt]


def finish(ladder, mirror, down, up, denominator, select, first_local, slab_virt):
    rows = ladder.shape[0]
    return pl.pallas_call(
        finish_kernel,
        out_shape=jax.ShapeDtypeStruct((rows, first_local, slab_virt), jnp.float32),
        in_specs=[pl.BlockSpec(memory_space=pltpu.VMEM)] * (4 + len(down) + len(up)),
        out_specs=pl.BlockSpec(memory_space=pltpu.VMEM),
        compiler_params=pltpu.CompilerParams(vmem_limit_bytes=6 * MIB),
        cost_estimate=pl.CostEstimate(flops=6 * rows * select.size, bytes_accessed=2 * select.size, transcendentals=0),
        name="finish",
    )(ladder, denominator, select, mirror, *down, *up)


def swap(values, axis, bits):
    return lax.ppermute(values, axis, [(p, p ^ bits) for p in range(lax.axis_size(axis))])


def local(amplitudes, integrals, virt_irrep, occ_energy, slab_energy):
    pair_count = lax.axis_size("pair")
    slab_count = lax.axis_size("slab")
    occ_local, occupied, virt_pairs = amplitudes.shape
    rows_local, cols_local = integrals.shape
    slab_virt = slab_energy.shape[0]
    first_local = slab_virt // slab_count
    assert occ_local == 1
    me = lax.axis_index("pair").astype(jnp.int32).reshape(1)
    slab = lax.axis_index("slab").astype(jnp.int32).reshape(1)

    shared = int(SHARE * rows_local) // 128 * 128
    amps = amplitudes.reshape(occupied, virt_pairs)
    chips = [2 * k for k in range(1, pair_count // 2)]

    def to_chips(parts):
        return [swap(part, "pair", bits) for part, bits in zip(parts, chips)]

    parts = pack(amps, me, slab, shared, "own", pair_count)
    own_amps = to_chips(parts)
    parts = pack(amps, me, slab, shared, "rest", pair_count, parts[-1])
    rest_amps = to_chips(parts)
    (home,) = pack(amps, me, slab, shared, "all", pair_count, parts[-1])

    own_amps, for_other = merge(own_amps, home)
    other_amps = swap(own_amps, "slab", 1)
    home_other = swap(for_other, "pair", 1)
    masked, select, denominator = mask(integrals, me, slab, virt_irrep, occ_energy, slab_energy, own_amps)
    rest_others = swap(for_other_core(rest_amps, denominator), "pair", 1)
    place = (home, home_other, masked, me, slab, shared)
    (partial,) = contract([own_amps], *place, "own")
    (partial,) = contract([*rest_amps, rest_others], *place, "rest", partial)
    even, odd = contract([other_amps, swap(other_amps, "pair", 1)], *place, "other", partial)

    parts = add_cores(even, swap(odd, "pair", 1))
    every = range(pair_count)
    pairs = [[(p, p ^ bits) for p in every if p ^ bits < p] for bits in chips]
    got = [lax.ppermute(part, "pair", down) for part, down in zip(parts[1:], pairs)]
    got += [lax.ppermute(part, "pair", [(q, p) for p, q in down]) for part, down in zip(parts[1:], pairs)]
    ladder, mirror = add_chips([parts[0], *got])
    steps = range(1, slab_count)
    down = [lax.ppermute(mirror, "slab", [(s, s - k) for s in range(k, slab_count)]) for k in steps]
    up = [lax.ppermute(mirror, "slab", [(s, s + slab_count - k) for s in range(k)]) for k in steps]
    update = finish(ladder, mirror, down, up, denominator, select, first_local, slab_virt)
    return update.reshape(occ_local, occupied, first_local, slab_virt)


def solution(mesh):
    placed = (P("pair", None, None), P("pair", "slab"), P(), P(), P())
    return jax.shard_map(
        local, mesh=mesh, in_specs=placed, out_specs=P("pair", None, "slab", None), check_vma=False
    )
```

```python
import functools
import math

import jax
import jax.numpy as jnp
from jax import lax
from jax.experimental import pallas as pl
from jax.experimental.pallas import tpu as pltpu
from jax.sharding import PartitionSpec as P

IRREPS = 8
MIB = 2**20
SHARE = 0.24
LATE_FLOPS = 10**10


def start_of(part, slab_ref, shared):
    parity = slab_ref[0] % 2
    return pl.multiple_of({"own": parity * shared, "other": (1 - parity) * shared, "rest": 2 * shared, "all": 0}[part], 128)


def pack_kernel(rows_local, shared, which, me_ref, slab_ref, amps_ref, after_ref, *refs):
    outs, (held, packed, sems) = refs[:-3], refs[-3:]
    _, _, size = packed.shape
    count = sems.shape[0]
    home = which == "all"
    me = me_ref[0]
    start = start_of(which, slab_ref, shared)
    loads, shifts = [], []
    for dest in range(count):
        first = dest * rows_local // 128 * 128
        shifts.append(dest * rows_local - first)
        width = -(-(shifts[dest] + size) // 128) * 128
        slot = dest ^ me if home else dest
        loads.append(
            pltpu.make_async_copy(
                amps_ref.at[:, pl.ds(start + first, width)], held.at[slot, :, pl.ds(0, width)], sems.at[dest]
            )
        )

    def wanted(dest):
        return (dest ^ me) // 2 == 0 if home else True

    for dest in range(count):
        pl.when(wanted(dest))(loads[dest].start)
    for dest in range(count):

        @pl.when(wanted(dest))
        def _():
            loads[dest].wait()
            packed[dest ^ me] = held[dest ^ me if home else dest, :, shifts[dest] : shifts[dest] + size]

    for k, out in enumerate(outs):
        slot = 0 if home else 2 * k + 2
        out[...] = packed[slot : slot + 2]


def pack(amps, me, slab, shared, which, pair_count, after=None):
    rows, virt_pairs = amps.shape
    rows_local = virt_pairs // pair_count
    home = which == "all"
    size = {"own": shared, "rest": rows_local - 2 * shared, "all": rows_local}[which]
    held = (2 if home else pair_count, rows, -(-size // 128) * 128 + 128)
    packed = (held[0], rows, size)
    outs = 1 if home else pair_count // 2 - 1
    vmem = 2 * MIB + 6 * held[0] * rows * held[2]
    return pl.pallas_call(
        functools.partial(pack_kernel, rows_local, shared, which),
        out_shape=[jax.ShapeDtypeStruct((2, rows, size), amps.dtype)] * outs,
        in_specs=[pl.BlockSpec(memory_space=pltpu.SMEM)] * 2
        + [pl.BlockSpec(memory_space=pltpu.HBM), pl.BlockSpec(memory_space=pl.ANY)],
        out_specs=[pl.BlockSpec(memory_space=pltpu.VMEM)] * outs,
        scratch_shapes=[
            pltpu.VMEM(held, amps.dtype),
            pltpu.VMEM(packed, amps.dtype),
            pltpu.SemaphoreType.DMA((pair_count,)),
        ],
        compiler_params=pltpu.CompilerParams(vmem_limit_bytes=vmem),
        cost_estimate=pl.CostEstimate(flops=0, bytes_accessed=4 * held[0] * rows * size, transcendentals=0),
        name="pack_home" if home else "pack_amplitudes",
    )(me, slab, pltpu.with_memory_space_constraint(amps, pltpu.HBM), me if after is None else after)


def mask_kernel(per_step, parts, me_ref, slab_ref, irrep_ref, occ_ref, virt_ref, row_ref, ints_ref, *refs):
    _, out_ref, select_ref, denominator_ref, table, padded, by_row = refs
    step = pl.program_id(0)
    chunk, cols = ints_ref.shape[1:]
    slab_virt = virt_ref.shape[0]
    first_local = cols // slab_virt
    bits = slab_virt.bit_length() - 1
    me, slab = me_ref[0], slab_ref[0]

    @pl.when(step == 0)
    def _():
        padded[:, : row_ref.shape[1]] = row_ref[...]
        for k in range(padded.shape[1] // 128):
            lanes = slice(k * 128, (k + 1) * 128)
            by_row[lanes] = jnp.transpose(jnp.broadcast_to(padded[:, lanes], (128, 128)))

        col = lax.broadcasted_iota(jnp.int32, (1, cols), 1)
        a_of, b_of = col >> bits, col & (slab_virt - 1)
        irrep_a = irrep_b = jnp.zeros_like(col)
        energy_a = energy_b = jnp.zeros(col.shape, jnp.float32)
        for a in range(first_local):
            irrep_a = jnp.where(a_of == a, irrep_ref[slab * first_local + a], irrep_a)
            energy_a = jnp.where(a_of == a, virt_ref[slab * first_local + a], energy_a)
        for b in range(slab_virt):
            irrep_b = jnp.where(b_of == b, irrep_ref[b], irrep_b)
            energy_b = jnp.where(b_of == b, virt_ref[b], energy_b)
        irrep_ab = irrep_a ^ irrep_b

        for part in range(parts):
            for lanes in (slice(k, k + 128) for k in range(0, cols, 128)):
                needed = by_row[part * chunk : (part + 1) * chunk] ^ irrep_ab[:, lanes]
                for irrep in range(IRREPS):
                    table[irrep * parts + part, :, lanes] = jnp.where(needed == irrep, 1.0, 0.0).astype(table.dtype)

        occupied = denominator_ref.shape[0]
        j_of = lax.broadcasted_iota(jnp.int32, (occupied, cols), 0)
        energy_j = jnp.zeros((occupied, cols), jnp.float32)
        for j in range(occupied):
            energy_j = jnp.where(j_of == j, occ_ref[j], energy_j)
        denominator_ref[...] = energy_a + energy_b - occ_ref[me] - energy_j

        row = lax.broadcasted_iota(jnp.int32, (cols, cols), 0)
        col = lax.broadcasted_iota(jnp.int32, (cols, cols), 1)
        same_a = (row & (slab_virt - 1)) == slab * first_local + (col >> bits)
        slab_count = select_ref.shape[0] // cols
        for t in range(slab_count):
            same_b = (slab + t) % slab_count * first_local + (row >> bits) == (col & (slab_virt - 1))
            chosen = jnp.where(same_a & same_b, 1.0, 0.0)
            select_ref[t * cols : (t + 1) * cols] = chosen.astype(select_ref.dtype)

    chunks = per_step * pl.num_programs(0)
    for k in range(per_step):
        index = me * chunks + step * per_step + k
        irrep_c = irrep_ref[index // parts]
        out_ref[k] = ints_ref[k] * table[irrep_c * parts + index % parts]


def in_hbm(array):
    return pltpu.with_memory_space_constraint(array, pltpu.HBM)


def mask(integrals, me, slab, virt_irrep, occ_energy, slab_energy, after):
    virtuals = virt_irrep.shape[0]
    slab_virt = slab_energy.shape[0]
    occupied = occ_energy.shape[0]
    rows_local, cols_local = integrals.shape
    chunk = math.gcd(virtuals, rows_local)
    parts = virtuals // chunk
    chunks = rows_local // chunk
    per_step = next(n for n in (10, 5, 4, 2, 1) if chunks % n == 0)
    padded = -(-virtuals // 128) * 128
    select_rows = slab_virt * slab_virt
    block = pl.BlockSpec((per_step, chunk, cols_local), lambda step: (step, 0, 0))
    scalars = pl.BlockSpec(memory_space=pltpu.SMEM)
    masked, select, denominator = pl.pallas_call(
        functools.partial(mask_kernel, per_step, parts),
        grid=(chunks // per_step,),
        in_specs=[scalars] * 5
        + [pl.BlockSpec((1, virtuals), lambda step: (0, 0)), block, pl.BlockSpec(memory_space=pl.ANY)],
        out_specs=[
            block,
            pl.BlockSpec((select_rows, cols_local), lambda step: (0, 0)),
            pl.BlockSpec((occupied, cols_local), lambda step: (0, 0)),
        ],
        scratch_shapes=[
            pltpu.VMEM((IRREPS * parts, chunk, cols_local), integrals.dtype),
            pltpu.VMEM((1, padded), jnp.int32),
            pltpu.VMEM((padded, 128), jnp.int32),
        ],
        out_shape=[
            pltpu.VMEM((chunks, chunk, cols_local), integrals.dtype),
            jax.ShapeDtypeStruct((select_rows, cols_local), jnp.bfloat16),
            jax.ShapeDtypeStruct((occupied, cols_local), jnp.float32),
        ],
        compiler_params=pltpu.CompilerParams(vmem_limit_bytes=16 * MIB),
        cost_estimate=pl.CostEstimate(
            flops=LATE_FLOPS, bytes_accessed=4 * rows_local * cols_local, transcendentals=0
        ),
        name="mask_integrals",
    )(
        me,
        slab,
        *(in_hbm(array) for array in (virt_irrep, occ_energy, slab_energy, virt_irrep.reshape(1, virtuals))),
        in_hbm(integrals.reshape(chunks, chunk, cols_local)),
        after,
    )
    return masked.reshape(rows_local, cols_local), select, denominator


def merge_kernel(*refs):
    parts, home_ref, all_ref, other_ref = refs[:-3], refs[-3], refs[-2], refs[-1]
    size = parts[0].shape[2]
    for k, part in enumerate(parts):
        all_ref[k] = part[...]
        other_ref[:, k * size : (k + 1) * size] = part[1]
    other_ref[:, len(parts) * size :] = home_ref[1]


def merge(parts, home):
    count = len(parts)
    _, rows, size = parts[0].shape
    other = (rows, count * size + home.shape[2])
    vmem = pl.BlockSpec(memory_space=pltpu.VMEM)
    return pl.pallas_call(
        merge_kernel,
        out_shape=[
            jax.ShapeDtypeStruct((count,) + parts[0].shape, home.dtype),
            jax.ShapeDtypeStruct(other, home.dtype),
        ],
        in_specs=[vmem] * (count + 1),
        out_specs=[vmem, vmem],
        compiler_params=pltpu.CompilerParams(vmem_limit_bytes=4 * MIB),
        cost_estimate=pl.CostEstimate(flops=0, bytes_accessed=6 * rows * other[1], transcendentals=0),
        name="merge",
    )(*parts, home)


def other_core_kernel(*refs):
    parts, out_ref = refs[:-2], refs[-1]
    for k, part in enumerate(parts):
        out_ref[k] = part[1]


def for_other_core(parts, after):
    vmem = pl.BlockSpec(memory_space=pltpu.VMEM)
    _, rows, size = parts[0].shape
    out = jax.ShapeDtypeStruct((len(parts), rows, size), parts[0].dtype)
    return pl.pallas_call(
        other_core_kernel,
        out_shape=out,
        in_specs=[vmem] * len(parts) + [pl.BlockSpec(memory_space=pl.ANY)],
        out_specs=vmem,
        compiler_params=pltpu.CompilerParams(vmem_limit_bytes=4 * MIB),
        cost_estimate=pl.CostEstimate(flops=LATE_FLOPS // 2, bytes_accessed=4 * out.size, transcendentals=0),
        name="for_other_core",
    )(*parts, after)


def contract_kernel(which, shared, slab_ref, me_ref, home_ref, home_other_ref, ints_ref, *refs):
    last = which == "other"
    lhs = refs[-2] if last else refs[-1]
    count, rows, size = lhs.shape
    chips = count // 2 - 1
    start = start_of(which, slab_ref, shared)
    home_first = home_other_ref.shape[1] - home_ref.shape[2]
    lhs[0] = home_ref[0, :, pl.ds(start, size)]
    lhs[1] = home_other_ref[:, pl.ds(home_first + start, size)]
    for k in range(chips):
        lhs[2 * k + 2] = refs[k][0] if which == "rest" else refs[0][k, 0]
        if which == "own":
            lhs[2 * k + 3] = home_other_ref[:, k * size : (k + 1) * size]
        elif which == "other":
            lhs[2 * k + 3] = refs[1][k, 1]
        else:
            lhs[2 * k + 3] = refs[chips][k]
    refs = refs[{"own": 1, "other": 2, "rest": chips + 1}[which] :]
    step = 2560
    total = None
    for first in range(0, size, step):
        width = min(step, size - first)
        block = lhs[:, :, first : first + width].reshape(count * rows, width)
        part = jnp.dot(block, ints_ref[pl.ds(start + first, width)], preferred_element_type=jnp.float32)
        total = part if total is None else total + part
    if not last:
        before, out_ref = refs[:-2], refs[-2]
        out_ref[...] = total + before[0][...] if before else total
        return
    before_ref, own_ref, other_ref, _, partial = refs
    me = me_ref[0]
    partial[:count, :rows] = (total + before_ref[...]).reshape(count, rows, total.shape[1])
    for i in range(count):
        block = partial[i ^ me, :rows]
        partial[count + (i ^ me), :rows] = block
        for j in range(rows):
            partial[count + (j ^ me), rows + i : rows + i + 1] = block[j : j + 1]
    for k in range(count // 2):
        own_ref[k] = partial[count + 2 * k]
        other_ref[k] = partial[count + 2 * k + 1]


def contract(amps, home, home_other, ints, me, slab, shared, which, before=None):
    occupied, size = amps[0].shape[-2:]
    cols = ints.shape[1]
    vmem = pl.BlockSpec(memory_space=pltpu.VMEM)
    operands = [*amps] + ([] if before is None else [before])
    scratch = [pltpu.VMEM((occupied, occupied, size), home.dtype)]
    if which == "other":
        out_shape = [jax.ShapeDtypeStruct((occupied // 2, 2 * occupied, cols), jnp.float32)] * 2
        scratch.append(pltpu.VMEM((2 * occupied, 2 * occupied, cols), jnp.float32))
    else:
        out_shape = [jax.ShapeDtypeStruct((occupied * occupied, cols), jnp.float32)]
    return pl.pallas_call(
        functools.partial(contract_kernel, which, shared),
        out_shape=out_shape,
        in_specs=[pl.BlockSpec(memory_space=pltpu.SMEM)] * 2 + [vmem] * (3 + len(operands)),
        out_specs=[vmem] * len(out_shape),
        scratch_shapes=scratch,
        compiler_params=pltpu.CompilerParams(
            vmem_limit_bytes=4 * MIB + 40 * occupied * occupied * cols + 4 * occupied * occupied * size
        ),
        cost_estimate=pl.CostEstimate(
            flops=2 * occupied * occupied * size * cols,
            bytes_accessed=2 * size * (cols + occupied * occupied),
            transcendentals=0,
        ),
        name="contract",
    )(slab, me, home, home_other, pltpu.with_memory_space_constraint(ints, pltpu.VMEM), *operands)


def select_exactly(values, select):
    rows = values.shape[0]
    high = values.astype(jnp.bfloat16)
    rest = values - high.astype(jnp.float32)
    middle = rest.astype(jnp.bfloat16)
    low = (rest - middle.astype(jnp.float32)).astype(jnp.bfloat16)
    terms = [jnp.dot(term, select, preferred_element_type=jnp.float32) for term in (high, middle, low)]
    return terms[0] + terms[1] + terms[2]


def add_cores_kernel(mine_ref, other_ref, *outs):
    for k, out in enumerate(outs):
        out[...] = mine_ref[k] + other_ref[k]


def add_cores(mine, other):
    count, rows, cols = mine.shape
    vmem = pl.BlockSpec(memory_space=pltpu.VMEM)
    return pl.pallas_call(
        add_cores_kernel,
        out_shape=[jax.ShapeDtypeStruct((rows, cols), jnp.float32)] * count,
        in_specs=[vmem, vmem],
        out_specs=[vmem] * count,
        compiler_params=pltpu.CompilerParams(vmem_limit_bytes=4 * MIB),
        cost_estimate=pl.CostEstimate(flops=mine.size, bytes_accessed=12 * mine.size, transcendentals=0),
        name="add_cores",
    )(mine, other)


def add_chips_kernel(*refs):
    parts, (ladder_ref, mirror_ref) = refs[:-2], refs[-2:]
    total = parts[0][...]
    for part in parts[1:]:
        total = total + part[...]
    half = total.shape[0] // 2
    ladder_ref[...] = total[:half]
    mirror_ref[...] = total[half:]


def add_chips(parts):
    rows, cols = parts[0].shape
    half = jax.ShapeDtypeStruct((rows // 2, cols), jnp.float32)
    vmem = pl.BlockSpec(memory_space=pltpu.VMEM)
    return pl.pallas_call(
        add_chips_kernel,
        out_shape=[half, half],
        in_specs=[vmem] * len(parts),
        out_specs=[vmem, vmem],
        compiler_params=pltpu.CompilerParams(vmem_limit_bytes=4 * MIB),
        cost_estimate=pl.CostEstimate(
            flops=len(parts) * rows * cols, bytes_accessed=4 * len(parts) * rows * cols, transcendentals=0
        ),
        name="add_chips",
    )(*parts)


def finish_kernel(ladder_ref, denominator_ref, select_ref, *refs):
    mirrors, out_ref = refs[:-1], refs[-1]
    mirror = select_exactly(jnp.concatenate([ref[...] for ref in mirrors], axis=1), select_ref[...])
    update = (ladder_ref[...] + mirror) / denominator_ref[...]
    _, first_local, slab_virt = out_ref.shape
    for a in range(first_local):
        out_ref[:, a, :] = update[:, a * slab_virt : (a + 1) * slab_virt]


def finish(ladder, mirrors, denominator, select, first_local, slab_virt):
    rows = ladder.shape[0]
    return pl.pallas_call(
        finish_kernel,
        out_shape=jax.ShapeDtypeStruct((rows, first_local, slab_virt), jnp.float32),
        in_specs=[pl.BlockSpec(memory_space=pltpu.VMEM)] * (3 + len(mirrors)),
        out_specs=pl.BlockSpec(memory_space=pltpu.VMEM),
        compiler_params=pltpu.CompilerParams(vmem_limit_bytes=6 * MIB),
        cost_estimate=pl.CostEstimate(flops=6 * rows * select.size, bytes_accessed=2 * select.size, transcendentals=0),
        name="finish",
    )(ladder, denominator, select, *mirrors)


def swap(values, axis, bits):
    return lax.ppermute(values, axis, [(p, p ^ bits) for p in range(lax.axis_size(axis))])


def local(amplitudes, integrals, virt_irrep, occ_energy, slab_energy):
    pair_count = lax.axis_size("pair")
    slab_count = lax.axis_size("slab")
    occ_local, occupied, virt_pairs = amplitudes.shape
    rows_local, cols_local = integrals.shape
    slab_virt = slab_energy.shape[0]
    first_local = slab_virt // slab_count
    assert occ_local == 1
    me = lax.axis_index("pair").astype(jnp.int32).reshape(1)
    slab = lax.axis_index("slab").astype(jnp.int32).reshape(1)

    shared = int(SHARE * rows_local) // 128 * 128
    amps = amplitudes.reshape(occupied, virt_pairs)
    chips = [2 * k for k in range(1, pair_count // 2)]

    def to_chips(parts):
        return [swap(part, "pair", bits) for part, bits in zip(parts, chips)]

    parts = pack(amps, me, slab, shared, "own", pair_count)
    own_amps = to_chips(parts)
    parts = pack(amps, me, slab, shared, "rest", pair_count, parts[-1])
    rest_amps = to_chips(parts)
    (home,) = pack(amps, me, slab, shared, "all", pair_count, parts[-1])

    own_amps, for_other = merge(own_amps, home)
    other_amps = swap(own_amps, "slab", 1)
    home_other = swap(for_other, "pair", 1)
    masked, select, denominator = mask(integrals, me, slab, virt_irrep, occ_energy, slab_energy, own_amps)
    rest_others = swap(for_other_core(rest_amps, denominator), "pair", 1)
    place = (home, home_other, masked, me, slab, shared)
    (partial,) = contract([own_amps], *place, "own")
    (partial,) = contract([*rest_amps, rest_others], *place, "rest", partial)
    even, odd = contract([other_amps, swap(other_amps, "pair", 1)], *place, "other", partial)

    parts = add_cores(even, swap(odd, "pair", 1))
    parts = [parts[0]] + [swap(parts[k], "pair", 2 * k) for k in reversed(range(1, pair_count // 2))]
    ladder, mirror = add_chips(parts)
    mirrors = [
        lax.ppermute(mirror, "slab", [(s, (s - k) % slab_count) for s in range(slab_count)])
        for k in reversed(range(1, slab_count))
    ]
    mirrors = [mirror] + mirrors[::-1]
    update = finish(ladder, mirrors, denominator, select, first_local, slab_virt)
    return update.reshape(occ_local, occupied, first_local, slab_virt)


def solution(mesh):
    placed = (P("pair", None, None), P("pair", "slab"), P(), P(), P())
    return jax.shard_map(
        local, mesh=mesh, in_specs=placed, out_specs=P("pair", None, "slab", None), check_vma=False
    )
```

```python
import functools
import math

import jax
import jax.numpy as jnp
from jax import lax
from jax.experimental import pallas as pl
from jax.experimental.pallas import tpu as pltpu
from jax.sharding import PartitionSpec as P

IRREPS = 8
MIB = 2**20
SHARE = 0.24
LATE_FLOPS = 10**10


def start_of(part, slab_ref, shared):
    parity = slab_ref[0] % 2
    return pl.multiple_of({"own": parity * shared, "other": (1 - parity) * shared, "rest": 2 * shared, "all": 0}[part], 128)


def pack_kernel(rows_local, shared, which, me_ref, slab_ref, amps_ref, after_ref, *refs):
    outs, (held, packed, sems) = refs[:-3], refs[-3:]
    _, _, size = packed.shape
    count = sems.shape[0]
    home = which == "all"
    me = me_ref[0]
    start = start_of(which, slab_ref, shared)
    loads, shifts = [], []
    for dest in range(count):
        first = dest * rows_local // 128 * 128
        shifts.append(dest * rows_local - first)
        width = -(-(shifts[dest] + size) // 128) * 128
        slot = dest ^ me if home else dest
        loads.append(
            pltpu.make_async_copy(
                amps_ref.at[:, pl.ds(start + first, width)], held.at[slot, :, pl.ds(0, width)], sems.at[dest]
            )
        )

    def wanted(dest):
        return (dest ^ me) // 2 == 0 if home else True

    for dest in range(count):
        pl.when(wanted(dest))(loads[dest].start)
    for dest in range(count):

        @pl.when(wanted(dest))
        def _():
            loads[dest].wait()
            packed[dest ^ me] = held[dest ^ me if home else dest, :, shifts[dest] : shifts[dest] + size]

    for k, out in enumerate(outs):
        slot = 0 if home else 2 * k + 2
        out[...] = packed[slot : slot + 2]


def pack(amps, me, slab, shared, which, pair_count, after=None):
    rows, virt_pairs = amps.shape
    rows_local = virt_pairs // pair_count
    home = which == "all"
    size = {"own": shared, "rest": rows_local - 2 * shared, "all": rows_local}[which]
    held = (2 if home else pair_count, rows, -(-size // 128) * 128 + 128)
    packed = (held[0], rows, size)
    outs = 1 if home else pair_count // 2 - 1
    vmem = 2 * MIB + 6 * held[0] * rows * held[2]
    return pl.pallas_call(
        functools.partial(pack_kernel, rows_local, shared, which),
        out_shape=[jax.ShapeDtypeStruct((2, rows, size), amps.dtype)] * outs,
        in_specs=[pl.BlockSpec(memory_space=pltpu.SMEM)] * 2
        + [pl.BlockSpec(memory_space=pltpu.HBM), pl.BlockSpec(memory_space=pl.ANY)],
        out_specs=[pl.BlockSpec(memory_space=pltpu.VMEM)] * outs,
        scratch_shapes=[
            pltpu.VMEM(held, amps.dtype),
            pltpu.VMEM(packed, amps.dtype),
            pltpu.SemaphoreType.DMA((pair_count,)),
        ],
        compiler_params=pltpu.CompilerParams(vmem_limit_bytes=vmem),
        cost_estimate=pl.CostEstimate(flops=0, bytes_accessed=4 * held[0] * rows * size, transcendentals=0),
        name="pack_home" if home else "pack_amplitudes",
    )(me, slab, pltpu.with_memory_space_constraint(amps, pltpu.HBM), me if after is None else after)


def mask_kernel(per_step, parts, me_ref, slab_ref, irrep_ref, occ_ref, virt_ref, row_ref, ints_ref, *refs):
    _, out_ref, select_ref, denominator_ref, table, padded, by_row = refs
    step = pl.program_id(0)
    chunk, cols = ints_ref.shape[1:]
    slab_virt = virt_ref.shape[0]
    first_local = cols // slab_virt
    bits = slab_virt.bit_length() - 1
    me, slab = me_ref[0], slab_ref[0]

    @pl.when(step == 0)
    def _():
        padded[:, : row_ref.shape[1]] = row_ref[...]
        for k in range(padded.shape[1] // 128):
            lanes = slice(k * 128, (k + 1) * 128)
            by_row[lanes] = jnp.transpose(jnp.broadcast_to(padded[:, lanes], (128, 128)))

        col = lax.broadcasted_iota(jnp.int32, (1, cols), 1)
        a_of, b_of = col >> bits, col & (slab_virt - 1)
        irrep_a = irrep_b = jnp.zeros_like(col)
        energy_a = energy_b = jnp.zeros(col.shape, jnp.float32)
        for a in range(first_local):
            irrep_a = jnp.where(a_of == a, irrep_ref[slab * first_local + a], irrep_a)
            energy_a = jnp.where(a_of == a, virt_ref[slab * first_local + a], energy_a)
        for b in range(slab_virt):
            irrep_b = jnp.where(b_of == b, irrep_ref[b], irrep_b)
            energy_b = jnp.where(b_of == b, virt_ref[b], energy_b)
        irrep_ab = irrep_a ^ irrep_b

        for part in range(parts):
            for lanes in (slice(k, k + 128) for k in range(0, cols, 128)):
                needed = by_row[part * chunk : (part + 1) * chunk] ^ irrep_ab[:, lanes]
                for irrep in range(IRREPS):
                    table[irrep * parts + part, :, lanes] = jnp.where(needed == irrep, 1.0, 0.0).astype(table.dtype)

        occupied = denominator_ref.shape[0]
        j_of = lax.broadcasted_iota(jnp.int32, (occupied, cols), 0)
        energy_j = jnp.zeros((occupied, cols), jnp.float32)
        for j in range(occupied):
            energy_j = jnp.where(j_of == j, occ_ref[j], energy_j)
        denominator_ref[...] = energy_a + energy_b - occ_ref[me] - energy_j

        row = lax.broadcasted_iota(jnp.int32, (cols, cols), 0)
        col = lax.broadcasted_iota(jnp.int32, (cols, cols), 1)
        same_a = (row & (slab_virt - 1)) == slab * first_local + (col >> bits)
        slab_count = select_ref.shape[0] // cols
        for t in range(slab_count):
            same_b = (slab + t) % slab_count * first_local + (row >> bits) == (col & (slab_virt - 1))
            chosen = jnp.where(same_a & same_b, 1.0, 0.0)
            select_ref[t * cols : (t + 1) * cols] = chosen.astype(select_ref.dtype)

    chunks = per_step * pl.num_programs(0)
    for k in range(per_step):
        index = me * chunks + step * per_step + k
        irrep_c = irrep_ref[index // parts]
        out_ref[k] = ints_ref[k] * table[irrep_c * parts + index % parts]


def in_hbm(array):
    return pltpu.with_memory_space_constraint(array, pltpu.HBM)


def mask(integrals, me, slab, virt_irrep, occ_energy, slab_energy, after):
    virtuals = virt_irrep.shape[0]
    slab_virt = slab_energy.shape[0]
    occupied = occ_energy.shape[0]
    rows_local, cols_local = integrals.shape
    chunk = math.gcd(virtuals, rows_local)
    parts = virtuals // chunk
    chunks = rows_local // chunk
    per_step = next(n for n in (10, 5, 4, 2, 1) if chunks % n == 0)
    padded = -(-virtuals // 128) * 128
    select_rows = slab_virt * slab_virt
    block = pl.BlockSpec((per_step, chunk, cols_local), lambda step: (step, 0, 0))
    scalars = pl.BlockSpec(memory_space=pltpu.SMEM)
    masked, select, denominator = pl.pallas_call(
        functools.partial(mask_kernel, per_step, parts),
        grid=(chunks // per_step,),
        in_specs=[scalars] * 5
        + [pl.BlockSpec((1, virtuals), lambda step: (0, 0)), block, pl.BlockSpec(memory_space=pl.ANY)],
        out_specs=[
            block,
            pl.BlockSpec((select_rows, cols_local), lambda step: (0, 0)),
            pl.BlockSpec((occupied, cols_local), lambda step: (0, 0)),
        ],
        scratch_shapes=[
            pltpu.VMEM((IRREPS * parts, chunk, cols_local), integrals.dtype),
            pltpu.VMEM((1, padded), jnp.int32),
            pltpu.VMEM((padded, 128), jnp.int32),
        ],
        out_shape=[
            pltpu.VMEM((chunks, chunk, cols_local), integrals.dtype),
            jax.ShapeDtypeStruct((select_rows, cols_local), jnp.bfloat16),
            jax.ShapeDtypeStruct((occupied, cols_local), jnp.float32),
        ],
        compiler_params=pltpu.CompilerParams(vmem_limit_bytes=16 * MIB),
        cost_estimate=pl.CostEstimate(
            flops=LATE_FLOPS, bytes_accessed=4 * rows_local * cols_local, transcendentals=0
        ),
        name="mask_integrals",
    )(
        me,
        slab,
        *(in_hbm(array) for array in (virt_irrep, occ_energy, slab_energy, virt_irrep.reshape(1, virtuals))),
        in_hbm(integrals.reshape(chunks, chunk, cols_local)),
        after,
    )
    return masked.reshape(rows_local, cols_local), select, denominator


def merge_kernel(*refs):
    parts, home_ref, all_ref, other_ref = refs[:-3], refs[-3], refs[-2], refs[-1]
    size = parts[0].shape[2]
    for k, part in enumerate(parts):
        all_ref[k] = part[...]
        other_ref[:, k * size : (k + 1) * size] = part[1]
    other_ref[:, len(parts) * size :] = home_ref[1]


def merge(parts, home):
    count = len(parts)
    _, rows, size = parts[0].shape
    other = (rows, count * size + home.shape[2])
    vmem = pl.BlockSpec(memory_space=pltpu.VMEM)
    return pl.pallas_call(
        merge_kernel,
        out_shape=[
            jax.ShapeDtypeStruct((count,) + parts[0].shape, home.dtype),
            jax.ShapeDtypeStruct(other, home.dtype),
        ],
        in_specs=[vmem] * (count + 1),
        out_specs=[vmem, vmem],
        compiler_params=pltpu.CompilerParams(vmem_limit_bytes=4 * MIB),
        cost_estimate=pl.CostEstimate(flops=0, bytes_accessed=6 * rows * other[1], transcendentals=0),
        name="merge",
    )(*parts, home)


def other_core_kernel(*refs):
    parts, out_ref = refs[:-2], refs[-1]
    for k, part in enumerate(parts):
        out_ref[k] = part[1]


def for_other_core(parts, after):
    vmem = pl.BlockSpec(memory_space=pltpu.VMEM)
    _, rows, size = parts[0].shape
    out = jax.ShapeDtypeStruct((len(parts), rows, size), parts[0].dtype)
    return pl.pallas_call(
        other_core_kernel,
        out_shape=out,
        in_specs=[vmem] * len(parts) + [pl.BlockSpec(memory_space=pl.ANY)],
        out_specs=vmem,
        compiler_params=pltpu.CompilerParams(vmem_limit_bytes=4 * MIB),
        cost_estimate=pl.CostEstimate(flops=LATE_FLOPS // 2, bytes_accessed=4 * out.size, transcendentals=0),
        name="for_other_core",
    )(*parts, after)


def contract_kernel(which, shared, slab_ref, me_ref, home_ref, home_other_ref, ints_ref, *refs):
    last = which == "rest"
    lhs = refs[-2] if last else refs[-1]
    count, rows, size = lhs.shape
    chips = count // 2 - 1
    start = start_of(which, slab_ref, shared)
    home_first = home_other_ref.shape[1] - home_ref.shape[2]
    lhs[0] = home_ref[0, :, pl.ds(start, size)]
    lhs[1] = home_other_ref[:, pl.ds(home_first + start, size)]
    for k in range(chips):
        lhs[2 * k + 2] = refs[k][0] if which == "rest" else refs[0][k, 0]
        if which == "own":
            lhs[2 * k + 3] = home_other_ref[:, k * size : (k + 1) * size]
        elif which == "other":
            lhs[2 * k + 3] = refs[1][k, 1]
        else:
            lhs[2 * k + 3] = refs[chips][k]
    refs = refs[{"own": 1, "other": 2, "rest": chips + 1}[which] :]
    step = 2560
    total = None
    for first in range(0, size, step):
        width = min(step, size - first)
        block = lhs[:, :, first : first + width].reshape(count * rows, width)
        part = jnp.dot(block, ints_ref[pl.ds(start + first, width)], preferred_element_type=jnp.float32)
        total = part if total is None else total + part
    if not last:
        before, out_ref = refs[:-2], refs[-2]
        out_ref[...] = total + before[0][...] if before else total
        return
    before_ref, own_ref, other_ref, _, partial = refs
    me = me_ref[0]
    partial[:count, :rows] = (total + before_ref[...]).reshape(count, rows, total.shape[1])
    for i in range(count):
        block = partial[i ^ me, :rows]
        partial[count + (i ^ me), :rows] = block
        for j in range(rows):
            partial[count + (j ^ me), rows + i : rows + i + 1] = block[j : j + 1]
    for k in range(count // 2):
        own_ref[k] = partial[count + 2 * k]
        other_ref[k] = partial[count + 2 * k + 1]


def contract(amps, home, home_other, ints, me, slab, shared, which, before=None):
    occupied, size = amps[0].shape[-2:]
    cols = ints.shape[1]
    vmem = pl.BlockSpec(memory_space=pltpu.VMEM)
    operands = [*amps] + ([] if before is None else [before])
    scratch = [pltpu.VMEM((occupied, occupied, size), home.dtype)]
    if which == "rest":
        out_shape = [jax.ShapeDtypeStruct((occupied // 2, 2 * occupied, cols), jnp.float32)] * 2
        scratch.append(pltpu.VMEM((2 * occupied, 2 * occupied, cols), jnp.float32))
    else:
        out_shape = [jax.ShapeDtypeStruct((occupied * occupied, cols), jnp.float32)]
    return pl.pallas_call(
        functools.partial(contract_kernel, which, shared),
        out_shape=out_shape,
        in_specs=[pl.BlockSpec(memory_space=pltpu.SMEM)] * 2 + [vmem] * (3 + len(operands)),
        out_specs=[vmem] * len(out_shape),
        scratch_shapes=scratch,
        compiler_params=pltpu.CompilerParams(
            vmem_limit_bytes=4 * MIB + 40 * occupied * occupied * cols + 4 * occupied * occupied * size
        ),
        cost_estimate=pl.CostEstimate(
            flops=2 * occupied * occupied * size * cols,
            bytes_accessed=2 * size * (cols + occupied * occupied),
            transcendentals=0,
        ),
        name="contract",
    )(slab, me, home, home_other, pltpu.with_memory_space_constraint(ints, pltpu.VMEM), *operands)


def select_exactly(values, select):
    rows = values.shape[0]
    high = values.astype(jnp.bfloat16)
    rest = values - high.astype(jnp.float32)
    middle = rest.astype(jnp.bfloat16)
    low = (rest - middle.astype(jnp.float32)).astype(jnp.bfloat16)
    terms = [jnp.dot(term, select, preferred_element_type=jnp.float32) for term in (high, middle, low)]
    return terms[0] + terms[1] + terms[2]


def add_cores_kernel(mine_ref, other_ref, *outs):
    for k, out in enumerate(outs):
        out[...] = mine_ref[k] + other_ref[k]


def add_cores(mine, other):
    count, rows, cols = mine.shape
    vmem = pl.BlockSpec(memory_space=pltpu.VMEM)
    return pl.pallas_call(
        add_cores_kernel,
        out_shape=[jax.ShapeDtypeStruct((rows, cols), jnp.float32)] * count,
        in_specs=[vmem, vmem],
        out_specs=[vmem] * count,
        compiler_params=pltpu.CompilerParams(vmem_limit_bytes=4 * MIB),
        cost_estimate=pl.CostEstimate(flops=mine.size, bytes_accessed=12 * mine.size, transcendentals=0),
        name="add_cores",
    )(mine, other)


def add_chips_kernel(*refs):
    parts, (ladder_ref, mirror_ref) = refs[:-2], refs[-2:]
    total = parts[0][...]
    for part in parts[1:]:
        total = total + part[...]
    half = total.shape[0] // 2
    ladder_ref[...] = total[:half]
    mirror_ref[...] = total[half:]


def add_chips(parts):
    rows, cols = parts[0].shape
    half = jax.ShapeDtypeStruct((rows // 2, cols), jnp.float32)
    vmem = pl.BlockSpec(memory_space=pltpu.VMEM)
    return pl.pallas_call(
        add_chips_kernel,
        out_shape=[half, half],
        in_specs=[vmem] * len(parts),
        out_specs=[vmem, vmem],
        compiler_params=pltpu.CompilerParams(vmem_limit_bytes=4 * MIB),
        cost_estimate=pl.CostEstimate(
            flops=len(parts) * rows * cols, bytes_accessed=4 * len(parts) * rows * cols, transcendentals=0
        ),
        name="add_chips",
    )(*parts)


def finish_kernel(ladder_ref, denominator_ref, select_ref, *refs):
    mirrors, out_ref = refs[:-1], refs[-1]
    mirror = select_exactly(jnp.concatenate([ref[...] for ref in mirrors], axis=1), select_ref[...])
    update = (ladder_ref[...] + mirror) / denominator_ref[...]
    _, first_local, slab_virt = out_ref.shape
    for a in range(first_local):
        out_ref[:, a, :] = update[:, a * slab_virt : (a + 1) * slab_virt]


def finish(ladder, mirrors, denominator, select, first_local, slab_virt):
    rows = ladder.shape[0]
    return pl.pallas_call(
        finish_kernel,
        out_shape=jax.ShapeDtypeStruct((rows, first_local, slab_virt), jnp.float32),
        in_specs=[pl.BlockSpec(memory_space=pltpu.VMEM)] * (3 + len(mirrors)),
        out_specs=pl.BlockSpec(memory_space=pltpu.VMEM),
        compiler_params=pltpu.CompilerParams(vmem_limit_bytes=6 * MIB),
        cost_estimate=pl.CostEstimate(flops=6 * rows * select.size, bytes_accessed=2 * select.size, transcendentals=0),
        name="finish",
    )(ladder, denominator, select, *mirrors)


def swap(values, axis, bits):
    return lax.ppermute(values, axis, [(p, p ^ bits) for p in range(lax.axis_size(axis))])


def local(amplitudes, integrals, virt_irrep, occ_energy, slab_energy):
    pair_count = lax.axis_size("pair")
    slab_count = lax.axis_size("slab")
    occ_local, occupied, virt_pairs = amplitudes.shape
    rows_local, cols_local = integrals.shape
    slab_virt = slab_energy.shape[0]
    first_local = slab_virt // slab_count
    assert occ_local == 1
    me = lax.axis_index("pair").astype(jnp.int32).reshape(1)
    slab = lax.axis_index("slab").astype(jnp.int32).reshape(1)

    shared = int(SHARE * rows_local) // 128 * 128
    amps = amplitudes.reshape(occupied, virt_pairs)
    chips = [2 * k for k in range(1, pair_count // 2)]

    def to_chips(parts):
        return [swap(part, "pair", bits) for part, bits in zip(parts, chips)]

    parts = pack(amps, me, slab, shared, "own", pair_count)
    own_amps = to_chips(parts)
    parts = pack(amps, me, slab, shared, "rest", pair_count, parts[-1])
    rest_amps = to_chips(parts)
    (home,) = pack(amps, me, slab, shared, "all", pair_count, parts[0])

    own_amps, for_other = merge(own_amps, home)
    other_amps = swap(own_amps, "slab", 1)
    home_other = swap(for_other, "pair", 1)
    masked, select, denominator = mask(integrals, me, slab, virt_irrep, occ_energy, slab_energy, own_amps)
    rest_others = swap(for_other_core(rest_amps, denominator), "pair", 1)
    place = (home, home_other, masked, me, slab, shared)
    (partial,) = contract([own_amps], *place, "own")
    (partial,) = contract([other_amps, swap(other_amps, "pair", 1)], *place, "other", partial)
    even, odd = contract([*rest_amps, rest_others], *place, "rest", partial)

    parts = add_cores(even, swap(odd, "pair", 1))
    parts = [parts[0]] + [swap(parts[k], "pair", 2 * k) for k in reversed(range(1, pair_count // 2))]
    ladder, mirror = add_chips(parts)
    mirrors = [
        lax.ppermute(mirror, "slab", [(s, (s - k) % slab_count) for s in range(slab_count)])
        for k in reversed(range(1, slab_count))
    ]
    mirrors = [mirror] + mirrors[::-1]
    update = finish(ladder, mirrors, denominator, select, first_local, slab_virt)
    return update.reshape(occ_local, occupied, first_local, slab_virt)


def solution(mesh):
    placed = (P("pair", None, None), P("pair", "slab"), P(), P(), P())
    return jax.shard_map(
        local, mesh=mesh, in_specs=placed, out_specs=P("pair", None, "slab", None), check_vma=False
    )
```

```python
import functools
import math

import jax
import jax.numpy as jnp
from jax import lax
from jax.experimental import pallas as pl
from jax.experimental.pallas import tpu as pltpu
from jax.sharding import PartitionSpec as P

IRREPS = 8
MIB = 2**20
SHARE = 0.28
LATE_FLOPS = 3 * 10**9
TIE_FLOPS = 6 * 10**9


def start_of(part, slab_ref, shared):
    parity = slab_ref[0] % 2
    return pl.multiple_of({"own": parity * shared, "other": (1 - parity) * shared, "rest": 2 * shared, "all": 0}[part], 128)


def pack_kernel(rows_local, shared, which, me_ref, slab_ref, amps_ref, other_ref, after_ref, *refs):
    outs, (held, packed, sems) = refs[:-3], refs[-3:]
    size = packed.shape[-1]
    count = sems.shape[0]
    me = me_ref[0]
    start = start_of(which, slab_ref, shared)
    sources = [amps_ref] if which == "own" else [amps_ref, other_ref]
    wanted = {
        "own": lambda dest: (dest ^ me) >= 2,
        "rest": lambda dest: jnp.logical_and(((dest ^ me) & 1) == 0, dest != me),
        "all": lambda dest: dest == me,
    }[which]
    slots = {"own": lambda dest: dest, "rest": lambda dest: dest // 2, "all": lambda dest: 0}[which]

    def load(dest, source):
        first = dest * rows_local // 128 * 128
        width = -(-(dest * rows_local - first + size) // 128) * 128
        return pltpu.make_async_copy(
            sources[source].at[:, pl.ds(start + first, width)],
            held.at[slots(dest), source, :, pl.ds(0, width)],
            sems.at[dest, source],
        )

    for dest in range(count):

        @pl.when(wanted(dest))
        def _():
            for source in range(len(sources)):
                load(dest, source).start()

    for dest in range(count):

        @pl.when(wanted(dest))
        def _():
            shift = dest * rows_local % 128
            for source in range(len(sources)):
                load(dest, source).wait()
                block = held[slots(dest), source, :, shift : shift + size]
                if which == "own":
                    packed[dest ^ me] = block
                elif which == "rest":
                    packed[(dest ^ me) // 2, source] = block
                else:
                    outs[0][source] = block

    if which == "own":
        for k, out in enumerate(outs):
            out[...] = packed[2 * k + 2 : 2 * k + 4]
    elif which == "rest":
        for k, out in enumerate(outs):
            out[...] = packed[k + 1]


def pack(amps, other, me, slab, shared, which, pair_count, after):
    rows, virt_pairs = amps.shape
    rows_local = virt_pairs // pair_count
    size = {"own": shared, "rest": rows_local - 2 * shared, "all": rows_local}[which]
    slots = {"own": pair_count, "rest": pair_count // 2, "all": 1}[which]
    sources = 1 if which == "own" else 2
    held = (slots, sources, rows, -(-size // 128) * 128 + 128)
    packed = {"own": (pair_count, rows, size), "rest": (pair_count // 2, 2, rows, size), "all": (1, rows, size)}[which]
    outs = 1 if which == "all" else pair_count // 2 - 1
    return pl.pallas_call(
        functools.partial(pack_kernel, rows_local, shared, which),
        out_shape=[jax.ShapeDtypeStruct((2, rows, size), amps.dtype)] * outs,
        in_specs=[pl.BlockSpec(memory_space=pltpu.SMEM)] * 2 + [pl.BlockSpec(memory_space=pl.ANY)] * 3,
        out_specs=[pl.BlockSpec(memory_space=pltpu.VMEM)] * outs,
        scratch_shapes=[
            pltpu.VMEM(held, amps.dtype),
            pltpu.VMEM(packed, amps.dtype),
            pltpu.SemaphoreType.DMA((pair_count, sources)),
        ],
        compiler_params=pltpu.CompilerParams(vmem_limit_bytes=2 * MIB + 6 * slots * sources * rows * held[3]),
        cost_estimate=pl.CostEstimate(
            flops=0, bytes_accessed=4 * slots * sources * rows * size, transcendentals=0
        ),
        name="pack_" + which,
    )(me, slab, pltpu.with_memory_space_constraint(amps, pltpu.HBM), other, after)


def mask_kernel(per_step, parts, me_ref, slab_ref, irrep_ref, occ_ref, virt_ref, row_ref, ints_ref, *refs):
    _, out_ref, select_ref, denominator_ref, table, padded, by_row = refs
    step = pl.program_id(0)
    chunk, cols = ints_ref.shape[1:]
    slab_virt = virt_ref.shape[0]
    first_local = cols // slab_virt
    bits = slab_virt.bit_length() - 1
    me, slab = me_ref[0], slab_ref[0]

    @pl.when(step == 0)
    def _():
        padded[:, : row_ref.shape[1]] = row_ref[...]
        for k in range(padded.shape[1] // 128):
            lanes = slice(k * 128, (k + 1) * 128)
            by_row[lanes] = jnp.transpose(jnp.broadcast_to(padded[:, lanes], (128, 128)))

        col = lax.broadcasted_iota(jnp.int32, (1, cols), 1)
        a_of, b_of = col >> bits, col & (slab_virt - 1)
        irrep_a = irrep_b = jnp.zeros_like(col)
        energy_a = energy_b = jnp.zeros(col.shape, jnp.float32)
        for a in range(first_local):
            irrep_a = jnp.where(a_of == a, irrep_ref[slab * first_local + a], irrep_a)
            energy_a = jnp.where(a_of == a, virt_ref[slab * first_local + a], energy_a)
        for b in range(slab_virt):
            irrep_b = jnp.where(b_of == b, irrep_ref[b], irrep_b)
            energy_b = jnp.where(b_of == b, virt_ref[b], energy_b)
        irrep_ab = irrep_a ^ irrep_b

        for part in range(parts):
            for lanes in (slice(k, k + 128) for k in range(0, cols, 128)):
                needed = by_row[part * chunk : (part + 1) * chunk] ^ irrep_ab[:, lanes]
                for irrep in range(IRREPS):
                    table[irrep * parts + part, :, lanes] = jnp.where(needed == irrep, 1.0, 0.0).astype(table.dtype)

        occupied = denominator_ref.shape[0]
        j_of = lax.broadcasted_iota(jnp.int32, (occupied, cols), 0)
        energy_j = jnp.zeros((occupied, cols), jnp.float32)
        for j in range(occupied):
            energy_j = jnp.where(j_of == j, occ_ref[j], energy_j)
        denominator_ref[...] = energy_a + energy_b - occ_ref[me] - energy_j

        row = lax.broadcasted_iota(jnp.int32, (cols, cols), 0)
        col = lax.broadcasted_iota(jnp.int32, (cols, cols), 1)
        same_a = (row & (slab_virt - 1)) == slab * first_local + (col >> bits)
        slab_count = select_ref.shape[0] // cols
        for t in range(slab_count):
            same_b = (slab + t) % slab_count * first_local + (row >> bits) == (col & (slab_virt - 1))
            chosen = jnp.where(same_a & same_b, 1.0, 0.0)
            select_ref[t * cols : (t + 1) * cols] = chosen.astype(select_ref.dtype)

    chunks = per_step * pl.num_programs(0)
    for k in range(per_step):
        index = me * chunks + step * per_step + k
        irrep_c = irrep_ref[index // parts]
        out_ref[k] = ints_ref[k] * table[irrep_c * parts + index % parts]


def in_hbm(array):
    return pltpu.with_memory_space_constraint(array, pltpu.HBM)


def mask(integrals, me, slab, virt_irrep, occ_energy, slab_energy, after):
    virtuals = virt_irrep.shape[0]
    slab_virt = slab_energy.shape[0]
    occupied = occ_energy.shape[0]
    rows_local, cols_local = integrals.shape
    chunk = math.gcd(virtuals, rows_local)
    parts = virtuals // chunk
    chunks = rows_local // chunk
    per_step = next(n for n in (10, 5, 4, 2, 1) if chunks % n == 0)
    padded = -(-virtuals // 128) * 128
    select_rows = slab_virt * slab_virt
    block = pl.BlockSpec((per_step, chunk, cols_local), lambda step: (step, 0, 0))
    scalars = pl.BlockSpec(memory_space=pltpu.SMEM)
    masked, select, denominator = pl.pallas_call(
        functools.partial(mask_kernel, per_step, parts),
        grid=(chunks // per_step,),
        in_specs=[scalars] * 5
        + [pl.BlockSpec((1, virtuals), lambda step: (0, 0)), block, pl.BlockSpec(memory_space=pl.ANY)],
        out_specs=[
            block,
            pl.BlockSpec((select_rows, cols_local), lambda step: (0, 0)),
            pl.BlockSpec((occupied, cols_local), lambda step: (0, 0)),
        ],
        scratch_shapes=[
            pltpu.VMEM((IRREPS * parts, chunk, cols_local), integrals.dtype),
            pltpu.VMEM((1, padded), jnp.int32),
            pltpu.VMEM((padded, 128), jnp.int32),
        ],
        out_shape=[
            pltpu.VMEM((chunks, chunk, cols_local), integrals.dtype),
            jax.ShapeDtypeStruct((select_rows, cols_local), jnp.bfloat16),
            jax.ShapeDtypeStruct((occupied, cols_local), jnp.float32),
        ],
        compiler_params=pltpu.CompilerParams(vmem_limit_bytes=16 * MIB),
        cost_estimate=pl.CostEstimate(
            flops=LATE_FLOPS, bytes_accessed=4 * rows_local * cols_local, transcendentals=0
        ),
        name="mask_integrals",
    )(
        me,
        slab,
        *(in_hbm(array) for array in (virt_irrep, occ_energy, slab_energy, virt_irrep.reshape(1, virtuals))),
        in_hbm(integrals.reshape(chunks, chunk, cols_local)),
        after,
    )
    return masked.reshape(rows_local, cols_local), select, denominator


def merge_kernel(*refs):
    parts, all_ref, other_ref = refs[:-3], refs[-2], refs[-1]
    for k, part in enumerate(parts):
        all_ref[k] = part[...]
        other_ref[k] = part[1]


def merge(parts, after):
    count = len(parts)
    _, rows, size = parts[0].shape
    vmem = pl.BlockSpec(memory_space=pltpu.VMEM)
    return pl.pallas_call(
        merge_kernel,
        out_shape=[
            jax.ShapeDtypeStruct((count,) + parts[0].shape, parts[0].dtype),
            jax.ShapeDtypeStruct((count, rows, size), parts[0].dtype),
        ],
        in_specs=[vmem] * count + [pl.BlockSpec(memory_space=pl.ANY)],
        out_specs=[vmem, vmem],
        compiler_params=pltpu.CompilerParams(vmem_limit_bytes=4 * MIB),
        cost_estimate=pl.CostEstimate(flops=0, bytes_accessed=6 * count * rows * size, transcendentals=0),
        name="merge",
    )(*parts, after)


def tie_kernel(*refs):
    del refs


def tie(parts, after):
    count = len(parts)
    anywhere = pl.BlockSpec(memory_space=pl.ANY)
    return pl.pallas_call(
        tie_kernel,
        out_shape=[pltpu.VMEM(part.shape, part.dtype) for part in parts],
        in_specs=[anywhere] * (count + 1),
        out_specs=[anywhere] * count,
        input_output_aliases={k: k for k in range(count)},
        compiler_params=pltpu.CompilerParams(vmem_limit_bytes=2 * MIB),
        cost_estimate=pl.CostEstimate(flops=TIE_FLOPS, bytes_accessed=0, transcendentals=0),
        name="tie",
    )(*(pltpu.with_memory_space_constraint(part, pltpu.VMEM) for part in parts), after)


def other_core_kernel(parts_ref, after_ref, out_ref):
    del after_ref
    out_ref[...] = parts_ref[:, 1]


def for_other_core(parts, after):
    vmem = pl.BlockSpec(memory_space=pltpu.VMEM)
    out = jax.ShapeDtypeStruct(parts.shape[:1] + parts.shape[2:], parts.dtype)
    return pl.pallas_call(
        other_core_kernel,
        out_shape=out,
        in_specs=[vmem, pl.BlockSpec(memory_space=pl.ANY)],
        out_specs=vmem,
        compiler_params=pltpu.CompilerParams(vmem_limit_bytes=4 * MIB),
        cost_estimate=pl.CostEstimate(flops=0, bytes_accessed=4 * out.size, transcendentals=0),
        name="for_other_core",
    )(parts, after)


def contract_kernel(which, shared, slab_ref, me_ref, home_ref, ints_ref, *refs):
    last = which == "other"
    lhs = refs[-2] if last else refs[-1]
    count, rows, size = lhs.shape
    chips = count // 2 - 1
    start = start_of(which, slab_ref, shared)
    lhs[:2] = home_ref[:, :, pl.ds(start, size)]
    for k in range(chips):
        if which == "rest":
            lhs[2 * k + 2 : 2 * k + 4] = refs[k][...]
        else:
            lhs[2 * k + 2] = refs[0][k, 0]
            lhs[2 * k + 3] = refs[1][k]
    refs = refs[chips if which == "rest" else 2 :]
    step = 2560
    total = None
    for first in range(0, size, step):
        width = min(step, size - first)
        block = lhs[:, :, first : first + width].reshape(count * rows, width)
        part = jnp.dot(block, ints_ref[pl.ds(start + first, width)], preferred_element_type=jnp.float32)
        total = part if total is None else total + part
    if not last:
        before, out_ref = refs[:-2], refs[-2]
        out_ref[...] = total + before[0][...] if before else total
        return
    before_ref, own_ref, other_ref, _, partial = refs
    me = me_ref[0]
    partial[:count, :rows] = (total + before_ref[...]).reshape(count, rows, total.shape[1])
    for i in range(count):
        block = partial[i ^ me, :rows]
        partial[count + (i ^ me), :rows] = block
        for j in range(rows):
            partial[count + (j ^ me), rows + i : rows + i + 1] = block[j : j + 1]
    for k in range(count // 2):
        own_ref[k] = partial[count + 2 * k]
        other_ref[k] = partial[count + 2 * k + 1]


def contract(amps, home, ints, me, slab, shared, which, before=None):
    occupied, size = amps[0].shape[-2:]
    cols = ints.shape[1]
    vmem = pl.BlockSpec(memory_space=pltpu.VMEM)
    operands = [*amps] + ([] if before is None else [before])
    scratch = [pltpu.VMEM((occupied, occupied, size), home.dtype)]
    if which == "other":
        out_shape = [jax.ShapeDtypeStruct((occupied // 2, 2 * occupied, cols), jnp.float32)] * 2
        scratch.append(pltpu.VMEM((2 * occupied, 2 * occupied, cols), jnp.float32))
    else:
        out_shape = [jax.ShapeDtypeStruct((occupied * occupied, cols), jnp.float32)]
    return pl.pallas_call(
        functools.partial(contract_kernel, which, shared),
        out_shape=out_shape,
        in_specs=[pl.BlockSpec(memory_space=pltpu.SMEM)] * 2 + [vmem] * (2 + len(operands)),
        out_specs=[vmem] * len(out_shape),
        scratch_shapes=scratch,
        compiler_params=pltpu.CompilerParams(
            vmem_limit_bytes=4 * MIB + 40 * occupied * occupied * cols + 4 * occupied * occupied * size
        ),
        cost_estimate=pl.CostEstimate(
            flops=2 * occupied * occupied * size * cols,
            bytes_accessed=2 * size * (cols + occupied * occupied),
            transcendentals=0,
        ),
        name="contract",
    )(slab, me, home, pltpu.with_memory_space_constraint(ints, pltpu.VMEM), *operands)


def select_exactly(values, select):
    rows = values.shape[0]
    high = values.astype(jnp.bfloat16)
    rest = values - high.astype(jnp.float32)
    middle = rest.astype(jnp.bfloat16)
    low = (rest - middle.astype(jnp.float32)).astype(jnp.bfloat16)
    terms = [jnp.dot(term, select, preferred_element_type=jnp.float32) for term in (high, middle, low)]
    return terms[0] + terms[1] + terms[2]


def add_cores_kernel(mine_ref, other_ref, *outs):
    for k, out in enumerate(outs):
        out[...] = mine_ref[k] + other_ref[k]


def add_cores(mine, other):
    count, rows, cols = mine.shape
    vmem = pl.BlockSpec(memory_space=pltpu.VMEM)
    return pl.pallas_call(
        add_cores_kernel,
        out_shape=[jax.ShapeDtypeStruct((rows, cols), jnp.float32)] * count,
        in_specs=[vmem, vmem],
        out_specs=[vmem] * count,
        compiler_params=pltpu.CompilerParams(vmem_limit_bytes=4 * MIB),
        cost_estimate=pl.CostEstimate(flops=mine.size, bytes_accessed=12 * mine.size, transcendentals=0),
        name="add_cores",
    )(mine, other)


def add_chips_kernel(*refs):
    parts, (ladder_ref, mirror_ref) = refs[:-2], refs[-2:]
    total = parts[0][...]
    for part in parts[1:]:
        total = total + part[...]
    half = total.shape[0] // 2
    ladder_ref[...] = total[:half]
    mirror_ref[...] = total[half:]


def add_chips(parts):
    rows, cols = parts[0].shape
    half = jax.ShapeDtypeStruct((rows // 2, cols), jnp.float32)
    vmem = pl.BlockSpec(memory_space=pltpu.VMEM)
    return pl.pallas_call(
        add_chips_kernel,
        out_shape=[half, half],
        in_specs=[vmem] * len(parts),
        out_specs=[vmem, vmem],
        compiler_params=pltpu.CompilerParams(vmem_limit_bytes=4 * MIB),
        cost_estimate=pl.CostEstimate(
            flops=len(parts) * rows * cols, bytes_accessed=4 * len(parts) * rows * cols, transcendentals=0
        ),
        name="add_chips",
    )(*parts)


def finish_kernel(ladder_ref, denominator_ref, select_ref, *refs):
    mirrors, out_ref = refs[:-1], refs[-1]
    mirror = select_exactly(jnp.concatenate([ref[...] for ref in mirrors], axis=1), select_ref[...])
    update = (ladder_ref[...] + mirror) / denominator_ref[...]
    _, first_local, slab_virt = out_ref.shape
    for a in range(first_local):
        out_ref[:, a, :] = update[:, a * slab_virt : (a + 1) * slab_virt]


def finish(ladder, mirrors, denominator, select, first_local, slab_virt):
    rows = ladder.shape[0]
    return pl.pallas_call(
        finish_kernel,
        out_shape=jax.ShapeDtypeStruct((rows, first_local, slab_virt), jnp.float32),
        in_specs=[pl.BlockSpec(memory_space=pltpu.VMEM)] * (3 + len(mirrors)),
        out_specs=pl.BlockSpec(memory_space=pltpu.VMEM),
        compiler_params=pltpu.CompilerParams(vmem_limit_bytes=6 * MIB),
        cost_estimate=pl.CostEstimate(flops=6 * rows * select.size, bytes_accessed=2 * select.size, transcendentals=0),
        name="finish",
    )(ladder, denominator, select, *mirrors)


def swap(values, axis, bits):
    return lax.ppermute(values, axis, [(p, p ^ bits) for p in range(lax.axis_size(axis))])


def local(amplitudes, integrals, virt_irrep, occ_energy, slab_energy):
    pair_count = lax.axis_size("pair")
    slab_count = lax.axis_size("slab")
    occ_local, occupied, virt_pairs = amplitudes.shape
    rows_local, cols_local = integrals.shape
    slab_virt = slab_energy.shape[0]
    first_local = slab_virt // slab_count
    assert occ_local == 1
    me = lax.axis_index("pair").astype(jnp.int32).reshape(1)
    slab = lax.axis_index("slab").astype(jnp.int32).reshape(1)

    shared = int(SHARE * rows_local) // 128 * 128
    amps = amplitudes.reshape(occupied, virt_pairs)
    chips = [2 * k for k in range(1, pair_count // 2)]

    def to_chips(parts):
        return [swap(part, "pair", bits) for part, bits in zip(parts, chips)]

    other = swap(amps, "pair", 1)
    parts = pack(amps, me, me, slab, shared, "own", pair_count, me)
    own_amps = to_chips(parts)
    parts = pack(amps, other, me, slab, shared, "rest", pair_count, parts[-1])
    rest_amps = to_chips(parts)
    (home,) = pack(amps, other, me, slab, shared, "all", pair_count, parts[-1])

    own_amps, for_other = merge(own_amps, home)
    other_amps = swap(own_amps, "slab", 1)
    masked, select, denominator = mask(integrals, me, slab, virt_irrep, occ_energy, slab_energy, own_amps)
    rest_amps = tie(rest_amps, denominator)
    place = (home, masked, me, slab, shared)
    (partial,) = contract([own_amps, swap(for_other, "pair", 1)], *place, "own")
    (partial,) = contract(rest_amps, *place, "rest", partial)
    from_other = swap(for_other_core(other_amps, rest_amps[0]), "pair", 1)
    even, odd = contract([other_amps, from_other], *place, "other", partial)

    parts = add_cores(even, swap(odd, "pair", 1))
    parts = [parts[0]] + [swap(parts[k], "pair", 2 * k) for k in reversed(range(1, pair_count // 2))]
    ladder, mirror = add_chips(parts)
    mirrors = [
        lax.ppermute(mirror, "slab", [(s, (s - k) % slab_count) for s in range(slab_count)])
        for k in reversed(range(1, slab_count))
    ]
    mirrors = [mirror] + mirrors[::-1]
    update = finish(ladder, mirrors, denominator, select, first_local, slab_virt)
    return update.reshape(occ_local, occupied, first_local, slab_virt)


def solution(mesh):
    placed = (P("pair", None, None), P("pair", "slab"), P(), P(), P())
    return jax.shard_map(
        local, mesh=mesh, in_specs=placed, out_specs=P("pair", None, "slab", None), check_vma=False
    )
```

```python
import functools
import math

import jax
import jax.numpy as jnp
from jax import lax
from jax.experimental import pallas as pl
from jax.experimental.pallas import tpu as pltpu
from jax.sharding import PartitionSpec as P

IRREPS = 8
MIB = 2**20
SHARE = 0.26
LATE_FLOPS = 3 * 10**9
TIE_FLOPS = 6 * 10**9


def start_of(part, slab_ref, shared):
    parity = slab_ref[0] % 2
    return pl.multiple_of({"own": parity * shared, "other": (1 - parity) * shared, "rest": 2 * shared, "all": 0}[part], 128)


def pack_kernel(rows_local, shared, which, me_ref, slab_ref, amps_ref, other_ref, after_ref, *refs):
    outs, (held, packed, sems) = refs[:-3], refs[-3:]
    size = packed.shape[-1]
    count = sems.shape[0]
    me = me_ref[0]
    start = start_of(which, slab_ref, shared)
    sources = [amps_ref] if which == "own" else [amps_ref, other_ref]
    wanted = {
        "own": lambda dest: (dest ^ me) >= 2,
        "rest": lambda dest: jnp.logical_and(((dest ^ me) & 1) == 0, dest != me),
        "all": lambda dest: dest == me,
    }[which]
    slots = {"own": lambda dest: dest, "rest": lambda dest: dest // 2, "all": lambda dest: 0}[which]

    def load(dest, source):
        first = dest * rows_local // 128 * 128
        width = -(-(dest * rows_local - first + size) // 128) * 128
        return pltpu.make_async_copy(
            sources[source].at[:, pl.ds(start + first, width)],
            held.at[slots(dest), source, :, pl.ds(0, width)],
            sems.at[dest, source],
        )

    for dest in range(count):

        @pl.when(wanted(dest))
        def _():
            for source in range(len(sources)):
                load(dest, source).start()

    for dest in range(count):

        @pl.when(wanted(dest))
        def _():
            shift = dest * rows_local % 128
            for source in range(len(sources)):
                load(dest, source).wait()
                block = held[slots(dest), source, :, shift : shift + size]
                if which == "own":
                    packed[dest ^ me] = block
                elif which == "rest":
                    packed[(dest ^ me) // 2, source] = block
                else:
                    outs[0][source] = block

    if which == "own":
        for k, out in enumerate(outs):
            out[...] = packed[2 * k + 2 : 2 * k + 4]
    elif which == "rest":
        for k, out in enumerate(outs):
            out[...] = packed[k + 1]


def pack(amps, other, me, slab, shared, which, pair_count, after):
    rows, virt_pairs = amps.shape
    rows_local = virt_pairs // pair_count
    size = {"own": shared, "rest": rows_local - 2 * shared, "all": rows_local}[which]
    slots = {"own": pair_count, "rest": pair_count // 2, "all": 1}[which]
    sources = 1 if which == "own" else 2
    held = (slots, sources, rows, -(-size // 128) * 128 + 128)
    packed = {"own": (pair_count, rows, size), "rest": (pair_count // 2, 2, rows, size), "all": (1, rows, size)}[which]
    outs = 1 if which == "all" else pair_count // 2 - 1
    return pl.pallas_call(
        functools.partial(pack_kernel, rows_local, shared, which),
        out_shape=[jax.ShapeDtypeStruct((2, rows, size), amps.dtype)] * outs,
        in_specs=[pl.BlockSpec(memory_space=pltpu.SMEM)] * 2 + [pl.BlockSpec(memory_space=pl.ANY)] * 3,
        out_specs=[pl.BlockSpec(memory_space=pltpu.VMEM)] * outs,
        scratch_shapes=[
            pltpu.VMEM(held, amps.dtype),
            pltpu.VMEM(packed, amps.dtype),
            pltpu.SemaphoreType.DMA((pair_count, sources)),
        ],
        compiler_params=pltpu.CompilerParams(vmem_limit_bytes=2 * MIB + 6 * slots * sources * rows * held[3]),
        cost_estimate=pl.CostEstimate(
            flops=0, bytes_accessed=4 * slots * sources * rows * size, transcendentals=0
        ),
        name="pack_" + which,
    )(me, slab, pltpu.with_memory_space_constraint(amps, pltpu.HBM), other, after)


def mask_kernel(per_step, parts, me_ref, slab_ref, irrep_ref, occ_ref, virt_ref, row_ref, ints_ref, *refs):
    _, out_ref, select_ref, denominator_ref, table, padded, by_row = refs
    step = pl.program_id(0)
    chunk, cols = ints_ref.shape[1:]
    slab_virt = virt_ref.shape[0]
    first_local = cols // slab_virt
    bits = slab_virt.bit_length() - 1
    me, slab = me_ref[0], slab_ref[0]

    @pl.when(step == 0)
    def _():
        padded[:, : row_ref.shape[1]] = row_ref[...]
        for k in range(padded.shape[1] // 128):
            lanes = slice(k * 128, (k + 1) * 128)
            by_row[lanes] = jnp.transpose(jnp.broadcast_to(padded[:, lanes], (128, 128)))

        col = lax.broadcasted_iota(jnp.int32, (1, cols), 1)
        a_of, b_of = col >> bits, col & (slab_virt - 1)
        irrep_a = irrep_b = jnp.zeros_like(col)
        energy_a = energy_b = jnp.zeros(col.shape, jnp.float32)
        for a in range(first_local):
            irrep_a = jnp.where(a_of == a, irrep_ref[slab * first_local + a], irrep_a)
            energy_a = jnp.where(a_of == a, virt_ref[slab * first_local + a], energy_a)
        for b in range(slab_virt):
            irrep_b = jnp.where(b_of == b, irrep_ref[b], irrep_b)
            energy_b = jnp.where(b_of == b, virt_ref[b], energy_b)
        irrep_ab = irrep_a ^ irrep_b

        for part in range(parts):
            for lanes in (slice(k, k + 128) for k in range(0, cols, 128)):
                needed = by_row[part * chunk : (part + 1) * chunk] ^ irrep_ab[:, lanes]
                for irrep in range(IRREPS):
                    table[irrep * parts + part, :, lanes] = jnp.where(needed == irrep, 1.0, 0.0).astype(table.dtype)

        occupied = denominator_ref.shape[0]
        j_of = lax.broadcasted_iota(jnp.int32, (occupied, cols), 0)
        energy_j = jnp.zeros((occupied, cols), jnp.float32)
        for j in range(occupied):
            energy_j = jnp.where(j_of == j, occ_ref[j], energy_j)
        denominator_ref[...] = energy_a + energy_b - occ_ref[me] - energy_j

        row = lax.broadcasted_iota(jnp.int32, (cols, cols), 0)
        col = lax.broadcasted_iota(jnp.int32, (cols, cols), 1)
        same_a = (row & (slab_virt - 1)) == slab * first_local + (col >> bits)
        slab_count = select_ref.shape[0] // cols
        for t in range(slab_count):
            same_b = (slab + t) % slab_count * first_local + (row >> bits) == (col & (slab_virt - 1))
            chosen = jnp.where(same_a & same_b, 1.0, 0.0)
            select_ref[t * cols : (t + 1) * cols] = chosen.astype(select_ref.dtype)

    chunks = per_step * pl.num_programs(0)
    for k in range(per_step):
        index = me * chunks + step * per_step + k
        irrep_c = irrep_ref[index // parts]
        out_ref[k] = ints_ref[k] * table[irrep_c * parts + index % parts]


def in_hbm(array):
    return pltpu.with_memory_space_constraint(array, pltpu.HBM)


def mask(integrals, me, slab, virt_irrep, occ_energy, slab_energy, after):
    virtuals = virt_irrep.shape[0]
    slab_virt = slab_energy.shape[0]
    occupied = occ_energy.shape[0]
    rows_local, cols_local = integrals.shape
    chunk = math.gcd(virtuals, rows_local)
    parts = virtuals // chunk
    chunks = rows_local // chunk
    per_step = next(n for n in (10, 5, 4, 2, 1) if chunks % n == 0)
    padded = -(-virtuals // 128) * 128
    select_rows = slab_virt * slab_virt
    block = pl.BlockSpec((per_step, chunk, cols_local), lambda step: (step, 0, 0))
    scalars = pl.BlockSpec(memory_space=pltpu.SMEM)
    masked, select, denominator = pl.pallas_call(
        functools.partial(mask_kernel, per_step, parts),
        grid=(chunks // per_step,),
        in_specs=[scalars] * 5
        + [pl.BlockSpec((1, virtuals), lambda step: (0, 0)), block, pl.BlockSpec(memory_space=pl.ANY)],
        out_specs=[
            block,
            pl.BlockSpec((select_rows, cols_local), lambda step: (0, 0)),
            pl.BlockSpec((occupied, cols_local), lambda step: (0, 0)),
        ],
        scratch_shapes=[
            pltpu.VMEM((IRREPS * parts, chunk, cols_local), integrals.dtype),
            pltpu.VMEM((1, padded), jnp.int32),
            pltpu.VMEM((padded, 128), jnp.int32),
        ],
        out_shape=[
            pltpu.VMEM((chunks, chunk, cols_local), integrals.dtype),
            jax.ShapeDtypeStruct((select_rows, cols_local), jnp.bfloat16),
            jax.ShapeDtypeStruct((occupied, cols_local), jnp.float32),
        ],
        compiler_params=pltpu.CompilerParams(vmem_limit_bytes=16 * MIB),
        cost_estimate=pl.CostEstimate(
            flops=LATE_FLOPS, bytes_accessed=4 * rows_local * cols_local, transcendentals=0
        ),
        name="mask_integrals",
    )(
        me,
        slab,
        *(in_hbm(array) for array in (virt_irrep, occ_energy, slab_energy, virt_irrep.reshape(1, virtuals))),
        in_hbm(integrals.reshape(chunks, chunk, cols_local)),
        after,
    )
    return masked.reshape(rows_local, cols_local), select, denominator


def merge_kernel(*refs):
    parts, all_ref, other_ref = refs[:-3], refs[-2], refs[-1]
    for k, part in enumerate(parts):
        all_ref[k] = part[...]
        other_ref[k] = part[1]


def merge(parts, after):
    count = len(parts)
    _, rows, size = parts[0].shape
    vmem = pl.BlockSpec(memory_space=pltpu.VMEM)
    return pl.pallas_call(
        merge_kernel,
        out_shape=[
            jax.ShapeDtypeStruct((count,) + parts[0].shape, parts[0].dtype),
            jax.ShapeDtypeStruct((count, rows, size), parts[0].dtype),
        ],
        in_specs=[vmem] * count + [pl.BlockSpec(memory_space=pl.ANY)],
        out_specs=[vmem, vmem],
        compiler_params=pltpu.CompilerParams(vmem_limit_bytes=4 * MIB),
        cost_estimate=pl.CostEstimate(flops=0, bytes_accessed=6 * count * rows * size, transcendentals=0),
        name="merge",
    )(*parts, after)


def tie_kernel(*refs):
    del refs


def tie(parts, after):
    count = len(parts)
    anywhere = pl.BlockSpec(memory_space=pl.ANY)
    return pl.pallas_call(
        tie_kernel,
        out_shape=[pltpu.VMEM(part.shape, part.dtype) for part in parts],
        in_specs=[anywhere] * (count + 1),
        out_specs=[anywhere] * count,
        input_output_aliases={k: k for k in range(count)},
        compiler_params=pltpu.CompilerParams(vmem_limit_bytes=2 * MIB),
        cost_estimate=pl.CostEstimate(flops=TIE_FLOPS, bytes_accessed=0, transcendentals=0),
        name="tie",
    )(*(pltpu.with_memory_space_constraint(part, pltpu.VMEM) for part in parts), after)


def other_core_kernel(parts_ref, after_ref, out_ref):
    del after_ref
    out_ref[...] = parts_ref[:, 1]


def for_other_core(parts, after):
    vmem = pl.BlockSpec(memory_space=pltpu.VMEM)
    out = jax.ShapeDtypeStruct(parts.shape[:1] + parts.shape[2:], parts.dtype)
    return pl.pallas_call(
        other_core_kernel,
        out_shape=out,
        in_specs=[vmem, pl.BlockSpec(memory_space=pl.ANY)],
        out_specs=vmem,
        compiler_params=pltpu.CompilerParams(vmem_limit_bytes=4 * MIB),
        cost_estimate=pl.CostEstimate(flops=0, bytes_accessed=4 * out.size, transcendentals=0),
        name="for_other_core",
    )(parts, after)


def contract_kernel(which, shared, slab_ref, me_ref, home_ref, ints_ref, *refs):
    last = which == "other"
    lhs = refs[-2] if last else refs[-1]
    count, rows, size = lhs.shape
    chips = count // 2 - 1
    start = start_of(which, slab_ref, shared)
    lhs[:2] = home_ref[:, :, pl.ds(start, size)]
    for k in range(chips):
        if which == "rest":
            lhs[2 * k + 2 : 2 * k + 4] = refs[k][...]
        else:
            lhs[2 * k + 2] = refs[0][k, 0]
            lhs[2 * k + 3] = refs[1][k]
    refs = refs[chips if which == "rest" else 2 :]
    step = 2560
    total = None
    for first in range(0, size, step):
        width = min(step, size - first)
        block = lhs[:, :, first : first + width].reshape(count * rows, width)
        part = jnp.dot(block, ints_ref[pl.ds(start + first, width)], preferred_element_type=jnp.float32)
        total = part if total is None else total + part
    if not last:
        before, out_ref = refs[:-2], refs[-2]
        out_ref[...] = total + before[0][...] if before else total
        return
    before_ref, own_ref, other_ref, _, partial = refs
    me = me_ref[0]
    partial[:count, :rows] = (total + before_ref[...]).reshape(count, rows, total.shape[1])
    for i in range(count):
        block = partial[i ^ me, :rows]
        partial[count + (i ^ me), :rows] = block
        for j in range(rows):
            partial[count + (j ^ me), rows + i : rows + i + 1] = block[j : j + 1]
    for k in range(count // 2):
        own_ref[k] = partial[count + 2 * k]
        other_ref[k] = partial[count + 2 * k + 1]


def contract(amps, home, ints, me, slab, shared, which, before=None):
    occupied, size = amps[0].shape[-2:]
    cols = ints.shape[1]
    vmem = pl.BlockSpec(memory_space=pltpu.VMEM)
    operands = [*amps] + ([] if before is None else [before])
    scratch = [pltpu.VMEM((occupied, occupied, size), home.dtype)]
    if which == "other":
        out_shape = [jax.ShapeDtypeStruct((occupied // 2, 2 * occupied, cols), jnp.float32)] * 2
        scratch.append(pltpu.VMEM((2 * occupied, 2 * occupied, cols), jnp.float32))
    else:
        out_shape = [jax.ShapeDtypeStruct((occupied * occupied, cols), jnp.float32)]
    return pl.pallas_call(
        functools.partial(contract_kernel, which, shared),
        out_shape=out_shape,
        in_specs=[pl.BlockSpec(memory_space=pltpu.SMEM)] * 2 + [vmem] * (2 + len(operands)),
        out_specs=[vmem] * len(out_shape),
        scratch_shapes=scratch,
        compiler_params=pltpu.CompilerParams(
            vmem_limit_bytes=4 * MIB + 40 * occupied * occupied * cols + 4 * occupied * occupied * size
        ),
        cost_estimate=pl.CostEstimate(
            flops=2 * occupied * occupied * size * cols,
            bytes_accessed=2 * size * (cols + occupied * occupied),
            transcendentals=0,
        ),
        name="contract",
    )(slab, me, home, pltpu.with_memory_space_constraint(ints, pltpu.VMEM), *operands)


def select_exactly(values, select):
    rows = values.shape[0]
    high = values.astype(jnp.bfloat16)
    rest = values - high.astype(jnp.float32)
    middle = rest.astype(jnp.bfloat16)
    low = (rest - middle.astype(jnp.float32)).astype(jnp.bfloat16)
    terms = [jnp.dot(term, select, preferred_element_type=jnp.float32) for term in (high, middle, low)]
    return terms[0] + terms[1] + terms[2]


def add_cores_kernel(mine_ref, other_ref, *outs):
    for k, out in enumerate(outs):
        out[...] = mine_ref[k] + other_ref[k]


def add_cores(mine, other):
    count, rows, cols = mine.shape
    vmem = pl.BlockSpec(memory_space=pltpu.VMEM)
    return pl.pallas_call(
        add_cores_kernel,
        out_shape=[jax.ShapeDtypeStruct((rows, cols), jnp.float32)] * count,
        in_specs=[vmem, vmem],
        out_specs=[vmem] * count,
        compiler_params=pltpu.CompilerParams(vmem_limit_bytes=4 * MIB),
        cost_estimate=pl.CostEstimate(flops=mine.size, bytes_accessed=12 * mine.size, transcendentals=0),
        name="add_cores",
    )(mine, other)


def add_chips_kernel(*refs):
    parts, (ladder_ref, mirror_ref) = refs[:-2], refs[-2:]
    total = parts[0][...]
    for part in parts[1:]:
        total = total + part[...]
    half = total.shape[0] // 2
    ladder_ref[...] = total[:half]
    mirror_ref[...] = total[half:]


def add_chips(parts):
    rows, cols = parts[0].shape
    half = jax.ShapeDtypeStruct((rows // 2, cols), jnp.float32)
    vmem = pl.BlockSpec(memory_space=pltpu.VMEM)
    return pl.pallas_call(
        add_chips_kernel,
        out_shape=[half, half],
        in_specs=[vmem] * len(parts),
        out_specs=[vmem, vmem],
        compiler_params=pltpu.CompilerParams(vmem_limit_bytes=4 * MIB),
        cost_estimate=pl.CostEstimate(
            flops=len(parts) * rows * cols, bytes_accessed=4 * len(parts) * rows * cols, transcendentals=0
        ),
        name="add_chips",
    )(*parts)


def finish_kernel(ladder_ref, denominator_ref, select_ref, *refs):
    mirrors, out_ref = refs[:-1], refs[-1]
    mirror = select_exactly(jnp.concatenate([ref[...] for ref in mirrors], axis=1), select_ref[...])
    update = (ladder_ref[...] + mirror) / denominator_ref[...]
    _, first_local, slab_virt = out_ref.shape
    for a in range(first_local):
        out_ref[:, a, :] = update[:, a * slab_virt : (a + 1) * slab_virt]


def finish(ladder, mirrors, denominator, select, first_local, slab_virt):
    rows = ladder.shape[0]
    return pl.pallas_call(
        finish_kernel,
        out_shape=jax.ShapeDtypeStruct((rows, first_local, slab_virt), jnp.float32),
        in_specs=[pl.BlockSpec(memory_space=pltpu.VMEM)] * (3 + len(mirrors)),
        out_specs=pl.BlockSpec(memory_space=pltpu.VMEM),
        compiler_params=pltpu.CompilerParams(vmem_limit_bytes=6 * MIB),
        cost_estimate=pl.CostEstimate(flops=6 * rows * select.size, bytes_accessed=2 * select.size, transcendentals=0),
        name="finish",
    )(ladder, denominator, select, *mirrors)


def swap(values, axis, bits):
    return lax.ppermute(values, axis, [(p, p ^ bits) for p in range(lax.axis_size(axis))])


def local(amplitudes, integrals, virt_irrep, occ_energy, slab_energy):
    pair_count = lax.axis_size("pair")
    slab_count = lax.axis_size("slab")
    occ_local, occupied, virt_pairs = amplitudes.shape
    rows_local, cols_local = integrals.shape
    slab_virt = slab_energy.shape[0]
    first_local = slab_virt // slab_count
    assert occ_local == 1
    me = lax.axis_index("pair").astype(jnp.int32).reshape(1)
    slab = lax.axis_index("slab").astype(jnp.int32).reshape(1)

    shared = int(SHARE * rows_local) // 128 * 128
    amps = amplitudes.reshape(occupied, virt_pairs)
    chips = [2 * k for k in range(1, pair_count // 2)]

    def to_chips(parts):
        return [swap(part, "pair", bits) for part, bits in zip(parts, chips)]

    other = swap(amps, "pair", 1)
    parts = pack(amps, me, me, slab, shared, "own", pair_count, me)
    own_amps = to_chips(parts)
    parts = pack(amps, other, me, slab, shared, "rest", pair_count, parts[-1])
    rest_amps = to_chips(parts)
    (home,) = pack(amps, other, me, slab, shared, "all", pair_count, parts[-1])

    own_amps, for_other = merge(own_amps, home)
    other_amps = swap(own_amps, "slab", 1)
    masked, select, denominator = mask(integrals, me, slab, virt_irrep, occ_energy, slab_energy, own_amps)
    rest_amps = tie(rest_amps, denominator)
    place = (home, masked, me, slab, shared)
    (partial,) = contract([own_amps, swap(for_other, "pair", 1)], *place, "own")
    (partial,) = contract(rest_amps, *place, "rest", partial)
    from_other = swap(for_other_core(other_amps, rest_amps[0]), "pair", 1)
    even, odd = contract([other_amps, from_other], *place, "other", partial)

    parts = add_cores(even, swap(odd, "pair", 1))
    parts = [parts[0]] + [swap(parts[k], "pair", 2 * k) for k in reversed(range(1, pair_count // 2))]
    ladder, mirror = add_chips(parts)
    mirrors = [
        lax.ppermute(mirror, "slab", [(s, (s - k) % slab_count) for s in range(slab_count)])
        for k in reversed(range(1, slab_count))
    ]
    mirrors = [mirror] + mirrors[::-1]
    update = finish(ladder, mirrors, denominator, select, first_local, slab_virt)
    return update.reshape(occ_local, occupied, first_local, slab_virt)


def solution(mesh):
    placed = (P("pair", None, None), P("pair", "slab"), P(), P(), P())
    return jax.shard_map(
        local, mesh=mesh, in_specs=placed, out_specs=P("pair", None, "slab", None), check_vma=False
    )
```

```python
import functools
import math

import jax
import jax.numpy as jnp
from jax import lax
from jax.experimental import pallas as pl
from jax.experimental.pallas import tpu as pltpu
from jax.sharding import PartitionSpec as P

IRREPS = 8
MIB = 2**20
SHARE = 0.24
TIE_FLOPS = 10**10


def start_of(part, slab_ref, shared):
    parity = slab_ref[0] % 2
    return pl.multiple_of({"own": parity * shared, "other": (1 - parity) * shared, "rest": 2 * shared, "all": 0}[part], 128)


def pack_kernel(rows_local, shared, which, me_ref, slab_ref, amps_ref, other_ref, after_ref, *refs):
    outs, (held, packed, sems) = refs[:-3], refs[-3:]
    size = packed.shape[-1]
    count = sems.shape[0]
    me = me_ref[0]
    start = start_of(which, slab_ref, shared)
    sources = [amps_ref] if which == "own" else [amps_ref, other_ref]
    wanted = {
        "own": lambda dest: (dest ^ me) >= 2,
        "rest": lambda dest: jnp.logical_and(((dest ^ me) & 1) == 0, dest != me),
        "all": lambda dest: dest == me,
    }[which]
    slots = {"own": lambda dest: dest, "rest": lambda dest: dest // 2, "all": lambda dest: 0}[which]

    def load(dest, source):
        first = dest * rows_local // 128 * 128
        width = -(-(dest * rows_local - first + size) // 128) * 128
        return pltpu.make_async_copy(
            sources[source].at[:, pl.ds(start + first, width)],
            held.at[slots(dest), source, :, pl.ds(0, width)],
            sems.at[dest, source],
        )

    for dest in range(count):

        @pl.when(wanted(dest))
        def _():
            for source in range(len(sources)):
                load(dest, source).start()

    for dest in range(count):

        @pl.when(wanted(dest))
        def _():
            shift = dest * rows_local % 128
            for source in range(len(sources)):
                load(dest, source).wait()
                block = held[slots(dest), source, :, shift : shift + size]
                if which == "own":
                    packed[dest ^ me] = block
                elif which == "rest":
                    packed[(dest ^ me) // 2, source] = block
                else:
                    outs[0][source] = block

    if which == "own":
        for k, out in enumerate(outs):
            out[...] = packed[2 * k + 2 : 2 * k + 4]
    elif which == "rest":
        for k, out in enumerate(outs):
            out[...] = packed[k + 1]


def pack(amps, other, me, slab, shared, which, pair_count, after):
    rows, virt_pairs = amps.shape
    rows_local = virt_pairs // pair_count
    size = {"own": shared, "rest": rows_local - 2 * shared, "all": rows_local}[which]
    slots = {"own": pair_count, "rest": pair_count // 2, "all": 1}[which]
    sources = 1 if which == "own" else 2
    held = (slots, sources, rows, -(-size // 128) * 128 + 128)
    packed = {"own": (pair_count, rows, size), "rest": (pair_count // 2, 2, rows, size), "all": (1, rows, size)}[which]
    outs = 1 if which == "all" else pair_count // 2 - 1
    return pl.pallas_call(
        functools.partial(pack_kernel, rows_local, shared, which),
        out_shape=[jax.ShapeDtypeStruct((2, rows, size), amps.dtype)] * outs,
        in_specs=[pl.BlockSpec(memory_space=pltpu.SMEM)] * 2 + [pl.BlockSpec(memory_space=pl.ANY)] * 3,
        out_specs=[pl.BlockSpec(memory_space=pltpu.VMEM)] * outs,
        scratch_shapes=[
            pltpu.VMEM(held, amps.dtype),
            pltpu.VMEM(packed, amps.dtype),
            pltpu.SemaphoreType.DMA((pair_count, sources)),
        ],
        compiler_params=pltpu.CompilerParams(vmem_limit_bytes=2 * MIB + 6 * slots * sources * rows * held[3]),
        cost_estimate=pl.CostEstimate(
            flops=0, bytes_accessed=4 * slots * sources * rows * size, transcendentals=0
        ),
        name="pack_" + which,
    )(me, slab, pltpu.with_memory_space_constraint(amps, pltpu.HBM), other, after)


def mask_kernel(per_step, parts, me_ref, slab_ref, irrep_ref, occ_ref, virt_ref, row_ref, ints_ref, *refs):
    _, out_ref, select_ref, denominator_ref, table, padded, by_row = refs
    step = pl.program_id(0)
    chunk, cols = ints_ref.shape[1:]
    slab_virt = virt_ref.shape[0]
    first_local = cols // slab_virt
    bits = slab_virt.bit_length() - 1
    me, slab = me_ref[0], slab_ref[0]

    @pl.when(step == 0)
    def _():
        padded[:, : row_ref.shape[1]] = row_ref[...]
        for k in range(padded.shape[1] // 128):
            lanes = slice(k * 128, (k + 1) * 128)
            by_row[lanes] = jnp.transpose(jnp.broadcast_to(padded[:, lanes], (128, 128)))

        col = lax.broadcasted_iota(jnp.int32, (1, cols), 1)
        a_of, b_of = col >> bits, col & (slab_virt - 1)
        irrep_a = irrep_b = jnp.zeros_like(col)
        energy_a = energy_b = jnp.zeros(col.shape, jnp.float32)
        for a in range(first_local):
            irrep_a = jnp.where(a_of == a, irrep_ref[slab * first_local + a], irrep_a)
            energy_a = jnp.where(a_of == a, virt_ref[slab * first_local + a], energy_a)
        for b in range(slab_virt):
            irrep_b = jnp.where(b_of == b, irrep_ref[b], irrep_b)
            energy_b = jnp.where(b_of == b, virt_ref[b], energy_b)
        irrep_ab = irrep_a ^ irrep_b

        for part in range(parts):
            for lanes in (slice(k, k + 128) for k in range(0, cols, 128)):
                needed = by_row[part * chunk : (part + 1) * chunk] ^ irrep_ab[:, lanes]
                for irrep in range(IRREPS):
                    table[irrep * parts + part, :, lanes] = jnp.where(needed == irrep, 1.0, 0.0).astype(table.dtype)

        occupied = denominator_ref.shape[0]
        j_of = lax.broadcasted_iota(jnp.int32, (occupied, cols), 0)
        energy_j = jnp.zeros((occupied, cols), jnp.float32)
        for j in range(occupied):
            energy_j = jnp.where(j_of == j, occ_ref[j], energy_j)
        denominator_ref[...] = energy_a + energy_b - occ_ref[me] - energy_j

        row = lax.broadcasted_iota(jnp.int32, (cols, cols), 0)
        col = lax.broadcasted_iota(jnp.int32, (cols, cols), 1)
        same_a = (row & (slab_virt - 1)) == slab * first_local + (col >> bits)
        slab_count = select_ref.shape[0] // cols
        for t in range(slab_count):
            same_b = (slab + t) % slab_count * first_local + (row >> bits) == (col & (slab_virt - 1))
            chosen = jnp.where(same_a & same_b, 1.0, 0.0)
            select_ref[t * cols : (t + 1) * cols] = chosen.astype(select_ref.dtype)

    chunks = per_step * pl.num_programs(0)
    for k in range(per_step):
        index = me * chunks + step * per_step + k
        irrep_c = irrep_ref[index // parts]
        out_ref[k] = ints_ref[k] * table[irrep_c * parts + index % parts]


def in_hbm(array):
    return pltpu.with_memory_space_constraint(array, pltpu.HBM)


def mask(integrals, me, slab, virt_irrep, occ_energy, slab_energy, after):
    virtuals = virt_irrep.shape[0]
    slab_virt = slab_energy.shape[0]
    occupied = occ_energy.shape[0]
    rows_local, cols_local = integrals.shape
    chunk = math.gcd(virtuals, rows_local)
    parts = virtuals // chunk
    chunks = rows_local // chunk
    per_step = next(n for n in (10, 5, 4, 2, 1) if chunks % n == 0)
    padded = -(-virtuals // 128) * 128
    select_rows = slab_virt * slab_virt
    block = pl.BlockSpec((per_step, chunk, cols_local), lambda step: (step, 0, 0))
    scalars = pl.BlockSpec(memory_space=pltpu.SMEM)
    masked, select, denominator = pl.pallas_call(
        functools.partial(mask_kernel, per_step, parts),
        grid=(chunks // per_step,),
        in_specs=[scalars] * 5
        + [pl.BlockSpec((1, virtuals), lambda step: (0, 0)), block, pl.BlockSpec(memory_space=pl.ANY)],
        out_specs=[
            block,
            pl.BlockSpec((select_rows, cols_local), lambda step: (0, 0)),
            pl.BlockSpec((occupied, cols_local), lambda step: (0, 0)),
        ],
        scratch_shapes=[
            pltpu.VMEM((IRREPS * parts, chunk, cols_local), integrals.dtype),
            pltpu.VMEM((1, padded), jnp.int32),
            pltpu.VMEM((padded, 128), jnp.int32),
        ],
        out_shape=[
            pltpu.VMEM((chunks, chunk, cols_local), integrals.dtype),
            jax.ShapeDtypeStruct((select_rows, cols_local), jnp.bfloat16),
            jax.ShapeDtypeStruct((occupied, cols_local), jnp.float32),
        ],
        compiler_params=pltpu.CompilerParams(vmem_limit_bytes=16 * MIB),
        cost_estimate=pl.CostEstimate(
            flops=0, bytes_accessed=0, transcendentals=0
        ),
        name="mask_integrals",
    )(
        me,
        slab,
        *(in_hbm(array) for array in (virt_irrep, occ_energy, slab_energy, virt_irrep.reshape(1, virtuals))),
        in_hbm(integrals.reshape(chunks, chunk, cols_local)),
        after,
    )
    return masked.reshape(rows_local, cols_local), select, denominator


def take_kernel(*refs):
    parts, out_ref = refs[:-2], refs[-1]
    for k, part in enumerate(parts):
        out_ref[k] = part[1]


def take_other(parts, after):
    count = len(parts)
    _, rows, size = parts[0].shape
    vmem = pl.BlockSpec(memory_space=pltpu.VMEM)
    return pl.pallas_call(
        take_kernel,
        out_shape=jax.ShapeDtypeStruct((count, rows, size), parts[0].dtype),
        in_specs=[vmem] * count + [pl.BlockSpec(memory_space=pl.ANY)],
        out_specs=vmem,
        compiler_params=pltpu.CompilerParams(vmem_limit_bytes=4 * MIB),
        cost_estimate=pl.CostEstimate(flops=0, bytes_accessed=4 * count * rows * size, transcendentals=0),
        name="take_other",
    )(*parts, after)


def join_kernel(*refs):
    parts, other_ref, out_ref = refs[:-2], refs[-2], refs[-1]
    for k, part in enumerate(parts):
        out_ref[k, 0] = part[0]
        out_ref[k, 1] = other_ref[k]


def join(parts, other):
    vmem = pl.BlockSpec(memory_space=pltpu.VMEM)
    return pl.pallas_call(
        join_kernel,
        out_shape=jax.ShapeDtypeStruct((len(parts),) + parts[0].shape, other.dtype),
        in_specs=[vmem] * (len(parts) + 1),
        out_specs=vmem,
        compiler_params=pltpu.CompilerParams(vmem_limit_bytes=4 * MIB),
        cost_estimate=pl.CostEstimate(flops=0, bytes_accessed=8 * other.size, transcendentals=0),
        name="join",
    )(*parts, other)


def tie_kernel(*refs):
    del refs


def tie(parts, after):
    count = len(parts)
    anywhere = pl.BlockSpec(memory_space=pl.ANY)
    return pl.pallas_call(
        tie_kernel,
        out_shape=[pltpu.VMEM(part.shape, part.dtype) for part in parts],
        in_specs=[anywhere] * (count + 1),
        out_specs=[anywhere] * count,
        input_output_aliases={k: k for k in range(count)},
        compiler_params=pltpu.CompilerParams(vmem_limit_bytes=2 * MIB),
        cost_estimate=pl.CostEstimate(flops=TIE_FLOPS, bytes_accessed=0, transcendentals=0),
        name="tie",
    )(*(pltpu.with_memory_space_constraint(part, pltpu.VMEM) for part in parts), after)


def contract_kernel(which, shared, slab_ref, me_ref, home_ref, ints_ref, *refs):
    last = which == "other"
    lhs = refs[-2] if last else refs[-1]
    count, rows, size = lhs.shape
    chips = count // 2 - 1
    start = start_of(which, slab_ref, shared)
    lhs[:2] = home_ref[:, :, pl.ds(start, size)]
    for k in range(chips):
        if which == "rest":
            lhs[2 * k + 2 : 2 * k + 4] = refs[k][...]
        else:
            lhs[2 * k + 2 : 2 * k + 4] = refs[0][k]
    refs = refs[chips if which == "rest" else 1 :]
    step = 2560
    total = None
    for first in range(0, size, step):
        width = min(step, size - first)
        block = lhs[:, :, first : first + width].reshape(count * rows, width)
        part = jnp.dot(block, ints_ref[pl.ds(start + first, width)], preferred_element_type=jnp.float32)
        total = part if total is None else total + part
    if not last:
        before, out_ref = refs[:-2], refs[-2]
        out_ref[...] = total + before[0][...] if before else total
        return
    before_ref, own_ref, other_ref, _, partial = refs
    me = me_ref[0]
    partial[:count, :rows] = (total + before_ref[...]).reshape(count, rows, total.shape[1])
    for i in range(count):
        block = partial[i ^ me, :rows]
        partial[count + (i ^ me), :rows] = block
        for j in range(rows):
            partial[count + (j ^ me), rows + i : rows + i + 1] = block[j : j + 1]
    for k in range(count // 2):
        own_ref[k] = partial[count + 2 * k]
        other_ref[k] = partial[count + 2 * k + 1]


def contract(amps, home, ints, me, slab, shared, which, before=None):
    occupied, size = amps[0].shape[-2:]
    cols = ints.shape[1]
    vmem = pl.BlockSpec(memory_space=pltpu.VMEM)
    operands = [*amps] + ([] if before is None else [before])
    scratch = [pltpu.VMEM((occupied, occupied, size), home.dtype)]
    if which == "other":
        out_shape = [jax.ShapeDtypeStruct((occupied // 2, 2 * occupied, cols), jnp.float32)] * 2
        scratch.append(pltpu.VMEM((2 * occupied, 2 * occupied, cols), jnp.float32))
    else:
        out_shape = [jax.ShapeDtypeStruct((occupied * occupied, cols), jnp.float32)]
    return pl.pallas_call(
        functools.partial(contract_kernel, which, shared),
        out_shape=out_shape,
        in_specs=[pl.BlockSpec(memory_space=pltpu.SMEM)] * 2 + [vmem] * (2 + len(operands)),
        out_specs=[vmem] * len(out_shape),
        scratch_shapes=scratch,
        compiler_params=pltpu.CompilerParams(
            vmem_limit_bytes=4 * MIB + 40 * occupied * occupied * cols + 4 * occupied * occupied * size
        ),
        cost_estimate=pl.CostEstimate(
            flops=2 * occupied * occupied * size * cols,
            bytes_accessed=2 * size * (cols + occupied * occupied),
            transcendentals=0,
        ),
        name="contract",
    )(slab, me, home, pltpu.with_memory_space_constraint(ints, pltpu.VMEM), *operands)


def select_exactly(values, select):
    rows = values.shape[0]
    high = values.astype(jnp.bfloat16)
    rest = values - high.astype(jnp.float32)
    middle = rest.astype(jnp.bfloat16)
    low = (rest - middle.astype(jnp.float32)).astype(jnp.bfloat16)
    terms = [jnp.dot(term, select, preferred_element_type=jnp.float32) for term in (high, middle, low)]
    return terms[0] + terms[1] + terms[2]


def add_cores_kernel(mine_ref, other_ref, *outs):
    for k, out in enumerate(outs):
        out[...] = mine_ref[k] + other_ref[k]


def add_cores(mine, other):
    count, rows, cols = mine.shape
    vmem = pl.BlockSpec(memory_space=pltpu.VMEM)
    return pl.pallas_call(
        add_cores_kernel,
        out_shape=[jax.ShapeDtypeStruct((rows, cols), jnp.float32)] * count,
        in_specs=[vmem, vmem],
        out_specs=[vmem] * count,
        compiler_params=pltpu.CompilerParams(vmem_limit_bytes=4 * MIB),
        cost_estimate=pl.CostEstimate(flops=mine.size, bytes_accessed=12 * mine.size, transcendentals=0),
        name="add_cores",
    )(mine, other)


def add_chips_kernel(*refs):
    parts, (ladder_ref, mirror_ref) = refs[:-2], refs[-2:]
    total = parts[0][...]
    for part in parts[1:]:
        total = total + part[...]
    half = total.shape[0] // 2
    ladder_ref[...] = total[:half]
    mirror_ref[...] = total[half:]


def add_chips(parts):
    rows, cols = parts[0].shape
    half = jax.ShapeDtypeStruct((rows // 2, cols), jnp.float32)
    vmem = pl.BlockSpec(memory_space=pltpu.VMEM)
    return pl.pallas_call(
        add_chips_kernel,
        out_shape=[half, half],
        in_specs=[vmem] * len(parts),
        out_specs=[vmem, vmem],
        compiler_params=pltpu.CompilerParams(vmem_limit_bytes=4 * MIB),
        cost_estimate=pl.CostEstimate(
            flops=len(parts) * rows * cols, bytes_accessed=4 * len(parts) * rows * cols, transcendentals=0
        ),
        name="add_chips",
    )(*parts)


def finish_kernel(ladder_ref, denominator_ref, select_ref, *refs):
    mirrors, out_ref = refs[:-1], refs[-1]
    mirror = select_exactly(jnp.concatenate([ref[...] for ref in mirrors], axis=1), select_ref[...])
    update = (ladder_ref[...] + mirror) / denominator_ref[...]
    _, first_local, slab_virt = out_ref.shape
    for a in range(first_local):
        out_ref[:, a, :] = update[:, a * slab_virt : (a + 1) * slab_virt]


def finish(ladder, mirrors, denominator, select, first_local, slab_virt):
    rows = ladder.shape[0]
    return pl.pallas_call(
        finish_kernel,
        out_shape=jax.ShapeDtypeStruct((rows, first_local, slab_virt), jnp.float32),
        in_specs=[pl.BlockSpec(memory_space=pltpu.VMEM)] * (3 + len(mirrors)),
        out_specs=pl.BlockSpec(memory_space=pltpu.VMEM),
        compiler_params=pltpu.CompilerParams(vmem_limit_bytes=6 * MIB),
        cost_estimate=pl.CostEstimate(flops=6 * rows * select.size, bytes_accessed=2 * select.size, transcendentals=0),
        name="finish",
    )(ladder, denominator, select, *mirrors)


def swap(values, axis, bits):
    return lax.ppermute(values, axis, [(p, p ^ bits) for p in range(lax.axis_size(axis))])


def local(amplitudes, integrals, virt_irrep, occ_energy, slab_energy):
    pair_count = lax.axis_size("pair")
    slab_count = lax.axis_size("slab")
    occ_local, occupied, virt_pairs = amplitudes.shape
    rows_local, cols_local = integrals.shape
    slab_virt = slab_energy.shape[0]
    first_local = slab_virt // slab_count
    assert occ_local == 1
    me = lax.axis_index("pair").astype(jnp.int32).reshape(1)
    slab = lax.axis_index("slab").astype(jnp.int32).reshape(1)

    shared = int(SHARE * rows_local) // 128 * 128
    amps = amplitudes.reshape(occupied, virt_pairs)
    chips = [2 * k for k in range(1, pair_count // 2)]

    def to_chips(parts):
        return [swap(part, "pair", bits) for part, bits in zip(parts, chips)]

    other = swap(amps, "pair", 1)
    parts = pack(amps, me, me, slab, shared, "own", pair_count, me)
    own_amps = to_chips(parts)
    parts = pack(amps, other, me, slab, shared, "rest", pair_count, parts[-1])
    rest_amps = to_chips(parts)
    (home,) = pack(amps, other, me, slab, shared, "all", pair_count, parts[-1])

    own_amps = join(own_amps, swap(take_other(own_amps, home), "pair", 1))
    other_amps = swap(own_amps, "slab", 1)
    masked, select, denominator = mask(integrals, me, slab, virt_irrep, occ_energy, slab_energy, own_amps)
    rest_amps = tie(rest_amps, denominator)
    place = (home, masked, me, slab, shared)
    (partial,) = contract([own_amps], *place, "own")
    (partial,) = contract(rest_amps, *place, "rest", partial)
    even, odd = contract([other_amps], *place, "other", partial)

    parts = add_cores(even, swap(odd, "pair", 1))
    parts = [parts[0]] + [swap(parts[k], "pair", 2 * k) for k in reversed(range(1, pair_count // 2))]
    ladder, mirror = add_chips(parts)
    mirrors = [
        lax.ppermute(mirror, "slab", [(s, (s - k) % slab_count) for s in range(slab_count)])
        for k in reversed(range(1, slab_count))
    ]
    mirrors = [mirror] + mirrors[::-1]
    update = finish(ladder, mirrors, denominator, select, first_local, slab_virt)
    return update.reshape(occ_local, occupied, first_local, slab_virt)


def solution(mesh):
    placed = (P("pair", None, None), P("pair", "slab"), P(), P(), P())
    return jax.shard_map(
        local, mesh=mesh, in_specs=placed, out_specs=P("pair", None, "slab", None), check_vma=False
    )
```

```python
import functools
import math

import jax
import jax.numpy as jnp
from jax import lax
from jax.experimental import pallas as pl
from jax.experimental.pallas import tpu as pltpu
from jax.sharding import PartitionSpec as P

IRREPS = 8
MIB = 2**20
SHARE = 0.25
TIE_FLOPS = 10**10


def start_of(part, slab_ref, shared):
    parity = slab_ref[0] % 2
    return pl.multiple_of({"own": parity * shared, "other": (1 - parity) * shared, "rest": 2 * shared, "all": 0}[part], 128)


def pack_kernel(rows_local, shared, which, me_ref, slab_ref, amps_ref, other_ref, after_ref, *refs):
    outs, (held, packed, sems) = refs[:-3], refs[-3:]
    size = packed.shape[-1]
    count = sems.shape[0]
    me = me_ref[0]
    start = start_of(which, slab_ref, shared)
    sources = [amps_ref] if which == "own" else [amps_ref, other_ref]
    wanted = {
        "own": lambda dest: (dest ^ me) >= 2,
        "rest": lambda dest: jnp.logical_and(((dest ^ me) & 1) == 0, dest != me),
        "all": lambda dest: dest == me,
    }[which]
    slots = {"own": lambda dest: dest, "rest": lambda dest: dest // 2, "all": lambda dest: 0}[which]

    def load(dest, source):
        first = dest * rows_local // 128 * 128
        width = -(-(dest * rows_local - first + size) // 128) * 128
        return pltpu.make_async_copy(
            sources[source].at[:, pl.ds(start + first, width)],
            held.at[slots(dest), source, :, pl.ds(0, width)],
            sems.at[dest, source],
        )

    for dest in range(count):

        @pl.when(wanted(dest))
        def _():
            for source in range(len(sources)):
                load(dest, source).start()

    for dest in range(count):

        @pl.when(wanted(dest))
        def _():
            shift = dest * rows_local % 128
            for source in range(len(sources)):
                load(dest, source).wait()
                block = held[slots(dest), source, :, shift : shift + size]
                if which == "own":
                    packed[dest ^ me] = block
                elif which == "rest":
                    packed[(dest ^ me) // 2, source] = block
                else:
                    outs[0][source] = block

    if which == "own":
        for k, out in enumerate(outs):
            out[...] = packed[2 * k + 2 : 2 * k + 4]
    elif which == "rest":
        for k, out in enumerate(outs):
            out[...] = packed[k + 1]


def pack(amps, other, me, slab, shared, which, pair_count, after):
    rows, virt_pairs = amps.shape
    rows_local = virt_pairs // pair_count
    size = {"own": shared, "rest": rows_local - 2 * shared, "all": rows_local}[which]
    slots = {"own": pair_count, "rest": pair_count // 2, "all": 1}[which]
    sources = 1 if which == "own" else 2
    held = (slots, sources, rows, -(-size // 128) * 128 + 128)
    packed = {"own": (pair_count, rows, size), "rest": (pair_count // 2, 2, rows, size), "all": (1, rows, size)}[which]
    outs = 1 if which == "all" else pair_count // 2 - 1
    return pl.pallas_call(
        functools.partial(pack_kernel, rows_local, shared, which),
        out_shape=[jax.ShapeDtypeStruct((2, rows, size), amps.dtype)] * outs,
        in_specs=[pl.BlockSpec(memory_space=pltpu.SMEM)] * 2 + [pl.BlockSpec(memory_space=pl.ANY)] * 3,
        out_specs=[pl.BlockSpec(memory_space=pltpu.VMEM)] * outs,
        scratch_shapes=[
            pltpu.VMEM(held, amps.dtype),
            pltpu.VMEM(packed, amps.dtype),
            pltpu.SemaphoreType.DMA((pair_count, sources)),
        ],
        compiler_params=pltpu.CompilerParams(vmem_limit_bytes=2 * MIB + 6 * slots * sources * rows * held[3]),
        cost_estimate=pl.CostEstimate(
            flops=0, bytes_accessed=4 * slots * sources * rows * size, transcendentals=0
        ),
        name="pack_" + which,
    )(me, slab, pltpu.with_memory_space_constraint(amps, pltpu.HBM), other, after)


def mask_kernel(per_step, parts, me_ref, slab_ref, irrep_ref, occ_ref, virt_ref, row_ref, ints_ref, *refs):
    _, out_ref, select_ref, denominator_ref, table, padded, by_row = refs
    step = pl.program_id(0)
    chunk, cols = ints_ref.shape[1:]
    slab_virt = virt_ref.shape[0]
    first_local = cols // slab_virt
    bits = slab_virt.bit_length() - 1
    me, slab = me_ref[0], slab_ref[0]

    @pl.when(step == 0)
    def _():
        padded[:, : row_ref.shape[1]] = row_ref[...]
        for k in range(padded.shape[1] // 128):
            lanes = slice(k * 128, (k + 1) * 128)
            by_row[lanes] = jnp.transpose(jnp.broadcast_to(padded[:, lanes], (128, 128)))

        col = lax.broadcasted_iota(jnp.int32, (1, cols), 1)
        a_of, b_of = col >> bits, col & (slab_virt - 1)
        irrep_a = irrep_b = jnp.zeros_like(col)
        energy_a = energy_b = jnp.zeros(col.shape, jnp.float32)
        for a in range(first_local):
            irrep_a = jnp.where(a_of == a, irrep_ref[slab * first_local + a], irrep_a)
            energy_a = jnp.where(a_of == a, virt_ref[slab * first_local + a], energy_a)
        for b in range(slab_virt):
            irrep_b = jnp.where(b_of == b, irrep_ref[b], irrep_b)
            energy_b = jnp.where(b_of == b, virt_ref[b], energy_b)
        irrep_ab = irrep_a ^ irrep_b

        for part in range(parts):
            for lanes in (slice(k, k + 128) for k in range(0, cols, 128)):
                needed = by_row[part * chunk : (part + 1) * chunk] ^ irrep_ab[:, lanes]
                for irrep in range(IRREPS):
                    table[irrep * parts + part, :, lanes] = jnp.where(needed == irrep, 1.0, 0.0).astype(table.dtype)

        occupied = denominator_ref.shape[0]
        j_of = lax.broadcasted_iota(jnp.int32, (occupied, cols), 0)
        energy_j = jnp.zeros((occupied, cols), jnp.float32)
        for j in range(occupied):
            energy_j = jnp.where(j_of == j, occ_ref[j], energy_j)
        denominator_ref[...] = energy_a + energy_b - occ_ref[me] - energy_j

        row = lax.broadcasted_iota(jnp.int32, (cols, cols), 0)
        col = lax.broadcasted_iota(jnp.int32, (cols, cols), 1)
        same_a = (row & (slab_virt - 1)) == slab * first_local + (col >> bits)
        slab_count = select_ref.shape[0] // cols
        for t in range(slab_count):
            same_b = (slab + t) % slab_count * first_local + (row >> bits) == (col & (slab_virt - 1))
            chosen = jnp.where(same_a & same_b, 1.0, 0.0)
            select_ref[t * cols : (t + 1) * cols] = chosen.astype(select_ref.dtype)

    chunks = per_step * pl.num_programs(0)
    for k in range(per_step):
        index = me * chunks + step * per_step + k
        irrep_c = irrep_ref[index // parts]
        out_ref[k] = ints_ref[k] * table[irrep_c * parts + index % parts]


def in_hbm(array):
    return pltpu.with_memory_space_constraint(array, pltpu.HBM)


def mask(integrals, me, slab, virt_irrep, occ_energy, slab_energy, after):
    virtuals = virt_irrep.shape[0]
    slab_virt = slab_energy.shape[0]
    occupied = occ_energy.shape[0]
    rows_local, cols_local = integrals.shape
    chunk = math.gcd(virtuals, rows_local)
    parts = virtuals // chunk
    chunks = rows_local // chunk
    per_step = next(n for n in (10, 5, 4, 2, 1) if chunks % n == 0)
    padded = -(-virtuals // 128) * 128
    select_rows = slab_virt * slab_virt
    block = pl.BlockSpec((per_step, chunk, cols_local), lambda step: (step, 0, 0))
    scalars = pl.BlockSpec(memory_space=pltpu.SMEM)
    masked, select, denominator = pl.pallas_call(
        functools.partial(mask_kernel, per_step, parts),
        grid=(chunks // per_step,),
        in_specs=[scalars] * 5
        + [pl.BlockSpec((1, virtuals), lambda step: (0, 0)), block, pl.BlockSpec(memory_space=pl.ANY)],
        out_specs=[
            block,
            pl.BlockSpec((select_rows, cols_local), lambda step: (0, 0)),
            pl.BlockSpec((occupied, cols_local), lambda step: (0, 0)),
        ],
        scratch_shapes=[
            pltpu.VMEM((IRREPS * parts, chunk, cols_local), integrals.dtype),
            pltpu.VMEM((1, padded), jnp.int32),
            pltpu.VMEM((padded, 128), jnp.int32),
        ],
        out_shape=[
            pltpu.VMEM((chunks, chunk, cols_local), integrals.dtype),
            jax.ShapeDtypeStruct((select_rows, cols_local), jnp.bfloat16),
            jax.ShapeDtypeStruct((occupied, cols_local), jnp.float32),
        ],
        compiler_params=pltpu.CompilerParams(vmem_limit_bytes=16 * MIB),
        cost_estimate=pl.CostEstimate(
            flops=0, bytes_accessed=0, transcendentals=0
        ),
        name="mask_integrals",
    )(
        me,
        slab,
        *(in_hbm(array) for array in (virt_irrep, occ_energy, slab_energy, virt_irrep.reshape(1, virtuals))),
        in_hbm(integrals.reshape(chunks, chunk, cols_local)),
        after,
    )
    return masked.reshape(rows_local, cols_local), select, denominator


def take_kernel(*refs):
    parts, out_ref = refs[:-2], refs[-1]
    for k, part in enumerate(parts):
        out_ref[k] = part[1]


def take_other(parts, after):
    count = len(parts)
    _, rows, size = parts[0].shape
    vmem = pl.BlockSpec(memory_space=pltpu.VMEM)
    return pl.pallas_call(
        take_kernel,
        out_shape=jax.ShapeDtypeStruct((count, rows, size), parts[0].dtype),
        in_specs=[vmem] * count + [pl.BlockSpec(memory_space=pl.ANY)],
        out_specs=vmem,
        compiler_params=pltpu.CompilerParams(vmem_limit_bytes=4 * MIB),
        cost_estimate=pl.CostEstimate(flops=0, bytes_accessed=4 * count * rows * size, transcendentals=0),
        name="take_other",
    )(*parts, after)


def join_kernel(*refs):
    parts, other_ref, out_ref = refs[:-2], refs[-2], refs[-1]
    for k, part in enumerate(parts):
        out_ref[k, 0] = part[0]
        out_ref[k, 1] = other_ref[k]


def join(parts, other):
    vmem = pl.BlockSpec(memory_space=pltpu.VMEM)
    return pl.pallas_call(
        join_kernel,
        out_shape=jax.ShapeDtypeStruct((len(parts),) + parts[0].shape, other.dtype),
        in_specs=[vmem] * (len(parts) + 1),
        out_specs=vmem,
        compiler_params=pltpu.CompilerParams(vmem_limit_bytes=4 * MIB),
        cost_estimate=pl.CostEstimate(flops=0, bytes_accessed=8 * other.size, transcendentals=0),
        name="join",
    )(*parts, other)


def tie_kernel(*refs):
    del refs


def tie(parts, after):
    count = len(parts)
    anywhere = pl.BlockSpec(memory_space=pl.ANY)
    return pl.pallas_call(
        tie_kernel,
        out_shape=[pltpu.VMEM(part.shape, part.dtype) for part in parts],
        in_specs=[anywhere] * (count + 1),
        out_specs=[anywhere] * count,
        input_output_aliases={k: k for k in range(count)},
        compiler_params=pltpu.CompilerParams(vmem_limit_bytes=2 * MIB),
        cost_estimate=pl.CostEstimate(flops=TIE_FLOPS, bytes_accessed=0, transcendentals=0),
        name="tie",
    )(*(pltpu.with_memory_space_constraint(part, pltpu.VMEM) for part in parts), after)


def contract_kernel(which, shared, slab_ref, me_ref, home_ref, ints_ref, *refs):
    last = which == "other"
    lhs = refs[-2] if last else refs[-1]
    count, rows, size = lhs.shape
    chips = count // 2 - 1
    start = start_of(which, slab_ref, shared)
    lhs[:2] = home_ref[:, :, pl.ds(start, size)]
    for k in range(chips):
        if which == "rest":
            lhs[2 * k + 2 : 2 * k + 4] = refs[k][...]
        else:
            lhs[2 * k + 2 : 2 * k + 4] = refs[0][k]
    refs = refs[chips if which == "rest" else 1 :]
    step = 2560
    total = None
    for first in range(0, size, step):
        width = min(step, size - first)
        block = lhs[:, :, first : first + width].reshape(count * rows, width)
        part = jnp.dot(block, ints_ref[pl.ds(start + first, width)], preferred_element_type=jnp.float32)
        total = part if total is None else total + part
    if not last:
        before, out_ref = refs[:-2], refs[-2]
        out_ref[...] = total + before[0][...] if before else total
        return
    before_ref, own_ref, other_ref, _, partial = refs
    me = me_ref[0]
    partial[:count, :rows] = (total + before_ref[...]).reshape(count, rows, total.shape[1])
    for i in range(count):
        block = partial[i ^ me, :rows]
        partial[count + (i ^ me), :rows] = block
        for j in range(rows):
            partial[count + (j ^ me), rows + i : rows + i + 1] = block[j : j + 1]
    for k in range(count // 2):
        own_ref[k] = partial[count + 2 * k]
        other_ref[k] = partial[count + 2 * k + 1]


def contract(amps, home, ints, me, slab, shared, which, before=None):
    occupied, size = amps[0].shape[-2:]
    cols = ints.shape[1]
    vmem = pl.BlockSpec(memory_space=pltpu.VMEM)
    operands = [*amps] + ([] if before is None else [before])
    scratch = [pltpu.VMEM((occupied, occupied, size), home.dtype)]
    if which == "other":
        out_shape = [jax.ShapeDtypeStruct((occupied // 2, 2 * occupied, cols), jnp.float32)] * 2
        scratch.append(pltpu.VMEM((2 * occupied, 2 * occupied, cols), jnp.float32))
    else:
        out_shape = [jax.ShapeDtypeStruct((occupied * occupied, cols), jnp.float32)]
    return pl.pallas_call(
        functools.partial(contract_kernel, which, shared),
        out_shape=out_shape,
        in_specs=[pl.BlockSpec(memory_space=pltpu.SMEM)] * 2 + [vmem] * (2 + len(operands)),
        out_specs=[vmem] * len(out_shape),
        scratch_shapes=scratch,
        compiler_params=pltpu.CompilerParams(
            vmem_limit_bytes=4 * MIB + 40 * occupied * occupied * cols + 4 * occupied * occupied * size
        ),
        cost_estimate=pl.CostEstimate(
            flops=2 * occupied * occupied * size * cols,
            bytes_accessed=2 * size * (cols + occupied * occupied),
            transcendentals=0,
        ),
        name="contract",
    )(slab, me, home, pltpu.with_memory_space_constraint(ints, pltpu.VMEM), *operands)


def select_exactly(values, select):
    rows = values.shape[0]
    high = values.astype(jnp.bfloat16)
    rest = values - high.astype(jnp.float32)
    middle = rest.astype(jnp.bfloat16)
    low = (rest - middle.astype(jnp.float32)).astype(jnp.bfloat16)
    terms = [jnp.dot(term, select, preferred_element_type=jnp.float32) for term in (high, middle, low)]
    return terms[0] + terms[1] + terms[2]


def add_cores_kernel(mine_ref, other_ref, *outs):
    for k, out in enumerate(outs):
        out[...] = mine_ref[k] + other_ref[k]


def add_cores(mine, other):
    count, rows, cols = mine.shape
    vmem = pl.BlockSpec(memory_space=pltpu.VMEM)
    return pl.pallas_call(
        add_cores_kernel,
        out_shape=[jax.ShapeDtypeStruct((rows, cols), jnp.float32)] * count,
        in_specs=[vmem, vmem],
        out_specs=[vmem] * count,
        compiler_params=pltpu.CompilerParams(vmem_limit_bytes=4 * MIB),
        cost_estimate=pl.CostEstimate(flops=mine.size, bytes_accessed=12 * mine.size, transcendentals=0),
        name="add_cores",
    )(mine, other)


def add_chips_kernel(*refs):
    parts, (ladder_ref, mirror_ref) = refs[:-2], refs[-2:]
    total = parts[0][...]
    for part in parts[1:]:
        total = total + part[...]
    half = total.shape[0] // 2
    ladder_ref[...] = total[:half]
    mirror_ref[...] = total[half:]


def add_chips(parts):
    rows, cols = parts[0].shape
    half = jax.ShapeDtypeStruct((rows // 2, cols), jnp.float32)
    vmem = pl.BlockSpec(memory_space=pltpu.VMEM)
    return pl.pallas_call(
        add_chips_kernel,
        out_shape=[half, half],
        in_specs=[vmem] * len(parts),
        out_specs=[vmem, vmem],
        compiler_params=pltpu.CompilerParams(vmem_limit_bytes=4 * MIB),
        cost_estimate=pl.CostEstimate(
            flops=len(parts) * rows * cols, bytes_accessed=4 * len(parts) * rows * cols, transcendentals=0
        ),
        name="add_chips",
    )(*parts)


def finish_kernel(ladder_ref, denominator_ref, select_ref, *refs):
    mirrors, out_ref = refs[:-1], refs[-1]
    mirror = select_exactly(jnp.concatenate([ref[...] for ref in mirrors], axis=1), select_ref[...])
    update = (ladder_ref[...] + mirror) / denominator_ref[...]
    _, first_local, slab_virt = out_ref.shape
    for a in range(first_local):
        out_ref[:, a, :] = update[:, a * slab_virt : (a + 1) * slab_virt]


def finish(ladder, mirrors, denominator, select, first_local, slab_virt):
    rows = ladder.shape[0]
    return pl.pallas_call(
        finish_kernel,
        out_shape=jax.ShapeDtypeStruct((rows, first_local, slab_virt), jnp.float32),
        in_specs=[pl.BlockSpec(memory_space=pltpu.VMEM)] * (3 + len(mirrors)),
        out_specs=pl.BlockSpec(memory_space=pltpu.VMEM),
        compiler_params=pltpu.CompilerParams(vmem_limit_bytes=6 * MIB),
        cost_estimate=pl.CostEstimate(flops=6 * rows * select.size, bytes_accessed=2 * select.size, transcendentals=0),
        name="finish",
    )(ladder, denominator, select, *mirrors)


def swap(values, axis, bits):
    return lax.ppermute(values, axis, [(p, p ^ bits) for p in range(lax.axis_size(axis))])


def local(amplitudes, integrals, virt_irrep, occ_energy, slab_energy):
    pair_count = lax.axis_size("pair")
    slab_count = lax.axis_size("slab")
    occ_local, occupied, virt_pairs = amplitudes.shape
    rows_local, cols_local = integrals.shape
    slab_virt = slab_energy.shape[0]
    first_local = slab_virt // slab_count
    assert occ_local == 1
    me = lax.axis_index("pair").astype(jnp.int32).reshape(1)
    slab = lax.axis_index("slab").astype(jnp.int32).reshape(1)

    shared = int(SHARE * rows_local) // 128 * 128
    amps = amplitudes.reshape(occupied, virt_pairs)
    chips = [2 * k for k in range(1, pair_count // 2)]

    def to_chips(parts):
        return [swap(part, "pair", bits) for part, bits in zip(parts, chips)]

    other = swap(amps, "pair", 1)
    parts = pack(amps, me, me, slab, shared, "own", pair_count, me)
    own_amps = to_chips(parts)
    parts = pack(amps, other, me, slab, shared, "rest", pair_count, parts[-1])
    rest_amps = to_chips(parts)
    (home,) = pack(amps, other, me, slab, shared, "all", pair_count, parts[-1])

    own_amps = join(own_amps, swap(take_other(own_amps, home), "pair", 1))
    other_amps = swap(own_amps, "slab", 1)
    masked, select, denominator = mask(integrals, me, slab, virt_irrep, occ_energy, slab_energy, own_amps)
    rest_amps = tie(rest_amps, denominator)
    place = (home, masked, me, slab, shared)
    (partial,) = contract([own_amps], *place, "own")
    (partial,) = contract(rest_amps, *place, "rest", partial)
    even, odd = contract([other_amps], *place, "other", partial)

    parts = add_cores(even, swap(odd, "pair", 1))
    parts = [parts[0]] + [swap(parts[k], "pair", 2 * k) for k in reversed(range(1, pair_count // 2))]
    ladder, mirror = add_chips(parts)
    mirrors = [
        lax.ppermute(mirror, "slab", [(s, (s - k) % slab_count) for s in range(slab_count)])
        for k in reversed(range(1, slab_count))
    ]
    mirrors = [mirror] + mirrors[::-1]
    update = finish(ladder, mirrors, denominator, select, first_local, slab_virt)
    return update.reshape(occ_local, occupied, first_local, slab_virt)


def solution(mesh):
    placed = (P("pair", None, None), P("pair", "slab"), P(), P(), P())
    return jax.shard_map(
        local, mesh=mesh, in_specs=placed, out_specs=P("pair", None, "slab", None), check_vma=False
    )
```

```python
import functools
import math

import jax
import jax.numpy as jnp
from jax import lax
from jax.experimental import pallas as pl
from jax.experimental.pallas import tpu as pltpu
from jax.sharding import PartitionSpec as P

IRREPS = 8
MIB = 2**20
SHARE = 0.25
TIE_FLOPS = 10**10


def start_of(part, slab_ref, shared):
    parity = slab_ref[0] % 2
    return pl.multiple_of({"own": parity * shared, "other": (1 - parity) * shared, "rest": 2 * shared, "all": 0}[part], 128)


def pack_kernel(rows_local, shared, which, me_ref, slab_ref, amps_ref, other_ref, after_ref, *refs):
    outs, (held, packed, sems) = refs[:-3], refs[-3:]
    size = packed.shape[-1]
    count = sems.shape[0]
    me = me_ref[0]
    start = start_of(which, slab_ref, shared)
    sources = [amps_ref] if which == "own" else [amps_ref, other_ref]
    wanted = {
        "own": lambda dest: (dest ^ me) >= 2,
        "rest": lambda dest: jnp.logical_and(((dest ^ me) & 1) == 0, dest != me),
        "all": lambda dest: dest == me,
    }[which]
    slots = {"own": lambda dest: dest, "rest": lambda dest: dest // 2, "all": lambda dest: 0}[which]

    def load(dest, source):
        first = dest * rows_local // 128 * 128
        width = -(-(dest * rows_local - first + size) // 128) * 128
        return pltpu.make_async_copy(
            sources[source].at[:, pl.ds(start + first, width)],
            held.at[slots(dest), source, :, pl.ds(0, width)],
            sems.at[dest, source],
        )

    for dest in range(count):

        @pl.when(wanted(dest))
        def _():
            for source in range(len(sources)):
                load(dest, source).start()

    for dest in range(count):

        @pl.when(wanted(dest))
        def _():
            shift = dest * rows_local % 128
            for source in range(len(sources)):
                load(dest, source).wait()
                block = held[slots(dest), source, :, shift : shift + size]
                if which == "own":
                    packed[dest ^ me] = block
                elif which == "rest":
                    packed[(dest ^ me) // 2, source] = block
                else:
                    outs[0][source] = block

    if which == "own":
        for k, out in enumerate(outs):
            out[...] = packed[2 * k + 2 : 2 * k + 4]
    elif which == "rest":
        for k, out in enumerate(outs):
            out[...] = packed[k + 1]


def pack(amps, other, me, slab, shared, which, pair_count, after):
    rows, virt_pairs = amps.shape
    rows_local = virt_pairs // pair_count
    size = {"own": shared, "rest": rows_local - 2 * shared, "all": rows_local}[which]
    slots = {"own": pair_count, "rest": pair_count // 2, "all": 1}[which]
    sources = 1 if which == "own" else 2
    held = (slots, sources, rows, -(-size // 128) * 128 + 128)
    packed = {"own": (pair_count, rows, size), "rest": (pair_count // 2, 2, rows, size), "all": (1, rows, size)}[which]
    outs = 1 if which == "all" else pair_count // 2 - 1
    return pl.pallas_call(
        functools.partial(pack_kernel, rows_local, shared, which),
        out_shape=[jax.ShapeDtypeStruct((2, rows, size), amps.dtype)] * outs,
        in_specs=[pl.BlockSpec(memory_space=pltpu.SMEM)] * 2 + [pl.BlockSpec(memory_space=pl.ANY)] * 3,
        out_specs=[pl.BlockSpec(memory_space=pltpu.VMEM)] * outs,
        scratch_shapes=[
            pltpu.VMEM(held, amps.dtype),
            pltpu.VMEM(packed, amps.dtype),
            pltpu.SemaphoreType.DMA((pair_count, sources)),
        ],
        compiler_params=pltpu.CompilerParams(vmem_limit_bytes=2 * MIB + 6 * slots * sources * rows * held[3]),
        cost_estimate=pl.CostEstimate(
            flops=0, bytes_accessed=4 * slots * sources * rows * size, transcendentals=0
        ),
        name="pack_" + which,
    )(me, slab, pltpu.with_memory_space_constraint(amps, pltpu.HBM), other, after)


def mask_kernel(per_step, parts, me_ref, slab_ref, irrep_ref, occ_ref, virt_ref, row_ref, ints_ref, *refs):
    _, out_ref, by_slab_ref, by_first_ref, denominator_ref, table, padded, by_row = refs
    step = pl.program_id(0)
    chunk, cols = ints_ref.shape[1:]
    slab_virt = virt_ref.shape[0]
    first_local = cols // slab_virt
    bits = slab_virt.bit_length() - 1
    me, slab = me_ref[0], slab_ref[0]

    @pl.when(step == 0)
    def _():
        padded[:, : row_ref.shape[1]] = row_ref[...]
        for k in range(padded.shape[1] // 128):
            lanes = slice(k * 128, (k + 1) * 128)
            by_row[lanes] = jnp.transpose(jnp.broadcast_to(padded[:, lanes], (128, 128)))

        col = lax.broadcasted_iota(jnp.int32, (1, cols), 1)
        a_of, b_of = col >> bits, col & (slab_virt - 1)
        irrep_a = irrep_b = jnp.zeros_like(col)
        energy_a = energy_b = jnp.zeros(col.shape, jnp.float32)
        for a in range(first_local):
            irrep_a = jnp.where(a_of == a, irrep_ref[slab * first_local + a], irrep_a)
            energy_a = jnp.where(a_of == a, virt_ref[slab * first_local + a], energy_a)
        for b in range(slab_virt):
            irrep_b = jnp.where(b_of == b, irrep_ref[b], irrep_b)
            energy_b = jnp.where(b_of == b, virt_ref[b], energy_b)
        irrep_ab = irrep_a ^ irrep_b

        for part in range(parts):
            for lanes in (slice(k, k + 128) for k in range(0, cols, 128)):
                needed = by_row[part * chunk : (part + 1) * chunk] ^ irrep_ab[:, lanes]
                for irrep in range(IRREPS):
                    table[irrep * parts + part, :, lanes] = jnp.where(needed == irrep, 1.0, 0.0).astype(table.dtype)

        occupied = denominator_ref.shape[0]
        j_of = lax.broadcasted_iota(jnp.int32, (occupied, cols), 0)
        energy_j = jnp.zeros((occupied, cols), jnp.float32)
        for j in range(occupied):
            energy_j = jnp.where(j_of == j, occ_ref[j], energy_j)
        denominator_ref[...] = energy_a + energy_b - occ_ref[me] - energy_j

        row = lax.broadcasted_iota(jnp.int32, (cols, cols), 0)
        col = lax.broadcasted_iota(jnp.int32, (cols, cols), 1)
        first_bits = first_local.bit_length() - 1
        low = first_local - 1
        slabs = slab_virt // first_local
        source = (((col >> first_bits) & low) << bits) + ((col >> (2 * first_bits)) << first_bits) + (col & low)
        by_slab_ref[...] = jnp.where(row == source, 1.0, 0.0).astype(by_slab_ref.dtype)
        source = (((col >> first_bits) & (slabs - 1)) << (2 * first_bits)) + ((col & low) << first_bits) + (col >> bits)
        by_first_ref[...] = jnp.where(row == source, 1.0, 0.0).astype(by_first_ref.dtype)

    chunks = per_step * pl.num_programs(0)
    for k in range(per_step):
        index = me * chunks + step * per_step + k
        irrep_c = irrep_ref[index // parts]
        out_ref[k] = ints_ref[k] * table[irrep_c * parts + index % parts]


def in_hbm(array):
    return pltpu.with_memory_space_constraint(array, pltpu.HBM)


def mask(integrals, me, slab, virt_irrep, occ_energy, slab_energy, after):
    virtuals = virt_irrep.shape[0]
    slab_virt = slab_energy.shape[0]
    occupied = occ_energy.shape[0]
    rows_local, cols_local = integrals.shape
    chunk = math.gcd(virtuals, rows_local)
    parts = virtuals // chunk
    chunks = rows_local // chunk
    per_step = next(n for n in (10, 5, 4, 2, 1) if chunks % n == 0)
    padded = -(-virtuals // 128) * 128
    square = jax.ShapeDtypeStruct((cols_local, cols_local), jnp.bfloat16)
    block = pl.BlockSpec((per_step, chunk, cols_local), lambda step: (step, 0, 0))
    scalars = pl.BlockSpec(memory_space=pltpu.SMEM)
    masked, by_slab, by_first, denominator = pl.pallas_call(
        functools.partial(mask_kernel, per_step, parts),
        grid=(chunks // per_step,),
        in_specs=[scalars] * 5
        + [pl.BlockSpec((1, virtuals), lambda step: (0, 0)), block, pl.BlockSpec(memory_space=pl.ANY)],
        out_specs=[
            block,
            pl.BlockSpec(square.shape, lambda step: (0, 0)),
            pl.BlockSpec(square.shape, lambda step: (0, 0)),
            pl.BlockSpec((occupied, cols_local), lambda step: (0, 0)),
        ],
        scratch_shapes=[
            pltpu.VMEM((IRREPS * parts, chunk, cols_local), integrals.dtype),
            pltpu.VMEM((1, padded), jnp.int32),
            pltpu.VMEM((padded, 128), jnp.int32),
        ],
        out_shape=[
            pltpu.VMEM((chunks, chunk, cols_local), integrals.dtype),
            square,
            square,
            jax.ShapeDtypeStruct((occupied, cols_local), jnp.float32),
        ],
        compiler_params=pltpu.CompilerParams(vmem_limit_bytes=16 * MIB),
        cost_estimate=pl.CostEstimate(
            flops=0, bytes_accessed=0, transcendentals=0
        ),
        name="mask_integrals",
    )(
        me,
        slab,
        *(in_hbm(array) for array in (virt_irrep, occ_energy, slab_energy, virt_irrep.reshape(1, virtuals))),
        in_hbm(integrals.reshape(chunks, chunk, cols_local)),
        after,
    )
    return masked.reshape(rows_local, cols_local), by_slab, by_first, denominator


def take_kernel(*refs):
    parts, out_ref = refs[:-2], refs[-1]
    for k, part in enumerate(parts):
        out_ref[k] = part[1]


def take_other(parts, after):
    count = len(parts)
    _, rows, size = parts[0].shape
    vmem = pl.BlockSpec(memory_space=pltpu.VMEM)
    return pl.pallas_call(
        take_kernel,
        out_shape=jax.ShapeDtypeStruct((count, rows, size), parts[0].dtype),
        in_specs=[vmem] * count + [pl.BlockSpec(memory_space=pl.ANY)],
        out_specs=vmem,
        compiler_params=pltpu.CompilerParams(vmem_limit_bytes=4 * MIB),
        cost_estimate=pl.CostEstimate(flops=0, bytes_accessed=4 * count * rows * size, transcendentals=0),
        name="take_other",
    )(*parts, after)


def join_kernel(*refs):
    parts, other_ref, out_ref = refs[:-2], refs[-2], refs[-1]
    for k, part in enumerate(parts):
        out_ref[k, 0] = part[0]
        out_ref[k, 1] = other_ref[k]


def join(parts, other):
    vmem = pl.BlockSpec(memory_space=pltpu.VMEM)
    return pl.pallas_call(
        join_kernel,
        out_shape=jax.ShapeDtypeStruct((len(parts),) + parts[0].shape, other.dtype),
        in_specs=[vmem] * (len(parts) + 1),
        out_specs=vmem,
        compiler_params=pltpu.CompilerParams(vmem_limit_bytes=4 * MIB),
        cost_estimate=pl.CostEstimate(flops=0, bytes_accessed=8 * other.size, transcendentals=0),
        name="join",
    )(*parts, other)


def tie_kernel(*refs):
    del refs


def tie(parts, after):
    count = len(parts)
    anywhere = pl.BlockSpec(memory_space=pl.ANY)
    return pl.pallas_call(
        tie_kernel,
        out_shape=[pltpu.VMEM(part.shape, part.dtype) for part in parts],
        in_specs=[anywhere] * (count + 1),
        out_specs=[anywhere] * count,
        input_output_aliases={k: k for k in range(count)},
        compiler_params=pltpu.CompilerParams(vmem_limit_bytes=2 * MIB),
        cost_estimate=pl.CostEstimate(flops=TIE_FLOPS, bytes_accessed=0, transcendentals=0),
        name="tie",
    )(*(pltpu.with_memory_space_constraint(part, pltpu.VMEM) for part in parts), after)


def select_exactly(values, select):
    rows = values.shape[0]
    high = values.astype(jnp.bfloat16)
    rest = values - high.astype(jnp.float32)
    middle = rest.astype(jnp.bfloat16)
    low = (rest - middle.astype(jnp.float32)).astype(jnp.bfloat16)
    terms = [jnp.dot(term, select, preferred_element_type=jnp.float32) for term in (high, middle, low)]
    return terms[0] + terms[1] + terms[2]


def contract_kernel(which, shared, slab_ref, me_ref, home_ref, ints_ref, *refs):
    last = which == "other"
    lhs = refs[-3] if last else refs[-1]
    count, rows, size = lhs.shape
    chips = count // 2 - 1
    start = start_of(which, slab_ref, shared)
    lhs[:2] = home_ref[:, :, pl.ds(start, size)]
    for k in range(chips):
        if which == "rest":
            lhs[2 * k + 2 : 2 * k + 4] = refs[k][...]
        else:
            lhs[2 * k + 2 : 2 * k + 4] = refs[0][k]
    refs = refs[chips if which == "rest" else 1 :]
    step = 2560
    total = None
    for first in range(0, size, step):
        width = min(step, size - first)
        block = lhs[:, :, first : first + width].reshape(count * rows, width)
        part = jnp.dot(block, ints_ref[pl.ds(start + first, width)], preferred_element_type=jnp.float32)
        total = part if total is None else total + part
    if not last:
        before, out_ref = refs[:-2], refs[-2]
        out_ref[...] = total + before[0][...] if before else total
        return
    before_ref, by_slab_ref, own_ref, other_ref, mirror_ref, _, partial, ordered = refs
    total = total + before_ref[...]
    partial[...] = total.reshape(partial.shape)
    for k in range(count // 2):
        own_ref[k] = partial[2 * k]
        other_ref[k] = partial[2 * k + 1]
    partial[...] = select_exactly(total, by_slab_ref[...]).reshape(partial.shape)
    for i in range(count):
        ordered[i] = partial[i ^ me_ref[0]]
    slabs = mirror_ref.shape[0] // count
    half, width = mirror_ref.shape[1], mirror_ref.shape[2] // 2
    for p in range(count):
        block = ordered[:, p, :]
        for s in range(slabs):
            part = block[:, s * width : (s + 1) * width]
            mirror_ref[p * slabs + s, :, :width] = part[:half]
            mirror_ref[p * slabs + s, :, width:] = part[half:]


def contract(amps, home, ints, me, slab, shared, which, before=None, by_slab=None, slab_count=None):
    occupied, size = amps[0].shape[-2:]
    cols = ints.shape[1]
    vmem = pl.BlockSpec(memory_space=pltpu.VMEM)
    operands = [operand for operand in (*amps, before, by_slab) if operand is not None]
    scratch = [pltpu.VMEM((occupied, occupied, size), home.dtype)]
    if which == "other":
        width = 2 * cols // slab_count
        out_shape = [jax.ShapeDtypeStruct((occupied // 2, occupied, cols), jnp.float32)] * 2
        out_shape.append(jax.ShapeDtypeStruct((occupied * slab_count, occupied // 2, width), jnp.float32))
        scratch += [pltpu.VMEM((occupied, occupied, cols), jnp.float32)] * 2
    else:
        out_shape = [jax.ShapeDtypeStruct((occupied * occupied, cols), jnp.float32)]
    return pl.pallas_call(
        functools.partial(contract_kernel, which, shared),
        out_shape=out_shape,
        in_specs=[pl.BlockSpec(memory_space=pltpu.SMEM)] * 2 + [vmem] * (2 + len(operands)),
        out_specs=[vmem] * len(out_shape),
        scratch_shapes=scratch,
        compiler_params=pltpu.CompilerParams(
            vmem_limit_bytes=4 * MIB + 40 * occupied * occupied * cols + 4 * occupied * occupied * size
        ),
        cost_estimate=pl.CostEstimate(
            flops=2 * occupied * occupied * size * cols,
            bytes_accessed=2 * size * (cols + occupied * occupied),
            transcendentals=0,
        ),
        name="contract",
    )(slab, me, home, pltpu.with_memory_space_constraint(ints, pltpu.VMEM), *operands)


def add_cores_kernel(mine_ref, other_ref, *outs):
    for k, out in enumerate(outs):
        out[...] = mine_ref[k] + other_ref[k]


def add_cores(mine, other):
    count, rows, cols = mine.shape
    vmem = pl.BlockSpec(memory_space=pltpu.VMEM)
    return pl.pallas_call(
        add_cores_kernel,
        out_shape=[jax.ShapeDtypeStruct((rows, cols), jnp.float32)] * count,
        in_specs=[vmem, vmem],
        out_specs=[vmem] * count,
        compiler_params=pltpu.CompilerParams(vmem_limit_bytes=4 * MIB),
        cost_estimate=pl.CostEstimate(flops=mine.size, bytes_accessed=12 * mine.size, transcendentals=0),
        name="add_cores",
    )(mine, other)


def finish_kernel(mirror_ref, denominator_ref, select_ref, *refs):
    parts, out_ref = refs[:-1], refs[-1]
    ladder = parts[0][...]
    for part in parts[1:]:
        ladder = ladder + part[...]
    _, first_local, slab_virt = out_ref.shape
    slab_count = slab_virt // first_local
    width = mirror_ref.shape[2] // 2
    blocks = []
    for s in range(slab_count):
        block = mirror_ref[s]
        for q in range(1, mirror_ref.shape[0] // slab_count):
            block = block + mirror_ref[q * slab_count + s]
        blocks += [jnp.concatenate([block[:, :width], block[:, width:]], axis=0)]
    mirror = select_exactly(jnp.concatenate(blocks, axis=1), select_ref[...])
    update = (ladder + mirror) / denominator_ref[...]
    for a in range(first_local):
        out_ref[:, a, :] = update[:, a * slab_virt : (a + 1) * slab_virt]


def finish(parts, mirror, denominator, select, first_local, slab_virt):
    rows = parts[0].shape[0]
    return pl.pallas_call(
        finish_kernel,
        out_shape=jax.ShapeDtypeStruct((rows, first_local, slab_virt), jnp.float32),
        in_specs=[pl.BlockSpec(memory_space=pltpu.VMEM)] * (3 + len(parts)),
        out_specs=pl.BlockSpec(memory_space=pltpu.VMEM),
        compiler_params=pltpu.CompilerParams(vmem_limit_bytes=6 * MIB),
        cost_estimate=pl.CostEstimate(flops=6 * rows * select.size, bytes_accessed=2 * select.size, transcendentals=0),
        name="finish",
    )(mirror, denominator, select, *parts)


def swap(values, axis, bits):
    return lax.ppermute(values, axis, [(p, p ^ bits) for p in range(lax.axis_size(axis))])


def local(amplitudes, integrals, virt_irrep, occ_energy, slab_energy):
    pair_count = lax.axis_size("pair")
    slab_count = lax.axis_size("slab")
    occ_local, occupied, virt_pairs = amplitudes.shape
    rows_local, cols_local = integrals.shape
    slab_virt = slab_energy.shape[0]
    first_local = slab_virt // slab_count
    assert occ_local == 1
    me = lax.axis_index("pair").astype(jnp.int32).reshape(1)
    slab = lax.axis_index("slab").astype(jnp.int32).reshape(1)

    shared = int(SHARE * rows_local) // 128 * 128
    amps = amplitudes.reshape(occupied, virt_pairs)
    chips = [2 * k for k in range(1, pair_count // 2)]

    def to_chips(parts):
        return [swap(part, "pair", bits) for part, bits in zip(parts, chips)]

    other = swap(amps, "pair", 1)
    parts = pack(amps, me, me, slab, shared, "own", pair_count, me)
    own_amps = to_chips(parts)
    parts = pack(amps, other, me, slab, shared, "rest", pair_count, parts[-1])
    rest_amps = to_chips(parts)
    (home,) = pack(amps, other, me, slab, shared, "all", pair_count, parts[-1])

    own_amps = join(own_amps, swap(take_other(own_amps, home), "pair", 1))
    other_amps = swap(own_amps, "slab", 1)
    masked, by_slab, by_first, denominator = mask(integrals, me, slab, virt_irrep, occ_energy, slab_energy, own_amps)
    rest_amps = tie(rest_amps, denominator)
    place = (home, masked, me, slab, shared)
    (partial,) = contract([own_amps], *place, "own")
    (partial,) = contract(rest_amps, *place, "rest", partial)
    even, odd, mirror = contract([other_amps], *place, "other", partial, by_slab, slab_count)

    mirror = lax.all_to_all(mirror, ("pair", "slab"), split_axis=0, concat_axis=0, tiled=True)
    parts = add_cores(even, swap(odd, "pair", 1))
    parts = [parts[0]] + [swap(parts[k], "pair", 2 * k) for k in reversed(range(1, pair_count // 2))]
    update = finish(parts, mirror, denominator, by_first, first_local, slab_virt)
    return update.reshape(occ_local, occupied, first_local, slab_virt)


def solution(mesh):
    placed = (P("pair", None, None), P("pair", "slab"), P(), P(), P())
    return jax.shard_map(
        local, mesh=mesh, in_specs=placed, out_specs=P("pair", None, "slab", None), check_vma=False
    )
```

```python
import functools
import math

import jax
import jax.numpy as jnp
from jax import lax
from jax.experimental import pallas as pl
from jax.experimental.pallas import tpu as pltpu
from jax.sharding import PartitionSpec as P

IRREPS = 8
MIB = 2**20
SHARE = 0.25
TIE_FLOPS = 10**10


def start_of(part, slab_ref, shared):
    parity = slab_ref[0] % 2
    return pl.multiple_of({"own": parity * shared, "other": (1 - parity) * shared, "rest": 2 * shared, "all": 0}[part], 128)


def pack_kernel(rows_local, shared, which, me_ref, slab_ref, amps_ref, other_ref, after_ref, *refs):
    outs, (held, packed, sems) = refs[:-3], refs[-3:]
    size = packed.shape[-1]
    count = sems.shape[0]
    me = me_ref[0]
    start = start_of(which, slab_ref, shared)
    sources = [amps_ref] if which == "own" else [amps_ref, other_ref]
    wanted = {
        "own": lambda dest: (dest ^ me) >= 2,
        "rest": lambda dest: jnp.logical_and(((dest ^ me) & 1) == 0, dest != me),
        "all": lambda dest: dest == me,
    }[which]
    slots = {"own": lambda dest: dest, "rest": lambda dest: dest // 2, "all": lambda dest: 0}[which]

    def load(dest, source):
        first = dest * rows_local // 128 * 128
        width = -(-(dest * rows_local - first + size) // 128) * 128
        return pltpu.make_async_copy(
            sources[source].at[:, pl.ds(start + first, width)],
            held.at[slots(dest), source, :, pl.ds(0, width)],
            sems.at[dest, source],
        )

    for dest in range(count):

        @pl.when(wanted(dest))
        def _():
            for source in range(len(sources)):
                load(dest, source).start()

    for dest in range(count):

        @pl.when(wanted(dest))
        def _():
            shift = dest * rows_local % 128
            for source in range(len(sources)):
                load(dest, source).wait()
                block = held[slots(dest), source, :, shift : shift + size]
                if which == "own":
                    packed[dest ^ me] = block
                elif which == "rest":
                    packed[(dest ^ me) // 2, source] = block
                else:
                    outs[0][source] = block

    if which == "own":
        for k, out in enumerate(outs):
            out[...] = packed[2 * k + 2 : 2 * k + 4]
    elif which == "rest":
        for k, out in enumerate(outs):
            out[...] = packed[k + 1]


def pack(amps, other, me, slab, shared, which, pair_count, after):
    rows, virt_pairs = amps.shape
    rows_local = virt_pairs // pair_count
    size = {"own": shared, "rest": rows_local - 2 * shared, "all": rows_local}[which]
    slots = {"own": pair_count, "rest": pair_count // 2, "all": 1}[which]
    sources = 1 if which == "own" else 2
    held = (slots, sources, rows, -(-size // 128) * 128 + 128)
    packed = {"own": (pair_count, rows, size), "rest": (pair_count // 2, 2, rows, size), "all": (1, rows, size)}[which]
    outs = 1 if which == "all" else pair_count // 2 - 1
    return pl.pallas_call(
        functools.partial(pack_kernel, rows_local, shared, which),
        out_shape=[jax.ShapeDtypeStruct((2, rows, size), amps.dtype)] * outs,
        in_specs=[pl.BlockSpec(memory_space=pltpu.SMEM)] * 2 + [pl.BlockSpec(memory_space=pl.ANY)] * 3,
        out_specs=[pl.BlockSpec(memory_space=pltpu.VMEM)] * outs,
        scratch_shapes=[
            pltpu.VMEM(held, amps.dtype),
            pltpu.VMEM(packed, amps.dtype),
            pltpu.SemaphoreType.DMA((pair_count, sources)),
        ],
        compiler_params=pltpu.CompilerParams(vmem_limit_bytes=2 * MIB + 6 * slots * sources * rows * held[3]),
        cost_estimate=pl.CostEstimate(
            flops=0, bytes_accessed=4 * slots * sources * rows * size, transcendentals=0
        ),
        name="pack_" + which,
    )(me, slab, pltpu.with_memory_space_constraint(amps, pltpu.HBM), other, after)


def mask_kernel(per_step, parts, me_ref, slab_ref, irrep_ref, occ_ref, virt_ref, row_ref, ints_ref, *refs):
    _, out_ref, by_slab_ref, by_first_ref, denominator_ref, table, padded, by_row = refs
    step = pl.program_id(0)
    chunk, cols = ints_ref.shape[1:]
    slab_virt = virt_ref.shape[0]
    first_local = cols // slab_virt
    bits = slab_virt.bit_length() - 1
    me, slab = me_ref[0], slab_ref[0]

    @pl.when(step == 0)
    def _():
        padded[:, : row_ref.shape[1]] = row_ref[...]
        for k in range(padded.shape[1] // 128):
            lanes = slice(k * 128, (k + 1) * 128)
            by_row[lanes] = jnp.transpose(jnp.broadcast_to(padded[:, lanes], (128, 128)))

        col = lax.broadcasted_iota(jnp.int32, (1, cols), 1)
        a_of, b_of = col >> bits, col & (slab_virt - 1)
        irrep_a = irrep_b = jnp.zeros_like(col)
        energy_a = energy_b = jnp.zeros(col.shape, jnp.float32)
        for a in range(first_local):
            irrep_a = jnp.where(a_of == a, irrep_ref[slab * first_local + a], irrep_a)
            energy_a = jnp.where(a_of == a, virt_ref[slab * first_local + a], energy_a)
        for b in range(slab_virt):
            irrep_b = jnp.where(b_of == b, irrep_ref[b], irrep_b)
            energy_b = jnp.where(b_of == b, virt_ref[b], energy_b)
        irrep_ab = irrep_a ^ irrep_b

        for part in range(parts):
            for lanes in (slice(k, k + 128) for k in range(0, cols, 128)):
                needed = by_row[part * chunk : (part + 1) * chunk] ^ irrep_ab[:, lanes]
                for irrep in range(IRREPS):
                    table[irrep * parts + part, :, lanes] = jnp.where(needed == irrep, 1.0, 0.0).astype(table.dtype)

        occupied = denominator_ref.shape[0]
        j_of = lax.broadcasted_iota(jnp.int32, (occupied, cols), 0)
        energy_j = jnp.zeros((occupied, cols), jnp.float32)
        for j in range(occupied):
            energy_j = jnp.where(j_of == j, occ_ref[j], energy_j)
        denominator_ref[...] = energy_a + energy_b - occ_ref[me] - energy_j

        row = lax.broadcasted_iota(jnp.int32, (cols, cols), 0)
        col = lax.broadcasted_iota(jnp.int32, (cols, cols), 1)
        first_bits = first_local.bit_length() - 1
        low = first_local - 1
        slabs = slab_virt // first_local
        source = (((col >> first_bits) & low) << bits) + ((col >> (2 * first_bits)) << first_bits) + (col & low)
        by_slab_ref[...] = jnp.where(row == source, 1.0, 0.0).astype(by_slab_ref.dtype)
        source = (((col >> first_bits) & (slabs - 1)) << (2 * first_bits)) + ((col & low) << first_bits) + (col >> bits)
        by_first_ref[...] = jnp.where(row == source, 1.0, 0.0).astype(by_first_ref.dtype)

    chunks = per_step * pl.num_programs(0)
    for k in range(per_step):
        index = me * chunks + step * per_step + k
        irrep_c = irrep_ref[index // parts]
        out_ref[k] = ints_ref[k] * table[irrep_c * parts + index % parts]


def in_hbm(array):
    return pltpu.with_memory_space_constraint(array, pltpu.HBM)


def mask(integrals, me, slab, virt_irrep, occ_energy, slab_energy, after):
    virtuals = virt_irrep.shape[0]
    slab_virt = slab_energy.shape[0]
    occupied = occ_energy.shape[0]
    rows_local, cols_local = integrals.shape
    chunk = math.gcd(virtuals, rows_local)
    parts = virtuals // chunk
    chunks = rows_local // chunk
    per_step = next(n for n in (10, 5, 4, 2, 1) if chunks % n == 0)
    padded = -(-virtuals // 128) * 128
    square = jax.ShapeDtypeStruct((cols_local, cols_local), jnp.bfloat16)
    block = pl.BlockSpec((per_step, chunk, cols_local), lambda step: (step, 0, 0))
    scalars = pl.BlockSpec(memory_space=pltpu.SMEM)
    masked, by_slab, by_first, denominator = pl.pallas_call(
        functools.partial(mask_kernel, per_step, parts),
        grid=(chunks // per_step,),
        in_specs=[scalars] * 5
        + [pl.BlockSpec((1, virtuals), lambda step: (0, 0)), block, pl.BlockSpec(memory_space=pl.ANY)],
        out_specs=[
            block,
            pl.BlockSpec(square.shape, lambda step: (0, 0)),
            pl.BlockSpec(square.shape, lambda step: (0, 0)),
            pl.BlockSpec((occupied, cols_local), lambda step: (0, 0)),
        ],
        scratch_shapes=[
            pltpu.VMEM((IRREPS * parts, chunk, cols_local), integrals.dtype),
            pltpu.VMEM((1, padded), jnp.int32),
            pltpu.VMEM((padded, 128), jnp.int32),
        ],
        out_shape=[
            pltpu.VMEM((chunks, chunk, cols_local), integrals.dtype),
            square,
            square,
            jax.ShapeDtypeStruct((occupied, cols_local), jnp.float32),
        ],
        compiler_params=pltpu.CompilerParams(vmem_limit_bytes=16 * MIB),
        cost_estimate=pl.CostEstimate(
            flops=0, bytes_accessed=0, transcendentals=0
        ),
        name="mask_integrals",
    )(
        me,
        slab,
        *(in_hbm(array) for array in (virt_irrep, occ_energy, slab_energy, virt_irrep.reshape(1, virtuals))),
        in_hbm(integrals.reshape(chunks, chunk, cols_local)),
        after,
    )
    return masked.reshape(rows_local, cols_local), by_slab, by_first, denominator


def take_kernel(*refs):
    parts, out_ref = refs[:-2], refs[-1]
    for k, part in enumerate(parts):
        out_ref[k] = part[1]


def take_other(parts, after):
    count = len(parts)
    _, rows, size = parts[0].shape
    vmem = pl.BlockSpec(memory_space=pltpu.VMEM)
    return pl.pallas_call(
        take_kernel,
        out_shape=jax.ShapeDtypeStruct((count, rows, size), parts[0].dtype),
        in_specs=[vmem] * count + [pl.BlockSpec(memory_space=pl.ANY)],
        out_specs=vmem,
        compiler_params=pltpu.CompilerParams(vmem_limit_bytes=4 * MIB),
        cost_estimate=pl.CostEstimate(flops=0, bytes_accessed=4 * count * rows * size, transcendentals=0),
        name="take_other",
    )(*parts, after)


def join_kernel(*refs):
    parts, other_ref, out_ref = refs[:-2], refs[-2], refs[-1]
    for k, part in enumerate(parts):
        out_ref[k, 0] = part[0]
        out_ref[k, 1] = other_ref[k]


def join(parts, other):
    vmem = pl.BlockSpec(memory_space=pltpu.VMEM)
    return pl.pallas_call(
        join_kernel,
        out_shape=jax.ShapeDtypeStruct((len(parts),) + parts[0].shape, other.dtype),
        in_specs=[vmem] * (len(parts) + 1),
        out_specs=vmem,
        compiler_params=pltpu.CompilerParams(vmem_limit_bytes=4 * MIB),
        cost_estimate=pl.CostEstimate(flops=0, bytes_accessed=8 * other.size, transcendentals=0),
        name="join",
    )(*parts, other)


def tie_kernel(*refs):
    del refs


def tie(parts, after):
    count = len(parts)
    anywhere = pl.BlockSpec(memory_space=pl.ANY)
    return pl.pallas_call(
        tie_kernel,
        out_shape=[pltpu.VMEM(part.shape, part.dtype) for part in parts],
        in_specs=[anywhere] * (count + 1),
        out_specs=[anywhere] * count,
        input_output_aliases={k: k for k in range(count)},
        compiler_params=pltpu.CompilerParams(vmem_limit_bytes=2 * MIB),
        cost_estimate=pl.CostEstimate(flops=TIE_FLOPS, bytes_accessed=0, transcendentals=0),
        name="tie",
    )(*(pltpu.with_memory_space_constraint(part, pltpu.VMEM) for part in parts), after)


def select_exactly(values, select):
    rows = values.shape[0]
    high = values.astype(jnp.bfloat16)
    rest = values - high.astype(jnp.float32)
    middle = rest.astype(jnp.bfloat16)
    low = (rest - middle.astype(jnp.float32)).astype(jnp.bfloat16)
    terms = [jnp.dot(term, select, preferred_element_type=jnp.float32) for term in (high, middle, low)]
    return terms[0] + terms[1] + terms[2]


def contract_kernel(which, shared, slab_ref, me_ref, home_ref, ints_ref, *refs):
    last = which == "other"
    lhs = refs[-2] if last else refs[-1]
    count, rows, size = lhs.shape
    chips = count // 2 - 1
    start = start_of(which, slab_ref, shared)
    lhs[:2] = home_ref[:, :, pl.ds(start, size)]
    for k in range(chips):
        if which == "rest":
            lhs[2 * k + 2 : 2 * k + 4] = refs[k][...]
        else:
            lhs[2 * k + 2 : 2 * k + 4] = refs[0][k]
    refs = refs[chips if which == "rest" else 1 :]
    step = 2560
    total = None
    for first in range(0, size, step):
        width = min(step, size - first)
        block = lhs[:, :, first : first + width].reshape(count * rows, width)
        part = jnp.dot(block, ints_ref[pl.ds(start + first, width)], preferred_element_type=jnp.float32)
        total = part if total is None else total + part
    if not last:
        before, out_ref = refs[:-2], refs[-2]
        out_ref[...] = total + before[0][...] if before else total
        return
    before_ref, own_ref, other_ref, total_ref, _, partial = refs
    total = total + before_ref[...]
    total_ref[...] = total
    partial[...] = total.reshape(partial.shape)
    for k in range(count // 2):
        own_ref[k] = partial[2 * k]
        other_ref[k] = partial[2 * k + 1]


def mirror_kernel(me_ref, total_ref, select_ref, out_ref, chosen, ordered):
    count = chosen.shape[0]
    chosen[...] = select_exactly(total_ref[...], select_ref[...]).reshape(chosen.shape)
    for i in range(count):
        ordered[i] = chosen[i ^ me_ref[0]]
    slabs = out_ref.shape[0] // count
    half, width = out_ref.shape[1], out_ref.shape[2] // 2
    for p in range(count):
        block = ordered[:, p, :]
        for s in range(slabs):
            part = block[:, s * width : (s + 1) * width]
            out_ref[p * slabs + s, :, :width] = part[:half]
            out_ref[p * slabs + s, :, width:] = part[half:]


def mirror_blocks(total, select, me, slab_count):
    cols = total.shape[1]
    count = math.isqrt(total.shape[0])
    vmem = pl.BlockSpec(memory_space=pltpu.VMEM)
    return pl.pallas_call(
        mirror_kernel,
        out_shape=jax.ShapeDtypeStruct((count * slab_count, count // 2, 2 * cols // slab_count), jnp.float32),
        in_specs=[pl.BlockSpec(memory_space=pltpu.SMEM), vmem, vmem],
        out_specs=vmem,
        scratch_shapes=[pltpu.VMEM((count, count, cols), jnp.float32)] * 2,
        compiler_params=pltpu.CompilerParams(vmem_limit_bytes=4 * MIB + 40 * total.size),
        cost_estimate=pl.CostEstimate(flops=6 * total.size * cols, bytes_accessed=8 * total.size, transcendentals=0),
        name="mirror_blocks",
    )(me, total, select)


def contract(amps, home, ints, me, slab, shared, which, before=None):
    occupied, size = amps[0].shape[-2:]
    cols = ints.shape[1]
    vmem = pl.BlockSpec(memory_space=pltpu.VMEM)
    operands = [*amps] + ([] if before is None else [before])
    scratch = [pltpu.VMEM((occupied, occupied, size), home.dtype)]
    if which == "other":
        out_shape = [jax.ShapeDtypeStruct((occupied // 2, occupied, cols), jnp.float32)] * 2
        out_shape.append(jax.ShapeDtypeStruct((occupied * occupied, cols), jnp.float32))
        scratch.append(pltpu.VMEM((occupied, occupied, cols), jnp.float32))
    else:
        out_shape = [jax.ShapeDtypeStruct((occupied * occupied, cols), jnp.float32)]
    return pl.pallas_call(
        functools.partial(contract_kernel, which, shared),
        out_shape=out_shape,
        in_specs=[pl.BlockSpec(memory_space=pltpu.SMEM)] * 2 + [vmem] * (2 + len(operands)),
        out_specs=[vmem] * len(out_shape),
        scratch_shapes=scratch,
        compiler_params=pltpu.CompilerParams(
            vmem_limit_bytes=4 * MIB + 40 * occupied * occupied * cols + 4 * occupied * occupied * size
        ),
        cost_estimate=pl.CostEstimate(
            flops=2 * occupied * occupied * size * cols,
            bytes_accessed=2 * size * (cols + occupied * occupied),
            transcendentals=0,
        ),
        name="contract",
    )(slab, me, home, pltpu.with_memory_space_constraint(ints, pltpu.VMEM), *operands)


def add_cores_kernel(mine_ref, other_ref, *outs):
    for k, out in enumerate(outs):
        out[...] = mine_ref[k] + other_ref[k]


def add_cores(mine, other):
    count, rows, cols = mine.shape
    vmem = pl.BlockSpec(memory_space=pltpu.VMEM)
    return pl.pallas_call(
        add_cores_kernel,
        out_shape=[jax.ShapeDtypeStruct((rows, cols), jnp.float32)] * count,
        in_specs=[vmem, vmem],
        out_specs=[vmem] * count,
        compiler_params=pltpu.CompilerParams(vmem_limit_bytes=4 * MIB),
        cost_estimate=pl.CostEstimate(flops=mine.size, bytes_accessed=12 * mine.size, transcendentals=0),
        name="add_cores",
    )(mine, other)


def finish_kernel(mirror_ref, denominator_ref, select_ref, *refs):
    parts, out_ref = refs[:-1], refs[-1]
    ladder = parts[0][...]
    for part in parts[1:]:
        ladder = ladder + part[...]
    _, first_local, slab_virt = out_ref.shape
    slab_count = slab_virt // first_local
    width = mirror_ref.shape[2] // 2
    blocks = []
    for s in range(slab_count):
        block = mirror_ref[s]
        for q in range(1, mirror_ref.shape[0] // slab_count):
            block = block + mirror_ref[q * slab_count + s]
        blocks += [jnp.concatenate([block[:, :width], block[:, width:]], axis=0)]
    mirror = select_exactly(jnp.concatenate(blocks, axis=1), select_ref[...])
    update = (ladder + mirror) / denominator_ref[...]
    for a in range(first_local):
        out_ref[:, a, :] = update[:, a * slab_virt : (a + 1) * slab_virt]


def finish(parts, mirror, denominator, select, first_local, slab_virt):
    rows = parts[0].shape[0]
    return pl.pallas_call(
        finish_kernel,
        out_shape=jax.ShapeDtypeStruct((rows, first_local, slab_virt), jnp.float32),
        in_specs=[pl.BlockSpec(memory_space=pltpu.VMEM)] * (3 + len(parts)),
        out_specs=pl.BlockSpec(memory_space=pltpu.VMEM),
        compiler_params=pltpu.CompilerParams(vmem_limit_bytes=6 * MIB),
        cost_estimate=pl.CostEstimate(flops=6 * rows * select.size, bytes_accessed=2 * select.size, transcendentals=0),
        name="finish",
    )(mirror, denominator, select, *parts)


def swap(values, axis, bits):
    return lax.ppermute(values, axis, [(p, p ^ bits) for p in range(lax.axis_size(axis))])


def local(amplitudes, integrals, virt_irrep, occ_energy, slab_energy):
    pair_count = lax.axis_size("pair")
    slab_count = lax.axis_size("slab")
    occ_local, occupied, virt_pairs = amplitudes.shape
    rows_local, cols_local = integrals.shape
    slab_virt = slab_energy.shape[0]
    first_local = slab_virt // slab_count
    assert occ_local == 1
    me = lax.axis_index("pair").astype(jnp.int32).reshape(1)
    slab = lax.axis_index("slab").astype(jnp.int32).reshape(1)

    shared = int(SHARE * rows_local) // 128 * 128
    amps = amplitudes.reshape(occupied, virt_pairs)
    chips = [2 * k for k in range(1, pair_count // 2)]

    def to_chips(parts):
        return [swap(part, "pair", bits) for part, bits in zip(parts, chips)]

    other = swap(amps, "pair", 1)
    parts = pack(amps, me, me, slab, shared, "own", pair_count, me)
    own_amps = to_chips(parts)
    parts = pack(amps, other, me, slab, shared, "rest", pair_count, parts[-1])
    rest_amps = to_chips(parts)
    (home,) = pack(amps, other, me, slab, shared, "all", pair_count, parts[-1])

    own_amps = join(own_amps, swap(take_other(own_amps, home), "pair", 1))
    other_amps = swap(own_amps, "slab", 1)
    masked, by_slab, by_first, denominator = mask(integrals, me, slab, virt_irrep, occ_energy, slab_energy, own_amps)
    rest_amps = tie(rest_amps, denominator)
    place = (home, masked, me, slab, shared)
    (partial,) = contract([own_amps], *place, "own")
    (partial,) = contract(rest_amps, *place, "rest", partial)
    even, odd, total = contract([other_amps], *place, "other", partial)

    mirror = mirror_blocks(total, by_slab, me, slab_count)
    mirror = lax.all_to_all(mirror, ("pair", "slab"), split_axis=0, concat_axis=0, tiled=True)
    parts = add_cores(even, swap(odd, "pair", 1))
    parts = [parts[0]] + [swap(parts[k], "pair", 2 * k) for k in reversed(range(1, pair_count // 2))]
    update = finish(parts, mirror, denominator, by_first, first_local, slab_virt)
    return update.reshape(occ_local, occupied, first_local, slab_virt)


def solution(mesh):
    placed = (P("pair", None, None), P("pair", "slab"), P(), P(), P())
    return jax.shard_map(
        local, mesh=mesh, in_specs=placed, out_specs=P("pair", None, "slab", None), check_vma=False
    )
```

```python
import functools
import math

import jax
import jax.numpy as jnp
from jax import lax
from jax.experimental import pallas as pl
from jax.experimental.pallas import tpu as pltpu
from jax.sharding import PartitionSpec as P

IRREPS = 8
MIB = 2**20
SHARE = 0.25
TIE_FLOPS = 10**10


def start_of(part, slab_ref, shared):
    parity = slab_ref[0] % 2
    return pl.multiple_of({"own": parity * shared, "other": (1 - parity) * shared, "rest": 2 * shared, "all": 0}[part], 128)


def pack_kernel(rows_local, shared, which, me_ref, slab_ref, amps_ref, other_ref, after_ref, *refs):
    outs, (held, packed, sems) = refs[:-3], refs[-3:]
    size = packed.shape[-1]
    count = sems.shape[0]
    me = me_ref[0]
    start = start_of(which, slab_ref, shared)
    sources = [amps_ref] if which == "own" else [amps_ref, other_ref]
    wanted = {
        "own": lambda dest: (dest ^ me) >= 2,
        "rest": lambda dest: jnp.logical_and(((dest ^ me) & 1) == 0, dest != me),
        "all": lambda dest: dest == me,
    }[which]
    slots = {"own": lambda dest: dest, "rest": lambda dest: dest // 2, "all": lambda dest: 0}[which]

    def load(dest, source):
        first = dest * rows_local // 128 * 128
        width = -(-(dest * rows_local - first + size) // 128) * 128
        return pltpu.make_async_copy(
            sources[source].at[:, pl.ds(start + first, width)],
            held.at[slots(dest), source, :, pl.ds(0, width)],
            sems.at[dest, source],
        )

    for dest in range(count):

        @pl.when(wanted(dest))
        def _():
            for source in range(len(sources)):
                load(dest, source).start()

    for dest in range(count):

        @pl.when(wanted(dest))
        def _():
            shift = dest * rows_local % 128
            for source in range(len(sources)):
                load(dest, source).wait()
                block = held[slots(dest), source, :, shift : shift + size]
                if which == "own":
                    packed[dest ^ me] = block
                elif which == "rest":
                    packed[(dest ^ me) // 2, source] = block
                else:
                    outs[0][source] = block

    if which == "own":
        for k, out in enumerate(outs):
            out[...] = packed[2 * k + 2 : 2 * k + 4]
    elif which == "rest":
        for k, out in enumerate(outs):
            out[...] = packed[k + 1]


def pack(amps, other, me, slab, shared, which, pair_count, after):
    rows, virt_pairs = amps.shape
    rows_local = virt_pairs // pair_count
    size = {"own": shared, "rest": rows_local - 2 * shared, "all": rows_local}[which]
    slots = {"own": pair_count, "rest": pair_count // 2, "all": 1}[which]
    sources = 1 if which == "own" else 2
    held = (slots, sources, rows, -(-size // 128) * 128 + 128)
    packed = {"own": (pair_count, rows, size), "rest": (pair_count // 2, 2, rows, size), "all": (1, rows, size)}[which]
    outs = 1 if which == "all" else pair_count // 2 - 1
    return pl.pallas_call(
        functools.partial(pack_kernel, rows_local, shared, which),
        out_shape=[jax.ShapeDtypeStruct((2, rows, size), amps.dtype)] * outs,
        in_specs=[pl.BlockSpec(memory_space=pltpu.SMEM)] * 2 + [pl.BlockSpec(memory_space=pl.ANY)] * 3,
        out_specs=[pl.BlockSpec(memory_space=pltpu.VMEM)] * outs,
        scratch_shapes=[
            pltpu.VMEM(held, amps.dtype),
            pltpu.VMEM(packed, amps.dtype),
            pltpu.SemaphoreType.DMA((pair_count, sources)),
        ],
        compiler_params=pltpu.CompilerParams(vmem_limit_bytes=2 * MIB + 6 * slots * sources * rows * held[3]),
        cost_estimate=pl.CostEstimate(
            flops=0, bytes_accessed=4 * slots * sources * rows * size, transcendentals=0
        ),
        name="pack_" + which,
    )(me, slab, pltpu.with_memory_space_constraint(amps, pltpu.HBM), other, after)


def mask_kernel(per_step, parts, me_ref, slab_ref, irrep_ref, occ_ref, virt_ref, row_ref, ints_ref, *refs):
    _, out_ref, by_slab_ref, by_first_ref, denominator_ref, table, padded, by_row = refs
    step = pl.program_id(0)
    chunk, cols = ints_ref.shape[1:]
    slab_virt = virt_ref.shape[0]
    first_local = cols // slab_virt
    bits = slab_virt.bit_length() - 1
    me, slab = me_ref[0], slab_ref[0]

    @pl.when(step == 0)
    def _():
        padded[:, : row_ref.shape[1]] = row_ref[...]
        for k in range(padded.shape[1] // 128):
            lanes = slice(k * 128, (k + 1) * 128)
            by_row[lanes] = jnp.transpose(jnp.broadcast_to(padded[:, lanes], (128, 128)))

        col = lax.broadcasted_iota(jnp.int32, (1, cols), 1)
        a_of, b_of = col >> bits, col & (slab_virt - 1)
        irrep_a = irrep_b = jnp.zeros_like(col)
        energy_a = energy_b = jnp.zeros(col.shape, jnp.float32)
        for a in range(first_local):
            irrep_a = jnp.where(a_of == a, irrep_ref[slab * first_local + a], irrep_a)
            energy_a = jnp.where(a_of == a, virt_ref[slab * first_local + a], energy_a)
        for b in range(slab_virt):
            irrep_b = jnp.where(b_of == b, irrep_ref[b], irrep_b)
            energy_b = jnp.where(b_of == b, virt_ref[b], energy_b)
        irrep_ab = irrep_a ^ irrep_b

        for part in range(parts):
            for lanes in (slice(k, k + 128) for k in range(0, cols, 128)):
                needed = by_row[part * chunk : (part + 1) * chunk] ^ irrep_ab[:, lanes]
                for irrep in range(IRREPS):
                    table[irrep * parts + part, :, lanes] = jnp.where(needed == irrep, 1.0, 0.0).astype(table.dtype)

        occupied = denominator_ref.shape[0]
        j_of = lax.broadcasted_iota(jnp.int32, (occupied, cols), 0)
        energy_j = jnp.zeros((occupied, cols), jnp.float32)
        for j in range(occupied):
            energy_j = jnp.where(j_of == j, occ_ref[j], energy_j)
        denominator_ref[...] = energy_a + energy_b - occ_ref[me] - energy_j

        row = lax.broadcasted_iota(jnp.int32, (cols, cols), 0)
        col = lax.broadcasted_iota(jnp.int32, (cols, cols), 1)
        first_bits = first_local.bit_length() - 1
        low = first_local - 1
        slabs = slab_virt // first_local
        source = (((col >> first_bits) & low) << bits) + ((col >> (2 * first_bits)) << first_bits) + (col & low)
        by_slab_ref[...] = jnp.where(row == source, 1.0, 0.0).astype(by_slab_ref.dtype)
        source = (((col >> first_bits) & (slabs - 1)) << (2 * first_bits)) + ((col & low) << first_bits) + (col >> bits)
        by_first_ref[...] = jnp.where(row == source, 1.0, 0.0).astype(by_first_ref.dtype)

    chunks = per_step * pl.num_programs(0)
    for k in range(per_step):
        index = me * chunks + step * per_step + k
        irrep_c = irrep_ref[index // parts]
        out_ref[k] = ints_ref[k] * table[irrep_c * parts + index % parts]


def in_hbm(array):
    return pltpu.with_memory_space_constraint(array, pltpu.HBM)


def mask(integrals, me, slab, virt_irrep, occ_energy, slab_energy, after):
    virtuals = virt_irrep.shape[0]
    slab_virt = slab_energy.shape[0]
    occupied = occ_energy.shape[0]
    rows_local, cols_local = integrals.shape
    chunk = math.gcd(virtuals, rows_local)
    parts = virtuals // chunk
    chunks = rows_local // chunk
    per_step = next(n for n in (10, 5, 4, 2, 1) if chunks % n == 0)
    padded = -(-virtuals // 128) * 128
    square = jax.ShapeDtypeStruct((cols_local, cols_local), jnp.bfloat16)
    block = pl.BlockSpec((per_step, chunk, cols_local), lambda step: (step, 0, 0))
    scalars = pl.BlockSpec(memory_space=pltpu.SMEM)
    masked, by_slab, by_first, denominator = pl.pallas_call(
        functools.partial(mask_kernel, per_step, parts),
        grid=(chunks // per_step,),
        in_specs=[scalars] * 5
        + [pl.BlockSpec((1, virtuals), lambda step: (0, 0)), block, pl.BlockSpec(memory_space=pl.ANY)],
        out_specs=[
            block,
            pl.BlockSpec(square.shape, lambda step: (0, 0)),
            pl.BlockSpec(square.shape, lambda step: (0, 0)),
            pl.BlockSpec((occupied, cols_local), lambda step: (0, 0)),
        ],
        scratch_shapes=[
            pltpu.VMEM((IRREPS * parts, chunk, cols_local), integrals.dtype),
            pltpu.VMEM((1, padded), jnp.int32),
            pltpu.VMEM((padded, 128), jnp.int32),
        ],
        out_shape=[
            pltpu.VMEM((chunks, chunk, cols_local), integrals.dtype),
            square,
            square,
            jax.ShapeDtypeStruct((occupied, cols_local), jnp.float32),
        ],
        compiler_params=pltpu.CompilerParams(vmem_limit_bytes=16 * MIB),
        cost_estimate=pl.CostEstimate(
            flops=0, bytes_accessed=0, transcendentals=0
        ),
        name="mask_integrals",
    )(
        me,
        slab,
        *(in_hbm(array) for array in (virt_irrep, occ_energy, slab_energy, virt_irrep.reshape(1, virtuals))),
        in_hbm(integrals.reshape(chunks, chunk, cols_local)),
        after,
    )
    return masked.reshape(rows_local, cols_local), by_slab, by_first, denominator


def take_kernel(*refs):
    parts, out_ref = refs[:-2], refs[-1]
    for k, part in enumerate(parts):
        out_ref[k] = part[1]


def take_other(parts, after):
    count = len(parts)
    _, rows, size = parts[0].shape
    vmem = pl.BlockSpec(memory_space=pltpu.VMEM)
    return pl.pallas_call(
        take_kernel,
        out_shape=jax.ShapeDtypeStruct((count, rows, size), parts[0].dtype),
        in_specs=[vmem] * count + [pl.BlockSpec(memory_space=pl.ANY)],
        out_specs=vmem,
        compiler_params=pltpu.CompilerParams(vmem_limit_bytes=4 * MIB),
        cost_estimate=pl.CostEstimate(flops=0, bytes_accessed=4 * count * rows * size, transcendentals=0),
        name="take_other",
    )(*parts, after)


def join_kernel(*refs):
    parts, other_ref, out_ref = refs[:-2], refs[-2], refs[-1]
    for k, part in enumerate(parts):
        out_ref[k, 0] = part[0]
        out_ref[k, 1] = other_ref[k]


def join(parts, other):
    vmem = pl.BlockSpec(memory_space=pltpu.VMEM)
    return pl.pallas_call(
        join_kernel,
        out_shape=jax.ShapeDtypeStruct((len(parts),) + parts[0].shape, other.dtype),
        in_specs=[vmem] * (len(parts) + 1),
        out_specs=vmem,
        compiler_params=pltpu.CompilerParams(vmem_limit_bytes=4 * MIB),
        cost_estimate=pl.CostEstimate(flops=0, bytes_accessed=8 * other.size, transcendentals=0),
        name="join",
    )(*parts, other)


def tie_kernel(*refs):
    del refs


def tie(parts, after):
    count = len(parts)
    anywhere = pl.BlockSpec(memory_space=pl.ANY)
    return pl.pallas_call(
        tie_kernel,
        out_shape=[pltpu.VMEM(part.shape, part.dtype) for part in parts],
        in_specs=[anywhere] * (count + 1),
        out_specs=[anywhere] * count,
        input_output_aliases={k: k for k in range(count)},
        compiler_params=pltpu.CompilerParams(vmem_limit_bytes=2 * MIB),
        cost_estimate=pl.CostEstimate(flops=TIE_FLOPS, bytes_accessed=0, transcendentals=0),
        name="tie",
    )(*(pltpu.with_memory_space_constraint(part, pltpu.VMEM) for part in parts), after)


def select_exactly(values, select):
    rows = values.shape[0]
    high = values.astype(jnp.bfloat16)
    rest = values - high.astype(jnp.float32)
    middle = rest.astype(jnp.bfloat16)
    low = (rest - middle.astype(jnp.float32)).astype(jnp.bfloat16)
    terms = [jnp.dot(term, select, preferred_element_type=jnp.float32) for term in (high, middle, low)]
    return terms[0] + terms[1] + terms[2]


def contract_kernel(which, shared, slab_ref, me_ref, home_ref, ints_ref, *refs):
    last = which == "other"
    lhs = refs[-2] if last else refs[-1]
    count, rows, size = lhs.shape
    chips = count // 2 - 1
    start = start_of(which, slab_ref, shared)
    lhs[:2] = home_ref[:, :, pl.ds(start, size)]
    for k in range(chips):
        if which == "rest":
            lhs[2 * k + 2 : 2 * k + 4] = refs[k][...]
        else:
            lhs[2 * k + 2 : 2 * k + 4] = refs[0][k]
    refs = refs[chips if which == "rest" else 1 :]
    step = 2560
    total = None
    for first in range(0, size, step):
        width = min(step, size - first)
        block = lhs[:, :, first : first + width].reshape(count * rows, width)
        part = jnp.dot(block, ints_ref[pl.ds(start + first, width)], preferred_element_type=jnp.float32)
        total = part if total is None else total + part
    if not last:
        before, out_ref = refs[:-2], refs[-2]
        out_ref[...] = total + before[0][...] if before else total
        return
    before_ref, own_ref, other_ref, total_ref, _, partial = refs
    total = total + before_ref[...]
    total_ref[...] = total
    partial[...] = total.reshape(partial.shape)
    for k in range(count // 2):
        own_ref[k] = partial[2 * k]
        other_ref[k] = partial[2 * k + 1]


def select_kernel(total_ref, select_ref, out_ref):
    out_ref[...] = select_exactly(total_ref[...], select_ref[...])


def select_columns(total, select):
    vmem = pl.BlockSpec(memory_space=pltpu.VMEM)
    return pl.pallas_call(
        select_kernel,
        out_shape=jax.ShapeDtypeStruct(total.shape, total.dtype),
        in_specs=[vmem, vmem],
        out_specs=vmem,
        compiler_params=pltpu.CompilerParams(vmem_limit_bytes=4 * MIB + 40 * total.size),
        cost_estimate=pl.CostEstimate(
            flops=6 * total.size * total.shape[1], bytes_accessed=8 * total.size, transcendentals=0
        ),
        name="select_columns",
    )(total, select)


def mirror_kernel(me_ref, chosen_ref, after_ref, out_ref, ordered):
    del after_ref
    count = chosen_ref.shape[0]
    for i in range(count):
        ordered[i] = chosen_ref[i ^ me_ref[0]]
    slabs = out_ref.shape[0] // count
    half, width = out_ref.shape[1], out_ref.shape[2] // 2
    for p in range(count):
        block = ordered[:, p, :]
        for s in range(slabs):
            part = block[:, s * width : (s + 1) * width]
            out_ref[p * slabs + s, :, :width] = part[:half]
            out_ref[p * slabs + s, :, width:] = part[half:]


def mirror_blocks(chosen, me, slab_count, after):
    cols = chosen.shape[1]
    count = math.isqrt(chosen.shape[0])
    vmem = pl.BlockSpec(memory_space=pltpu.VMEM)
    return pl.pallas_call(
        mirror_kernel,
        out_shape=jax.ShapeDtypeStruct((count * slab_count, count // 2, 2 * cols // slab_count), jnp.float32),
        in_specs=[pl.BlockSpec(memory_space=pltpu.SMEM), vmem, pl.BlockSpec(memory_space=pl.ANY)],
        out_specs=vmem,
        scratch_shapes=[pltpu.VMEM((count, count, cols), jnp.float32)],
        compiler_params=pltpu.CompilerParams(vmem_limit_bytes=4 * MIB + 24 * chosen.size),
        cost_estimate=pl.CostEstimate(flops=0, bytes_accessed=8 * chosen.size, transcendentals=0),
        name="mirror_blocks",
    )(me, chosen.reshape(count, count, cols), after)


def contract(amps, home, ints, me, slab, shared, which, before=None):
    occupied, size = amps[0].shape[-2:]
    cols = ints.shape[1]
    vmem = pl.BlockSpec(memory_space=pltpu.VMEM)
    operands = [*amps] + ([] if before is None else [before])
    scratch = [pltpu.VMEM((occupied, occupied, size), home.dtype)]
    if which == "other":
        out_shape = [jax.ShapeDtypeStruct((occupied // 2, occupied, cols), jnp.float32)] * 2
        out_shape.append(jax.ShapeDtypeStruct((occupied * occupied, cols), jnp.float32))
        scratch.append(pltpu.VMEM((occupied, occupied, cols), jnp.float32))
    else:
        out_shape = [jax.ShapeDtypeStruct((occupied * occupied, cols), jnp.float32)]
    return pl.pallas_call(
        functools.partial(contract_kernel, which, shared),
        out_shape=out_shape,
        in_specs=[pl.BlockSpec(memory_space=pltpu.SMEM)] * 2 + [vmem] * (2 + len(operands)),
        out_specs=[vmem] * len(out_shape),
        scratch_shapes=scratch,
        compiler_params=pltpu.CompilerParams(
            vmem_limit_bytes=4 * MIB + 40 * occupied * occupied * cols + 4 * occupied * occupied * size
        ),
        cost_estimate=pl.CostEstimate(
            flops=2 * occupied * occupied * size * cols,
            bytes_accessed=2 * size * (cols + occupied * occupied),
            transcendentals=0,
        ),
        name="contract",
    )(slab, me, home, pltpu.with_memory_space_constraint(ints, pltpu.VMEM), *operands)


def add_cores_kernel(mine_ref, other_ref, *outs):
    for k, out in enumerate(outs):
        out[...] = mine_ref[k] + other_ref[k]


def add_cores(mine, other):
    count, rows, cols = mine.shape
    vmem = pl.BlockSpec(memory_space=pltpu.VMEM)
    return pl.pallas_call(
        add_cores_kernel,
        out_shape=[jax.ShapeDtypeStruct((rows, cols), jnp.float32)] * count,
        in_specs=[vmem, vmem],
        out_specs=[vmem] * count,
        compiler_params=pltpu.CompilerParams(vmem_limit_bytes=4 * MIB),
        cost_estimate=pl.CostEstimate(flops=mine.size, bytes_accessed=12 * mine.size, transcendentals=0),
        name="add_cores",
    )(mine, other)


def finish_kernel(mirror_ref, denominator_ref, select_ref, *refs):
    parts, out_ref = refs[:-1], refs[-1]
    ladder = parts[0][...]
    for part in parts[1:]:
        ladder = ladder + part[...]
    _, first_local, slab_virt = out_ref.shape
    slab_count = slab_virt // first_local
    width = mirror_ref.shape[2] // 2
    blocks = []
    for s in range(slab_count):
        block = mirror_ref[s]
        for q in range(1, mirror_ref.shape[0] // slab_count):
            block = block + mirror_ref[q * slab_count + s]
        blocks += [jnp.concatenate([block[:, :width], block[:, width:]], axis=0)]
    mirror = select_exactly(jnp.concatenate(blocks, axis=1), select_ref[...])
    update = (ladder + mirror) / denominator_ref[...]
    for a in range(first_local):
        out_ref[:, a, :] = update[:, a * slab_virt : (a + 1) * slab_virt]


def finish(parts, mirror, denominator, select, first_local, slab_virt):
    rows = parts[0].shape[0]
    return pl.pallas_call(
        finish_kernel,
        out_shape=jax.ShapeDtypeStruct((rows, first_local, slab_virt), jnp.float32),
        in_specs=[pl.BlockSpec(memory_space=pltpu.VMEM)] * (3 + len(parts)),
        out_specs=pl.BlockSpec(memory_space=pltpu.VMEM),
        compiler_params=pltpu.CompilerParams(vmem_limit_bytes=6 * MIB),
        cost_estimate=pl.CostEstimate(flops=6 * rows * select.size, bytes_accessed=2 * select.size, transcendentals=0),
        name="finish",
    )(mirror, denominator, select, *parts)


def swap(values, axis, bits):
    return lax.ppermute(values, axis, [(p, p ^ bits) for p in range(lax.axis_size(axis))])


def local(amplitudes, integrals, virt_irrep, occ_energy, slab_energy):
    pair_count = lax.axis_size("pair")
    slab_count = lax.axis_size("slab")
    occ_local, occupied, virt_pairs = amplitudes.shape
    rows_local, cols_local = integrals.shape
    slab_virt = slab_energy.shape[0]
    first_local = slab_virt // slab_count
    assert occ_local == 1
    me = lax.axis_index("pair").astype(jnp.int32).reshape(1)
    slab = lax.axis_index("slab").astype(jnp.int32).reshape(1)

    shared = int(SHARE * rows_local) // 128 * 128
    amps = amplitudes.reshape(occupied, virt_pairs)
    chips = [2 * k for k in range(1, pair_count // 2)]

    def to_chips(parts):
        return [swap(part, "pair", bits) for part, bits in zip(parts, chips)]

    other = swap(amps, "pair", 1)
    parts = pack(amps, me, me, slab, shared, "own", pair_count, me)
    own_amps = to_chips(parts)
    parts = pack(amps, other, me, slab, shared, "rest", pair_count, parts[-1])
    rest_amps = to_chips(parts)
    (home,) = pack(amps, other, me, slab, shared, "all", pair_count, parts[-1])

    own_amps = join(own_amps, swap(take_other(own_amps, home), "pair", 1))
    other_amps = swap(own_amps, "slab", 1)
    masked, by_slab, by_first, denominator = mask(integrals, me, slab, virt_irrep, occ_energy, slab_energy, own_amps)
    rest_amps = tie(rest_amps, denominator)
    place = (home, masked, me, slab, shared)
    (partial,) = contract([own_amps], *place, "own")
    (partial,) = contract(rest_amps, *place, "rest", partial)
    even, odd, total = contract([other_amps], *place, "other", partial)

    odd = swap(odd, "pair", 1)
    mirror = mirror_blocks(select_columns(total, by_slab), me, slab_count, odd)
    mirror = lax.all_to_all(mirror, ("pair", "slab"), split_axis=0, concat_axis=0, tiled=True)
    parts = add_cores(even, odd)
    parts = [parts[0]] + [swap(parts[k], "pair", 2 * k) for k in reversed(range(1, pair_count // 2))]
    update = finish(parts, mirror, denominator, by_first, first_local, slab_virt)
    return update.reshape(occ_local, occupied, first_local, slab_virt)


def solution(mesh):
    placed = (P("pair", None, None), P("pair", "slab"), P(), P(), P())
    return jax.shard_map(
        local, mesh=mesh, in_specs=placed, out_specs=P("pair", None, "slab", None), check_vma=False
    )
```

```python
import functools
import math

import jax
import jax.numpy as jnp
from jax import lax
from jax.experimental import pallas as pl
from jax.experimental.pallas import tpu as pltpu
from jax.sharding import PartitionSpec as P

IRREPS = 8
MIB = 2**20
SHARE = 0.25
TIE_FLOPS = 10**10


def start_of(part, slab_ref, shared):
    parity = slab_ref[0] % 2
    return pl.multiple_of({"own": parity * shared, "other": (1 - parity) * shared, "rest": 2 * shared, "all": 0}[part], 128)


def pack_kernel(rows_local, shared, which, me_ref, slab_ref, amps_ref, other_ref, after_ref, *refs):
    outs, (held, packed, sems) = refs[:-3], refs[-3:]
    size = packed.shape[-1]
    count = sems.shape[0]
    me = me_ref[0]
    start = start_of(which, slab_ref, shared)
    sources = [amps_ref] if which == "own" else [amps_ref, other_ref]
    wanted = {
        "own": lambda dest: (dest ^ me) >= 2,
        "rest": lambda dest: jnp.logical_and(((dest ^ me) & 1) == 0, dest != me),
        "all": lambda dest: dest == me,
    }[which]
    slots = {"own": lambda dest: dest, "rest": lambda dest: dest // 2, "all": lambda dest: 0}[which]

    def load(dest, source):
        first = dest * rows_local // 128 * 128
        width = -(-(dest * rows_local - first + size) // 128) * 128
        return pltpu.make_async_copy(
            sources[source].at[:, pl.ds(start + first, width)],
            held.at[slots(dest), source, :, pl.ds(0, width)],
            sems.at[dest, source],
        )

    for dest in range(count):

        @pl.when(wanted(dest))
        def _():
            for source in range(len(sources)):
                load(dest, source).start()

    for dest in range(count):

        @pl.when(wanted(dest))
        def _():
            shift = dest * rows_local % 128
            for source in range(len(sources)):
                load(dest, source).wait()
                block = held[slots(dest), source, :, shift : shift + size]
                if which == "own":
                    packed[dest ^ me] = block
                elif which == "rest":
                    packed[(dest ^ me) // 2, source] = block
                else:
                    outs[0][source] = block

    if which == "own":
        for k, out in enumerate(outs):
            out[...] = packed[2 * k + 2 : 2 * k + 4]
    elif which == "rest":
        for k, out in enumerate(outs):
            out[...] = packed[k + 1]


def pack(amps, other, me, slab, shared, which, pair_count, after):
    rows, virt_pairs = amps.shape
    rows_local = virt_pairs // pair_count
    size = {"own": shared, "rest": rows_local - 2 * shared, "all": rows_local}[which]
    slots = {"own": pair_count, "rest": pair_count // 2, "all": 1}[which]
    sources = 1 if which == "own" else 2
    held = (slots, sources, rows, -(-size // 128) * 128 + 128)
    packed = {"own": (pair_count, rows, size), "rest": (pair_count // 2, 2, rows, size), "all": (1, rows, size)}[which]
    outs = 1 if which == "all" else pair_count // 2 - 1
    return pl.pallas_call(
        functools.partial(pack_kernel, rows_local, shared, which),
        out_shape=[jax.ShapeDtypeStruct((2, rows, size), amps.dtype)] * outs,
        in_specs=[pl.BlockSpec(memory_space=pltpu.SMEM)] * 2 + [pl.BlockSpec(memory_space=pl.ANY)] * 3,
        out_specs=[pl.BlockSpec(memory_space=pltpu.VMEM)] * outs,
        scratch_shapes=[
            pltpu.VMEM(held, amps.dtype),
            pltpu.VMEM(packed, amps.dtype),
            pltpu.SemaphoreType.DMA((pair_count, sources)),
        ],
        compiler_params=pltpu.CompilerParams(vmem_limit_bytes=2 * MIB + 6 * slots * sources * rows * held[3]),
        cost_estimate=pl.CostEstimate(
            flops=0, bytes_accessed=4 * slots * sources * rows * size, transcendentals=0
        ),
        name="pack_" + which,
    )(me, slab, pltpu.with_memory_space_constraint(amps, pltpu.HBM), other, after)


def mask_kernel(per_step, parts, me_ref, slab_ref, irrep_ref, occ_ref, virt_ref, row_ref, ints_ref, *refs):
    _, out_ref, by_slab_ref, by_first_ref, denominator_ref, table, padded, by_row = refs
    step = pl.program_id(0)
    chunk, cols = ints_ref.shape[1:]
    slab_virt = virt_ref.shape[0]
    first_local = cols // slab_virt
    bits = slab_virt.bit_length() - 1
    me, slab = me_ref[0], slab_ref[0]

    @pl.when(step == 0)
    def _():
        padded[:, : row_ref.shape[1]] = row_ref[...]
        for k in range(padded.shape[1] // 128):
            lanes = slice(k * 128, (k + 1) * 128)
            by_row[lanes] = jnp.transpose(jnp.broadcast_to(padded[:, lanes], (128, 128)))

        col = lax.broadcasted_iota(jnp.int32, (1, cols), 1)
        a_of, b_of = col >> bits, col & (slab_virt - 1)
        irrep_a = irrep_b = jnp.zeros_like(col)
        energy_a = energy_b = jnp.zeros(col.shape, jnp.float32)
        for a in range(first_local):
            irrep_a = jnp.where(a_of == a, irrep_ref[slab * first_local + a], irrep_a)
            energy_a = jnp.where(a_of == a, virt_ref[slab * first_local + a], energy_a)
        for b in range(slab_virt):
            irrep_b = jnp.where(b_of == b, irrep_ref[b], irrep_b)
            energy_b = jnp.where(b_of == b, virt_ref[b], energy_b)
        irrep_ab = irrep_a ^ irrep_b

        for part in range(parts):
            for lanes in (slice(k, k + 128) for k in range(0, cols, 128)):
                needed = by_row[part * chunk : (part + 1) * chunk] ^ irrep_ab[:, lanes]
                for irrep in range(IRREPS):
                    table[irrep * parts + part, :, lanes] = jnp.where(needed == irrep, 1.0, 0.0).astype(table.dtype)

        occupied = denominator_ref.shape[0]
        j_of = lax.broadcasted_iota(jnp.int32, (occupied, cols), 0)
        energy_j = jnp.zeros((occupied, cols), jnp.float32)
        for j in range(occupied):
            energy_j = jnp.where(j_of == j, occ_ref[j], energy_j)
        denominator_ref[...] = energy_a + energy_b - occ_ref[me] - energy_j

        row = lax.broadcasted_iota(jnp.int32, (cols, cols), 0)
        col = lax.broadcasted_iota(jnp.int32, (cols, cols), 1)
        first_bits = first_local.bit_length() - 1
        low = first_local - 1
        slabs = slab_virt // first_local
        source = (((col >> first_bits) & low) << bits) + ((col >> (2 * first_bits)) << first_bits) + (col & low)
        by_slab_ref[...] = jnp.where(row == source, 1.0, 0.0).astype(by_slab_ref.dtype)
        source = (((col >> first_bits) & (slabs - 1)) << (2 * first_bits)) + ((col & low) << first_bits) + (col >> bits)
        by_first_ref[...] = jnp.where(row == source, 1.0, 0.0).astype(by_first_ref.dtype)

    chunks = per_step * pl.num_programs(0)
    for k in range(per_step):
        index = me * chunks + step * per_step + k
        irrep_c = irrep_ref[index // parts]
        out_ref[k] = ints_ref[k] * table[irrep_c * parts + index % parts]


def in_hbm(array):
    return pltpu.with_memory_space_constraint(array, pltpu.HBM)


def mask(integrals, me, slab, virt_irrep, occ_energy, slab_energy, after):
    virtuals = virt_irrep.shape[0]
    slab_virt = slab_energy.shape[0]
    occupied = occ_energy.shape[0]
    rows_local, cols_local = integrals.shape
    chunk = math.gcd(virtuals, rows_local)
    parts = virtuals // chunk
    chunks = rows_local // chunk
    per_step = next(n for n in (10, 5, 4, 2, 1) if chunks % n == 0)
    padded = -(-virtuals // 128) * 128
    square = jax.ShapeDtypeStruct((cols_local, cols_local), jnp.bfloat16)
    block = pl.BlockSpec((per_step, chunk, cols_local), lambda step: (step, 0, 0))
    scalars = pl.BlockSpec(memory_space=pltpu.SMEM)
    masked, by_slab, by_first, denominator = pl.pallas_call(
        functools.partial(mask_kernel, per_step, parts),
        grid=(chunks // per_step,),
        in_specs=[scalars] * 5
        + [pl.BlockSpec((1, virtuals), lambda step: (0, 0)), block, pl.BlockSpec(memory_space=pl.ANY)],
        out_specs=[
            block,
            pl.BlockSpec(square.shape, lambda step: (0, 0)),
            pl.BlockSpec(square.shape, lambda step: (0, 0)),
            pl.BlockSpec((occupied, cols_local), lambda step: (0, 0)),
        ],
        scratch_shapes=[
            pltpu.VMEM((IRREPS * parts, chunk, cols_local), integrals.dtype),
            pltpu.VMEM((1, padded), jnp.int32),
            pltpu.VMEM((padded, 128), jnp.int32),
        ],
        out_shape=[
            pltpu.VMEM((chunks, chunk, cols_local), integrals.dtype),
            square,
            square,
            jax.ShapeDtypeStruct((occupied, cols_local), jnp.float32),
        ],
        compiler_params=pltpu.CompilerParams(vmem_limit_bytes=16 * MIB),
        cost_estimate=pl.CostEstimate(
            flops=0, bytes_accessed=0, transcendentals=0
        ),
        name="mask_integrals",
    )(
        me,
        slab,
        *(in_hbm(array) for array in (virt_irrep, occ_energy, slab_energy, virt_irrep.reshape(1, virtuals))),
        in_hbm(integrals.reshape(chunks, chunk, cols_local)),
        after,
    )
    return masked.reshape(rows_local, cols_local), by_slab, by_first, denominator


def take_kernel(*refs):
    parts, out_ref = refs[:-2], refs[-1]
    for k, part in enumerate(parts):
        out_ref[k] = part[1]


def take_other(parts, after):
    count = len(parts)
    _, rows, size = parts[0].shape
    vmem = pl.BlockSpec(memory_space=pltpu.VMEM)
    return pl.pallas_call(
        take_kernel,
        out_shape=jax.ShapeDtypeStruct((count, rows, size), parts[0].dtype),
        in_specs=[vmem] * count + [pl.BlockSpec(memory_space=pl.ANY)],
        out_specs=vmem,
        compiler_params=pltpu.CompilerParams(vmem_limit_bytes=4 * MIB),
        cost_estimate=pl.CostEstimate(flops=0, bytes_accessed=4 * count * rows * size, transcendentals=0),
        name="take_other",
    )(*parts, after)


def join_kernel(*refs):
    parts, other_ref, out_ref = refs[:-2], refs[-2], refs[-1]
    for k, part in enumerate(parts):
        out_ref[k, 0] = part[0]
        out_ref[k, 1] = other_ref[k]


def join(parts, other):
    vmem = pl.BlockSpec(memory_space=pltpu.VMEM)
    return pl.pallas_call(
        join_kernel,
        out_shape=jax.ShapeDtypeStruct((len(parts),) + parts[0].shape, other.dtype),
        in_specs=[vmem] * (len(parts) + 1),
        out_specs=vmem,
        compiler_params=pltpu.CompilerParams(vmem_limit_bytes=4 * MIB),
        cost_estimate=pl.CostEstimate(flops=0, bytes_accessed=8 * other.size, transcendentals=0),
        name="join",
    )(*parts, other)


def tie_kernel(*refs):
    del refs


def tie(parts, after, flops=0):
    count = len(parts)
    anywhere = pl.BlockSpec(memory_space=pl.ANY)
    return pl.pallas_call(
        tie_kernel,
        out_shape=[pltpu.VMEM(part.shape, part.dtype) for part in parts],
        in_specs=[anywhere] * (count + 1),
        out_specs=[anywhere] * count,
        input_output_aliases={k: k for k in range(count)},
        compiler_params=pltpu.CompilerParams(vmem_limit_bytes=2 * MIB),
        cost_estimate=pl.CostEstimate(flops=flops, bytes_accessed=0, transcendentals=0),
        name="tie",
    )(*(pltpu.with_memory_space_constraint(part, pltpu.VMEM) for part in parts), after)


def select_exactly(values, select):
    rows = values.shape[0]
    high = values.astype(jnp.bfloat16)
    rest = values - high.astype(jnp.float32)
    middle = rest.astype(jnp.bfloat16)
    low = (rest - middle.astype(jnp.float32)).astype(jnp.bfloat16)
    terms = [jnp.dot(term, select, preferred_element_type=jnp.float32) for term in (high, middle, low)]
    return terms[0] + terms[1] + terms[2]


def contract_kernel(which, shared, slab_ref, me_ref, home_ref, ints_ref, *refs):
    last = which == "other"
    lhs = refs[-2] if last else refs[-1]
    count, rows, size = lhs.shape
    chips = count // 2 - 1
    start = start_of(which, slab_ref, shared)
    lhs[:2] = home_ref[:, :, pl.ds(start, size)]
    for k in range(chips):
        if which == "rest":
            lhs[2 * k + 2 : 2 * k + 4] = refs[k][...]
        else:
            lhs[2 * k + 2 : 2 * k + 4] = refs[0][k]
    refs = refs[chips if which == "rest" else 1 :]
    step = 2560
    total = None
    for first in range(0, size, step):
        width = min(step, size - first)
        block = lhs[:, :, first : first + width].reshape(count * rows, width)
        part = jnp.dot(block, ints_ref[pl.ds(start + first, width)], preferred_element_type=jnp.float32)
        total = part if total is None else total + part
    if not last:
        before, out_ref = refs[:-2], refs[-2]
        out_ref[...] = total + before[0][...] if before else total
        return
    before_ref, own_ref, other_ref, total_ref, _, partial = refs
    total = total + before_ref[...]
    total_ref[...] = total
    partial[...] = total.reshape(partial.shape)
    for k in range(count // 2):
        own_ref[k] = partial[2 * k]
        other_ref[k] = partial[2 * k + 1]


def mirror_kernel(me_ref, total_ref, select_ref, out_ref, chosen, ordered):
    count = chosen.shape[0]
    chosen[...] = select_exactly(total_ref[...], select_ref[...]).reshape(chosen.shape)
    for i in range(count):
        ordered[i] = chosen[i ^ me_ref[0]]
    slabs = out_ref.shape[0] // count
    half, width = out_ref.shape[1], out_ref.shape[2] // 2
    for p in range(count):
        block = ordered[:, p, :]
        for s in range(slabs):
            part = block[:, s * width : (s + 1) * width]
            out_ref[p * slabs + s, :, :width] = part[:half]
            out_ref[p * slabs + s, :, width:] = part[half:]


def mirror_blocks(total, select, me, slab_count):
    cols = total.shape[1]
    count = math.isqrt(total.shape[0])
    vmem = pl.BlockSpec(memory_space=pltpu.VMEM)
    return pl.pallas_call(
        mirror_kernel,
        out_shape=jax.ShapeDtypeStruct((count * slab_count, count // 2, 2 * cols // slab_count), jnp.float32),
        in_specs=[pl.BlockSpec(memory_space=pltpu.SMEM), vmem, vmem],
        out_specs=vmem,
        scratch_shapes=[pltpu.VMEM((count, count, cols), jnp.float32)] * 2,
        compiler_params=pltpu.CompilerParams(vmem_limit_bytes=4 * MIB + 40 * total.size),
        cost_estimate=pl.CostEstimate(flops=6 * total.size * cols, bytes_accessed=8 * total.size, transcendentals=0),
        name="mirror_blocks",
    )(me, total, select)


def contract(amps, home, ints, me, slab, shared, which, before=None):
    occupied, size = amps[0].shape[-2:]
    cols = ints.shape[1]
    vmem = pl.BlockSpec(memory_space=pltpu.VMEM)
    operands = [*amps] + ([] if before is None else [before])
    scratch = [pltpu.VMEM((occupied, occupied, size), home.dtype)]
    if which == "other":
        out_shape = [jax.ShapeDtypeStruct((occupied // 2, occupied, cols), jnp.float32)] * 2
        out_shape.append(jax.ShapeDtypeStruct((occupied * occupied, cols), jnp.float32))
        scratch.append(pltpu.VMEM((occupied, occupied, cols), jnp.float32))
    else:
        out_shape = [jax.ShapeDtypeStruct((occupied * occupied, cols), jnp.float32)]
    return pl.pallas_call(
        functools.partial(contract_kernel, which, shared),
        out_shape=out_shape,
        in_specs=[pl.BlockSpec(memory_space=pltpu.SMEM)] * 2 + [vmem] * (2 + len(operands)),
        out_specs=[vmem] * len(out_shape),
        scratch_shapes=scratch,
        compiler_params=pltpu.CompilerParams(
            vmem_limit_bytes=4 * MIB + 40 * occupied * occupied * cols + 4 * occupied * occupied * size
        ),
        cost_estimate=pl.CostEstimate(
            flops=2 * occupied * occupied * size * cols,
            bytes_accessed=2 * size * (cols + occupied * occupied),
            transcendentals=0,
        ),
        name="contract",
    )(slab, me, home, pltpu.with_memory_space_constraint(ints, pltpu.VMEM), *operands)


def add_cores_kernel(mine_ref, other_ref, *outs):
    for k, out in enumerate(outs):
        out[...] = mine_ref[k] + other_ref[k]


def add_cores(mine, other):
    count, rows, cols = mine.shape
    vmem = pl.BlockSpec(memory_space=pltpu.VMEM)
    return pl.pallas_call(
        add_cores_kernel,
        out_shape=[jax.ShapeDtypeStruct((rows, cols), jnp.float32)] * count,
        in_specs=[vmem, vmem],
        out_specs=[vmem] * count,
        compiler_params=pltpu.CompilerParams(vmem_limit_bytes=4 * MIB),
        cost_estimate=pl.CostEstimate(flops=mine.size, bytes_accessed=12 * mine.size, transcendentals=0),
        name="add_cores",
    )(mine, other)


def finish_kernel(mirror_ref, denominator_ref, select_ref, *refs):
    parts, out_ref = refs[:-1], refs[-1]
    ladder = parts[0][...]
    for part in parts[1:]:
        ladder = ladder + part[...]
    _, first_local, slab_virt = out_ref.shape
    slab_count = slab_virt // first_local
    width = mirror_ref.shape[2] // 2
    blocks = []
    for s in range(slab_count):
        block = mirror_ref[s]
        for q in range(1, mirror_ref.shape[0] // slab_count):
            block = block + mirror_ref[q * slab_count + s]
        blocks += [jnp.concatenate([block[:, :width], block[:, width:]], axis=0)]
    mirror = select_exactly(jnp.concatenate(blocks, axis=1), select_ref[...])
    update = (ladder + mirror) / denominator_ref[...]
    for a in range(first_local):
        out_ref[:, a, :] = update[:, a * slab_virt : (a + 1) * slab_virt]


def finish(parts, mirror, denominator, select, first_local, slab_virt):
    rows = parts[0].shape[0]
    return pl.pallas_call(
        finish_kernel,
        out_shape=jax.ShapeDtypeStruct((rows, first_local, slab_virt), jnp.float32),
        in_specs=[pl.BlockSpec(memory_space=pltpu.VMEM)] * (3 + len(parts)),
        out_specs=pl.BlockSpec(memory_space=pltpu.VMEM),
        compiler_params=pltpu.CompilerParams(vmem_limit_bytes=6 * MIB),
        cost_estimate=pl.CostEstimate(flops=6 * rows * select.size, bytes_accessed=2 * select.size, transcendentals=0),
        name="finish",
    )(mirror, denominator, select, *parts)


def swap(values, axis, bits):
    return lax.ppermute(values, axis, [(p, p ^ bits) for p in range(lax.axis_size(axis))])


def local(amplitudes, integrals, virt_irrep, occ_energy, slab_energy):
    pair_count = lax.axis_size("pair")
    slab_count = lax.axis_size("slab")
    occ_local, occupied, virt_pairs = amplitudes.shape
    rows_local, cols_local = integrals.shape
    slab_virt = slab_energy.shape[0]
    first_local = slab_virt // slab_count
    assert occ_local == 1
    me = lax.axis_index("pair").astype(jnp.int32).reshape(1)
    slab = lax.axis_index("slab").astype(jnp.int32).reshape(1)

    shared = int(SHARE * rows_local) // 128 * 128
    amps = amplitudes.reshape(occupied, virt_pairs)
    chips = [2 * k for k in range(1, pair_count // 2)]

    def to_chips(parts):
        return [swap(part, "pair", bits) for part, bits in zip(parts, chips)]

    other = swap(amps, "pair", 1)
    parts = pack(amps, me, me, slab, shared, "own", pair_count, me)
    own_amps = to_chips(parts)
    parts = pack(amps, other, me, slab, shared, "rest", pair_count, parts[-1])
    rest_amps = to_chips(parts)
    (home,) = pack(amps, other, me, slab, shared, "all", pair_count, parts[-1])

    own_amps = join(own_amps, swap(take_other(own_amps, home), "pair", 1))
    other_amps = swap(own_amps, "slab", 1)
    masked, by_slab, by_first, denominator = mask(integrals, me, slab, virt_irrep, occ_energy, slab_energy, own_amps)
    rest_amps = tie(rest_amps, denominator, TIE_FLOPS)
    place = (home, masked, me, slab, shared)
    (partial,) = contract([own_amps], *place, "own")
    (partial,) = contract(rest_amps, *place, "rest", partial)
    even, odd, total = contract([other_amps], *place, "other", partial)

    odd = swap(odd, "pair", 1)
    (mirror,) = tie([mirror_blocks(total, by_slab, me, slab_count)], odd)
    mirror = lax.all_to_all(mirror, ("pair", "slab"), split_axis=0, concat_axis=0, tiled=True)
    parts = add_cores(even, odd)
    parts = [parts[0]] + [swap(parts[k], "pair", 2 * k) for k in reversed(range(1, pair_count // 2))]
    update = finish(parts, mirror, denominator, by_first, first_local, slab_virt)
    return update.reshape(occ_local, occupied, first_local, slab_virt)


def solution(mesh):
    placed = (P("pair", None, None), P("pair", "slab"), P(), P(), P())
    return jax.shard_map(
        local, mesh=mesh, in_specs=placed, out_specs=P("pair", None, "slab", None), check_vma=False
    )
```

```python
import functools
import math

import jax
import jax.numpy as jnp
from jax import lax
from jax.experimental import pallas as pl
from jax.experimental.pallas import tpu as pltpu
from jax.sharding import PartitionSpec as P

IRREPS = 8
MIB = 2**20
SHARE = 0.25
TIE_FLOPS = 10**10


def start_of(part, slab_ref, shared):
    parity = slab_ref[0] % 2
    return pl.multiple_of({"own": parity * shared, "other": (1 - parity) * shared, "rest": 2 * shared, "all": 0}[part], 128)


def pack_kernel(rows_local, shared, which, me_ref, slab_ref, amps_ref, other_ref, after_ref, *refs):
    outs, (held, packed, sems) = refs[:-3], refs[-3:]
    size = packed.shape[-1]
    count = sems.shape[0]
    me = me_ref[0]
    start = start_of(which, slab_ref, shared)
    sources = [amps_ref] if which == "own" else [amps_ref, other_ref]
    wanted = {
        "own": lambda dest: (dest ^ me) >= 2,
        "rest": lambda dest: jnp.logical_and(((dest ^ me) & 1) == 0, dest != me),
        "all": lambda dest: dest == me,
    }[which]
    slots = {"own": lambda dest: dest, "rest": lambda dest: dest // 2, "all": lambda dest: 0}[which]

    def load(dest, source):
        first = dest * rows_local // 128 * 128
        width = -(-(dest * rows_local - first + size) // 128) * 128
        return pltpu.make_async_copy(
            sources[source].at[:, pl.ds(start + first, width)],
            held.at[slots(dest), source, :, pl.ds(0, width)],
            sems.at[dest, source],
        )

    for dest in range(count):

        @pl.when(wanted(dest))
        def _():
            for source in range(len(sources)):
                load(dest, source).start()

    for dest in range(count):

        @pl.when(wanted(dest))
        def _():
            shift = dest * rows_local % 128
            for source in range(len(sources)):
                load(dest, source).wait()
                block = held[slots(dest), source, :, shift : shift + size]
                if which == "own":
                    for k, out in enumerate(outs):

                        @pl.when((dest ^ me) // 2 == k + 1)
                        def _():
                            out[(dest ^ me) & 1] = block

                elif which == "rest":
                    packed[(dest ^ me) // 2, source] = block
                else:
                    outs[0][source] = block

    if which == "rest":
        for k, out in enumerate(outs):
            out[...] = packed[k + 1]


def pack(amps, other, me, slab, shared, which, pair_count, after):
    rows, virt_pairs = amps.shape
    rows_local = virt_pairs // pair_count
    size = {"own": shared, "rest": rows_local - 2 * shared, "all": rows_local}[which]
    slots = {"own": pair_count, "rest": pair_count // 2, "all": 1}[which]
    sources = 1 if which == "own" else 2
    held = (slots, sources, rows, -(-size // 128) * 128 + 128)
    packed = {"own": (1, rows, size), "rest": (pair_count // 2, 2, rows, size), "all": (1, rows, size)}[which]
    outs = 1 if which == "all" else pair_count // 2 - 1
    return pl.pallas_call(
        functools.partial(pack_kernel, rows_local, shared, which),
        out_shape=[jax.ShapeDtypeStruct((2, rows, size), amps.dtype)] * outs,
        in_specs=[pl.BlockSpec(memory_space=pltpu.SMEM)] * 2 + [pl.BlockSpec(memory_space=pl.ANY)] * 3,
        out_specs=[pl.BlockSpec(memory_space=pltpu.VMEM)] * outs,
        scratch_shapes=[
            pltpu.VMEM(held, amps.dtype),
            pltpu.VMEM(packed, amps.dtype),
            pltpu.SemaphoreType.DMA((pair_count, sources)),
        ],
        compiler_params=pltpu.CompilerParams(vmem_limit_bytes=2 * MIB + 6 * slots * sources * rows * held[3]),
        cost_estimate=pl.CostEstimate(
            flops=0, bytes_accessed=4 * slots * sources * rows * size, transcendentals=0
        ),
        name="pack_" + which,
    )(me, slab, pltpu.with_memory_space_constraint(amps, pltpu.HBM), other, after)


def mask_kernel(per_step, parts, me_ref, slab_ref, irrep_ref, occ_ref, virt_ref, row_ref, ints_ref, *refs):
    _, out_ref, by_slab_ref, by_first_ref, denominator_ref, table, padded, by_row = refs
    step = pl.program_id(0)
    chunk, cols = ints_ref.shape[1:]
    slab_virt = virt_ref.shape[0]
    first_local = cols // slab_virt
    bits = slab_virt.bit_length() - 1
    me, slab = me_ref[0], slab_ref[0]

    @pl.when(step == 0)
    def _():
        padded[:, : row_ref.shape[1]] = row_ref[...]
        for k in range(padded.shape[1] // 128):
            lanes = slice(k * 128, (k + 1) * 128)
            by_row[lanes] = jnp.transpose(jnp.broadcast_to(padded[:, lanes], (128, 128)))

        col = lax.broadcasted_iota(jnp.int32, (1, cols), 1)
        a_of, b_of = col >> bits, col & (slab_virt - 1)
        irrep_a = irrep_b = jnp.zeros_like(col)
        energy_a = energy_b = jnp.zeros(col.shape, jnp.float32)
        for a in range(first_local):
            irrep_a = jnp.where(a_of == a, irrep_ref[slab * first_local + a], irrep_a)
            energy_a = jnp.where(a_of == a, virt_ref[slab * first_local + a], energy_a)
        for b in range(slab_virt):
            irrep_b = jnp.where(b_of == b, irrep_ref[b], irrep_b)
            energy_b = jnp.where(b_of == b, virt_ref[b], energy_b)
        irrep_ab = irrep_a ^ irrep_b

        for part in range(parts):
            for lanes in (slice(k, k + 128) for k in range(0, cols, 128)):
                needed = by_row[part * chunk : (part + 1) * chunk] ^ irrep_ab[:, lanes]
                for irrep in range(IRREPS):
                    table[irrep * parts + part, :, lanes] = jnp.where(needed == irrep, 1.0, 0.0).astype(table.dtype)

        occupied = denominator_ref.shape[0]
        j_of = lax.broadcasted_iota(jnp.int32, (occupied, cols), 0)
        energy_j = jnp.zeros((occupied, cols), jnp.float32)
        for j in range(occupied):
            energy_j = jnp.where(j_of == j, occ_ref[j], energy_j)
        denominator_ref[...] = energy_a + energy_b - occ_ref[me] - energy_j

        row = lax.broadcasted_iota(jnp.int32, (cols, cols), 0)
        col = lax.broadcasted_iota(jnp.int32, (cols, cols), 1)
        first_bits = first_local.bit_length() - 1
        low = first_local - 1
        slabs = slab_virt // first_local
        source = (((col >> first_bits) & low) << bits) + ((col >> (2 * first_bits)) << first_bits) + (col & low)
        by_slab_ref[...] = jnp.where(row == source, 1.0, 0.0).astype(by_slab_ref.dtype)
        source = (((col >> first_bits) & (slabs - 1)) << (2 * first_bits)) + ((col & low) << first_bits) + (col >> bits)
        by_first_ref[...] = jnp.where(row == source, 1.0, 0.0).astype(by_first_ref.dtype)

    chunks = per_step * pl.num_programs(0)
    for k in range(per_step):
        index = me * chunks + step * per_step + k
        irrep_c = irrep_ref[index // parts]
        out_ref[k] = ints_ref[k] * table[irrep_c * parts + index % parts]


def in_hbm(array):
    return pltpu.with_memory_space_constraint(array, pltpu.HBM)


def mask(integrals, me, slab, virt_irrep, occ_energy, slab_energy, after):
    virtuals = virt_irrep.shape[0]
    slab_virt = slab_energy.shape[0]
    occupied = occ_energy.shape[0]
    rows_local, cols_local = integrals.shape
    chunk = math.gcd(virtuals, rows_local)
    parts = virtuals // chunk
    chunks = rows_local // chunk
    per_step = next(n for n in (10, 5, 4, 2, 1) if chunks % n == 0)
    padded = -(-virtuals // 128) * 128
    square = jax.ShapeDtypeStruct((cols_local, cols_local), jnp.bfloat16)
    block = pl.BlockSpec((per_step, chunk, cols_local), lambda step: (step, 0, 0))
    scalars = pl.BlockSpec(memory_space=pltpu.SMEM)
    masked, by_slab, by_first, denominator = pl.pallas_call(
        functools.partial(mask_kernel, per_step, parts),
        grid=(chunks // per_step,),
        in_specs=[scalars] * 5
        + [pl.BlockSpec((1, virtuals), lambda step: (0, 0)), block, pl.BlockSpec(memory_space=pl.ANY)],
        out_specs=[
            block,
            pl.BlockSpec(square.shape, lambda step: (0, 0)),
            pl.BlockSpec(square.shape, lambda step: (0, 0)),
            pl.BlockSpec((occupied, cols_local), lambda step: (0, 0)),
        ],
        scratch_shapes=[
            pltpu.VMEM((IRREPS * parts, chunk, cols_local), integrals.dtype),
            pltpu.VMEM((1, padded), jnp.int32),
            pltpu.VMEM((padded, 128), jnp.int32),
        ],
        out_shape=[
            pltpu.VMEM((chunks, chunk, cols_local), integrals.dtype),
            square,
            square,
            jax.ShapeDtypeStruct((occupied, cols_local), jnp.float32),
        ],
        compiler_params=pltpu.CompilerParams(vmem_limit_bytes=16 * MIB),
        cost_estimate=pl.CostEstimate(
            flops=0, bytes_accessed=0, transcendentals=0
        ),
        name="mask_integrals",
    )(
        me,
        slab,
        *(in_hbm(array) for array in (virt_irrep, occ_energy, slab_energy, virt_irrep.reshape(1, virtuals))),
        in_hbm(integrals.reshape(chunks, chunk, cols_local)),
        after,
    )
    return masked.reshape(rows_local, cols_local), by_slab, by_first, denominator


def take_kernel(*refs):
    parts, out_ref = refs[:-2], refs[-1]
    for k, part in enumerate(parts):
        out_ref[k] = part[1]


def take_other(parts, after):
    count = len(parts)
    _, rows, size = parts[0].shape
    vmem = pl.BlockSpec(memory_space=pltpu.VMEM)
    return pl.pallas_call(
        take_kernel,
        out_shape=jax.ShapeDtypeStruct((count, rows, size), parts[0].dtype),
        in_specs=[vmem] * count + [pl.BlockSpec(memory_space=pl.ANY)],
        out_specs=vmem,
        compiler_params=pltpu.CompilerParams(vmem_limit_bytes=4 * MIB),
        cost_estimate=pl.CostEstimate(flops=0, bytes_accessed=4 * count * rows * size, transcendentals=0),
        name="take_other",
    )(*parts, after)


def join_kernel(*refs):
    parts, other_ref, out_ref = refs[:-2], refs[-2], refs[-1]
    for k, part in enumerate(parts):
        out_ref[k, 0] = part[0]
        out_ref[k, 1] = other_ref[k]


def join(parts, other):
    vmem = pl.BlockSpec(memory_space=pltpu.VMEM)
    return pl.pallas_call(
        join_kernel,
        out_shape=jax.ShapeDtypeStruct((len(parts),) + parts[0].shape, other.dtype),
        in_specs=[vmem] * (len(parts) + 1),
        out_specs=vmem,
        compiler_params=pltpu.CompilerParams(vmem_limit_bytes=4 * MIB),
        cost_estimate=pl.CostEstimate(flops=0, bytes_accessed=8 * other.size, transcendentals=0),
        name="join",
    )(*parts, other)


def tie_kernel(*refs):
    del refs


def tie(parts, after, flops=0):
    count = len(parts)
    anywhere = pl.BlockSpec(memory_space=pl.ANY)
    return pl.pallas_call(
        tie_kernel,
        out_shape=[pltpu.VMEM(part.shape, part.dtype) for part in parts],
        in_specs=[anywhere] * (count + 1),
        out_specs=[anywhere] * count,
        input_output_aliases={k: k for k in range(count)},
        compiler_params=pltpu.CompilerParams(vmem_limit_bytes=2 * MIB),
        cost_estimate=pl.CostEstimate(flops=flops, bytes_accessed=0, transcendentals=0),
        name="tie",
    )(*(pltpu.with_memory_space_constraint(part, pltpu.VMEM) for part in parts), after)


def select_exactly(values, select):
    rows = values.shape[0]
    high = values.astype(jnp.bfloat16)
    rest = values - high.astype(jnp.float32)
    middle = rest.astype(jnp.bfloat16)
    low = (rest - middle.astype(jnp.float32)).astype(jnp.bfloat16)
    terms = [jnp.dot(term, select, preferred_element_type=jnp.float32) for term in (high, middle, low)]
    return terms[0] + terms[1] + terms[2]


def contract_kernel(which, shared, slab_ref, me_ref, home_ref, ints_ref, *refs):
    last = which == "other"
    lhs = refs[-2] if last else refs[-1]
    count, rows, size = lhs.shape
    chips = count // 2 - 1
    start = start_of(which, slab_ref, shared)
    lhs[:2] = home_ref[:, :, pl.ds(start, size)]
    for k in range(chips):
        if which == "rest":
            lhs[2 * k + 2 : 2 * k + 4] = refs[k][...]
        else:
            lhs[2 * k + 2 : 2 * k + 4] = refs[0][k]
    refs = refs[chips if which == "rest" else 1 :]
    step = 2560
    total = None
    for first in range(0, size, step):
        width = min(step, size - first)
        block = lhs[:, :, first : first + width].reshape(count * rows, width)
        part = jnp.dot(block, ints_ref[pl.ds(start + first, width)], preferred_element_type=jnp.float32)
        total = part if total is None else total + part
    if not last:
        before, out_ref = refs[:-2], refs[-2]
        out_ref[...] = total + before[0][...] if before else total
        return
    before_ref, own_ref, other_ref, total_ref, _, partial = refs
    total = total + before_ref[...]
    total_ref[...] = total
    partial[...] = total.reshape(partial.shape)
    for k in range(count // 2):
        own_ref[k] = partial[2 * k]
        other_ref[k] = partial[2 * k + 1]


def mirror_kernel(me_ref, total_ref, select_ref, out_ref, chosen, ordered):
    count = chosen.shape[0]
    chosen[...] = select_exactly(total_ref[...], select_ref[...]).reshape(chosen.shape)
    for i in range(count):
        ordered[i] = chosen[i ^ me_ref[0]]
    slabs = out_ref.shape[0] // count
    half, width = out_ref.shape[1], out_ref.shape[2] // 2
    for p in range(count):
        block = ordered[:, p, :]
        for s in range(slabs):
            part = block[:, s * width : (s + 1) * width]
            out_ref[p * slabs + s, :, :width] = part[:half]
            out_ref[p * slabs + s, :, width:] = part[half:]


def mirror_blocks(total, select, me, slab_count):
    cols = total.shape[1]
    count = math.isqrt(total.shape[0])
    vmem = pl.BlockSpec(memory_space=pltpu.VMEM)
    return pl.pallas_call(
        mirror_kernel,
        out_shape=jax.ShapeDtypeStruct((count * slab_count, count // 2, 2 * cols // slab_count), jnp.float32),
        in_specs=[pl.BlockSpec(memory_space=pltpu.SMEM), vmem, vmem],
        out_specs=vmem,
        scratch_shapes=[pltpu.VMEM((count, count, cols), jnp.float32)] * 2,
        compiler_params=pltpu.CompilerParams(vmem_limit_bytes=4 * MIB + 40 * total.size),
        cost_estimate=pl.CostEstimate(flops=6 * total.size * cols, bytes_accessed=8 * total.size, transcendentals=0),
        name="mirror_blocks",
    )(me, total, select)


def contract(amps, home, ints, me, slab, shared, which, before=None):
    occupied, size = amps[0].shape[-2:]
    cols = ints.shape[1]
    vmem = pl.BlockSpec(memory_space=pltpu.VMEM)
    operands = [*amps] + ([] if before is None else [before])
    scratch = [pltpu.VMEM((occupied, occupied, size), home.dtype)]
    if which == "other":
        out_shape = [jax.ShapeDtypeStruct((occupied // 2, occupied, cols), jnp.float32)] * 2
        out_shape.append(jax.ShapeDtypeStruct((occupied * occupied, cols), jnp.float32))
        scratch.append(pltpu.VMEM((occupied, occupied, cols), jnp.float32))
    else:
        out_shape = [jax.ShapeDtypeStruct((occupied * occupied, cols), jnp.float32)]
    return pl.pallas_call(
        functools.partial(contract_kernel, which, shared),
        out_shape=out_shape,
        in_specs=[pl.BlockSpec(memory_space=pltpu.SMEM)] * 2 + [vmem] * (2 + len(operands)),
        out_specs=[vmem] * len(out_shape),
        scratch_shapes=scratch,
        compiler_params=pltpu.CompilerParams(
            vmem_limit_bytes=4 * MIB + 40 * occupied * occupied * cols + 4 * occupied * occupied * size
        ),
        cost_estimate=pl.CostEstimate(
            flops=2 * occupied * occupied * size * cols,
            bytes_accessed=2 * size * (cols + occupied * occupied),
            transcendentals=0,
        ),
        name="contract",
    )(slab, me, home, pltpu.with_memory_space_constraint(ints, pltpu.VMEM), *operands)


def add_cores_kernel(mine_ref, other_ref, *outs):
    for k, out in enumerate(outs):
        out[...] = mine_ref[k] + other_ref[k]


def add_cores(mine, other):
    count, rows, cols = mine.shape
    vmem = pl.BlockSpec(memory_space=pltpu.VMEM)
    return pl.pallas_call(
        add_cores_kernel,
        out_shape=[jax.ShapeDtypeStruct((rows, cols), jnp.float32)] * count,
        in_specs=[vmem, vmem],
        out_specs=[vmem] * count,
        compiler_params=pltpu.CompilerParams(vmem_limit_bytes=4 * MIB),
        cost_estimate=pl.CostEstimate(flops=mine.size, bytes_accessed=12 * mine.size, transcendentals=0),
        name="add_cores",
    )(mine, other)


def finish_kernel(mirror_ref, denominator_ref, select_ref, *refs):
    parts, out_ref = refs[:-1], refs[-1]
    ladder = parts[0][...]
    for part in parts[1:]:
        ladder = ladder + part[...]
    _, first_local, slab_virt = out_ref.shape
    slab_count = slab_virt // first_local
    width = mirror_ref.shape[2] // 2
    blocks = []
    for s in range(slab_count):
        block = mirror_ref[s]
        for q in range(1, mirror_ref.shape[0] // slab_count):
            block = block + mirror_ref[q * slab_count + s]
        blocks += [jnp.concatenate([block[:, :width], block[:, width:]], axis=0)]
    mirror = select_exactly(jnp.concatenate(blocks, axis=1), select_ref[...])
    update = (ladder + mirror) / denominator_ref[...]
    for a in range(first_local):
        out_ref[:, a, :] = update[:, a * slab_virt : (a + 1) * slab_virt]


def finish(parts, mirror, denominator, select, first_local, slab_virt):
    rows = parts[0].shape[0]
    return pl.pallas_call(
        finish_kernel,
        out_shape=jax.ShapeDtypeStruct((rows, first_local, slab_virt), jnp.float32),
        in_specs=[pl.BlockSpec(memory_space=pltpu.VMEM)] * (3 + len(parts)),
        out_specs=pl.BlockSpec(memory_space=pltpu.VMEM),
        compiler_params=pltpu.CompilerParams(vmem_limit_bytes=6 * MIB),
        cost_estimate=pl.CostEstimate(flops=6 * rows * select.size, bytes_accessed=2 * select.size, transcendentals=0),
        name="finish",
    )(mirror, denominator, select, *parts)


def swap(values, axis, bits):
    return lax.ppermute(values, axis, [(p, p ^ bits) for p in range(lax.axis_size(axis))])


def local(amplitudes, integrals, virt_irrep, occ_energy, slab_energy):
    pair_count = lax.axis_size("pair")
    slab_count = lax.axis_size("slab")
    occ_local, occupied, virt_pairs = amplitudes.shape
    rows_local, cols_local = integrals.shape
    slab_virt = slab_energy.shape[0]
    first_local = slab_virt // slab_count
    assert occ_local == 1
    me = lax.axis_index("pair").astype(jnp.int32).reshape(1)
    slab = lax.axis_index("slab").astype(jnp.int32).reshape(1)

    shared = int(SHARE * rows_local) // 128 * 128
    amps = amplitudes.reshape(occupied, virt_pairs)
    chips = [2 * k for k in range(1, pair_count // 2)]

    def to_chips(parts):
        return [swap(part, "pair", bits) for part, bits in zip(parts, chips)]

    other = swap(amps, "pair", 1)
    parts = pack(amps, me, me, slab, shared, "own", pair_count, me)
    own_amps = to_chips(parts)
    parts = pack(amps, other, me, slab, shared, "rest", pair_count, parts[-1])
    rest_amps = to_chips(parts)
    (home,) = pack(amps, other, me, slab, shared, "all", pair_count, parts[-1])

    own_amps = join(own_amps, swap(take_other(own_amps, home), "pair", 1))
    other_amps = swap(own_amps, "slab", 1)
    masked, by_slab, by_first, denominator = mask(integrals, me, slab, virt_irrep, occ_energy, slab_energy, own_amps)
    rest_amps = tie(rest_amps, denominator, TIE_FLOPS)
    place = (home, masked, me, slab, shared)
    (partial,) = contract([own_amps], *place, "own")
    (partial,) = contract(rest_amps, *place, "rest", partial)
    even, odd, total = contract([other_amps], *place, "other", partial)

    odd = swap(odd, "pair", 1)
    (mirror,) = tie([mirror_blocks(total, by_slab, me, slab_count)], odd)
    mirror = lax.all_to_all(mirror, ("pair", "slab"), split_axis=0, concat_axis=0, tiled=True)
    parts = add_cores(even, odd)
    parts = [parts[0]] + [swap(parts[k], "pair", 2 * k) for k in reversed(range(1, pair_count // 2))]
    update = finish(parts, mirror, denominator, by_first, first_local, slab_virt)
    return update.reshape(occ_local, occupied, first_local, slab_virt)


def solution(mesh):
    placed = (P("pair", None, None), P("pair", "slab"), P(), P(), P())
    return jax.shard_map(
        local, mesh=mesh, in_specs=placed, out_specs=P("pair", None, "slab", None), check_vma=False
    )
```

```python
import functools
import math

import jax
import jax.numpy as jnp
from jax import lax
from jax.experimental import pallas as pl
from jax.experimental.pallas import tpu as pltpu
from jax.sharding import PartitionSpec as P

IRREPS = 8
MIB = 2**20
SHARE = 0.25
TIE_FLOPS = 10**10


def start_of(part, slab_ref, shared):
    parity = slab_ref[0] % 2
    return pl.multiple_of({"own": parity * shared, "other": (1 - parity) * shared, "rest": 2 * shared, "all": 0}[part], 128)


def pack_kernel(rows_local, shared, which, me_ref, slab_ref, amps_ref, other_ref, after_ref, *refs):
    outs, (held, packed, sems) = refs[:-3], refs[-3:]
    size = packed.shape[-1]
    count = sems.shape[0]
    me = me_ref[0]
    start = start_of(which, slab_ref, shared)
    sources = [amps_ref] if which == "own" else [amps_ref, other_ref]
    wanted = {
        "own": lambda dest: (dest ^ me) >= 2,
        "rest": lambda dest: jnp.logical_and(((dest ^ me) & 1) == 0, dest != me),
        "all": lambda dest: dest == me,
    }[which]
    slots = {"own": lambda dest: dest, "rest": lambda dest: dest // 2, "all": lambda dest: 0}[which]

    def load(dest, source):
        first = dest * rows_local // 128 * 128
        width = -(-(dest * rows_local - first + size) // 128) * 128
        return pltpu.make_async_copy(
            sources[source].at[:, pl.ds(start + first, width)],
            held.at[slots(dest), source, :, pl.ds(0, width)],
            sems.at[dest, source],
        )

    for dest in range(count):

        @pl.when(wanted(dest))
        def _():
            for source in range(len(sources)):
                load(dest, source).start()

    for dest in range(count):

        @pl.when(wanted(dest))
        def _():
            shift = dest * rows_local % 128
            for source in range(len(sources)):
                load(dest, source).wait()
                block = held[slots(dest), source, :, shift : shift + size]
                if which == "own":
                    for k, out in enumerate(outs):

                        @pl.when((dest ^ me) // 2 == k + 1)
                        def _():
                            out[(dest ^ me) & 1] = block

                elif which == "rest":
                    packed[(dest ^ me) // 2, source] = block
                else:
                    outs[0][source] = block

    if which == "rest":
        for k, out in enumerate(outs):
            out[...] = packed[k + 1]


def pack(amps, other, me, slab, shared, which, pair_count, after):
    rows, virt_pairs = amps.shape
    rows_local = virt_pairs // pair_count
    size = {"own": shared, "rest": rows_local - 2 * shared, "all": rows_local}[which]
    slots = {"own": pair_count, "rest": pair_count // 2, "all": 1}[which]
    sources = 1 if which == "own" else 2
    held = (slots, sources, rows, -(-size // 128) * 128 + 128)
    packed = {"own": (1, rows, size), "rest": (pair_count // 2, 2, rows, size), "all": (1, rows, size)}[which]
    outs = 1 if which == "all" else pair_count // 2 - 1
    return pl.pallas_call(
        functools.partial(pack_kernel, rows_local, shared, which),
        out_shape=[jax.ShapeDtypeStruct((2, rows, size), amps.dtype)] * outs,
        in_specs=[pl.BlockSpec(memory_space=pltpu.SMEM)] * 2 + [pl.BlockSpec(memory_space=pl.ANY)] * 3,
        out_specs=[pl.BlockSpec(memory_space=pltpu.VMEM)] * outs,
        scratch_shapes=[
            pltpu.VMEM(held, amps.dtype),
            pltpu.VMEM(packed, amps.dtype),
            pltpu.SemaphoreType.DMA((pair_count, sources)),
        ],
        compiler_params=pltpu.CompilerParams(vmem_limit_bytes=2 * MIB + 6 * slots * sources * rows * held[3]),
        cost_estimate=pl.CostEstimate(
            flops=0, bytes_accessed=4 * slots * sources * rows * size, transcendentals=0
        ),
        name="pack_" + which,
    )(me, slab, pltpu.with_memory_space_constraint(amps, pltpu.HBM), other, after)


def mask_kernel(per_step, parts, me_ref, slab_ref, irrep_ref, occ_ref, virt_ref, row_ref, ints_ref, *refs):
    _, out_ref, by_slab_ref, by_first_ref, denominator_ref, table, padded, by_row = refs
    step = pl.program_id(0)
    chunk, cols = ints_ref.shape[1:]
    slab_virt = virt_ref.shape[0]
    first_local = cols // slab_virt
    bits = slab_virt.bit_length() - 1
    me, slab = me_ref[0], slab_ref[0]

    @pl.when(step == 0)
    def _():
        padded[:, : row_ref.shape[1]] = row_ref[...]
        for k in range(padded.shape[1] // 128):
            lanes = slice(k * 128, (k + 1) * 128)
            by_row[lanes] = jnp.transpose(jnp.broadcast_to(padded[:, lanes], (128, 128)))

        col = lax.broadcasted_iota(jnp.int32, (1, cols), 1)
        a_of, b_of = col >> bits, col & (slab_virt - 1)
        irrep_a = irrep_b = jnp.zeros_like(col)
        energy_a = energy_b = jnp.zeros(col.shape, jnp.float32)
        for a in range(first_local):
            irrep_a = jnp.where(a_of == a, irrep_ref[slab * first_local + a], irrep_a)
            energy_a = jnp.where(a_of == a, virt_ref[slab * first_local + a], energy_a)
        for b in range(slab_virt):
            irrep_b = jnp.where(b_of == b, irrep_ref[b], irrep_b)
            energy_b = jnp.where(b_of == b, virt_ref[b], energy_b)
        irrep_ab = irrep_a ^ irrep_b

        for part in range(parts):
            for lanes in (slice(k, k + 128) for k in range(0, cols, 128)):
                needed = by_row[part * chunk : (part + 1) * chunk] ^ irrep_ab[:, lanes]
                for irrep in range(IRREPS):
                    table[irrep * parts + part, :, lanes] = jnp.where(needed == irrep, 1.0, 0.0).astype(table.dtype)

        occupied = denominator_ref.shape[0]
        j_of = lax.broadcasted_iota(jnp.int32, (occupied, cols), 0)
        energy_j = jnp.zeros((occupied, cols), jnp.float32)
        for j in range(occupied):
            energy_j = jnp.where(j_of == j, occ_ref[j], energy_j)
        denominator_ref[...] = energy_a + energy_b - occ_ref[me] - energy_j

        row = lax.broadcasted_iota(jnp.int32, (cols, cols), 0)
        col = lax.broadcasted_iota(jnp.int32, (cols, cols), 1)
        first_bits = first_local.bit_length() - 1
        low = first_local - 1
        slabs = slab_virt // first_local
        source = (((col >> first_bits) & low) << bits) + ((col >> (2 * first_bits)) << first_bits) + (col & low)
        by_slab_ref[...] = jnp.where(row == source, 1.0, 0.0).astype(by_slab_ref.dtype)
        source = (((col >> first_bits) & (slabs - 1)) << (2 * first_bits)) + ((col & low) << first_bits) + (col >> bits)
        by_first_ref[...] = jnp.where(row == source, 1.0, 0.0).astype(by_first_ref.dtype)

    chunks = per_step * pl.num_programs(0)
    for k in range(per_step):
        index = me * chunks + step * per_step + k
        irrep_c = irrep_ref[index // parts]
        out_ref[k] = ints_ref[k] * table[irrep_c * parts + index % parts]


def in_hbm(array):
    return pltpu.with_memory_space_constraint(array, pltpu.HBM)


def mask(integrals, me, slab, virt_irrep, occ_energy, slab_energy, after):
    virtuals = virt_irrep.shape[0]
    slab_virt = slab_energy.shape[0]
    occupied = occ_energy.shape[0]
    rows_local, cols_local = integrals.shape
    chunk = math.gcd(virtuals, rows_local)
    parts = virtuals // chunk
    chunks = rows_local // chunk
    per_step = next(n for n in (10, 5, 4, 2, 1) if chunks % n == 0)
    padded = -(-virtuals // 128) * 128
    square = jax.ShapeDtypeStruct((cols_local, cols_local), jnp.bfloat16)
    block = pl.BlockSpec((per_step, chunk, cols_local), lambda step: (step, 0, 0))
    scalars = pl.BlockSpec(memory_space=pltpu.SMEM)
    masked, by_slab, by_first, denominator = pl.pallas_call(
        functools.partial(mask_kernel, per_step, parts),
        grid=(chunks // per_step,),
        in_specs=[scalars] * 5
        + [pl.BlockSpec((1, virtuals), lambda step: (0, 0)), block, pl.BlockSpec(memory_space=pl.ANY)],
        out_specs=[
            block,
            pl.BlockSpec(square.shape, lambda step: (0, 0)),
            pl.BlockSpec(square.shape, lambda step: (0, 0)),
            pl.BlockSpec((occupied, cols_local), lambda step: (0, 0)),
        ],
        scratch_shapes=[
            pltpu.VMEM((IRREPS * parts, chunk, cols_local), integrals.dtype),
            pltpu.VMEM((1, padded), jnp.int32),
            pltpu.VMEM((padded, 128), jnp.int32),
        ],
        out_shape=[
            pltpu.VMEM((chunks, chunk, cols_local), integrals.dtype),
            square,
            square,
            jax.ShapeDtypeStruct((occupied, cols_local), jnp.float32),
        ],
        compiler_params=pltpu.CompilerParams(vmem_limit_bytes=16 * MIB),
        cost_estimate=pl.CostEstimate(
            flops=0, bytes_accessed=0, transcendentals=0
        ),
        name="mask_integrals",
    )(
        me,
        slab,
        *(in_hbm(array) for array in (virt_irrep, occ_energy, slab_energy, virt_irrep.reshape(1, virtuals))),
        in_hbm(integrals.reshape(chunks, chunk, cols_local)),
        after,
    )
    return masked.reshape(rows_local, cols_local), by_slab, by_first, denominator


def take_kernel(*refs):
    parts, out_ref = refs[:-2], refs[-1]
    for k, part in enumerate(parts):
        out_ref[k] = part[1]


def take_other(parts, after):
    count = len(parts)
    _, rows, size = parts[0].shape
    vmem = pl.BlockSpec(memory_space=pltpu.VMEM)
    return pl.pallas_call(
        take_kernel,
        out_shape=jax.ShapeDtypeStruct((count, rows, size), parts[0].dtype),
        in_specs=[vmem] * count + [pl.BlockSpec(memory_space=pl.ANY)],
        out_specs=vmem,
        compiler_params=pltpu.CompilerParams(vmem_limit_bytes=4 * MIB),
        cost_estimate=pl.CostEstimate(flops=0, bytes_accessed=4 * count * rows * size, transcendentals=0),
        name="take_other",
    )(*parts, after)


def join_kernel(*refs):
    parts, other_ref, out_ref = refs[:-2], refs[-2], refs[-1]
    for k, part in enumerate(parts):
        out_ref[k, 0] = part[0]
        out_ref[k, 1] = other_ref[k]


def join(parts, other):
    vmem = pl.BlockSpec(memory_space=pltpu.VMEM)
    return pl.pallas_call(
        join_kernel,
        out_shape=jax.ShapeDtypeStruct((len(parts),) + parts[0].shape, other.dtype),
        in_specs=[vmem] * (len(parts) + 1),
        out_specs=vmem,
        compiler_params=pltpu.CompilerParams(vmem_limit_bytes=4 * MIB),
        cost_estimate=pl.CostEstimate(flops=0, bytes_accessed=8 * other.size, transcendentals=0),
        name="join",
    )(*parts, other)


def tie_kernel(*refs):
    del refs


def tie(parts, after, flops=0):
    count = len(parts)
    anywhere = pl.BlockSpec(memory_space=pl.ANY)
    return pl.pallas_call(
        tie_kernel,
        out_shape=[pltpu.VMEM(part.shape, part.dtype) for part in parts],
        in_specs=[anywhere] * (count + 1),
        out_specs=[anywhere] * count,
        input_output_aliases={k: k for k in range(count)},
        compiler_params=pltpu.CompilerParams(vmem_limit_bytes=2 * MIB),
        cost_estimate=pl.CostEstimate(flops=flops, bytes_accessed=0, transcendentals=0),
        name="tie",
    )(*(pltpu.with_memory_space_constraint(part, pltpu.VMEM) for part in parts), after)


def select_exactly(values, select):
    rows = values.shape[0]
    high = values.astype(jnp.bfloat16)
    rest = values - high.astype(jnp.float32)
    middle = rest.astype(jnp.bfloat16)
    low = (rest - middle.astype(jnp.float32)).astype(jnp.bfloat16)
    terms = [jnp.dot(term, select, preferred_element_type=jnp.float32) for term in (high, middle, low)]
    return terms[0] + terms[1] + terms[2]


def contract_kernel(passes, shared, slab_ref, me_ref, home_ref, ints_ref, *refs):
    last = len(passes) > 1
    lhs = refs[-2] if last else refs[-1]
    count, rows, _ = lhs.shape
    chips = count // 2 - 1
    total = None
    for which in passes:
        start = start_of(which, slab_ref, shared)
        size = ints_ref.shape[0] - 2 * shared if which == "rest" else shared
        lhs[:2, :, :size] = home_ref[:, :, pl.ds(start, size)]
        for k in range(chips):
            lhs[2 * k + 2 : 2 * k + 4, :, :size] = refs[k][...] if which == "rest" else refs[0][k]
        refs = refs[chips if which == "rest" else 1 :]
        step = 2560
        for first in range(0, size, step):
            width = min(step, size - first)
            block = lhs[:, :, first : first + width].reshape(count * rows, width)
            part = jnp.dot(block, ints_ref[pl.ds(start + first, width)], preferred_element_type=jnp.float32)
            total = part if total is None else total + part
    if not last:
        before, out_ref = refs[:-2], refs[-2]
        out_ref[...] = total + before[0][...] if before else total
        return
    before_ref, own_ref, other_ref, total_ref, _, partial = refs
    total = total + before_ref[...]
    total_ref[...] = total
    partial[...] = total.reshape(partial.shape)
    for k in range(count // 2):
        own_ref[k] = partial[2 * k]
        other_ref[k] = partial[2 * k + 1]


def mirror_kernel(me_ref, total_ref, select_ref, out_ref, chosen, ordered):
    count = chosen.shape[0]
    chosen[...] = select_exactly(total_ref[...], select_ref[...]).reshape(chosen.shape)
    for i in range(count):
        ordered[i] = chosen[i ^ me_ref[0]]
    slabs = out_ref.shape[0] // count
    half, width = out_ref.shape[1], out_ref.shape[2] // 2
    for p in range(count):
        block = ordered[:, p, :]
        for s in range(slabs):
            part = block[:, s * width : (s + 1) * width]
            out_ref[p * slabs + s, :, :width] = part[:half]
            out_ref[p * slabs + s, :, width:] = part[half:]


def mirror_blocks(total, select, me, slab_count):
    cols = total.shape[1]
    count = math.isqrt(total.shape[0])
    vmem = pl.BlockSpec(memory_space=pltpu.VMEM)
    return pl.pallas_call(
        mirror_kernel,
        out_shape=jax.ShapeDtypeStruct((count * slab_count, count // 2, 2 * cols // slab_count), jnp.float32),
        in_specs=[pl.BlockSpec(memory_space=pltpu.SMEM), vmem, vmem],
        out_specs=vmem,
        scratch_shapes=[pltpu.VMEM((count, count, cols), jnp.float32)] * 2,
        compiler_params=pltpu.CompilerParams(vmem_limit_bytes=4 * MIB + 40 * total.size),
        cost_estimate=pl.CostEstimate(flops=6 * total.size * cols, bytes_accessed=8 * total.size, transcendentals=0),
        name="mirror_blocks",
    )(me, total, select)


def contract(amps, home, ints, me, slab, shared, passes, before=None):
    occupied = home.shape[1]
    size = max(array.shape[-1] for array in amps)
    cols = ints.shape[1]
    vmem = pl.BlockSpec(memory_space=pltpu.VMEM)
    operands = [*amps] + ([] if before is None else [before])
    scratch = [pltpu.VMEM((occupied, occupied, size), home.dtype)]
    if len(passes) > 1:
        out_shape = [jax.ShapeDtypeStruct((occupied // 2, occupied, cols), jnp.float32)] * 2
        out_shape.append(jax.ShapeDtypeStruct((occupied * occupied, cols), jnp.float32))
        scratch.append(pltpu.VMEM((occupied, occupied, cols), jnp.float32))
    else:
        out_shape = [jax.ShapeDtypeStruct((occupied * occupied, cols), jnp.float32)]
    return pl.pallas_call(
        functools.partial(contract_kernel, passes, shared),
        out_shape=out_shape,
        in_specs=[pl.BlockSpec(memory_space=pltpu.SMEM)] * 2 + [vmem] * (2 + len(operands)),
        out_specs=[vmem] * len(out_shape),
        scratch_shapes=scratch,
        compiler_params=pltpu.CompilerParams(
            vmem_limit_bytes=4 * MIB + 40 * occupied * occupied * cols + 4 * occupied * occupied * size
        ),
        cost_estimate=pl.CostEstimate(
            flops=2 * occupied * occupied * size * cols,
            bytes_accessed=2 * size * (cols + occupied * occupied),
            transcendentals=0,
        ),
        name="contract",
    )(slab, me, home, pltpu.with_memory_space_constraint(ints, pltpu.VMEM), *operands)


def add_cores_kernel(mine_ref, other_ref, *outs):
    for k, out in enumerate(outs):
        out[...] = mine_ref[k] + other_ref[k]


def add_cores(mine, other):
    count, rows, cols = mine.shape
    vmem = pl.BlockSpec(memory_space=pltpu.VMEM)
    return pl.pallas_call(
        add_cores_kernel,
        out_shape=[jax.ShapeDtypeStruct((rows, cols), jnp.float32)] * count,
        in_specs=[vmem, vmem],
        out_specs=[vmem] * count,
        compiler_params=pltpu.CompilerParams(vmem_limit_bytes=4 * MIB),
        cost_estimate=pl.CostEstimate(flops=mine.size, bytes_accessed=12 * mine.size, transcendentals=0),
        name="add_cores",
    )(mine, other)


def finish_kernel(mirror_ref, denominator_ref, select_ref, *refs):
    parts, out_ref = refs[:-1], refs[-1]
    ladder = parts[0][...]
    for part in parts[1:]:
        ladder = ladder + part[...]
    _, first_local, slab_virt = out_ref.shape
    slab_count = slab_virt // first_local
    width = mirror_ref.shape[2] // 2
    blocks = []
    for s in range(slab_count):
        block = mirror_ref[s]
        for q in range(1, mirror_ref.shape[0] // slab_count):
            block = block + mirror_ref[q * slab_count + s]
        blocks += [jnp.concatenate([block[:, :width], block[:, width:]], axis=0)]
    mirror = select_exactly(jnp.concatenate(blocks, axis=1), select_ref[...])
    update = (ladder + mirror) / denominator_ref[...]
    for a in range(first_local):
        out_ref[:, a, :] = update[:, a * slab_virt : (a + 1) * slab_virt]


def finish(parts, mirror, denominator, select, first_local, slab_virt):
    rows = parts[0].shape[0]
    return pl.pallas_call(
        finish_kernel,
        out_shape=jax.ShapeDtypeStruct((rows, first_local, slab_virt), jnp.float32),
        in_specs=[pl.BlockSpec(memory_space=pltpu.VMEM)] * (3 + len(parts)),
        out_specs=pl.BlockSpec(memory_space=pltpu.VMEM),
        compiler_params=pltpu.CompilerParams(vmem_limit_bytes=6 * MIB),
        cost_estimate=pl.CostEstimate(flops=6 * rows * select.size, bytes_accessed=2 * select.size, transcendentals=0),
        name="finish",
    )(mirror, denominator, select, *parts)


def swap(values, axis, bits):
    return lax.ppermute(values, axis, [(p, p ^ bits) for p in range(lax.axis_size(axis))])


def local(amplitudes, integrals, virt_irrep, occ_energy, slab_energy):
    pair_count = lax.axis_size("pair")
    slab_count = lax.axis_size("slab")
    occ_local, occupied, virt_pairs = amplitudes.shape
    rows_local, cols_local = integrals.shape
    slab_virt = slab_energy.shape[0]
    first_local = slab_virt // slab_count
    assert occ_local == 1
    me = lax.axis_index("pair").astype(jnp.int32).reshape(1)
    slab = lax.axis_index("slab").astype(jnp.int32).reshape(1)

    shared = int(SHARE * rows_local) // 128 * 128
    amps = amplitudes.reshape(occupied, virt_pairs)
    chips = [2 * k for k in range(1, pair_count // 2)]

    def to_chips(parts):
        return [swap(part, "pair", bits) for part, bits in zip(parts, chips)]

    other = swap(amps, "pair", 1)
    parts = pack(amps, me, me, slab, shared, "own", pair_count, me)
    own_amps = to_chips(parts)
    parts = pack(amps, other, me, slab, shared, "rest", pair_count, parts[-1])
    rest_amps = to_chips(parts)
    (home,) = pack(amps, other, me, slab, shared, "all", pair_count, parts[-1])

    own_amps = join(own_amps, swap(take_other(own_amps, home), "pair", 1))
    other_amps = swap(own_amps, "slab", 1)
    masked, by_slab, by_first, denominator = mask(integrals, me, slab, virt_irrep, occ_energy, slab_energy, own_amps)
    rest_amps = tie(rest_amps, denominator, TIE_FLOPS)
    place = (home, masked, me, slab, shared)
    (partial,) = contract([own_amps], *place, ["own"])
    even, odd, total = contract([*rest_amps, other_amps], *place, ["rest", "other"], partial)

    odd = swap(odd, "pair", 1)
    (mirror,) = tie([mirror_blocks(total, by_slab, me, slab_count)], odd)
    mirror = lax.all_to_all(mirror, ("pair", "slab"), split_axis=0, concat_axis=0, tiled=True)
    parts = add_cores(even, odd)
    parts = [parts[0]] + [swap(parts[k], "pair", 2 * k) for k in reversed(range(1, pair_count // 2))]
    update = finish(parts, mirror, denominator, by_first, first_local, slab_virt)
    return update.reshape(occ_local, occupied, first_local, slab_virt)


def solution(mesh):
    placed = (P("pair", None, None), P("pair", "slab"), P(), P(), P())
    return jax.shard_map(
        local, mesh=mesh, in_specs=placed, out_specs=P("pair", None, "slab", None), check_vma=False
    )
```

```python
import functools
import math

import jax
import jax.numpy as jnp
from jax import lax
from jax.experimental import pallas as pl
from jax.experimental.pallas import tpu as pltpu
from jax.sharding import PartitionSpec as P

IRREPS = 8
MIB = 2**20
SHARE = 0.245
TIE_FLOPS = 10**10


def start_of(part, slab_ref, shared):
    parity = slab_ref[0] % 2
    return pl.multiple_of({"own": parity * shared, "other": (1 - parity) * shared, "rest": 2 * shared, "all": 0}[part], 128)


def pack_kernel(rows_local, shared, which, me_ref, slab_ref, amps_ref, other_ref, after_ref, *refs):
    outs, (held, packed, sems) = refs[:-3], refs[-3:]
    size = packed.shape[-1]
    count = sems.shape[0]
    me = me_ref[0]
    start = start_of(which, slab_ref, shared)
    sources = [amps_ref] if which == "own" else [amps_ref, other_ref]
    wanted = {
        "own": lambda dest: (dest ^ me) >= 2,
        "rest": lambda dest: jnp.logical_and(((dest ^ me) & 1) == 0, dest != me),
        "all": lambda dest: dest == me,
    }[which]
    slots = {"own": lambda dest: dest, "rest": lambda dest: dest // 2, "all": lambda dest: 0}[which]

    def load(dest, source):
        first = dest * rows_local // 128 * 128
        width = -(-(dest * rows_local - first + size) // 128) * 128
        return pltpu.make_async_copy(
            sources[source].at[:, pl.ds(start + first, width)],
            held.at[slots(dest), source, :, pl.ds(0, width)],
            sems.at[dest, source],
        )

    for dest in range(count):

        @pl.when(wanted(dest))
        def _():
            for source in range(len(sources)):
                load(dest, source).start()

    for dest in range(count):

        @pl.when(wanted(dest))
        def _():
            shift = dest * rows_local % 128
            for source in range(len(sources)):
                load(dest, source).wait()
                block = held[slots(dest), source, :, shift : shift + size]
                if which == "own":
                    for k, out in enumerate(outs):

                        @pl.when((dest ^ me) // 2 == k + 1)
                        def _():
                            out[(dest ^ me) & 1] = block

                elif which == "rest":
                    packed[(dest ^ me) // 2, source] = block
                else:
                    outs[0][source] = block

    if which == "rest":
        for k, out in enumerate(outs):
            out[...] = packed[k + 1]


def pack(amps, other, me, slab, shared, which, pair_count, after):
    rows, virt_pairs = amps.shape
    rows_local = virt_pairs // pair_count
    size = {"own": shared, "rest": rows_local - 2 * shared, "all": rows_local}[which]
    slots = {"own": pair_count, "rest": pair_count // 2, "all": 1}[which]
    sources = 1 if which == "own" else 2
    held = (slots, sources, rows, -(-size // 128) * 128 + 128)
    packed = {"own": (1, rows, size), "rest": (pair_count // 2, 2, rows, size), "all": (1, rows, size)}[which]
    outs = 1 if which == "all" else pair_count // 2 - 1
    return pl.pallas_call(
        functools.partial(pack_kernel, rows_local, shared, which),
        out_shape=[jax.ShapeDtypeStruct((2, rows, size), amps.dtype)] * outs,
        in_specs=[pl.BlockSpec(memory_space=pltpu.SMEM)] * 2 + [pl.BlockSpec(memory_space=pl.ANY)] * 3,
        out_specs=[pl.BlockSpec(memory_space=pltpu.VMEM)] * outs,
        scratch_shapes=[
            pltpu.VMEM(held, amps.dtype),
            pltpu.VMEM(packed, amps.dtype),
            pltpu.SemaphoreType.DMA((pair_count, sources)),
        ],
        compiler_params=pltpu.CompilerParams(vmem_limit_bytes=2 * MIB + 6 * slots * sources * rows * held[3]),
        cost_estimate=pl.CostEstimate(
            flops=0, bytes_accessed=4 * slots * sources * rows * size, transcendentals=0
        ),
        name="pack_" + which,
    )(me, slab, pltpu.with_memory_space_constraint(amps, pltpu.HBM), other, after)


def mask_kernel(per_step, parts, me_ref, slab_ref, irrep_ref, occ_ref, virt_ref, row_ref, ints_ref, *refs):
    _, out_ref, by_slab_ref, by_first_ref, denominator_ref, table, padded, by_row = refs
    step = pl.program_id(0)
    chunk, cols = ints_ref.shape[1:]
    slab_virt = virt_ref.shape[0]
    first_local = cols // slab_virt
    bits = slab_virt.bit_length() - 1
    me, slab = me_ref[0], slab_ref[0]

    @pl.when(step == 0)
    def _():
        padded[:, : row_ref.shape[1]] = row_ref[...]
        for k in range(padded.shape[1] // 128):
            lanes = slice(k * 128, (k + 1) * 128)
            by_row[lanes] = jnp.transpose(jnp.broadcast_to(padded[:, lanes], (128, 128)))

        col = lax.broadcasted_iota(jnp.int32, (1, cols), 1)
        a_of, b_of = col >> bits, col & (slab_virt - 1)
        irrep_a = irrep_b = jnp.zeros_like(col)
        energy_a = energy_b = jnp.zeros(col.shape, jnp.float32)
        for a in range(first_local):
            irrep_a = jnp.where(a_of == a, irrep_ref[slab * first_local + a], irrep_a)
            energy_a = jnp.where(a_of == a, virt_ref[slab * first_local + a], energy_a)
        for b in range(slab_virt):
            irrep_b = jnp.where(b_of == b, irrep_ref[b], irrep_b)
            energy_b = jnp.where(b_of == b, virt_ref[b], energy_b)
        irrep_ab = irrep_a ^ irrep_b

        for part in range(parts):
            for lanes in (slice(k, k + 128) for k in range(0, cols, 128)):
                needed = by_row[part * chunk : (part + 1) * chunk] ^ irrep_ab[:, lanes]
                for irrep in range(IRREPS):
                    table[irrep * parts + part, :, lanes] = jnp.where(needed == irrep, 1.0, 0.0).astype(table.dtype)

        occupied = denominator_ref.shape[0]
        j_of = lax.broadcasted_iota(jnp.int32, (occupied, cols), 0)
        energy_j = jnp.zeros((occupied, cols), jnp.float32)
        for j in range(occupied):
            energy_j = jnp.where(j_of == j, occ_ref[j], energy_j)
        denominator_ref[...] = energy_a + energy_b - occ_ref[me] - energy_j

        row = lax.broadcasted_iota(jnp.int32, (cols, cols), 0)
        col = lax.broadcasted_iota(jnp.int32, (cols, cols), 1)
        first_bits = first_local.bit_length() - 1
        low = first_local - 1
        slabs = slab_virt // first_local
        source = (((col >> first_bits) & low) << bits) + ((col >> (2 * first_bits)) << first_bits) + (col & low)
        by_slab_ref[...] = jnp.where(row == source, 1.0, 0.0).astype(by_slab_ref.dtype)
        source = (((col >> first_bits) & (slabs - 1)) << (2 * first_bits)) + ((col & low) << first_bits) + (col >> bits)
        by_first_ref[...] = jnp.where(row == source, 1.0, 0.0).astype(by_first_ref.dtype)

    chunks = per_step * pl.num_programs(0)
    for k in range(per_step):
        index = me * chunks + step * per_step + k
        irrep_c = irrep_ref[index // parts]
        out_ref[k] = ints_ref[k] * table[irrep_c * parts + index % parts]


def in_hbm(array):
    return pltpu.with_memory_space_constraint(array, pltpu.HBM)


def mask(integrals, me, slab, virt_irrep, occ_energy, slab_energy, after):
    virtuals = virt_irrep.shape[0]
    slab_virt = slab_energy.shape[0]
    occupied = occ_energy.shape[0]
    rows_local, cols_local = integrals.shape
    chunk = math.gcd(virtuals, rows_local)
    parts = virtuals // chunk
    chunks = rows_local // chunk
    per_step = next(n for n in (10, 5, 4, 2, 1) if chunks % n == 0)
    padded = -(-virtuals // 128) * 128
    square = jax.ShapeDtypeStruct((cols_local, cols_local), jnp.bfloat16)
    block = pl.BlockSpec((per_step, chunk, cols_local), lambda step: (step, 0, 0))
    scalars = pl.BlockSpec(memory_space=pltpu.SMEM)
    masked, by_slab, by_first, denominator = pl.pallas_call(
        functools.partial(mask_kernel, per_step, parts),
        grid=(chunks // per_step,),
        in_specs=[scalars] * 5
        + [pl.BlockSpec((1, virtuals), lambda step: (0, 0)), block, pl.BlockSpec(memory_space=pl.ANY)],
        out_specs=[
            block,
            pl.BlockSpec(square.shape, lambda step: (0, 0)),
            pl.BlockSpec(square.shape, lambda step: (0, 0)),
            pl.BlockSpec((occupied, cols_local), lambda step: (0, 0)),
        ],
        scratch_shapes=[
            pltpu.VMEM((IRREPS * parts, chunk, cols_local), integrals.dtype),
            pltpu.VMEM((1, padded), jnp.int32),
            pltpu.VMEM((padded, 128), jnp.int32),
        ],
        out_shape=[
            pltpu.VMEM((chunks, chunk, cols_local), integrals.dtype),
            square,
            square,
            jax.ShapeDtypeStruct((occupied, cols_local), jnp.float32),
        ],
        compiler_params=pltpu.CompilerParams(vmem_limit_bytes=16 * MIB),
        cost_estimate=pl.CostEstimate(
            flops=0, bytes_accessed=0, transcendentals=0
        ),
        name="mask_integrals",
    )(
        me,
        slab,
        *(in_hbm(array) for array in (virt_irrep, occ_energy, slab_energy, virt_irrep.reshape(1, virtuals))),
        in_hbm(integrals.reshape(chunks, chunk, cols_local)),
        after,
    )
    return masked.reshape(rows_local, cols_local), by_slab, by_first, denominator


def take_kernel(*refs):
    parts, out_ref = refs[:-2], refs[-1]
    for k, part in enumerate(parts):
        out_ref[k] = part[1]


def take_other(parts, after):
    count = len(parts)
    _, rows, size = parts[0].shape
    vmem = pl.BlockSpec(memory_space=pltpu.VMEM)
    return pl.pallas_call(
        take_kernel,
        out_shape=jax.ShapeDtypeStruct((count, rows, size), parts[0].dtype),
        in_specs=[vmem] * count + [pl.BlockSpec(memory_space=pl.ANY)],
        out_specs=vmem,
        compiler_params=pltpu.CompilerParams(vmem_limit_bytes=4 * MIB),
        cost_estimate=pl.CostEstimate(flops=0, bytes_accessed=4 * count * rows * size, transcendentals=0),
        name="take_other",
    )(*parts, after)


def join_kernel(*refs):
    parts, other_ref, out_ref = refs[:-2], refs[-2], refs[-1]
    for k, part in enumerate(parts):
        out_ref[k, 0] = part[0]
        out_ref[k, 1] = other_ref[k]


def join(parts, other):
    vmem = pl.BlockSpec(memory_space=pltpu.VMEM)
    return pl.pallas_call(
        join_kernel,
        out_shape=jax.ShapeDtypeStruct((len(parts),) + parts[0].shape, other.dtype),
        in_specs=[vmem] * (len(parts) + 1),
        out_specs=vmem,
        compiler_params=pltpu.CompilerParams(vmem_limit_bytes=4 * MIB),
        cost_estimate=pl.CostEstimate(flops=0, bytes_accessed=8 * other.size, transcendentals=0),
        name="join",
    )(*parts, other)


def tie_kernel(*refs):
    del refs


def tie(parts, after, flops=0):
    count = len(parts)
    anywhere = pl.BlockSpec(memory_space=pl.ANY)
    return pl.pallas_call(
        tie_kernel,
        out_shape=[pltpu.VMEM(part.shape, part.dtype) for part in parts],
        in_specs=[anywhere] * (count + 1),
        out_specs=[anywhere] * count,
        input_output_aliases={k: k for k in range(count)},
        compiler_params=pltpu.CompilerParams(vmem_limit_bytes=2 * MIB),
        cost_estimate=pl.CostEstimate(flops=flops, bytes_accessed=0, transcendentals=0),
        name="tie",
    )(*(pltpu.with_memory_space_constraint(part, pltpu.VMEM) for part in parts), after)


def select_exactly(values, select):
    rows = values.shape[0]
    high = values.astype(jnp.bfloat16)
    rest = values - high.astype(jnp.float32)
    middle = rest.astype(jnp.bfloat16)
    low = (rest - middle.astype(jnp.float32)).astype(jnp.bfloat16)
    terms = [jnp.dot(term, select, preferred_element_type=jnp.float32) for term in (high, middle, low)]
    return terms[0] + terms[1] + terms[2]


def contract_kernel(which, shared, slab_ref, me_ref, home_ref, ints_ref, *refs):
    last = which == "other"
    lhs = refs[-2] if last else refs[-1]
    count, rows, size = lhs.shape
    chips = count // 2 - 1
    start = start_of(which, slab_ref, shared)
    lhs[:2] = home_ref[:, :, pl.ds(start, size)]
    for k in range(chips):
        if which == "rest":
            lhs[2 * k + 2 : 2 * k + 4] = refs[k][...]
        else:
            lhs[2 * k + 2 : 2 * k + 4] = refs[0][k]
    refs = refs[chips if which == "rest" else 1 :]
    step = 2560
    total = None
    for first in range(0, size, step):
        width = min(step, size - first)
        block = lhs[:, :, first : first + width].reshape(count * rows, width)
        part = jnp.dot(block, ints_ref[pl.ds(start + first, width)], preferred_element_type=jnp.float32)
        total = part if total is None else total + part
    if not last:
        before, out_ref = refs[:-2], refs[-2]
        out_ref[...] = total + before[0][...] if before else total
        return
    before_ref, own_ref, other_ref, total_ref, _, partial = refs
    total = total + before_ref[...]
    total_ref[...] = total
    partial[...] = total.reshape(partial.shape)
    for k in range(count // 2):
        own_ref[k] = partial[2 * k]
        other_ref[k] = partial[2 * k + 1]


def mirror_kernel(me_ref, total_ref, select_ref, out_ref, chosen, ordered):
    count = chosen.shape[0]
    chosen[...] = select_exactly(total_ref[...], select_ref[...]).reshape(chosen.shape)
    for i in range(count):
        ordered[i] = chosen[i ^ me_ref[0]]
    slabs = out_ref.shape[0] // count
    half, width = out_ref.shape[1], out_ref.shape[2] // 2
    for p in range(count):
        block = ordered[:, p, :]
        for s in range(slabs):
            part = block[:, s * width : (s + 1) * width]
            out_ref[p * slabs + s, :, :width] = part[:half]
            out_ref[p * slabs + s, :, width:] = part[half:]


def mirror_blocks(total, select, me, slab_count):
    cols = total.shape[1]
    count = math.isqrt(total.shape[0])
    vmem = pl.BlockSpec(memory_space=pltpu.VMEM)
    return pl.pallas_call(
        mirror_kernel,
        out_shape=jax.ShapeDtypeStruct((count * slab_count, count // 2, 2 * cols // slab_count), jnp.float32),
        in_specs=[pl.BlockSpec(memory_space=pltpu.SMEM), vmem, vmem],
        out_specs=vmem,
        scratch_shapes=[pltpu.VMEM((count, count, cols), jnp.float32)] * 2,
        compiler_params=pltpu.CompilerParams(vmem_limit_bytes=4 * MIB + 40 * total.size),
        cost_estimate=pl.CostEstimate(flops=6 * total.size * cols, bytes_accessed=8 * total.size, transcendentals=0),
        name="mirror_blocks",
    )(me, total, select)


def contract(amps, home, ints, me, slab, shared, which, before=None):
    occupied, size = amps[0].shape[-2:]
    cols = ints.shape[1]
    vmem = pl.BlockSpec(memory_space=pltpu.VMEM)
    operands = [*amps] + ([] if before is None else [before])
    scratch = [pltpu.VMEM((occupied, occupied, size), home.dtype)]
    if which == "other":
        out_shape = [jax.ShapeDtypeStruct((occupied // 2, occupied, cols), jnp.float32)] * 2
        out_shape.append(jax.ShapeDtypeStruct((occupied * occupied, cols), jnp.float32))
        scratch.append(pltpu.VMEM((occupied, occupied, cols), jnp.float32))
    else:
        out_shape = [jax.ShapeDtypeStruct((occupied * occupied, cols), jnp.float32)]
    return pl.pallas_call(
        functools.partial(contract_kernel, which, shared),
        out_shape=out_shape,
        in_specs=[pl.BlockSpec(memory_space=pltpu.SMEM)] * 2 + [vmem] * (2 + len(operands)),
        out_specs=[vmem] * len(out_shape),
        scratch_shapes=scratch,
        compiler_params=pltpu.CompilerParams(
            vmem_limit_bytes=4 * MIB + 40 * occupied * occupied * cols + 4 * occupied * occupied * size
        ),
        cost_estimate=pl.CostEstimate(
            flops=2 * occupied * occupied * size * cols,
            bytes_accessed=2 * size * (cols + occupied * occupied),
            transcendentals=0,
        ),
        name="contract",
    )(slab, me, home, pltpu.with_memory_space_constraint(ints, pltpu.VMEM), *operands)


def add_cores_kernel(mine_ref, other_ref, *outs):
    for k, out in enumerate(outs):
        out[...] = mine_ref[k] + other_ref[k]


def add_cores(mine, other):
    count, rows, cols = mine.shape
    vmem = pl.BlockSpec(memory_space=pltpu.VMEM)
    return pl.pallas_call(
        add_cores_kernel,
        out_shape=[jax.ShapeDtypeStruct((rows, cols), jnp.float32)] * count,
        in_specs=[vmem, vmem],
        out_specs=[vmem] * count,
        compiler_params=pltpu.CompilerParams(vmem_limit_bytes=4 * MIB),
        cost_estimate=pl.CostEstimate(flops=mine.size, bytes_accessed=12 * mine.size, transcendentals=0),
        name="add_cores",
    )(mine, other)


def finish_kernel(mirror_ref, denominator_ref, select_ref, *refs):
    parts, out_ref = refs[:-1], refs[-1]
    ladder = parts[0][...]
    for part in parts[1:]:
        ladder = ladder + part[...]
    _, first_local, slab_virt = out_ref.shape
    slab_count = slab_virt // first_local
    width = mirror_ref.shape[2] // 2
    blocks = []
    for s in range(slab_count):
        block = mirror_ref[s]
        for q in range(1, mirror_ref.shape[0] // slab_count):
            block = block + mirror_ref[q * slab_count + s]
        blocks += [jnp.concatenate([block[:, :width], block[:, width:]], axis=0)]
    mirror = select_exactly(jnp.concatenate(blocks, axis=1), select_ref[...])
    update = (ladder + mirror) / denominator_ref[...]
    for a in range(first_local):
        out_ref[:, a, :] = update[:, a * slab_virt : (a + 1) * slab_virt]


def finish(parts, mirror, denominator, select, first_local, slab_virt):
    rows = parts[0].shape[0]
    return pl.pallas_call(
        finish_kernel,
        out_shape=jax.ShapeDtypeStruct((rows, first_local, slab_virt), jnp.float32),
        in_specs=[pl.BlockSpec(memory_space=pltpu.VMEM)] * (3 + len(parts)),
        out_specs=pl.BlockSpec(memory_space=pltpu.VMEM),
        compiler_params=pltpu.CompilerParams(vmem_limit_bytes=6 * MIB),
        cost_estimate=pl.CostEstimate(flops=6 * rows * select.size, bytes_accessed=2 * select.size, transcendentals=0),
        name="finish",
    )(mirror, denominator, select, *parts)


def swap(values, axis, bits):
    return lax.ppermute(values, axis, [(p, p ^ bits) for p in range(lax.axis_size(axis))])


def local(amplitudes, integrals, virt_irrep, occ_energy, slab_energy):
    pair_count = lax.axis_size("pair")
    slab_count = lax.axis_size("slab")
    occ_local, occupied, virt_pairs = amplitudes.shape
    rows_local, cols_local = integrals.shape
    slab_virt = slab_energy.shape[0]
    first_local = slab_virt // slab_count
    assert occ_local == 1
    me = lax.axis_index("pair").astype(jnp.int32).reshape(1)
    slab = lax.axis_index("slab").astype(jnp.int32).reshape(1)

    shared = int(SHARE * rows_local) // 128 * 128
    amps = amplitudes.reshape(occupied, virt_pairs)
    chips = [2 * k for k in range(1, pair_count // 2)]

    def to_chips(parts):
        return [swap(part, "pair", bits) for part, bits in zip(parts, chips)]

    other = swap(amps, "pair", 1)
    parts = pack(amps, me, me, slab, shared, "own", pair_count, me)
    own_amps = to_chips(parts)
    parts = pack(amps, other, me, slab, shared, "rest", pair_count, parts[-1])
    rest_amps = to_chips(parts)
    (home,) = pack(amps, other, me, slab, shared, "all", pair_count, parts[-1])

    own_amps = join(own_amps, swap(take_other(own_amps, home), "pair", 1))
    other_amps = swap(own_amps, "slab", 1)
    masked, by_slab, by_first, denominator = mask(integrals, me, slab, virt_irrep, occ_energy, slab_energy, own_amps)
    rest_amps = tie(rest_amps, denominator, TIE_FLOPS)
    place = (home, masked, me, slab, shared)
    (partial,) = contract([own_amps], *place, "own")
    (partial,) = contract(rest_amps, *place, "rest", partial)
    even, odd, total = contract([other_amps], *place, "other", partial)

    odd = swap(odd, "pair", 1)
    (mirror,) = tie([mirror_blocks(total, by_slab, me, slab_count)], odd)
    mirror = lax.all_to_all(mirror, ("pair", "slab"), split_axis=0, concat_axis=0, tiled=True)
    parts = add_cores(even, odd)
    parts = [parts[0]] + [swap(parts[k], "pair", 2 * k) for k in reversed(range(1, pair_count // 2))]
    update = finish(parts, mirror, denominator, by_first, first_local, slab_virt)
    return update.reshape(occ_local, occupied, first_local, slab_virt)


def solution(mesh):
    placed = (P("pair", None, None), P("pair", "slab"), P(), P(), P())
    return jax.shard_map(
        local, mesh=mesh, in_specs=placed, out_specs=P("pair", None, "slab", None), check_vma=False
    )
```
